32 devices in a mesh: frame: 16 (over z, y, core), rep: 2 (over x).
Axes of the slice: x: 2, y: 2, z: 4, core: 2. Of those that a mesh axis runs over, the one named last changes fastest.
Arguments:
- clean: float32 [2, 16, 16, 256], P('rep', 'frame'), may hold values from -6 to 6
- noise: float32 [2, 16, 16, 256], P('rep', 'frame'), may hold values from -6 to 6
- levels: int32 [2, 16], P('rep', 'frame'), may hold values from 1 to 31
- flags: int32 [2, 16], P('rep', 'frame'), may hold values 0 or 1
- frame_map: int32 [2, 16], replicated, may hold values from 0 to 15, each once within a row
- block_slot: int32 [768], replicated, may hold values from 0 to 767, each once
- step_count: int32 [1], replicated, may hold values from 2 to 20
- mat_weight: float32 [768, 128, 128], P(('frame', 'rep')), may hold values from -0.1875 to 0.1875
- mat_ema: float32 [768, 128, 128], P(('frame', 'rep')), may hold values from -0.1875 to 0.1875
- stat_left: float32 [768, 128, 128], P(('frame', 'rep')), as said below
- stat_right: float32 [768, 128, 128], P(('frame', 'rep')), as said below
- root_left: float32 [768, 128, 128], P(('frame', 'rep')), as said below
- root_right: float32 [768, 128, 128], P(('frame', 'rep')), as said below
- mod_table: float32 [32, 8192], replicated, may hold values from -3 to 3
- mod_mom: float32 [32, 8192], replicated, may hold values from -2.670288e-05 to 2.670288e-05
- mod_var: float32 [32, 8192], replicated, may hold values from 1.6895545e-13 to 1.3516436e-12
- mod_ema: float32 [32, 8192], replicated, may hold values from -3 to 3
- io_weight: float32 [33, 1024], replicated, may hold values from -0.75 to 0.75
- io_mom: float32 [33, 1024], replicated, may hold values from -0.00030517578 to 0.00030517578
- io_var: float32 [33, 1024], replicated, may hold values from 1.6895546e-11 to 2.7032873e-10
- io_ema: float32 [33, 1024], replicated, may hold values from -0.75 to 0.75
Outputs:
- loss_sum: float32 [], replicated
- noised_count: float32 [], replicated
- grad_norm: float32 [], replicated
- mat_grad: float32 [768, 128, 128], P(('frame', 'rep'))
- new_mat_weight: float32 [768, 128, 128], P(('frame', 'rep'))
- new_stat_left: float32 [768, 128, 128], P(('frame', 'rep'))
- new_stat_right: float32 [768, 128, 128], P(('frame', 'rep'))
- new_mat_ema: float32 [768, 128, 128], P(('frame', 'rep'))
- new_mod_table: float32 [32, 8192], replicated
- new_mod_mom: float32 [32, 8192], replicated
- new_mod_var: float32 [32, 8192], replicated
- new_mod_ema: float32 [32, 8192], replicated
- new_io_weight: float32 [33, 1024], replicated
- new_io_mom: float32 [33, 1024], replicated
- new_io_var: float32 [33, 1024], replicated
- new_io_ema: float32 [33, 1024], replicated
The draws below stay inside these ranges and needn't reach their ends.
Inputs may be any that keep to these rules, and one draw needn't show every extreme that they name: `stat_left`: symmetric blocks with positive diagonal, each strictly diagonally dominant. `stat_right`: symmetric blocks with positive diagonal, each strictly diagonally dominant. `root_left`: symmetric blocks with positive diagonal, each strictly diagonally dominant. `root_right`: symmetric blocks with positive diagonal, each strictly diagonally dominant.
All inputs are finite; a program needn't handle non-finite values. No bound on the sum of `flags` on one device may be relied on, other than what follows from the above.
Results may differ from the reference program's by a relative error of at most 0.01.
Values may be sent and summed in bfloat16 or wider, within the bound.
A program may use at most 640 MiB of HBM per device.

```python
import math
import jax
import jax.numpy as jnp
from jax import lax

D = 1024
HEADS = 16
HEAD_DIM = 64
FFN = 4096
PIN = 16
GRID = 16
BLOCK = 128
LEVELS = 32
FRAMES = 16
CLIPS = 2
NBLOCKS = 768
NPARAMS = 12878848
NSMALL = 295936


def dominant_blocks(key, center, low_factor, high_factor):
    diag_key, other_key = jax.random.split(key)
    diagonal = center * jax.random.uniform(diag_key, (NBLOCKS, BLOCK), jnp.float32, low_factor, high_factor)
    off_diagonal = jax.random.uniform(other_key, (NBLOCKS, BLOCK, BLOCK), jnp.float32, -1.0, 1.0)
    off_diagonal = 0.5 * (off_diagonal + jnp.swapaxes(off_diagonal, 1, 2)) * (0.9 * low_factor * center / BLOCK)
    identity = jnp.eye(BLOCK, dtype=jnp.float32)
    return off_diagonal * (1.0 - identity) + diagonal[:, :, None] * identity


def statistic_scale():
    return (1.0 - 0.95) / 0.95 * BLOCK * 0.0001 / NPARAMS


def draw_stat_left(key, part):
    return dominant_blocks(jax.random.fold_in(key, 11), statistic_scale(), 1.0, 4.0)


def draw_stat_right(key, part):
    return dominant_blocks(jax.random.fold_in(key, 12), statistic_scale(), 1.0, 4.0)


def draw_root_left(key, part):
    return dominant_blocks(jax.random.fold_in(key, 13), statistic_scale() ** (-0.25), 0.7, 1.4)


def draw_root_right(key, part):
    return dominant_blocks(jax.random.fold_in(key, 14), statistic_scale() ** (-0.25), 0.7, 1.4)


def with_ends(array, stream_key, smallest, top_value):
    spot = [jax.random.randint(jax.random.fold_in(stream_key, axis), (), 0, length) for axis, length in enumerate(array.shape)]
    longest = array.shape.index(max(array.shape))
    beside = spot[:longest] + [(spot[longest] + 1) % array.shape[longest]] + spot[longest + 1:]
    return array.at[tuple(spot)].set(smallest).at[tuple(beside)].set(top_value)


def shard_levels(rng, dims, shards, smallest, top_value):
    level = 1.0
    for position, blocks in shards:
        draws = jax.random.uniform(jax.random.fold_in(jax.random.fold_in(rng, 6), position), (blocks,), jnp.float32, smallest / len(shards), top_value / len(shards))
        level = level * jnp.repeat(jnp.exp(draws), dims[position] // blocks).reshape((-1,) + (1,) * (len(dims) - 1 - position))
    return level


def bell_draw(own_key, dims, spread, limit, cuts=(), held_as=jnp.bfloat16):
    loudness = shard_levels(own_key, dims, cuts, -0.22, 0.18) if cuts else 1.0
    array = jax.random.normal(own_key, dims, jnp.float32) * spread * loudness
    return jnp.minimum(jnp.maximum(array, -limit), limit).astype(held_as)


def setup_inputs(seed: int = 0) -> dict:
    arg_keys = jax.random.split(jax.random.key(seed), 22)
    return {
        "clean": bell_draw(arg_keys[0], (CLIPS, FRAMES, PIN, GRID * GRID), 1.0, 6.0, ((0, 2), (1, 16)), jnp.float32),
        "noise": bell_draw(arg_keys[1], (CLIPS, FRAMES, PIN, GRID * GRID), 1.0, 6.0, ((0, 2), (1, 16)), jnp.float32),
        "levels": with_ends(jax.random.randint(arg_keys[2], (CLIPS, FRAMES), 1, LEVELS), jax.random.fold_in(arg_keys[2], 1), 1, LEVELS - 1).astype(jnp.int32),
        "flags": with_ends((jax.random.randint(arg_keys[3], (CLIPS, FRAMES), 0, 4) < 1).astype(jnp.int32), jax.random.fold_in(arg_keys[3], 1), 0, 1),
        "frame_map": jax.vmap(lambda own: jax.random.permutation(own, FRAMES))(jax.random.split(arg_keys[4], CLIPS)).reshape((CLIPS, FRAMES)).astype(jnp.int32),
        "block_slot": jax.random.permutation(arg_keys[5], NBLOCKS).astype(jnp.int32),
        "step_count": jax.random.randint(arg_keys[6], (1,), 2, 21).astype(jnp.int32),
        "mat_weight": bell_draw(arg_keys[7], (NBLOCKS, BLOCK, BLOCK), D ** -0.5, 0.1875, ((0, 32),), jnp.float32),
        "mat_ema": bell_draw(arg_keys[8], (NBLOCKS, BLOCK, BLOCK), D ** -0.5, 0.1875, ((0, 32),), jnp.float32),
        "stat_left": draw_stat_left(jax.random.fold_in(arg_keys[21], 71), 0),
        "stat_right": draw_stat_right(jax.random.fold_in(arg_keys[21], 71), 0),
        "root_left": draw_root_left(jax.random.fold_in(arg_keys[21], 71), 0),
        "root_right": draw_root_right(jax.random.fold_in(arg_keys[21], 71), 0),
        "mod_table": bell_draw(arg_keys[13], (LEVELS, 8 * D), 0.5, 3.0, (), jnp.float32),
        "mod_mom": bell_draw(arg_keys[14], (LEVELS, 8 * D), (0.001 * NSMALL ** -0.5), 2.6702880859375e-05, (), jnp.float32),
        "mod_var": jnp.clip(jnp.exp(jax.random.uniform(arg_keys[15], (LEVELS, 8 * D), jnp.float32, math.log(1.6895545292688885e-13), math.log(1.3516436234151108e-12))), 1.6895545292688885e-13, 1.3516436234151108e-12),
        "mod_ema": bell_draw(arg_keys[16], (LEVELS, 8 * D), 0.5, 3.0, (), jnp.float32),
        "io_weight": bell_draw(arg_keys[17], (2 * PIN + 1, D), 64 ** -0.5, 0.75, (), jnp.float32),
        "io_mom": bell_draw(arg_keys[18], (2 * PIN + 1, D), (0.0111 * NSMALL ** -0.5), 0.00030517578, (), jnp.float32),
        "io_var": jnp.clip(jnp.exp(jax.random.uniform(arg_keys[19], (2 * PIN + 1, D), jnp.float32, math.log(1.6895545726369754e-11), math.log(2.7032873162191606e-10))), 1.6895545726369754e-11, 2.7032873162191606e-10),
        "io_ema": bell_draw(arg_keys[20], (2 * PIN + 1, D), 64 ** -0.5, 0.75, (), jnp.float32),
    }


LN_EPS = 1e-06
ROPE_BASE = 10000.0
CLIP_NORM = 0.01
BETA_ONE = 0.9
BETA_TWO = 0.999
ADAM_EPS = 1e-08
ADAM_RATE = 0.1
DECAY_RATE = 0.1
STAT_BETA = 0.95
SHAMPOO_RATE = 0.01
EMA_DECAY = 0.9
TOP_PRECISION = lax.Precision.HIGHEST

@jax.custom_vjp
def low(v):
    return lax.optimization_barrier(v.astype(jnp.bfloat16)).astype(jnp.float32)

@jax.custom_vjp
def low_back(v):
    return v

def low_keep(v):
    return (low(v), None)

def low_pass(kept, grad):
    return (grad,)

def back_keep(v):
    return (v, None)

def back_low(kept, grad):
    return (low(grad),)
low.defvjp(low_keep, low_pass)
low_back.defvjp(back_keep, back_low)

def matmul(left, right):
    return jnp.dot(left, right, precision=TOP_PRECISION, preferred_element_type=jnp.float32)

def layer_norm(hidden):
    centered = hidden - lax.optimization_barrier(jnp.mean(hidden, axis=-1, keepdims=True))
    return centered * lax.rsqrt(lax.optimization_barrier(jnp.mean(centered * centered, axis=-1, keepdims=True)) + LN_EPS)

def frequencies(width):
    return ROPE_BASE ** (-jnp.arange(width, dtype=jnp.float32) / width)

def rope_tables(frame_ids):
    pairs = HEAD_DIM // 2
    time_pairs = pairs // 4
    row_pairs = (pairs - time_pairs) // 2
    column_pairs = pairs - time_pairs - row_pairs
    frames = frame_ids.shape[0]
    tok_frame = GRID * GRID
    token_pos = jnp.arange(tok_frame, dtype=jnp.int32)
    row_pos = (token_pos // GRID).astype(jnp.float32)
    column_pos = (token_pos % GRID).astype(jnp.float32)
    time_angle = frame_ids.astype(jnp.float32)[:, None, None] * frequencies(time_pairs)[None, None, :]
    row_angle = row_pos[None, :, None] * frequencies(row_pairs)[None, None, :]
    column_angle = column_pos[None, :, None] * frequencies(column_pairs)[None, None, :]
    angles = jnp.concatenate([jnp.broadcast_to(time_angle, (frames, tok_frame, time_pairs)), jnp.broadcast_to(row_angle, (frames, tok_frame, row_pairs)), jnp.broadcast_to(column_angle, (frames, tok_frame, column_pairs))], axis=-1)
    angles = angles.reshape(frames * tok_frame, pairs)
    return (jnp.cos(angles), jnp.sin(angles))

def rotate(values, cosine, sine):
    pairs = HEAD_DIM // 2
    first, second = (values[..., :pairs], values[..., pairs:])
    cosine = cosine[:, None, :]
    sine = sine[:, None, :]
    return jnp.concatenate([first * cosine - second * sine, first * sine + second * cosine], axis=-1)

def attend(queries, keys, values, frame_of_row):
    total_rows = queries.shape[0]
    block_rows = math.gcd(total_rows, 512)

    def one_block(block_in):
        query_block, query_frames = block_in
        scores = jnp.einsum('qhd,khd->hqk', query_block, keys, precision=TOP_PRECISION) * HEAD_DIM ** (-0.5)
        scores = low_back(scores)
        visible = frame_of_row[None, None, :] <= query_frames[None, :, None]
        scores = jnp.where(visible, scores, -jnp.inf)
        log_total = jax.nn.logsumexp(scores, axis=-1, keepdims=True)
        probs = low(jnp.exp(scores - log_total))
        return jnp.einsum('hqk,khd->qhd', probs, values, precision=TOP_PRECISION)
    stacked = (queries.reshape(total_rows // block_rows, block_rows, HEADS, HEAD_DIM), frame_of_row.reshape(total_rows // block_rows, block_rows))
    result = lax.map(jax.checkpoint(one_block), stacked)
    return result.reshape(total_rows, HEADS * HEAD_DIM)

def clip_loss(weights, clean, noise, levels, flags, frame_ids):
    attn_w, out_w, up_w, down_w, table, io_rows = weights
    frames = clean.shape[0]
    tok_frame = GRID * GRID
    noised = 1 - flags
    level_now = levels * noised
    fraction = level_now.astype(jnp.float32) / LEVELS
    keep_coef = jnp.cos(0.5 * jnp.pi * fraction)
    noise_coef = jnp.sin(0.5 * jnp.pi * fraction)
    frames_in = keep_coef[:, None, None] * clean + noise_coef[:, None, None] * noise
    inputs = jnp.swapaxes(frames_in, 1, 2).reshape(-1, PIN)
    targets = jnp.swapaxes(noise, 1, 2).reshape(-1, PIN)
    modulation = table[level_now].reshape(frames, 8, 1, D)
    embed = low(io_rows[:PIN])
    head = low(io_rows[PIN:2 * PIN])
    bias = io_rows[2 * PIN]

    def per_frame(flat):
        return flat.reshape(frames, tok_frame, -1)

    def per_row(blocked):
        return blocked.reshape(frames * tok_frame, -1)

    def split_heads(flat):
        return flat.reshape(-1, HEADS, HEAD_DIM)
    start = per_frame(low_back(matmul(low(inputs), embed) + bias))
    normed = per_row(low(layer_norm(start) * (1 + modulation[:, 1]) + modulation[:, 0]))
    projected = low_back(matmul(normed, low(attn_w)))
    cosine, sine = rope_tables(frame_ids)
    queries = low(rotate(split_heads(projected[:, :D]), cosine, sine))
    keys = low(rotate(split_heads(projected[:, D:2 * D]), cosine, sine))
    values = low(split_heads(projected[:, 2 * D:]))
    attended = low(low_back(attend(queries, keys, values, jnp.repeat(frame_ids, tok_frame))))
    branch = per_frame(low_back(matmul(attended, low(out_w))))
    middle = start + modulation[:, 2] * branch
    normed_two = per_row(low(layer_norm(middle) * (1 + modulation[:, 4]) + modulation[:, 3]))
    upper = low_back(matmul(normed_two, low(up_w)))
    activated = low(jax.nn.gelu(upper, approximate=True))
    lower = per_frame(low_back(matmul(activated, low(down_w))))
    final = middle + modulation[:, 5] * lower
    normed_three = per_row(low(layer_norm(final) * (1 + modulation[:, 7]) + modulation[:, 6]))
    predicted = low_back(matmul(normed_three, head.T))
    row_weight = jnp.repeat(noised, tok_frame).astype(jnp.float32)
    return jnp.sum(row_weight[:, None] * (predicted - targets) ** 2)

def matrix_shapes():
    return ((D, 3 * D), (D, D), (D, FFN), (FFN, D))

def from_blocks(natural):
    matrices = []
    offset = 0
    for rows_in, cols_in in matrix_shapes():
        count_in = rows_in // BLOCK * (cols_in // BLOCK)
        part_blocks = natural[offset:offset + count_in]
        matrices.append(part_blocks.reshape(rows_in // BLOCK, cols_in // BLOCK, BLOCK, BLOCK).transpose(0, 2, 1, 3).reshape(rows_in, cols_in))
        offset = offset + count_in
    return matrices

def to_blocks(matrix):
    rows_in, cols_in = matrix.shape
    return matrix.reshape(rows_in // BLOCK, BLOCK, cols_in // BLOCK, BLOCK).transpose(0, 2, 1, 3).reshape(-1, BLOCK, BLOCK)

def shampoo(grads, weights, average, left, right, left_root, right_root):
    new_left = STAT_BETA * left + (1 - STAT_BETA) * jnp.einsum('bij,bkj->bik', grads, grads, precision=TOP_PRECISION)
    new_right = STAT_BETA * right + (1 - STAT_BETA) * jnp.einsum('bji,bjk->bik', grads, grads, precision=TOP_PRECISION)
    direction = jnp.einsum('bij,bjk->bik', left_root, grads, precision=TOP_PRECISION)
    direction = jnp.einsum('bij,bjk->bik', direction, right_root, precision=TOP_PRECISION)
    direction = direction * lax.rsqrt(lax.optimization_barrier(jnp.mean(direction * direction, axis=(1, 2), keepdims=True)) + 1e-06)
    new_weights = weights - SHAMPOO_RATE * (direction + DECAY_RATE * weights)
    new_average = EMA_DECAY * average + (1 - EMA_DECAY) * new_weights
    return (new_weights, new_left, new_right, new_average)

def adamw(grads, weights, first, second, average, step):
    new_first = BETA_ONE * first + (1 - BETA_ONE) * grads
    new_second = BETA_TWO * second + (1 - BETA_TWO) * grads * grads
    first_hat = new_first / (1 - BETA_ONE ** step)
    second_hat = new_second / (1 - BETA_TWO ** step)
    new_weights = weights - ADAM_RATE * (first_hat / (jnp.sqrt(second_hat) + ADAM_EPS) + DECAY_RATE * weights)
    new_average = EMA_DECAY * average + (1 - EMA_DECAY) * new_weights
    return (new_weights, new_first, new_second, new_average)

def reference(clean, noise, levels, flags, frame_map, block_slot, step_count, mat_weight, mat_ema, stat_left, stat_right, root_left, root_right, mod_table, mod_mom, mod_var, mod_ema, io_weight, io_mom, io_var, io_ema):
    natural = jnp.zeros_like(mat_weight).at[block_slot].set(mat_weight)
    weights = tuple(from_blocks(natural)) + (mod_table, io_weight)
    noised_total = jnp.maximum(jnp.sum((1 - flags).astype(jnp.float32)), 1.0)

    def objective(params):
        summed = jnp.zeros((), jnp.float32)
        for clip in range(CLIPS):
            summed = summed + clip_loss(params, clean[clip], noise[clip], levels[clip], flags[clip], frame_map[clip])
        return summed / (noised_total * GRID * GRID * PIN)
    total_loss, pullback = jax.vjp(objective, weights)
    grads = pullback(jnp.ones_like(total_loss))[0]
    grad_natural = jnp.concatenate([to_blocks(grads[0]), to_blocks(grads[1]), to_blocks(grads[2]), to_blocks(grads[3])], 0)
    grad_slot = grad_natural[block_slot]
    block_limit = CLIP_NORM * BLOCK * NPARAMS ** (-0.5)
    block_norm = jnp.sqrt(lax.optimization_barrier(jnp.sum(grad_slot * grad_slot, axis=(1, 2), keepdims=True)))
    mat_grad = grad_slot * (block_limit / jnp.maximum(block_norm, block_limit))
    grad_norm = jnp.sqrt(jnp.sum(grads[4] * grads[4]) + jnp.sum(grads[5] * grads[5]))
    factor = CLIP_NORM / jnp.maximum(grad_norm, CLIP_NORM)
    new_mat_weight, new_stat_left, new_stat_right, new_mat_ema = shampoo(mat_grad, mat_weight, mat_ema, stat_left, stat_right, root_left, root_right)
    step = step_count[0].astype(jnp.float32)
    new_mod = adamw(grads[4] * factor, mod_table, mod_mom, mod_var, mod_ema, step)
    new_io = adamw(grads[5] * factor, io_weight, io_mom, io_var, io_ema, step)
    return (total_loss * noised_total, noised_total, grad_norm, mat_grad, new_mat_weight, new_stat_left, new_stat_right, new_mat_ema, new_mod[0], new_mod[1], new_mod[2], new_mod[3], new_io[0], new_io[1], new_io[2], new_io[3])
```

```python
from functools import partial
import math

import jax
import jax.numpy as jnp
from jax import lax
from jax.experimental import pallas as pl
from jax.experimental.pallas import tpu as pltpu
from jax.sharding import PartitionSpec as P

D = 1024
HEADS = 16
HEAD_DIM = 64
FFN = 4096
PIN = 16
GRID = 16
BLOCK = 128
LEVELS = 32
FR_DEV = 1
NPARAMS = 12878848


LN_EPS = 1e-06
ROPE_BASE = 10000.0
CLIP_NORM = 0.01
BETA_ONE = 0.9
BETA_TWO = 0.999
ADAM_EPS = 1e-08
ADAM_RATE = 0.1
DECAY_RATE = 0.1
STAT_BETA = 0.95
SHAMPOO_RATE = 0.01
EMA_DECAY = 0.9
TOP_PRECISION = lax.Precision.HIGHEST


def matmul(left, right):
    return jnp.dot(left, right, preferred_element_type=jnp.float32)


def layer_norm(hidden):
    centered = hidden - jnp.mean(hidden, axis=-1, keepdims=True)
    inverse = lax.rsqrt(jnp.mean(centered * centered, axis=-1, keepdims=True) + LN_EPS)
    return (centered * inverse, inverse)


def norm_back(grad_hat, normed, inverse):
    return inverse * (
        grad_hat
        - jnp.mean(grad_hat, axis=-1, keepdims=True)
        - normed * jnp.mean(grad_hat * normed, axis=-1, keepdims=True)
    )


def gelu_back(upper, grad_act):
    return jax.vjp(partial(jax.nn.gelu, approximate=True), upper)[1](grad_act)[0]


def frequencies(width):
    return ROPE_BASE ** (-jnp.arange(width, dtype=jnp.float32) / width)


def rope_tables(frame_ids):
    pairs = HEAD_DIM // 2
    time_pairs = pairs // 4
    row_pairs = (pairs - time_pairs) // 2
    column_pairs = pairs - time_pairs - row_pairs
    frames = frame_ids.shape[0]
    tok_frame = GRID * GRID
    token_pos = jnp.arange(tok_frame, dtype=jnp.int32)
    row_pos = (token_pos // GRID).astype(jnp.float32)
    column_pos = (token_pos % GRID).astype(jnp.float32)
    time_angle = (
        frame_ids.astype(jnp.float32)[:, None, None] * frequencies(time_pairs)[None, None, :]
    )
    row_angle = row_pos[None, :, None] * frequencies(row_pairs)[None, None, :]
    column_angle = column_pos[None, :, None] * frequencies(column_pairs)[None, None, :]
    angles = jnp.concatenate(
        [jnp.broadcast_to(time_angle, (frames, tok_frame, time_pairs)), row_angle, column_angle],
        axis=-1,
    )
    angles = angles.reshape(frames * tok_frame, pairs)
    return (jnp.cos(angles), jnp.sin(angles))


def rotate(values, cosine, sine):
    pairs = HEAD_DIM // 2
    first, second = (values[..., :pairs], values[..., pairs:])
    cosine = cosine[:, None, :]
    sine = sine[:, None, :]
    return jnp.concatenate(
        [first * cosine - second * sine, first * sine + second * cosine], axis=-1
    )


def split_heads(flat):
    return flat.reshape(flat.shape[0], HEADS, HEAD_DIM)


def matrix_shapes():
    return ((D, 3 * D), (D, D), (D, FFN), (FFN, D))


def from_blocks(natural):
    matrices = []
    offset = 0
    for rows_in, cols_in in matrix_shapes():
        count_in = rows_in // BLOCK * (cols_in // BLOCK)
        part_blocks = natural[offset : offset + count_in]
        matrices.append(
            part_blocks.reshape(rows_in // BLOCK, cols_in // BLOCK, BLOCK, BLOCK)
            .transpose(0, 2, 1, 3)
            .reshape(rows_in, cols_in)
        )
        offset = offset + count_in
    return matrices


def to_blocks(matrix):
    rows_in, cols_in = matrix.shape
    return (
        matrix.reshape(rows_in // BLOCK, BLOCK, cols_in // BLOCK, BLOCK)
        .transpose(0, 2, 1, 3)
        .reshape(-1, BLOCK, BLOCK)
    )


def score_block(queries, key_block, query_frames, key_frames):
    scores = jnp.einsum(
        "qhd,khd->hqk", queries, key_block, preferred_element_type=jnp.float32
    ) * HEAD_DIM ** (-0.5)
    visible = key_frames[None, None, :] <= query_frames[None, :, None]
    return jnp.where(visible, scores, -jnp.inf)


def stack_keys(key_rows, value_rows, frame_rows):
    total_rows = key_rows.shape[0]
    block_rows = math.gcd(total_rows, 512)
    blocks = total_rows // block_rows
    return (
        (
            key_rows.reshape(blocks, block_rows, HEADS, HEAD_DIM),
            value_rows.reshape(blocks, block_rows, HEADS, HEAD_DIM),
            frame_rows.reshape(blocks, block_rows),
        ),
        block_rows,
    )


def keep_state(previous):
    return previous


def fold_keys(state, shard_rows, queries, query_frames, key_frames_all):
    key_rows, value_rows = shard_rows
    stacks, block_rows = stack_keys(key_rows, value_rows, key_frames_all)
    top_query = jnp.max(query_frames)

    def fold_step_block(carried, block_in):
        key_block, value_block, key_frames = block_in

        def fold_compute(previous):
            running, denominator, accumulated = previous
            scores = score_block(queries, key_block, query_frames, key_frames)
            new_max = jnp.maximum(running, jnp.max(scores, axis=-1))
            weights = jnp.exp(scores - new_max[..., None])
            rescale = jnp.exp(running - new_max)
            contrib = jnp.einsum(
                "hqk,khd->hqd",
                weights.astype(jnp.bfloat16),
                value_block,
                preferred_element_type=jnp.float32,
            )
            return (
                new_max,
                denominator * rescale + jnp.sum(weights, axis=-1),
                accumulated * rescale[..., None] + contrib,
            )

        return (lax.cond(jnp.min(key_frames) <= top_query, fold_compute, keep_state, carried), None)

    state, unused = lax.scan(fold_step_block, state, stacks)
    return state


def grad_parts(
    queries, grad_heads, delta, log_total, query_frames, key_block, value_block, key_frames
):
    probs = jnp.exp(
        score_block(queries, key_block, query_frames, key_frames) - log_total[..., None]
    )
    grad_probs = jnp.einsum(
        "qhd,khd->hqk", grad_heads, value_block, preferred_element_type=jnp.float32
    )
    grad_scores = (probs * (grad_probs - delta[..., None])).astype(jnp.bfloat16)
    return (probs, grad_scores)


def key_value_block(
    queries, grad_heads, delta, log_total, query_frames, key_block, value_block, key_frames
):
    block_rows = key_block.shape[0]
    probs, grad_scores = grad_parts(
        queries, grad_heads, delta, log_total, query_frames, key_block, value_block, key_frames
    )
    key_grad = jnp.einsum(
        "hqk,qhd->khd", grad_scores, queries, preferred_element_type=jnp.float32
    ) * HEAD_DIM ** (-0.5)
    value_grad = jnp.einsum(
        "hqk,qhd->khd", probs.astype(jnp.bfloat16), grad_heads, preferred_element_type=jnp.float32
    )
    return jnp.concatenate(
        [key_grad.reshape(block_rows, D), value_grad.reshape(block_rows, D)], axis=1
    )


def query_grads(
    queries, grad_heads, delta, log_total, query_frames, key_all, value_all, key_frames_all
):
    stacks, block_rows = stack_keys(key_all, value_all, key_frames_all)
    top_query = jnp.max(query_frames)

    def query_step_block(carried, block_in):
        key_block, value_block, key_frames = block_in

        def query_compute(previous):
            probs, grad_scores = grad_parts(
                queries,
                grad_heads,
                delta,
                log_total,
                query_frames,
                key_block,
                value_block,
                key_frames,
            )
            return previous + jnp.einsum(
                "hqk,khd->qhd", grad_scores, key_block, preferred_element_type=jnp.float32
            )

        return (
            lax.cond(jnp.min(key_frames) <= top_query, query_compute, keep_state, carried),
            None,
        )

    initial = jnp.zeros(queries.shape, jnp.float32)
    result, unused = lax.scan(query_step_block, initial, stacks)
    return result * HEAD_DIM ** (-0.5)


def key_terms(
    row_count,
    queries,
    grad_heads,
    delta,
    log_total,
    query_frames,
    key_all,
    value_all,
    key_frames_all,
):
    stacks, block_rows = stack_keys(key_all, value_all, key_frames_all)
    top_query = jnp.max(query_frames)

    def one_block(block_in):
        key_block, value_block, key_frames = block_in

        def one_compute(unused):
            return key_value_block(
                queries,
                grad_heads,
                delta,
                log_total,
                query_frames,
                key_block,
                value_block,
                key_frames,
            )

        def nothing(unused):
            return jnp.zeros((block_rows, 2 * D), jnp.float32)

        return lax.cond(jnp.min(key_frames) <= top_query, one_compute, nothing, 0)

    return lax.map(one_block, stacks).reshape(row_count, 2 * D)


def shampoo(grads, weights, average, left, right, left_root, right_root):
    new_left = STAT_BETA * left + (1 - STAT_BETA) * jnp.einsum(
        "bij,bkj->bik", grads, grads, precision=TOP_PRECISION
    )
    new_right = STAT_BETA * right + (1 - STAT_BETA) * jnp.einsum(
        "bji,bjk->bik", grads, grads, precision=TOP_PRECISION
    )
    direction = jnp.einsum("bij,bjk->bik", left_root, grads, precision=TOP_PRECISION)
    direction = jnp.einsum("bij,bjk->bik", direction, right_root, precision=TOP_PRECISION)
    direction = direction * lax.rsqrt(
        jnp.mean(direction * direction, axis=(1, 2), keepdims=True) + 1e-06
    )
    new_weights = weights - SHAMPOO_RATE * (direction + DECAY_RATE * weights)
    new_average = EMA_DECAY * average + (1 - EMA_DECAY) * new_weights
    return (new_weights, new_left, new_right, new_average)


def adamw(grads, weights, first, second, average, step):
    new_first = BETA_ONE * first + (1 - BETA_ONE) * grads
    new_second = BETA_TWO * second + (1 - BETA_TWO) * grads * grads
    first_hat = new_first / (1 - BETA_ONE**step)
    second_hat = new_second / (1 - BETA_TWO**step)
    new_weights = weights - ADAM_RATE * (
        first_hat / (jnp.sqrt(second_hat) + ADAM_EPS) + DECAY_RATE * weights
    )
    new_average = EMA_DECAY * average + (1 - EMA_DECAY) * new_weights
    return (new_weights, new_first, new_second, new_average)


def on_device(
    clean,
    noise,
    levels,
    flags,
    frame_map,
    block_slot,
    step_count,
    mat_weight,
    mat_ema,
    stat_left,
    stat_right,
    root_left,
    root_right,
    mod_table,
    mod_mom,
    mod_var,
    mod_ema,
    io_weight,
    io_mom,
    io_var,
    io_ema,
):
    tok_frame = GRID * GRID
    local_rows = FR_DEV * tok_frame
    noised = (1 - flags[0]).astype(jnp.float32)
    noised_total = jnp.maximum(lax.psum(jnp.sum(noised), ("frame", "rep")), 1.0)
    gathered = lax.all_gather(mat_weight.astype(jnp.bfloat16), ("frame", "rep"), axis=0, tiled=True)
    natural = jnp.zeros_like(gathered).at[block_slot].set(gathered)
    attn_w, out_w, up_w, down_w = from_blocks(natural)
    clip_map = lax.dynamic_index_in_dim(frame_map, lax.axis_index("rep"), 0, keepdims=False)
    my_frames = lax.dynamic_slice_in_dim(clip_map, lax.axis_index("frame") * FR_DEV, FR_DEV)
    key_frames_all = jnp.repeat(clip_map, tok_frame)
    query_frames = jnp.repeat(my_frames, tok_frame)
    level_now = levels[0] * (1 - flags[0])
    fraction = level_now.astype(jnp.float32) / LEVELS
    keep_coef = jnp.cos(0.5 * jnp.pi * fraction)
    noise_coef = jnp.sin(0.5 * jnp.pi * fraction)
    frames_in = keep_coef[:, None, None] * clean[0] + noise_coef[:, None, None] * noise[0]
    inputs = jnp.swapaxes(frames_in, 1, 2).reshape(local_rows, PIN).astype(jnp.bfloat16)
    targets = jnp.swapaxes(noise[0], 1, 2).reshape(local_rows, PIN)
    selector = (level_now[:, None] == jnp.arange(LEVELS, dtype=jnp.int32)[None, :]).astype(
        jnp.float32
    )
    modulation = jnp.dot(selector, mod_table, precision=TOP_PRECISION).reshape(FR_DEV, 8, 1, D)
    io_low = io_weight.astype(jnp.bfloat16)
    embed = io_low[:PIN]
    head = io_low[PIN : 2 * PIN]
    start = (matmul(inputs, embed) + io_weight[2 * PIN]).reshape(FR_DEV, tok_frame, D)
    hat_one, inv_one = layer_norm(start)
    normed = (
        (hat_one * (1 + modulation[:, 1]) + modulation[:, 0])
        .reshape(local_rows, D)
        .astype(jnp.bfloat16)
    )
    projected = matmul(normed, attn_w)
    cosine, sine = rope_tables(my_frames)
    queries = rotate(split_heads(projected[:, :D]), cosine, sine).astype(jnp.bfloat16)
    key_flat = (
        rotate(split_heads(projected[:, D : 2 * D]), cosine, sine)
        .astype(jnp.bfloat16)
        .reshape(local_rows, D)
    )
    value_flat = projected[:, 2 * D :].astype(jnp.bfloat16)
    initial = (
        jnp.full((HEADS, local_rows), -1e30, jnp.float32),
        jnp.zeros((HEADS, local_rows), jnp.float32),
        jnp.zeros((HEADS, local_rows, HEAD_DIM), jnp.float32),
    )
    running, denominator, accumulated = fold_keys(
        initial,
        (
            lax.all_gather(key_flat, "frame", axis=0, tiled=True),
            lax.all_gather(value_flat, "frame", axis=0, tiled=True),
        ),
        queries,
        query_frames,
        key_frames_all,
    )
    attended = jnp.transpose(accumulated / denominator[..., None], (1, 0, 2)).reshape(local_rows, D)
    log_total = running + jnp.log(denominator)
    attended_low = attended.astype(jnp.bfloat16)
    branch = matmul(attended_low, out_w).reshape(FR_DEV, tok_frame, D)
    middle = start + modulation[:, 2] * branch
    hat_two, inv_two = layer_norm(middle)
    normed_two = (
        (hat_two * (1 + modulation[:, 4]) + modulation[:, 3])
        .reshape(local_rows, D)
        .astype(jnp.bfloat16)
    )
    upper = matmul(normed_two, up_w)
    activated = jax.nn.gelu(upper, approximate=True).astype(jnp.bfloat16)
    lower = matmul(activated, down_w).reshape(FR_DEV, tok_frame, D)
    final = middle + modulation[:, 5] * lower
    hat_three, inv_three = layer_norm(final)
    normed_three = (
        (hat_three * (1 + modulation[:, 7]) + modulation[:, 6])
        .reshape(local_rows, D)
        .astype(jnp.bfloat16)
    )
    predicted = matmul(normed_three, head.T)
    row_weight = jnp.repeat(noised, tok_frame)[:, None]
    inv_scale = 1.0 / (noised_total * tok_frame * PIN)
    difference = predicted - targets
    loss_part = jnp.sum(row_weight * difference * difference) * inv_scale
    grad_pred = (2.0 * inv_scale * row_weight * difference).astype(jnp.bfloat16)
    grad_head = jnp.dot(grad_pred.T, normed_three, preferred_element_type=jnp.float32)
    grad_norm_three = matmul(grad_pred, head).reshape(FR_DEV, tok_frame, D)
    grad_final = norm_back(grad_norm_three * (1 + modulation[:, 7]), hat_three, inv_three)
    grad_lower = (grad_final * modulation[:, 5]).reshape(local_rows, D).astype(jnp.bfloat16)
    grad_down = jnp.dot(activated.T, grad_lower, preferred_element_type=jnp.float32)
    grad_upper = gelu_back(upper, matmul(grad_lower, down_w.T)).astype(jnp.bfloat16)
    grad_up = jnp.dot(normed_two.T, grad_upper, preferred_element_type=jnp.float32)
    grad_norm_two = matmul(grad_upper, up_w.T).reshape(FR_DEV, tok_frame, D)
    grad_middle = grad_final + norm_back(grad_norm_two * (1 + modulation[:, 4]), hat_two, inv_two)
    grad_branch = (grad_middle * modulation[:, 2]).reshape(local_rows, D).astype(jnp.bfloat16)
    grad_out_w = jnp.dot(attended_low.T, grad_branch, preferred_element_type=jnp.float32)
    grad_heads = split_heads(matmul(grad_branch, out_w.T).astype(jnp.bfloat16))
    delta = jnp.sum(grad_heads.astype(jnp.float32) * split_heads(attended), axis=-1).T
    key_all, value_all = (
        lax.all_gather(key_flat, "frame", axis=0, tiled=True),
        lax.all_gather(value_flat, "frame", axis=0, tiled=True),
    )
    grad_query = query_grads(
        queries, grad_heads, delta, log_total, query_frames, key_all, value_all, key_frames_all
    )
    key_value_grad = lax.psum_scatter(
        key_terms(
            lax.axis_size("frame") * local_rows,
            queries,
            grad_heads,
            delta,
            log_total,
            query_frames,
            key_all,
            value_all,
            key_frames_all,
        ),
        "frame",
        scatter_dimension=0,
        tiled=True,
    )
    grad_q = rotate(grad_query, cosine, -sine).reshape(local_rows, D)
    grad_k = rotate(split_heads(key_value_grad[:, :D]), cosine, -sine).reshape(local_rows, D)
    grad_proj = jnp.concatenate([grad_q, grad_k, key_value_grad[:, D:]], axis=1).astype(
        jnp.bfloat16
    )
    grad_attn_w = jnp.dot(normed.T, grad_proj, preferred_element_type=jnp.float32)
    grad_norm_one = matmul(grad_proj, attn_w.T).reshape(FR_DEV, tok_frame, D)
    grad_start = grad_middle + norm_back(grad_norm_one * (1 + modulation[:, 1]), hat_one, inv_one)
    grad_start_low = grad_start.reshape(local_rows, D).astype(jnp.bfloat16)
    grad_embed = jnp.dot(inputs.T, grad_start_low, preferred_element_type=jnp.float32)
    grad_bias = jnp.sum(grad_start_low.astype(jnp.float32), axis=0)
    mod_terms = [
        grad_norm_one,
        grad_norm_one * hat_one,
        grad_middle * branch,
        grad_norm_two,
        grad_norm_two * hat_two,
        grad_final * lower,
        grad_norm_three,
        grad_norm_three * hat_three,
    ]
    mod_grads = jnp.stack([jnp.sum(term, axis=1) for term in mod_terms], axis=1).reshape(
        FR_DEV, 8 * D
    )
    grad_table = jnp.dot(selector.T, mod_grads, precision=TOP_PRECISION)
    grad_io = jnp.concatenate([grad_embed, grad_head, grad_bias[None, :]], axis=0)
    grad_table, grad_io, total_loss = lax.psum((grad_table, grad_io, loss_part), ("frame", "rep"))
    grad_blocks = jnp.concatenate(
        [to_blocks(grad_attn_w), to_blocks(grad_out_w), to_blocks(grad_up), to_blocks(grad_down)], 0
    )
    owned = lax.psum_scatter(
        grad_blocks[block_slot], ("frame", "rep"), scatter_dimension=0, tiled=True
    )
    block_limit = CLIP_NORM * BLOCK * NPARAMS ** (-0.5)
    block_norm = jnp.sqrt(jnp.sum(owned * owned, axis=(1, 2), keepdims=True))
    mat_grad = owned * (block_limit / jnp.maximum(block_norm, block_limit))
    grad_norm = jnp.sqrt(jnp.sum(grad_table * grad_table) + jnp.sum(grad_io * grad_io))
    factor = CLIP_NORM / jnp.maximum(grad_norm, CLIP_NORM)
    new_mat_weight, new_stat_left, new_stat_right, new_mat_ema = shampoo(
        mat_grad, mat_weight, mat_ema, stat_left, stat_right, root_left, root_right
    )
    step = step_count[0].astype(jnp.float32)
    new_mod = adamw(grad_table * factor, mod_table, mod_mom, mod_var, mod_ema, step)
    new_io = adamw(grad_io * factor, io_weight, io_mom, io_var, io_ema, step)
    return (
        total_loss * noised_total,
        noised_total,
        grad_norm,
        mat_grad,
        new_mat_weight,
        new_stat_left,
        new_stat_right,
        new_mat_ema,
        new_mod[0],
        new_mod[1],
        new_mod[2],
        new_mod[3],
        new_io[0],
        new_io[1],
        new_io[2],
        new_io[3],
    )


MESH = pl.DeviceIdType.MESH
GRAN = 4
NSLOT = 24
ORDERS = ("xzy", "xzy", "yzx", "yzx", "zxy", "zyx")

def place():
    frame = lax.axis_index("frame")
    return frame // 4, (frame // 2) % 2, frame % 2, lax.axis_index("rep")

def device(z, y, c, x):
    return ((z * 2 + y) * 2 + c, x)

def owner_of(z, y, c, x):
    return ((z * 2 + y) * 2 + c) * 2 + x

def plane_of(z, y, x):
    return (z * 2 + y) * 2 + x

def route_keys():
    keys = [
        (part, dx, dy, dz)
        for part in range(len(ORDERS))
        for dx in (0, 1)
        for dy in (0, 1)
        for dz in range(-3, 4)
    ]
    return sorted(keys, key=lambda k: (k[1] + k[2] + abs(k[3]), k[0]))

def onward(order, dx, dy, dz):
    moved = {"x": dx, "y": dy, "z": dz}
    last = max((order.index(k) for k in order if moved[k]), default=-1)
    links = []
    if last >= 0 and order[last] == "z":
        links.append("u" if dz < 0 else "w")
    for k in order[last + 1 :]:
        links.extend("uw" if k == "z" else k)
    return links

def can(link, z):
    return {"u": z < 3, "w": z > 0}.get(link)

def partner(link, z, y, c, x):
    return {
        "x": device(z, y, c, 1 - x),
        "y": device(z, 1 - y, c, x),
        "u": device(z + 1, y, c, x),
        "w": device(z - 1, y, c, x),
        "c": device(z, y, 1 - c, x),
    }[link]

def when(cond, fn):
    if cond is None:
        fn()
    else:
        pl.when(cond)(fn)

def both(a, b):
    return b if a is None else a if b is None else jnp.logical_and(a, b)

def gather_kernel(w_ref, meta_ref, out_ref, meta_out, send, recv, csend, crecv, local, msend, mrecv):
    z, y, c, x = place()
    mine = owner_of(z, y, c, x)
    flat = lax.axis_index("frame") * 2 + lax.axis_index("rep")
    barrier = pltpu.get_barrier_semaphore()
    def others(fn):
        def body(step, carry):
            peer = lax.rem(flat + step, 32)
            fn(step, peer, (peer // 2, lax.rem(peer, 2)))
            return carry
        lax.fori_loop(1, 32, body, 0)
    others(lambda step, peer, dev: pl.semaphore_signal(barrier, inc=1, device_id=dev, device_id_type=MESH))
    pl.semaphore_wait(barrier, 31)
    own = pltpu.make_async_copy(w_ref, out_ref.at[mine], local.at[0])
    own.start()
    links = ("x", "y", "u", "w")
    pending = []
    def hop(link, part, src, owner, plane):
        return pltpu.make_async_remote_copy(
            src_ref=src, dst_ref=out_ref.at[owner, pl.ds(part * GRAN, GRAN)],
            send_sem=send.at[links.index(link), part, plane], recv_sem=recv.at[part, plane],
            device_id=partner(link, z, y, c, x), device_id_type=MESH)
    def core(src, owner, plane):
        return pltpu.make_async_remote_copy(src_ref=src, dst_ref=out_ref.at[owner],
            send_sem=csend.at[plane], recv_sem=crecv.at[plane],
            device_id=partner("c", z, y, c, x), device_id_type=MESH)
    def meta(step, peer, dev):
        return pltpu.make_async_remote_copy(src_ref=meta_ref, dst_ref=meta_out.at[flat],
            send_sem=msend.at[step], recv_sem=mrecv.at[step], device_id=dev, device_id_type=MESH)
    keys = route_keys()
    last_key = {}
    for k in keys:
        last_key[k[1:]] = k
    for k in keys:
        part, dx, dy, dz = k
        if (dx, dy, dz) == (0, 0, 0):
            for link in onward(ORDERS[part], 0, 0, 0):
                src = w_ref.at[pl.ds(part * GRAN, GRAN)]
                plane = plane_of(z, y, x)
                def go(link=link, part=part, src=src, plane=plane):
                    hop(link, part, src, mine, plane).start()
                when(can(link, z), go)
                pending.append((can(link, z), hop, (link, part, src, mine, plane)))
    core(w_ref, mine, plane_of(z, y, x)).start()
    pending.append((None, core, (w_ref, mine, plane_of(z, y, x))))
    mown = pltpu.make_async_copy(meta_ref, meta_out.at[flat], local.at[1])
    mown.start()
    others(lambda step, peer, dev: meta(step, peer, dev).start())
    for k in keys:
        part, dx, dy, dz = k
        if (dx, dy, dz) == (0, 0, 0):
            continue
        oz, oy, ox = z + dz, (1 - y if dy else y), (1 - x if dx else x)
        cond = None if dz == 0 else (oz <= 3 if dz > 0 else oz >= 0)
        owner, plane = owner_of(oz, oy, c, ox), plane_of(oz, oy, ox)
        src = out_ref.at[owner, pl.ds(part * GRAN, GRAN)]
        outs = onward(ORDERS[part], dx, dy, dz)
        def act(part=part, owner=owner, plane=plane, src=src, outs=outs, k=k):
            hop("x", part, src, owner, plane).wait_recv()
            for link in outs:
                when(can(link, z), lambda link=link: hop(link, part, src, owner, plane).start())
            if last_key[k[1:]] == k:
                core(out_ref.at[owner], owner, plane).start()
        when(cond, act)
        for link in outs:
            pending.append((both(cond, can(link, z)), hop, (link, part, src, owner, plane)))
        if last_key[k[1:]] == k:
            pending.append((cond, core, (out_ref.at[owner], owner, plane)))
    for cond, make, args in pending:
        when(cond, lambda make=make, args=args: make(*args).wait_send())
    own.wait()
    mown.wait()
    for plane in range(16):
        owner = owner_of(plane // 4, (plane // 2) % 2, 1 - c, plane % 2)
        core(out_ref.at[owner], owner, plane).wait_recv()
    others(lambda step, peer, dev: meta(step, peer, dev).wait())

def gather_weights(blocks, meta):
    anyspace = pl.BlockSpec(memory_space=pl.ANY)
    return pl.pallas_call(
        gather_kernel,
        out_shape=(jax.ShapeDtypeStruct((32, NSLOT, 128, 128), jnp.bfloat16), jax.ShapeDtypeStruct((32,) + meta.shape, meta.dtype)),
        in_specs=[anyspace, anyspace], out_specs=(anyspace, anyspace),
        scratch_shapes=[
            pltpu.SemaphoreType.DMA((4, 6, 16)), pltpu.SemaphoreType.DMA((6, 16)),
            pltpu.SemaphoreType.DMA((16,)), pltpu.SemaphoreType.DMA((16,)), pltpu.SemaphoreType.DMA((2,)),
            pltpu.SemaphoreType.DMA((32,)), pltpu.SemaphoreType.DMA((32,)),
        ],
        compiler_params=pltpu.CompilerParams(collective_id=1, has_side_effects=True),
    )(blocks, meta)

def inbox_rows(order, link):
    dim = "z" if link in "uw" else link
    dims = order[: order.index(dim)]
    return dims + "z" if dim == "z" else dims

def inbox_layout(link):
    starts, total = [], 0
    for order in ORDERS:
        starts.append(total)
        size = 1
        for d in inbox_rows(order, link):
            size *= 4 if d == "z" else 2
        total += size
    return starts, total

def inbox_index(link, part, oz, oy, ox):
    starts, _ = inbox_layout(link)
    index = 0
    for d in inbox_rows(ORDERS[part], link):
        index = index * (4 if d == "z" else 2) + {"z": oz, "y": oy, "x": ox}[d]
    return starts[part] + index

def toward(order, dx, dy, dz):
    moved = {"x": dx, "y": dy, "z": dz}
    last = [k for k in order if moved[k]][-1]
    if last == "z":
        return ("w", "u") if dz < 0 else ("u", "w")
    return last, last

def scatter_kernel(g_ref, out_ref, acc, sib, inx, iny, inu, inw, send, rx, ry, ru, rw, csend, crecv, local):
    z, y, c, x = place()
    boxes = {"x": (inx, rx), "y": (iny, ry), "u": (inu, ru), "w": (inw, rw)}
    barrier = pltpu.get_barrier_semaphore()
    for link in "xyuwc":
        when(can(link, z), lambda link=link: pl.semaphore_signal(
            barrier, inc=1, device_id=partner(link, z, y, c, x), device_id_type=MESH))
    ends = jnp.logical_or(z == 0, z == 3)
    pl.when(ends)(lambda: pl.semaphore_wait(barrier, 4))
    pl.when(jnp.logical_not(ends))(lambda: pl.semaphore_wait(barrier, 5))
    keys = [(k[0], k[1], k[2], k[3]) for k in reversed(route_keys())]
    def owner_at(dx, dy, dz):
        oz, oy, ox = z + dz, (1 - y if dy else y), (1 - x if dx else x)
        cond = None if dz == 0 else (oz <= 3 if dz > 0 else oz >= 0)
        return oz, oy, ox, cond
    def core(oz, oy, ox):
        plane = plane_of(oz, oy, ox)
        return pltpu.make_async_remote_copy(
            src_ref=g_ref.at[owner_of(oz, oy, 1 - c, ox)], dst_ref=sib.at[plane],
            send_sem=csend.at[plane], recv_sem=crecv.at[plane],
            device_id=partner("c", z, y, c, x), device_id_type=MESH)
    def load(oz, oy, ox):
        plane = plane_of(oz, oy, ox)
        return pltpu.make_async_copy(g_ref.at[owner_of(oz, oy, c, ox)], acc.at[plane], local.at[plane])
    seen = []
    for part, dx, dy, dz in keys:
        if (dx, dy, dz) not in seen:
            seen.append((dx, dy, dz))
    for off in seen:
        oz, oy, ox, cond = owner_at(*off)
        def begin(oz=oz, oy=oy, ox=ox):
            core(oz, oy, ox).start()
            load(oz, oy, ox).start()
        when(cond, begin)
    def clear(box):
        def body(i, carry):
            box[i] = jnp.zeros((GRAN, 128, 128), jnp.bfloat16)
            return carry
        lax.fori_loop(0, box.shape[0], body, 0)
    pl.when(z == 3)(lambda: clear(inu))
    pl.when(z == 0)(lambda: clear(inw))
    def hop(part, off):
        oz, oy, ox, cond = owner_at(*off)
        plane = plane_of(oz, oy, ox)
        link, seen_as = toward(ORDERS[part], *off)
        box, sems = boxes[seen_as]
        index = inbox_index(seen_as, part, oz, oy, ox)
        return pltpu.make_async_remote_copy(
            src_ref=acc.at[plane, pl.ds(part * GRAN, GRAN)], dst_ref=box.at[index],
            send_sem=send.at[part, plane], recv_sem=sems.at[index],
            device_id=partner(link, z, y, c, x), device_id_type=MESH)
    fresh = set()
    for part, dx, dy, dz in keys:
        off = (dx, dy, dz)
        oz, oy, ox, cond = owner_at(*off)
        plane = plane_of(oz, oy, ox)
        links = onward(ORDERS[part], *off)
        first = off not in fresh
        fresh.add(off)
        def act(part=part, off=off, oz=oz, oy=oy, ox=ox, plane=plane, links=links, first=first):
            if first:
                core(oz, oy, ox).wait_recv()
                load(oz, oy, ox).wait()
            sources = []
            for link in links:
                box, sems = boxes[link]
                index = inbox_index(link, part, oz, oy, ox)
                sources.append((box, index))
                def arrive(box=box, index=index, sems=sems, link=link):
                    pltpu.make_async_remote_copy(
                        src_ref=box.at[index], dst_ref=box.at[index], send_sem=csend.at[0], recv_sem=sems.at[index],
                        device_id=partner("c", z, y, c, x), device_id_type=MESH).wait_recv()
                when(can(link, z), arrive)
            def add(i, carry):
                row = part * GRAN + i
                total = acc[plane, row].astype(jnp.float32) + sib[plane, row].astype(jnp.float32)
                for box, index in sources:
                    total = total + box[index, i].astype(jnp.float32)
                if off == (0, 0, 0):
                    out_ref[row] = total
                else:
                    acc[plane, row] = total.astype(jnp.bfloat16)
                return carry
            lax.fori_loop(0, GRAN, add, 0)
            if off != (0, 0, 0):
                hop(part, off).start()
        when(cond, act)
    for part, dx, dy, dz in keys:
        if (dx, dy, dz) != (0, 0, 0):
            cond = owner_at(dx, dy, dz)[3]
            when(cond, lambda part=part, off=(dx, dy, dz): hop(part, off).wait_send())
    for plane in range(16):
        core(plane // 4, (plane // 2) % 2, plane % 2).wait_send()

def scatter_grads(grads):
    totals = {link: inbox_layout(link)[1] for link in "xyuw"}
    box = lambda n: pltpu.VMEM((n, GRAN, 128, 128), jnp.bfloat16)
    return pl.pallas_call(
        scatter_kernel,
        out_shape=jax.ShapeDtypeStruct((NSLOT, 128, 128), jnp.float32),
        in_specs=[pl.BlockSpec(memory_space=pl.ANY)], out_specs=pl.BlockSpec(memory_space=pltpu.VMEM),
        scratch_shapes=[
            pltpu.VMEM((16, NSLOT, 128, 128), jnp.bfloat16), pltpu.VMEM((16, NSLOT, 128, 128), jnp.bfloat16),
            box(totals["x"]), box(totals["y"]), box(totals["u"]), box(totals["w"]),
            pltpu.SemaphoreType.DMA((6, 16)),
            pltpu.SemaphoreType.DMA((totals["x"],)), pltpu.SemaphoreType.DMA((totals["y"],)),
            pltpu.SemaphoreType.DMA((totals["u"],)), pltpu.SemaphoreType.DMA((totals["w"],)),
            pltpu.SemaphoreType.DMA((16,)), pltpu.SemaphoreType.DMA((16,)), pltpu.SemaphoreType.DMA((16,)),
        ],
        compiler_params=pltpu.CompilerParams(collective_id=2, has_side_effects=True, vmem_limit_bytes=60 * 2**20),
    )(grads)


TOK=256; HD=64
def dotg(a,b,ca,cb):
    return lax.dot_general(a,b,(((ca,),(cb,)),((),())),preferred_element_type=jnp.float32)

def attend_kernel(order_ref, qkv_ref, low_ref, full_ref, lse_ref):
    t = pl.program_id(0)
    slot = order_ref[t]
    q = qkv_ref[slot, 0] * jnp.bfloat16(0.125)
    def fold(state, keys, values):
        top, total, acc = state
        s = dotg(keys, q, 0, 0)
        new = jnp.maximum(top, jnp.max(s, axis=0, keepdims=True))
        p = jnp.exp(s - new)
        shrink = jnp.exp(top - new)
        return (new, total * shrink + jnp.sum(p, axis=0, keepdims=True),
                acc * shrink + dotg(values, p.astype(jnp.bfloat16), 1, 0))
    def one(i, state):
        src = order_ref[i]
        return fold(state, qkv_ref[src, 1], qkv_ref[src, 2])
    def two(i, state):
        a, b = order_ref[2 * i], order_ref[2 * i + 1]
        keys = jnp.concatenate([qkv_ref[a, 1], qkv_ref[b, 1]], axis=1)
        values = jnp.concatenate([qkv_ref[a, 2], qkv_ref[b, 2]], axis=1)
        return fold(state, keys, values)
    state = (jnp.full((1, TOK), -1e30, jnp.float32), jnp.zeros((1, TOK), jnp.float32), jnp.zeros((HD, TOK), jnp.float32))
    n = t + 1
    state = lax.fori_loop(0, n // 2, two, state)
    top, total, acc = lax.fori_loop(2 * (n // 2), n, one, state)
    out = acc / total
    full_ref[slot] = out
    low_ref[slot] = out.astype(jnp.bfloat16)
    lse_ref[slot] = top + jnp.log(total)

def attend(order, qkv):
    frames = qkv.shape[0]
    whole = lambda shape: pl.BlockSpec(shape, lambda t, order: (0,) * len(shape))
    return pl.pallas_call(
        attend_kernel,
        grid_spec=pltpu.PrefetchScalarGridSpec(
            num_scalar_prefetch=1, grid=(frames,),
            in_specs=[whole(qkv.shape)],
            out_specs=[whole((frames, HD, TOK)), whole((frames, HD, TOK)), whole((frames, 1, TOK))]),
        out_shape=[jax.ShapeDtypeStruct((frames, HD, TOK), jnp.bfloat16), jax.ShapeDtypeStruct((frames, HD, TOK), jnp.float32), jax.ShapeDtypeStruct((frames, 1, TOK), jnp.float32)],
        compiler_params=pltpu.CompilerParams(vmem_limit_bytes=40*2**20),
    )(order, qkv)

def attend_back_kernel(order_ref, qkv_ref, do_ref, full_ref, lse_ref, cos_ref, sin_ref, out_ref, dq, delta):
    t = pl.program_id(0)
    frames = pl.num_programs(0)
    @pl.when(t == 0)
    def _():
        def start(i, carry):
            dq[i] = jnp.zeros((HD, TOK), jnp.float32)
            delta[i] = jnp.sum(do_ref[i].astype(jnp.float32) * full_ref[i], axis=0, keepdims=True)
            return carry
        lax.fori_loop(0, frames, start, 0)
    slot = order_ref[t]
    keys = qkv_ref[slot, 1]; values = qkv_ref[slot, 2]
    def fold(state, qs):
        dk, dv = state
        q = jnp.concatenate([qkv_ref[a, 0] for a in qs], axis=1) if len(qs) > 1 else qkv_ref[qs[0], 0]
        do = jnp.concatenate([do_ref[a] for a in qs], axis=1) if len(qs) > 1 else do_ref[qs[0]]
        lse = jnp.concatenate([lse_ref[a] for a in qs], axis=1) if len(qs) > 1 else lse_ref[qs[0]]
        dl = jnp.concatenate([delta[a] for a in qs], axis=1) if len(qs) > 1 else delta[qs[0]]
        s = dotg(keys, q * jnp.bfloat16(0.125), 0, 0)
        p = jnp.exp(s - lse)
        dp = dotg(values, do, 0, 0)
        ds = (p * (dp - dl)).astype(jnp.bfloat16)
        dv = dv + dotg(do, p.astype(jnp.bfloat16), 1, 1)
        dk = dk + dotg(q, ds, 1, 1)
        dqn = dotg(keys, ds, 1, 0)
        for j, a in enumerate(qs):
            dq[a] = dq[a] + dqn[:, j * TOK:(j + 1) * TOK]
        return dk, dv
    def one(i, state):
        return fold(state, [order_ref[i]])
    def two(i, state):
        j = t + 2 * i
        return fold(state, [order_ref[j], order_ref[j + 1]])
    zero = jnp.zeros((HD, TOK), jnp.float32)
    n = frames - t
    state = lax.fori_loop(0, n // 2, two, (zero, zero))
    dk, dv = lax.fori_loop(t + 2 * (n // 2), frames, one, state)
    def unturn(g, i):
        c, s = cos_ref[i], sin_ref[i]
        u1, u2 = g[:HD // 2], g[HD // 2:]
        return jnp.concatenate([u1 * c + u2 * s, u2 * c - u1 * s], axis=0)
    out_ref[slot, 1] = unturn(dk * 0.125, slot).astype(jnp.bfloat16)
    out_ref[slot, 2] = dv.astype(jnp.bfloat16)
    @pl.when(t == frames - 1)
    def _():
        def finish(i, carry):
            out_ref[i, 0] = unturn(dq[i] * 0.125, i).astype(jnp.bfloat16)
            return carry
        lax.fori_loop(0, frames, finish, 0)

def attend_back(order, qkv, do, full, lse, cos, sin):
    frames = qkv.shape[0]
    whole = lambda shape: pl.BlockSpec(shape, lambda t, order: (0,) * len(shape))
    return pl.pallas_call(
        attend_back_kernel,
        grid_spec=pltpu.PrefetchScalarGridSpec(
            num_scalar_prefetch=1, grid=(frames,),
            in_specs=[whole(a.shape) for a in (qkv, do, full, lse, cos, sin)],
            out_specs=whole(qkv.shape),
            scratch_shapes=[pltpu.VMEM((frames, HD, TOK), jnp.float32), pltpu.VMEM((frames, 1, TOK), jnp.float32)]),
        out_shape=jax.ShapeDtypeStruct(qkv.shape, jnp.bfloat16),
        compiler_params=pltpu.CompilerParams(vmem_limit_bytes=48*2**20),
    )(order, qkv, do, full, lse, cos, sin)


def matrix_starts():
    starts, total = [], 0
    for rows_in, cols_in in matrix_shapes():
        starts.append(total)
        total += rows_in // BLOCK * (cols_in // BLOCK)
    return starts, total


def block_view(ref, index, cols_in):
    across = cols_in // BLOCK
    row = pl.multiple_of(index // across * BLOCK, BLOCK)
    col = pl.multiple_of(index % across * BLOCK, BLOCK)
    return ref.at[pl.ds(row, BLOCK), pl.ds(col, BLOCK)]


def assemble_kernel(slot_ref, blocks_ref, *refs):
    held, sems, out_sems = refs[4:8], refs[8], refs[9]
    starts, _ = matrix_starts()
    for m, (rows_in, cols_in) in enumerate(matrix_shapes()):
        def one(i, carry):
            pltpu.make_async_copy(
                blocks_ref.at[slot_ref[starts[m] + i]], block_view(held[m], i, cols_in), sems.at[m]
            ).start()
            return carry

        lax.fori_loop(0, rows_in // BLOCK * (cols_in // BLOCK), one, 0)
    for m in range(4):
        pltpu.make_async_copy(held[m], held[m], sems.at[m]).wait()
        pltpu.make_async_copy(held[m], refs[m], out_sems.at[m]).start()
    for m in range(4):
        pltpu.make_async_copy(held[m], refs[m], out_sems.at[m]).wait()


def held_matrices():
    return [pltpu.VMEM(s, jnp.bfloat16) for s in matrix_shapes()]


def assemble(slots, blocks):
    anyspace = pl.BlockSpec(memory_space=pl.ANY)
    return pl.pallas_call(
        assemble_kernel,
        in_specs=[pl.BlockSpec(memory_space=pltpu.SMEM), anyspace],
        out_specs=[anyspace] * 4,
        out_shape=[jax.ShapeDtypeStruct(s, jnp.bfloat16) for s in matrix_shapes()],
        scratch_shapes=held_matrices() + [pltpu.SemaphoreType.DMA((4,)), pltpu.SemaphoreType.DMA((4,))],
        compiler_params=pltpu.CompilerParams(vmem_limit_bytes=40 * 2**20),
    )(slots, blocks)


def disassemble_kernel(slot_ref, *refs):
    out_ref, held, sem, in_sems = refs[4], refs[5:9], refs[9], refs[10]
    starts, _ = matrix_starts()
    for m in range(4):
        pltpu.make_async_copy(refs[m], held[m], in_sems.at[m]).start()
    for m, (rows_in, cols_in) in enumerate(matrix_shapes()):
        pltpu.make_async_copy(refs[m], held[m], in_sems.at[m]).wait()
        def one(i, carry):
            pltpu.make_async_copy(
                block_view(held[m], i, cols_in), out_ref.at[slot_ref[starts[m] + i]], sem.at[0]
            ).start()
            return carry

        lax.fori_loop(0, rows_in // BLOCK * (cols_in // BLOCK), one, 0)
    pltpu.make_async_copy(out_ref, out_ref, sem.at[0]).wait()


def disassemble(slots, matrices):
    anyspace = pl.BlockSpec(memory_space=pl.ANY)
    return pl.pallas_call(
        disassemble_kernel,
        in_specs=[pl.BlockSpec(memory_space=pltpu.SMEM)] + [anyspace] * 4,
        out_specs=anyspace,
        out_shape=jax.ShapeDtypeStruct((matrix_starts()[1], BLOCK, BLOCK), jnp.bfloat16),
        scratch_shapes=held_matrices() + [pltpu.SemaphoreType.DMA((1,)), pltpu.SemaphoreType.DMA((4,))],
        compiler_params=pltpu.CompilerParams(vmem_limit_bytes=40 * 2**20),
    )(slots, *matrices)


def turn(values, cosine, sine):
    first, second = values[:, : HEAD_DIM // 2], values[:, HEAD_DIM // 2 :]
    return jnp.concatenate(
        [first * cosine - second * sine, first * sine + second * cosine], axis=1
    )


def rope_columns(frame_ids):
    pairs = HEAD_DIM // 2
    time_pairs = pairs // 4
    row_pairs = (pairs - time_pairs) // 2
    column_pairs = pairs - time_pairs - row_pairs
    shape = (frame_ids.shape[0], pairs, GRID * GRID)
    token = jnp.arange(GRID * GRID, dtype=jnp.int32)
    groups = (
        (time_pairs, frame_ids[:, None, None].astype(jnp.float32)),
        (row_pairs, (token // GRID)[None, None, :].astype(jnp.float32)),
        (column_pairs, (token % GRID)[None, None, :].astype(jnp.float32)),
    )
    angles = jnp.concatenate(
        [
            jnp.broadcast_to(pos * frequencies(n)[None, :, None], (shape[0], n, shape[2]))
            for n, pos in groups
        ],
        axis=1,
    )
    return (jnp.cos(angles), jnp.sin(angles))


def on_grid(
    clean,
    noise,
    levels,
    flags,
    frame_map,
    block_slot,
    step_count,
    mat_weight,
    mat_ema,
    stat_left,
    stat_right,
    root_left,
    root_right,
    mod_table,
    mod_mom,
    mod_var,
    mod_ema,
    io_weight,
    io_mom,
    io_var,
    io_ema,
):
    axes = ("frame", "rep")
    tok_frame = GRID * GRID
    level_now = levels[0, 0] * (1 - flags[0, 0])
    noised = (1 - flags[0, 0]).astype(jnp.float32)
    meta = jnp.concatenate(
        [
            jnp.full((1, 128), noised),
            jnp.full((7, 128), level_now.astype(jnp.float32)),
        ]
    )
    gathered, meta_all = gather_weights(mat_weight.astype(jnp.bfloat16), meta)
    slots = jnp.zeros_like(block_slot).at[block_slot].set(
        jnp.arange(block_slot.shape[0], dtype=jnp.int32)
    )
    attn_w, out_w, up_w, down_w = assemble(slots, gathered.reshape(-1, BLOCK, BLOCK))
    noised_total = jnp.maximum(jnp.sum(meta_all[:, 0, 0]), 1.0)
    selector = (
        meta_all[:, 1, 0].astype(jnp.int32)[None, :] == jnp.arange(LEVELS, dtype=jnp.int32)[:, None]
    ).astype(jnp.float32)
    clip_map = lax.dynamic_index_in_dim(frame_map, lax.axis_index("rep"), 0, keepdims=False)
    my_frame = lax.dynamic_slice_in_dim(clip_map, lax.axis_index("frame"), 1)
    order = jnp.zeros_like(clip_map).at[clip_map].set(
        jnp.arange(clip_map.shape[0], dtype=jnp.int32)
    )
    fraction = level_now.astype(jnp.float32) / LEVELS
    frames_in = (
        jnp.cos(0.5 * jnp.pi * fraction) * clean[0, 0] + jnp.sin(0.5 * jnp.pi * fraction) * noise[0, 0]
    )
    inputs = frames_in.T.astype(jnp.bfloat16)
    targets = noise[0, 0].T
    modulation = lax.dynamic_index_in_dim(mod_table, level_now, 0, keepdims=False).reshape(8, 1, D)
    io_low = io_weight.astype(jnp.bfloat16)
    embed = io_low[:PIN]
    head = io_low[PIN : 2 * PIN]
    start = matmul(inputs, embed) + io_weight[2 * PIN]
    hat_one, inv_one = layer_norm(start)
    normed = (hat_one * (1 + modulation[1]) + modulation[0]).astype(jnp.bfloat16)
    projected = dotg(attn_w, normed, 0, 1)
    cosine, sine = rope_columns(clip_map)
    my_cos = lax.dynamic_index_in_dim(cosine, lax.axis_index("frame"), 0, keepdims=False)
    my_sin = lax.dynamic_index_in_dim(sine, lax.axis_index("frame"), 0, keepdims=False)
    parts = projected.reshape(3, HEADS, HEAD_DIM, tok_frame)
    parts = jnp.stack(
        [turn(parts[0], my_cos, my_sin), turn(parts[1], my_cos, my_sin), parts[2]], axis=1
    ).astype(jnp.bfloat16)
    mine = lax.all_to_all(parts, "frame", 0, 0, tiled=True)
    low, full, lse = attend(order, mine)
    attended = lax.all_to_all(low, "frame", 0, 0, tiled=True).reshape(D, tok_frame)
    branch = dotg(attended, out_w, 0, 0)
    middle = start + modulation[2] * branch
    hat_two, inv_two = layer_norm(middle)
    normed_two = (hat_two * (1 + modulation[4]) + modulation[3]).astype(jnp.bfloat16)
    upper = matmul(normed_two, up_w)
    activated = jax.nn.gelu(upper, approximate=True).astype(jnp.bfloat16)
    lower = matmul(activated, down_w)
    final = middle + modulation[5] * lower
    hat_three, inv_three = layer_norm(final)
    normed_three = (hat_three * (1 + modulation[7]) + modulation[6]).astype(jnp.bfloat16)
    predicted = matmul(normed_three, head.T)
    inv_scale = 1.0 / (noised_total * tok_frame * PIN)
    difference = predicted - targets
    loss_part = jnp.sum(noised * difference * difference) * inv_scale
    grad_pred = (2.0 * inv_scale * noised * difference).astype(jnp.bfloat16)
    grad_head = dotg(grad_pred, normed_three, 0, 0)
    grad_norm_three = matmul(grad_pred, head)
    grad_final = norm_back(grad_norm_three * (1 + modulation[7]), hat_three, inv_three)
    grad_lower = (grad_final * modulation[5]).astype(jnp.bfloat16)
    grad_down = dotg(activated, grad_lower, 0, 0).astype(jnp.bfloat16)
    grad_upper = gelu_back(upper, matmul(grad_lower, down_w.T)).astype(jnp.bfloat16)
    grad_up = dotg(normed_two, grad_upper, 0, 0).astype(jnp.bfloat16)
    grad_norm_two = matmul(grad_upper, up_w.T)
    grad_middle = grad_final + norm_back(grad_norm_two * (1 + modulation[4]), hat_two, inv_two)
    grad_branch = (grad_middle * modulation[2]).astype(jnp.bfloat16)
    grad_out_w = jnp.dot(attended, grad_branch, preferred_element_type=jnp.float32).astype(jnp.bfloat16)
    grad_heads = dotg(out_w, grad_branch, 1, 1).astype(jnp.bfloat16)
    grad_mine = lax.all_to_all(
        grad_heads.reshape(HEADS, HEAD_DIM, tok_frame), "frame", 0, 0, tiled=True
    )
    back = attend_back(order, mine, grad_mine, full, lse, cosine, sine)
    grad_proj = (
        lax.all_to_all(back, "frame", 0, 0, tiled=True).swapaxes(0, 1).reshape(3 * D, tok_frame)
    )
    grad_attn_w = dotg(normed, grad_proj, 0, 1).astype(jnp.bfloat16)
    grad_norm_one = dotg(grad_proj, attn_w, 0, 1)
    grad_start = grad_middle + norm_back(grad_norm_one * (1 + modulation[1]), hat_one, inv_one)
    grad_start_low = grad_start.astype(jnp.bfloat16)
    grad_embed = dotg(inputs, grad_start_low, 0, 0)
    grad_bias = jnp.sum(grad_start_low.astype(jnp.float32), axis=0)
    mod_terms = [
        grad_norm_one,
        grad_norm_one * hat_one,
        grad_middle * branch,
        grad_norm_two,
        grad_norm_two * hat_two,
        grad_final * lower,
        grad_norm_three,
        grad_norm_three * hat_three,
    ]
    mod_grads = jnp.concatenate([jnp.sum(term, axis=0) for term in mod_terms])[None]
    mod_rows = lax.all_gather(mod_grads, axes, axis=0, tiled=True)
    grad_table = jnp.dot(selector, mod_rows, precision=TOP_PRECISION)
    grad_io = jnp.concatenate([grad_embed, grad_head, grad_bias[None, :]], axis=0)
    grad_io, total_loss = lax.psum((grad_io, loss_part), axes)
    grad_blocks = disassemble(slots, (grad_attn_w, grad_out_w, grad_up, grad_down))
    owned = scatter_grads(grad_blocks.reshape(32, -1, BLOCK, BLOCK))
    block_limit = CLIP_NORM * BLOCK * NPARAMS ** (-0.5)
    block_norm = jnp.sqrt(jnp.sum(owned * owned, axis=(1, 2), keepdims=True))
    mat_grad = owned * (block_limit / jnp.maximum(block_norm, block_limit))
    grad_norm = jnp.sqrt(jnp.sum(grad_table * grad_table) + jnp.sum(grad_io * grad_io))
    factor = CLIP_NORM / jnp.maximum(grad_norm, CLIP_NORM)
    new_mat_weight, new_stat_left, new_stat_right, new_mat_ema = shampoo(
        mat_grad, mat_weight, mat_ema, stat_left, stat_right, root_left, root_right
    )
    step = step_count[0].astype(jnp.float32)
    new_mod = adamw(grad_table * factor, mod_table, mod_mom, mod_var, mod_ema, step)
    new_io = adamw(grad_io * factor, io_weight, io_mom, io_var, io_ema, step)
    return (
        total_loss * noised_total,
        noised_total,
        grad_norm,
        mat_grad,
        new_mat_weight,
        new_stat_left,
        new_stat_right,
        new_mat_ema,
        new_mod[0],
        new_mod[1],
        new_mod[2],
        new_mod[3],
        new_io[0],
        new_io[1],
        new_io[2],
        new_io[3],
    )


def solution(mesh):
    tuned = dict(mesh.shape) == {"frame": 16, "rep": 2}
    body = on_grid if tuned else on_device
    in_specs = (
        P("rep", "frame", None, None),
        P("rep", "frame", None, None),
        P("rep", "frame"),
        P("rep", "frame"),
        P(),
        P(),
        P(),
        P(("frame", "rep"), None, None),
        P(("frame", "rep"), None, None),
        P(("frame", "rep"), None, None),
        P(("frame", "rep"), None, None),
        P(("frame", "rep"), None, None),
        P(("frame", "rep"), None, None),
        P(),
        P(),
        P(),
        P(),
        P(),
        P(),
        P(),
        P(),
    )
    out_specs = (
        P(),
        P(),
        P(),
        P(("frame", "rep"), None, None),
        P(("frame", "rep"), None, None),
        P(("frame", "rep"), None, None),
        P(("frame", "rep"), None, None),
        P(("frame", "rep"), None, None),
        P(),
        P(),
        P(),
        P(),
        P(),
        P(),
        P(),
        P(),
    )
    return jax.shard_map(
        body, mesh=mesh, in_specs=in_specs, out_specs=out_specs, check_vma=False
    )
```

```python
from functools import partial
import math

import jax
import jax.numpy as jnp
from jax import lax
from jax.experimental import pallas as pl
from jax.experimental.pallas import tpu as pltpu
from jax.sharding import PartitionSpec as P

D = 1024
HEADS = 16
HEAD_DIM = 64
FFN = 4096
PIN = 16
GRID = 16
BLOCK = 128
LEVELS = 32
FR_DEV = 1
NPARAMS = 12878848


LN_EPS = 1e-06
ROPE_BASE = 10000.0
CLIP_NORM = 0.01
BETA_ONE = 0.9
BETA_TWO = 0.999
ADAM_EPS = 1e-08
ADAM_RATE = 0.1
DECAY_RATE = 0.1
STAT_BETA = 0.95
SHAMPOO_RATE = 0.01
EMA_DECAY = 0.9
TOP_PRECISION = lax.Precision.HIGHEST


def matmul(left, right):
    return jnp.dot(left, right, preferred_element_type=jnp.float32)


def layer_norm(hidden):
    centered = hidden - jnp.mean(hidden, axis=-1, keepdims=True)
    inverse = lax.rsqrt(jnp.mean(centered * centered, axis=-1, keepdims=True) + LN_EPS)
    return (centered * inverse, inverse)


def norm_back(grad_hat, normed, inverse):
    return inverse * (
        grad_hat
        - jnp.mean(grad_hat, axis=-1, keepdims=True)
        - normed * jnp.mean(grad_hat * normed, axis=-1, keepdims=True)
    )


def gelu_back(upper, grad_act):
    return jax.vjp(partial(jax.nn.gelu, approximate=True), upper)[1](grad_act)[0]


def frequencies(width):
    return ROPE_BASE ** (-jnp.arange(width, dtype=jnp.float32) / width)


def rope_tables(frame_ids):
    pairs = HEAD_DIM // 2
    time_pairs = pairs // 4
    row_pairs = (pairs - time_pairs) // 2
    column_pairs = pairs - time_pairs - row_pairs
    frames = frame_ids.shape[0]
    tok_frame = GRID * GRID
    token_pos = jnp.arange(tok_frame, dtype=jnp.int32)
    row_pos = (token_pos // GRID).astype(jnp.float32)
    column_pos = (token_pos % GRID).astype(jnp.float32)
    time_angle = (
        frame_ids.astype(jnp.float32)[:, None, None] * frequencies(time_pairs)[None, None, :]
    )
    row_angle = row_pos[None, :, None] * frequencies(row_pairs)[None, None, :]
    column_angle = column_pos[None, :, None] * frequencies(column_pairs)[None, None, :]
    angles = jnp.concatenate(
        [jnp.broadcast_to(time_angle, (frames, tok_frame, time_pairs)), row_angle, column_angle],
        axis=-1,
    )
    angles = angles.reshape(frames * tok_frame, pairs)
    return (jnp.cos(angles), jnp.sin(angles))


def rotate(values, cosine, sine):
    pairs = HEAD_DIM // 2
    first, second = (values[..., :pairs], values[..., pairs:])
    cosine = cosine[:, None, :]
    sine = sine[:, None, :]
    return jnp.concatenate(
        [first * cosine - second * sine, first * sine + second * cosine], axis=-1
    )


def split_heads(flat):
    return flat.reshape(flat.shape[0], HEADS, HEAD_DIM)


def matrix_shapes():
    return ((D, 3 * D), (D, D), (D, FFN), (FFN, D))


def from_blocks(natural):
    matrices = []
    offset = 0
    for rows_in, cols_in in matrix_shapes():
        count_in = rows_in // BLOCK * (cols_in // BLOCK)
        part_blocks = natural[offset : offset + count_in]
        matrices.append(
            part_blocks.reshape(rows_in // BLOCK, cols_in // BLOCK, BLOCK, BLOCK)
            .transpose(0, 2, 1, 3)
            .reshape(rows_in, cols_in)
        )
        offset = offset + count_in
    return matrices


def to_blocks(matrix):
    rows_in, cols_in = matrix.shape
    return (
        matrix.reshape(rows_in // BLOCK, BLOCK, cols_in // BLOCK, BLOCK)
        .transpose(0, 2, 1, 3)
        .reshape(-1, BLOCK, BLOCK)
    )


def score_block(queries, key_block, query_frames, key_frames):
    scores = jnp.einsum(
        "qhd,khd->hqk", queries, key_block, preferred_element_type=jnp.float32
    ) * HEAD_DIM ** (-0.5)
    visible = key_frames[None, None, :] <= query_frames[None, :, None]
    return jnp.where(visible, scores, -jnp.inf)


def stack_keys(key_rows, value_rows, frame_rows):
    total_rows = key_rows.shape[0]
    block_rows = math.gcd(total_rows, 512)
    blocks = total_rows // block_rows
    return (
        (
            key_rows.reshape(blocks, block_rows, HEADS, HEAD_DIM),
            value_rows.reshape(blocks, block_rows, HEADS, HEAD_DIM),
            frame_rows.reshape(blocks, block_rows),
        ),
        block_rows,
    )


def keep_state(previous):
    return previous


def fold_keys(state, shard_rows, queries, query_frames, key_frames_all):
    key_rows, value_rows = shard_rows
    stacks, block_rows = stack_keys(key_rows, value_rows, key_frames_all)
    top_query = jnp.max(query_frames)

    def fold_step_block(carried, block_in):
        key_block, value_block, key_frames = block_in

        def fold_compute(previous):
            running, denominator, accumulated = previous
            scores = score_block(queries, key_block, query_frames, key_frames)
            new_max = jnp.maximum(running, jnp.max(scores, axis=-1))
            weights = jnp.exp(scores - new_max[..., None])
            rescale = jnp.exp(running - new_max)
            contrib = jnp.einsum(
                "hqk,khd->hqd",
                weights.astype(jnp.bfloat16),
                value_block,
                preferred_element_type=jnp.float32,
            )
            return (
                new_max,
                denominator * rescale + jnp.sum(weights, axis=-1),
                accumulated * rescale[..., None] + contrib,
            )

        return (lax.cond(jnp.min(key_frames) <= top_query, fold_compute, keep_state, carried), None)

    state, unused = lax.scan(fold_step_block, state, stacks)
    return state


def grad_parts(
    queries, grad_heads, delta, log_total, query_frames, key_block, value_block, key_frames
):
    probs = jnp.exp(
        score_block(queries, key_block, query_frames, key_frames) - log_total[..., None]
    )
    grad_probs = jnp.einsum(
        "qhd,khd->hqk", grad_heads, value_block, preferred_element_type=jnp.float32
    )
    grad_scores = (probs * (grad_probs - delta[..., None])).astype(jnp.bfloat16)
    return (probs, grad_scores)


def key_value_block(
    queries, grad_heads, delta, log_total, query_frames, key_block, value_block, key_frames
):
    block_rows = key_block.shape[0]
    probs, grad_scores = grad_parts(
        queries, grad_heads, delta, log_total, query_frames, key_block, value_block, key_frames
    )
    key_grad = jnp.einsum(
        "hqk,qhd->khd", grad_scores, queries, preferred_element_type=jnp.float32
    ) * HEAD_DIM ** (-0.5)
    value_grad = jnp.einsum(
        "hqk,qhd->khd", probs.astype(jnp.bfloat16), grad_heads, preferred_element_type=jnp.float32
    )
    return jnp.concatenate(
        [key_grad.reshape(block_rows, D), value_grad.reshape(block_rows, D)], axis=1
    )


def query_grads(
    queries, grad_heads, delta, log_total, query_frames, key_all, value_all, key_frames_all
):
    stacks, block_rows = stack_keys(key_all, value_all, key_frames_all)
    top_query = jnp.max(query_frames)

    def query_step_block(carried, block_in):
        key_block, value_block, key_frames = block_in

        def query_compute(previous):
            probs, grad_scores = grad_parts(
                queries,
                grad_heads,
                delta,
                log_total,
                query_frames,
                key_block,
                value_block,
                key_frames,
            )
            return previous + jnp.einsum(
                "hqk,khd->qhd", grad_scores, key_block, preferred_element_type=jnp.float32
            )

        return (
            lax.cond(jnp.min(key_frames) <= top_query, query_compute, keep_state, carried),
            None,
        )

    initial = jnp.zeros(queries.shape, jnp.float32)
    result, unused = lax.scan(query_step_block, initial, stacks)
    return result * HEAD_DIM ** (-0.5)


def key_terms(
    row_count,
    queries,
    grad_heads,
    delta,
    log_total,
    query_frames,
    key_all,
    value_all,
    key_frames_all,
):
    stacks, block_rows = stack_keys(key_all, value_all, key_frames_all)
    top_query = jnp.max(query_frames)

    def one_block(block_in):
        key_block, value_block, key_frames = block_in

        def one_compute(unused):
            return key_value_block(
                queries,
                grad_heads,
                delta,
                log_total,
                query_frames,
                key_block,
                value_block,
                key_frames,
            )

        def nothing(unused):
            return jnp.zeros((block_rows, 2 * D), jnp.float32)

        return lax.cond(jnp.min(key_frames) <= top_query, one_compute, nothing, 0)

    return lax.map(one_block, stacks).reshape(row_count, 2 * D)


def shampoo(grads, weights, average, left, right, left_root, right_root):
    new_left = STAT_BETA * left + (1 - STAT_BETA) * jnp.einsum(
        "bij,bkj->bik", grads, grads, precision=TOP_PRECISION
    )
    new_right = STAT_BETA * right + (1 - STAT_BETA) * jnp.einsum(
        "bji,bjk->bik", grads, grads, precision=TOP_PRECISION
    )
    direction = jnp.einsum("bij,bjk->bik", left_root, grads, precision=TOP_PRECISION)
    direction = jnp.einsum("bij,bjk->bik", direction, right_root, precision=TOP_PRECISION)
    direction = direction * lax.rsqrt(
        jnp.mean(direction * direction, axis=(1, 2), keepdims=True) + 1e-06
    )
    new_weights = weights - SHAMPOO_RATE * (direction + DECAY_RATE * weights)
    new_average = EMA_DECAY * average + (1 - EMA_DECAY) * new_weights
    return (new_weights, new_left, new_right, new_average)


def adamw(grads, weights, first, second, average, step):
    new_first = BETA_ONE * first + (1 - BETA_ONE) * grads
    new_second = BETA_TWO * second + (1 - BETA_TWO) * grads * grads
    first_hat = new_first / (1 - BETA_ONE**step)
    second_hat = new_second / (1 - BETA_TWO**step)
    new_weights = weights - ADAM_RATE * (
        first_hat / (jnp.sqrt(second_hat) + ADAM_EPS) + DECAY_RATE * weights
    )
    new_average = EMA_DECAY * average + (1 - EMA_DECAY) * new_weights
    return (new_weights, new_first, new_second, new_average)


def on_device(
    clean,
    noise,
    levels,
    flags,
    frame_map,
    block_slot,
    step_count,
    mat_weight,
    mat_ema,
    stat_left,
    stat_right,
    root_left,
    root_right,
    mod_table,
    mod_mom,
    mod_var,
    mod_ema,
    io_weight,
    io_mom,
    io_var,
    io_ema,
):
    tok_frame = GRID * GRID
    local_rows = FR_DEV * tok_frame
    noised = (1 - flags[0]).astype(jnp.float32)
    noised_total = jnp.maximum(lax.psum(jnp.sum(noised), ("frame", "rep")), 1.0)
    gathered = lax.all_gather(mat_weight.astype(jnp.bfloat16), ("frame", "rep"), axis=0, tiled=True)
    natural = jnp.zeros_like(gathered).at[block_slot].set(gathered)
    attn_w, out_w, up_w, down_w = from_blocks(natural)
    clip_map = lax.dynamic_index_in_dim(frame_map, lax.axis_index("rep"), 0, keepdims=False)
    my_frames = lax.dynamic_slice_in_dim(clip_map, lax.axis_index("frame") * FR_DEV, FR_DEV)
    key_frames_all = jnp.repeat(clip_map, tok_frame)
    query_frames = jnp.repeat(my_frames, tok_frame)
    level_now = levels[0] * (1 - flags[0])
    fraction = level_now.astype(jnp.float32) / LEVELS
    keep_coef = jnp.cos(0.5 * jnp.pi * fraction)
    noise_coef = jnp.sin(0.5 * jnp.pi * fraction)
    frames_in = keep_coef[:, None, None] * clean[0] + noise_coef[:, None, None] * noise[0]
    inputs = jnp.swapaxes(frames_in, 1, 2).reshape(local_rows, PIN).astype(jnp.bfloat16)
    targets = jnp.swapaxes(noise[0], 1, 2).reshape(local_rows, PIN)
    selector = (level_now[:, None] == jnp.arange(LEVELS, dtype=jnp.int32)[None, :]).astype(
        jnp.float32
    )
    modulation = jnp.dot(selector, mod_table, precision=TOP_PRECISION).reshape(FR_DEV, 8, 1, D)
    io_low = io_weight.astype(jnp.bfloat16)
    embed = io_low[:PIN]
    head = io_low[PIN : 2 * PIN]
    start = (matmul(inputs, embed) + io_weight[2 * PIN]).reshape(FR_DEV, tok_frame, D)
    hat_one, inv_one = layer_norm(start)
    normed = (
        (hat_one * (1 + modulation[:, 1]) + modulation[:, 0])
        .reshape(local_rows, D)
        .astype(jnp.bfloat16)
    )
    projected = matmul(normed, attn_w)
    cosine, sine = rope_tables(my_frames)
    queries = rotate(split_heads(projected[:, :D]), cosine, sine).astype(jnp.bfloat16)
    key_flat = (
        rotate(split_heads(projected[:, D : 2 * D]), cosine, sine)
        .astype(jnp.bfloat16)
        .reshape(local_rows, D)
    )
    value_flat = projected[:, 2 * D :].astype(jnp.bfloat16)
    initial = (
        jnp.full((HEADS, local_rows), -1e30, jnp.float32),
        jnp.zeros((HEADS, local_rows), jnp.float32),
        jnp.zeros((HEADS, local_rows, HEAD_DIM), jnp.float32),
    )
    running, denominator, accumulated = fold_keys(
        initial,
        (
            lax.all_gather(key_flat, "frame", axis=0, tiled=True),
            lax.all_gather(value_flat, "frame", axis=0, tiled=True),
        ),
        queries,
        query_frames,
        key_frames_all,
    )
    attended = jnp.transpose(accumulated / denominator[..., None], (1, 0, 2)).reshape(local_rows, D)
    log_total = running + jnp.log(denominator)
    attended_low = attended.astype(jnp.bfloat16)
    branch = matmul(attended_low, out_w).reshape(FR_DEV, tok_frame, D)
    middle = start + modulation[:, 2] * branch
    hat_two, inv_two = layer_norm(middle)
    normed_two = (
        (hat_two * (1 + modulation[:, 4]) + modulation[:, 3])
        .reshape(local_rows, D)
        .astype(jnp.bfloat16)
    )
    upper = matmul(normed_two, up_w)
    activated = jax.nn.gelu(upper, approximate=True).astype(jnp.bfloat16)
    lower = matmul(activated, down_w).reshape(FR_DEV, tok_frame, D)
    final = middle + modulation[:, 5] * lower
    hat_three, inv_three = layer_norm(final)
    normed_three = (
        (hat_three * (1 + modulation[:, 7]) + modulation[:, 6])
        .reshape(local_rows, D)
        .astype(jnp.bfloat16)
    )
    predicted = matmul(normed_three, head.T)
    row_weight = jnp.repeat(noised, tok_frame)[:, None]
    inv_scale = 1.0 / (noised_total * tok_frame * PIN)
    difference = predicted - targets
    loss_part = jnp.sum(row_weight * difference * difference) * inv_scale
    grad_pred = (2.0 * inv_scale * row_weight * difference).astype(jnp.bfloat16)
    grad_head = jnp.dot(grad_pred.T, normed_three, preferred_element_type=jnp.float32)
    grad_norm_three = matmul(grad_pred, head).reshape(FR_DEV, tok_frame, D)
    grad_final = norm_back(grad_norm_three * (1 + modulation[:, 7]), hat_three, inv_three)
    grad_lower = (grad_final * modulation[:, 5]).reshape(local_rows, D).astype(jnp.bfloat16)
    grad_down = jnp.dot(activated.T, grad_lower, preferred_element_type=jnp.float32)
    grad_upper = gelu_back(upper, matmul(grad_lower, down_w.T)).astype(jnp.bfloat16)
    grad_up = jnp.dot(normed_two.T, grad_upper, preferred_element_type=jnp.float32)
    grad_norm_two = matmul(grad_upper, up_w.T).reshape(FR_DEV, tok_frame, D)
    grad_middle = grad_final + norm_back(grad_norm_two * (1 + modulation[:, 4]), hat_two, inv_two)
    grad_branch = (grad_middle * modulation[:, 2]).reshape(local_rows, D).astype(jnp.bfloat16)
    grad_out_w = jnp.dot(attended_low.T, grad_branch, preferred_element_type=jnp.float32)
    grad_heads = split_heads(matmul(grad_branch, out_w.T).astype(jnp.bfloat16))
    delta = jnp.sum(grad_heads.astype(jnp.float32) * split_heads(attended), axis=-1).T
    key_all, value_all = (
        lax.all_gather(key_flat, "frame", axis=0, tiled=True),
        lax.all_gather(value_flat, "frame", axis=0, tiled=True),
    )
    grad_query = query_grads(
        queries, grad_heads, delta, log_total, query_frames, key_all, value_all, key_frames_all
    )
    key_value_grad = lax.psum_scatter(
        key_terms(
            lax.axis_size("frame") * local_rows,
            queries,
            grad_heads,
            delta,
            log_total,
            query_frames,
            key_all,
            value_all,
            key_frames_all,
        ),
        "frame",
        scatter_dimension=0,
        tiled=True,
    )
    grad_q = rotate(grad_query, cosine, -sine).reshape(local_rows, D)
    grad_k = rotate(split_heads(key_value_grad[:, :D]), cosine, -sine).reshape(local_rows, D)
    grad_proj = jnp.concatenate([grad_q, grad_k, key_value_grad[:, D:]], axis=1).astype(
        jnp.bfloat16
    )
    grad_attn_w = jnp.dot(normed.T, grad_proj, preferred_element_type=jnp.float32)
    grad_norm_one = matmul(grad_proj, attn_w.T).reshape(FR_DEV, tok_frame, D)
    grad_start = grad_middle + norm_back(grad_norm_one * (1 + modulation[:, 1]), hat_one, inv_one)
    grad_start_low = grad_start.reshape(local_rows, D).astype(jnp.bfloat16)
    grad_embed = jnp.dot(inputs.T, grad_start_low, preferred_element_type=jnp.float32)
    grad_bias = jnp.sum(grad_start_low.astype(jnp.float32), axis=0)
    mod_terms = [
        grad_norm_one,
        grad_norm_one * hat_one,
        grad_middle * branch,
        grad_norm_two,
        grad_norm_two * hat_two,
        grad_final * lower,
        grad_norm_three,
        grad_norm_three * hat_three,
    ]
    mod_grads = jnp.stack([jnp.sum(term, axis=1) for term in mod_terms], axis=1).reshape(
        FR_DEV, 8 * D
    )
    grad_table = jnp.dot(selector.T, mod_grads, precision=TOP_PRECISION)
    grad_io = jnp.concatenate([grad_embed, grad_head, grad_bias[None, :]], axis=0)
    grad_table, grad_io, total_loss = lax.psum((grad_table, grad_io, loss_part), ("frame", "rep"))
    grad_blocks = jnp.concatenate(
        [to_blocks(grad_attn_w), to_blocks(grad_out_w), to_blocks(grad_up), to_blocks(grad_down)], 0
    )
    owned = lax.psum_scatter(
        grad_blocks[block_slot], ("frame", "rep"), scatter_dimension=0, tiled=True
    )
    block_limit = CLIP_NORM * BLOCK * NPARAMS ** (-0.5)
    block_norm = jnp.sqrt(jnp.sum(owned * owned, axis=(1, 2), keepdims=True))
    mat_grad = owned * (block_limit / jnp.maximum(block_norm, block_limit))
    grad_norm = jnp.sqrt(jnp.sum(grad_table * grad_table) + jnp.sum(grad_io * grad_io))
    factor = CLIP_NORM / jnp.maximum(grad_norm, CLIP_NORM)
    new_mat_weight, new_stat_left, new_stat_right, new_mat_ema = shampoo(
        mat_grad, mat_weight, mat_ema, stat_left, stat_right, root_left, root_right
    )
    step = step_count[0].astype(jnp.float32)
    new_mod = adamw(grad_table * factor, mod_table, mod_mom, mod_var, mod_ema, step)
    new_io = adamw(grad_io * factor, io_weight, io_mom, io_var, io_ema, step)
    return (
        total_loss * noised_total,
        noised_total,
        grad_norm,
        mat_grad,
        new_mat_weight,
        new_stat_left,
        new_stat_right,
        new_mat_ema,
        new_mod[0],
        new_mod[1],
        new_mod[2],
        new_mod[3],
        new_io[0],
        new_io[1],
        new_io[2],
        new_io[3],
    )


MESH = pl.DeviceIdType.MESH
NSLOT = 24
DATA = NSLOT
SMALL_ROWS = 40
GATHER_PARTS = (
    ("xzy", 0, 4),
    ("xzy", 4, 4),
    ("yzx", 8, 4),
    ("yzx", 12, 4),
    ("zxy", 16, 4),
    ("zyx", 20, 5),
)
SCATTER_PARTS = (
    ("xzy", 0, 4),
    ("xzy", 4, 4),
    ("yzx", 8, 4),
    ("yzx", 12, 4),
    ("zxy", 16, 4),
    ("zyx", 20, 4),
)


def place():
    frame = lax.axis_index("frame")
    return frame // 4, (frame // 2) % 2, frame % 2, lax.axis_index("rep")


def device(z, y, c, x):
    return ((z * 2 + y) * 2 + c, x)


def owner_of(z, y, c, x):
    return ((z * 2 + y) * 2 + c) * 2 + x


def plane_of(z, y, x):
    return (z * 2 + y) * 2 + x


def offsets():
    return [(dx, dy, dz) for dx in (0, 1) for dy in (0, 1) for dz in range(-3, 4)]


def hops(off):
    return off[0] + off[1] + abs(off[2])


def route_keys(parts):
    keys = [(part, off) for part in range(len(parts)) for off in offsets()]
    return sorted(keys, key=lambda k: (hops(k[1]), k[0]))


def onward(order, off):
    moved = dict(zip("xyz", off))
    last = max((order.index(k) for k in order if moved[k]), default=-1)
    links = []
    if last >= 0 and order[last] == "z":
        links.append("u" if off[2] < 0 else "w")
    for k in order[last + 1 :]:
        links.extend("uw" if k == "z" else k)
    return links


def toward(order, off):
    moved = dict(zip("xyz", off))
    last = [k for k in order if moved[k]][-1]
    if last == "z":
        return ("w", "u") if off[2] < 0 else ("u", "w")
    return last, last


def can(link, z):
    return {"u": z < 3, "w": z > 0}.get(link)


def partner(link, z, y, c, x):
    return {
        "x": device(z, y, c, 1 - x),
        "y": device(z, 1 - y, c, x),
        "u": device(z + 1, y, c, x),
        "w": device(z - 1, y, c, x),
        "c": device(z, y, 1 - c, x),
    }[link]


def when(cond, fn):
    if cond is None:
        fn()
    else:
        pl.when(cond)(fn)


def both(a, b):
    return b if a is None else a if b is None else jnp.logical_and(a, b)


def owner_at(off, z, y, x):
    dx, dy, dz = off
    oz = z + dz
    cond = None if dz == 0 else (oz <= 3 if dz > 0 else oz >= 0)
    return oz, (1 - y if dy else y), (1 - x if dx else x), cond


def greet(z, y, c, x, far=()):
    barrier = pltpu.get_barrier_semaphore()
    for link in "xyuwc":
        when(
            can(link, z),
            lambda link=link: pl.semaphore_signal(
                barrier, inc=1, device_id=partner(link, z, y, c, x), device_id_type=MESH
            ),
        )
    for dev in far:
        pl.semaphore_signal(barrier, inc=1, device_id=dev, device_id_type=MESH)
    ends = jnp.logical_or(z == 0, z == 3)
    pl.when(ends)(lambda: pl.semaphore_wait(barrier, 4 + len(far)))
    pl.when(jnp.logical_not(ends))(lambda: pl.semaphore_wait(barrier, 5 + len(far)))


class Gather:
    def __init__(self, parts, src, out, sems, where, core=True):
        self.parts, self.src, self.out, self.where, self.core = parts, src, out, where, core
        self.send, self.recv, self.csend, self.crecv = sems
        self.keys = route_keys(parts)
        self.last = {}
        for key in self.keys:
            self.last[key[1]] = key
        self.sent = []

    @staticmethod
    def sems(parts):
        n = len(parts)
        return [
            pltpu.SemaphoreType.DMA((4, n, 16)),
            pltpu.SemaphoreType.DMA((n, 16)),
            pltpu.SemaphoreType.DMA((16,)),
            pltpu.SemaphoreType.DMA((16,)),
        ]

    def hop(self, link, part, src, owner, plane):
        _, first, count = self.parts[part]
        return pltpu.make_async_remote_copy(
            src_ref=src.at[pl.ds(first, count)],
            dst_ref=self.out.at[owner, pl.ds(first, count)],
            send_sem=self.send.at["xyuw".index(link), part, plane],
            recv_sem=self.recv.at[part, plane],
            device_id=partner(link, *self.where),
            device_id_type=MESH,
        )

    def across(self, src, owner, plane):
        return pltpu.make_async_remote_copy(
            src_ref=src,
            dst_ref=self.out.at[owner],
            send_sem=self.csend.at[plane],
            recv_sem=self.crecv.at[plane],
            device_id=partner("c", *self.where),
            device_id_type=MESH,
        )

    def step(self, key):
        part, off = key
        z, y, c, x = self.where
        oz, oy, ox, cond = owner_at(off, z, y, x)
        owner, plane = owner_of(oz, oy, c, ox), plane_of(oz, oy, ox)
        own = off == (0, 0, 0)
        src = self.src if own else self.out.at[owner]
        links = onward(self.parts[part][0], off)

        def act():
            if not own:
                self.hop("x", part, src, owner, plane).wait_recv()
            for link in links:
                when(can(link, z), lambda link=link: self.hop(link, part, src, owner, plane).start())
            if self.core and self.last[off] == key:
                self.across(src, owner, plane).start()

        when(cond, act)
        for link in links:
            self.sent.append(
                (both(cond, can(link, z)), lambda link=link: self.hop(link, part, src, owner, plane))
            )
        if self.core and self.last[off] == key:
            self.sent.append((cond, lambda: self.across(src, owner, plane)))

    def finish(self):
        for cond, make in self.sent:
            when(cond, lambda make=make: make().wait_send())
        if self.core:
            c = self.where[2]
            for plane in range(16):
                owner = owner_of(plane // 4, (plane // 2) % 2, 1 - c, plane % 2)
                self.across(self.out.at[owner], owner, plane).wait_recv()


def gather_kernel(perm_ref, w_ref, data_ref, out_ref, stage, local, *sems):
    where = place()
    z, y, c, x = where

    def take(i, carry):
        stage[i] = w_ref[perm_ref[i]].astype(jnp.bfloat16)
        return carry

    lax.fori_loop(0, NSLOT, take, 0)
    stage[DATA] = data_ref[...]
    greet(*where)
    own = pltpu.make_async_copy(stage, out_ref.at[owner_of(z, y, c, x)], local.at[0])
    own.start()
    gather = Gather(GATHER_PARTS, stage, out_ref, sems, where)
    for key in gather.keys:
        gather.step(key)
    gather.finish()
    own.wait()


def gather_weights(perm, blocks, data):
    vmem = pl.BlockSpec(memory_space=pltpu.VMEM)
    return pl.pallas_call(
        gather_kernel,
        out_shape=jax.ShapeDtypeStruct((32, NSLOT + 1, 128, 128), jnp.bfloat16),
        in_specs=[pl.BlockSpec(memory_space=pltpu.SMEM), vmem, vmem],
        out_specs=pl.BlockSpec(memory_space=pltpu.HBM),
        scratch_shapes=[
            pltpu.VMEM((NSLOT + 1, 128, 128), jnp.bfloat16),
            pltpu.SemaphoreType.DMA((1,)),
        ]
        + Gather.sems(GATHER_PARTS),
        compiler_params=pltpu.CompilerParams(
            collective_id=1, has_side_effects=True, vmem_limit_bytes=60 * 2**20
        ),
    )(perm, blocks, data)


def inbox_axes(order, link):
    dim = "z" if link in "uw" else link
    axes = order[: order.index(dim)]
    return axes + "z" if dim == "z" else axes


def inbox_starts(parts, link):
    starts, total = [], 0
    for order, _, count in parts:
        starts.append(total)
        size = count
        for d in inbox_axes(order, link):
            size *= 4 if d == "z" else 2
        total += size
    return starts, total


class Scatter:
    def __init__(self, parts, acc, sib, boxes, send, recvs, where, ready, store):
        self.parts, self.acc, self.sib, self.where = parts, acc, sib, where
        self.boxes = dict(zip("xyuw", boxes))
        self.recvs = dict(zip("xyuw", recvs))
        self.send, self.ready, self.store = send, ready, store
        self.keys = list(reversed(route_keys(parts)))
        self.seen = []
        for _, off in self.keys:
            if off not in self.seen:
                self.seen.append(off)
        self.fresh = set()

    @staticmethod
    def boxes_of(parts):
        return [
            pltpu.VMEM((inbox_starts(parts, link)[1], 128, 128), jnp.bfloat16) for link in "xyuw"
        ]

    @staticmethod
    def sems(parts):
        return [pltpu.SemaphoreType.DMA((len(parts), 16))] + [
            pltpu.SemaphoreType.DMA((len(parts), 16)) for _ in "xyuw"
        ]

    def inbox(self, link, part, oz, oy, ox):
        order, _, count = self.parts[part]
        index = 0
        for d in inbox_axes(order, link):
            index = index * (4 if d == "z" else 2) + {"z": oz, "y": oy, "x": ox}[d]
        return inbox_starts(self.parts, link)[0][part] + index * count

    def clear_ends(self):
        z = self.where[0]

        def clear(box):
            def body(i, carry):
                box[i] = jnp.zeros((128, 128), jnp.bfloat16)
                return carry

            lax.fori_loop(0, box.shape[0], body, 0)

        pl.when(z == 3)(lambda: clear(self.boxes["u"]))
        pl.when(z == 0)(lambda: clear(self.boxes["w"]))

    def hop(self, part, off):
        z, y, c, x = self.where
        oz, oy, ox, _ = owner_at(off, z, y, x)
        plane = plane_of(oz, oy, ox)
        order, first, count = self.parts[part]
        link, named = toward(order, off)
        return pltpu.make_async_remote_copy(
            src_ref=self.acc.at[plane, pl.ds(first, count)],
            dst_ref=self.boxes[named].at[pl.ds(self.inbox(named, part, oz, oy, ox), count)],
            send_sem=self.send.at[part, plane],
            recv_sem=self.recvs[named].at[part, plane],
            device_id=partner(link, *self.where),
            device_id_type=MESH,
        )

    def step(self, key):
        part, off = key
        z, y, c, x = self.where
        oz, oy, ox, cond = owner_at(off, z, y, x)
        plane = plane_of(oz, oy, ox)
        order, first, count = self.parts[part]
        new = off not in self.fresh
        self.fresh.add(off)

        def act():
            if new:
                self.ready(oz, oy, ox)
            sources = []
            for link in onward(order, off):
                start = self.inbox(link, part, oz, oy, ox)
                sources.append((self.boxes[link], start))

                def arrive(link=link, start=start):
                    view = self.boxes[link].at[pl.ds(start, count)]
                    pltpu.make_async_remote_copy(
                        src_ref=view,
                        dst_ref=view,
                        send_sem=self.send.at[part, plane],
                        recv_sem=self.recvs[link].at[part, plane],
                        device_id=partner("c", *self.where),
                        device_id_type=MESH,
                    ).wait_recv()

                when(can(link, z), arrive)

            def add(i, carry):
                total = self.acc[plane, first + i].astype(jnp.float32) + self.sib[
                    plane, first + i
                ].astype(jnp.float32)
                for box, start in sources:
                    total = total + box[start + i].astype(jnp.float32)
                if off == (0, 0, 0):
                    self.store(first + i, total)
                else:
                    self.acc[plane, first + i] = total.astype(jnp.bfloat16)
                return carry

            lax.fori_loop(0, count, add, 0)
            if off != (0, 0, 0):
                self.hop(part, off).start()

        when(cond, act)

    def finish(self):
        z, y, c, x = self.where
        for part, off in self.keys:
            if off != (0, 0, 0):
                cond = owner_at(off, z, y, x)[3]
                when(cond, lambda part=part, off=off: self.hop(part, off).wait_send())


class SmallSums:
    def __init__(self, row, io, rows_out, io_out, mine, inbox, sems, where):
        self.row, self.io, self.rows, self.io_out = row, io, rows_out, io_out
        self.mine, self.inbox, self.where = mine, inbox, where
        self.gsend, self.grecv, self.osend, self.orecv, self.bsend, self.brecv, self.local = sems
        self.order = "zyx"
        self.sent = []

    @staticmethod
    def sems():
        dma = pltpu.SemaphoreType.DMA
        return [dma((4, 16)), dma((16,)), dma((6,)), dma((6,)), dma((1,)), dma((1,)), dma((1,))]

    def far(self):
        z, y, c, x = self.where
        return device(z + 2 - 4 * (z // 2), y, c, x)

    def peer(self, turn):
        z, y, c, x = self.where
        if turn == 3:
            return device(z + 1 - 2 * (z % 2), y, c, x)
        if turn == 4:
            return self.far()
        return partner("cxyyyc"[turn], *self.where)

    def swap(self, turn):
        c = self.where[2]
        if turn == 0:
            src, dst = self.io.at[1 - c], self.inbox.at[0]
        elif turn == 5:
            src, dst = self.mine.at[5], self.io_out.at[c]
        else:
            src, dst = self.mine.at[turn], self.inbox.at[turn]
        return pltpu.make_async_remote_copy(
            src_ref=src,
            dst_ref=dst,
            send_sem=self.osend.at[turn],
            recv_sem=self.orecv.at[turn],
            device_id=self.peer(turn),
            device_id_type=MESH,
        )

    def hop(self, link, src, plane):
        return pltpu.make_async_remote_copy(
            src_ref=src,
            dst_ref=self.rows.at[self.where[2], plane],
            send_sem=self.gsend.at["xyuw".index(link), plane],
            recv_sem=self.grecv.at[plane],
            device_id=partner(link, *self.where),
            device_id_type=MESH,
        )

    def bulk(self, core):
        return pltpu.make_async_remote_copy(
            src_ref=self.rows.at[core],
            dst_ref=self.rows.at[core],
            send_sem=self.bsend.at[0],
            recv_sem=self.brecv.at[0],
            device_id=partner("c", *self.where),
            device_id_type=MESH,
        )

    def row_step(self, off):
        z, y, c, x = self.where
        oz, oy, ox, cond = owner_at(off, z, y, x)
        plane = plane_of(oz, oy, ox)
        own = off == (0, 0, 0)
        src = self.row if own else self.rows.at[c, plane]
        links = onward(self.order, off)

        def act():
            if not own:
                self.hop("x", src, plane).wait_recv()
            for link in links:
                when(can(link, z), lambda link=link: self.hop(link, src, plane).start())

        when(cond, act)
        for link in links:
            self.sent.append(
                (both(cond, can(link, z)), lambda link=link: self.hop(link, src, plane))
            )

    def begin(self):
        z, y, c, x = self.where
        self.own = pltpu.make_async_copy(
            self.row, self.rows.at[c, plane_of(z, y, x)], self.local.at[0]
        )
        self.own.start()
        self.swap(0).start()
        self.row_step((0, 0, 0))

    def turn(self, turn):
        c = self.where[2]
        self.swap(turn).wait_recv()
        if turn < 5:
            before = self.io[c] if turn == 0 else self.mine[turn]
            self.mine[turn + 1] = before + self.inbox[turn]
            if turn == 4:
                self.io_out[c] = self.mine[5]
            self.swap(turn + 1).start()

    def tasks(self):
        todo = [
            lambda off=off: self.row_step(off)
            for off in sorted(offsets(), key=hops)
            if off != (0, 0, 0)
        ]
        for turn in range(6):
            todo.insert(4 * turn + 3, lambda turn=turn: self.turn(turn))

        def last():
            self.own.wait()
            self.bulk(self.where[2]).start()

        return todo + [last]

    def finish(self):
        c = self.where[2]
        self.bulk(1 - c).wait_recv()
        self.bulk(c).wait_send()
        for turn in range(6):
            self.swap(turn).wait_send()
        for cond, make in self.sent:
            when(cond, lambda make=make: make().wait_send())


def scatter_kernel(rank_ref, g_ref, row_ref, io_ref, out_ref, rows_out, io_out, *refs):
    acc, sib, total = refs[:3]
    boxes, refs = refs[3:7], refs[7:]
    mine, inbox = refs[:2]
    csend, crecv, local, send = refs[2:6]
    recvs, small_sems = refs[6:10], refs[10:]
    where = place()
    z, y, c, x = where
    small = SmallSums(row_ref, io_ref, rows_out, io_out, mine, inbox, small_sems, where)
    greet(*where, far=(small.far(),))
    small.begin()

    def core(oz, oy, ox):
        plane = plane_of(oz, oy, ox)
        return pltpu.make_async_remote_copy(
            src_ref=g_ref.at[owner_of(oz, oy, 1 - c, ox)],
            dst_ref=sib.at[plane],
            send_sem=csend.at[plane],
            recv_sem=crecv.at[plane],
            device_id=partner("c", *where),
            device_id_type=MESH,
        )

    def load(oz, oy, ox):
        plane = plane_of(oz, oy, ox)
        return pltpu.make_async_copy(
            g_ref.at[owner_of(oz, oy, c, ox)], acc.at[plane], local.at[plane]
        )

    def ready(oz, oy, ox):
        core(oz, oy, ox).wait_recv()
        load(oz, oy, ox).wait()

    def store(row, value):
        total[row] = value

    scatter = Scatter(SCATTER_PARTS, acc, sib, boxes, send, recvs, where, ready, store)
    for off in scatter.seen:
        oz, oy, ox, cond = owner_at(off, z, y, x)

        def begin(oz=oz, oy=oy, ox=ox):
            core(oz, oy, ox).start()
            load(oz, oy, ox).start()

        when(cond, begin)
    scatter.clear_ends()
    tasks = small.tasks()
    for i, key in enumerate(scatter.keys):
        scatter.step(key)
        if i % 3 == 2 and tasks:
            tasks.pop(0)()
    for task in tasks:
        task()

    def put(i, carry):
        out_ref[i] = total[rank_ref[i]]
        return carry

    lax.fori_loop(0, NSLOT, put, 0)
    scatter.finish()
    for plane in range(16):
        core(plane // 4, (plane // 2) % 2, plane % 2).wait_send()
    small.finish()


def scatter_grads(ranks, grads, row, io):
    vmem = pl.BlockSpec(memory_space=pltpu.VMEM)
    dma = pltpu.SemaphoreType.DMA
    held = pltpu.VMEM((16, NSLOT, 128, 128), jnp.bfloat16)
    half = (SMALL_ROWS, D // 2)
    return pl.pallas_call(
        scatter_kernel,
        out_shape=(
            jax.ShapeDtypeStruct((NSLOT, 128, 128), jnp.float32),
            jax.ShapeDtypeStruct((2, 16) + row.shape, jnp.float32),
            jax.ShapeDtypeStruct((2,) + half, jnp.float32),
        ),
        in_specs=[
            pl.BlockSpec(memory_space=pltpu.SMEM),
            pl.BlockSpec(memory_space=pl.ANY),
            vmem,
            vmem,
        ],
        out_specs=(vmem, vmem, vmem),
        scratch_shapes=[held, held, pltpu.VMEM((NSLOT, 128, 128), jnp.float32)]
        + Scatter.boxes_of(SCATTER_PARTS)
        + [pltpu.VMEM((6,) + half, jnp.float32), pltpu.VMEM((6,) + half, jnp.float32)]
        + [dma((16,)), dma((16,)), dma((16,))]
        + Scatter.sems(SCATTER_PARTS)
        + SmallSums.sems(),
        compiler_params=pltpu.CompilerParams(
            collective_id=2, has_side_effects=True, vmem_limit_bytes=58 * 2**20
        ),
    )(ranks, grads, row, io)


TOK = GRID * GRID
GROUP = 4


def fold_rows(values, op):
    return op(values.reshape(values.shape[0] // 8, 8, values.shape[1]), axis=0)


def side_by_side(ref, first, count, kind):
    parts = [ref[first + j, kind] for j in range(count)]
    return jnp.concatenate(parts, axis=1) if count > 1 else parts[0]


def attend_frame(t, qkv, scores, full, lse):
    q = qkv[t, 0] * jnp.bfloat16(HEAD_DIM**-0.5)

    def score(k, top):
        s = dotg(qkv[k, 1], q, 0, 0)
        scores[k] = s
        return jnp.maximum(top, fold_rows(s, jnp.max))

    top = lax.fori_loop(
        0, t + 1, score, jnp.full((8, TOK), -1e30, jnp.float32), unroll=min(GROUP, t + 1)
    )
    top = jnp.max(top, axis=0, keepdims=True)
    total = jnp.zeros((8, TOK), jnp.float32)
    acc = jnp.zeros((HEAD_DIM, TOK), jnp.float32)
    for k in range(0, t + 1, GROUP):
        count = min(GROUP, t + 1 - k)
        probs = []
        for j in range(count):
            p = jnp.exp(scores[k + j] - top)
            total = total + fold_rows(p, jnp.sum)
            probs.append(p.astype(jnp.bfloat16))
        acc = acc + dotg(side_by_side(qkv, k, count, 2), jnp.concatenate(probs, axis=0), 1, 0)
    total = jnp.sum(total, axis=0, keepdims=True)
    out = acc / total
    full[t] = out
    lse[t] = top + jnp.log(total)
    return out.astype(jnp.bfloat16)


def turn_back(values, cosine, sine):
    first, second = values[: HEAD_DIM // 2], values[HEAD_DIM // 2 :]
    return jnp.concatenate(
        [first * cosine + second * sine, second * cosine - first * sine], axis=0
    )


def attend_frame_back(t, qkv, do_ref, full, lse, cos, sin, dk_ref, dv_ref):
    q = qkv[t, 0] * jnp.bfloat16(HEAD_DIM**-0.5)
    do = do_ref[t]
    delta = jnp.sum(do.astype(jnp.float32) * full[t], axis=0, keepdims=True)
    dq = jnp.zeros((HEAD_DIM, TOK), jnp.float32)
    for k in range(0, t + 1, GROUP):
        count = min(GROUP, t + 1 - k)
        keys = side_by_side(qkv, k, count, 1)
        p = jnp.exp(dotg(keys, q, 0, 0) - lse[t])
        dp = dotg(side_by_side(qkv, k, count, 2), do, 0, 0)
        ds = (p * (dp - delta)).astype(jnp.bfloat16)
        dq = dq + dotg(keys, ds, 1, 0)
        dk = dotg(q, ds, 1, 1)
        dv = dotg(do, p.astype(jnp.bfloat16), 1, 1)
        for j in range(count):
            dk_ref[k + j] += dk[:, j * TOK : (j + 1) * TOK]
            dv_ref[k + j] += dv[:, j * TOK : (j + 1) * TOK]
    return (
        turn_back(dq * HEAD_DIM**-0.5, cos[t], sin[t]).astype(jnp.bfloat16),
        turn_back(dk_ref[t], cos[t], sin[t]).astype(jnp.bfloat16),
        dv_ref[t].astype(jnp.bfloat16),
    )


def attend_kernel(qkv_ref, low_ref, full_ref, lse_ref, scores):
    for t in range(qkv_ref.shape[0]):
        low_ref[t] = attend_frame(t, qkv_ref, scores, full_ref, lse_ref)


def attend(qkv):
    frames = qkv.shape[0]
    vmem = pl.BlockSpec(memory_space=pltpu.VMEM)
    return pl.pallas_call(
        attend_kernel,
        in_specs=[vmem],
        out_specs=[vmem] * 3,
        out_shape=[
            jax.ShapeDtypeStruct((frames, HEAD_DIM, TOK), jnp.bfloat16),
            jax.ShapeDtypeStruct((frames, HEAD_DIM, TOK), jnp.float32),
            jax.ShapeDtypeStruct((frames, 1, TOK), jnp.float32),
        ],
        scratch_shapes=[pltpu.VMEM((frames, TOK, TOK), jnp.float32)],
        compiler_params=pltpu.CompilerParams(vmem_limit_bytes=32 * 2**20),
    )(qkv)


def attend_back_kernel(qkv_ref, do_ref, full_ref, lse_ref, cos_ref, sin_ref, out_ref, dk, dv):
    dk[...] = jnp.zeros_like(dk)
    dv[...] = jnp.zeros_like(dv)
    for t in reversed(range(qkv_ref.shape[0])):
        parts = attend_frame_back(t, qkv_ref, do_ref, full_ref, lse_ref, cos_ref, sin_ref, dk, dv)
        for i in range(3):
            out_ref[t, i] = parts[i]


def attend_back(qkv, do, full, lse, cos, sin):
    frames = qkv.shape[0]
    vmem = pl.BlockSpec(memory_space=pltpu.VMEM)
    return pl.pallas_call(
        attend_back_kernel,
        in_specs=[vmem] * 6,
        out_specs=vmem,
        out_shape=jax.ShapeDtypeStruct(qkv.shape, jnp.bfloat16),
        scratch_shapes=[pltpu.VMEM((frames, HEAD_DIM, TOK), jnp.float32)] * 2,
        compiler_params=pltpu.CompilerParams(vmem_limit_bytes=32 * 2**20),
    )(qkv, do, full, lse, cos, sin)


TILE = 512
RING = 4


def dotg(left, right, left_dim, right_dim):
    return lax.dot_general(
        left, right, (((left_dim,), (right_dim,)), ((), ())), preferred_element_type=jnp.float32
    )


def place_of(start, across, row, col):
    return start + row * across + col


def fetch_tile(places, blocks, held, sem, start, across, row, rows, col, cols):
    def one(i, carry):
        r, c = row + i // cols, col + i % cols
        spot = places[place_of(start, across, r, c)]
        pltpu.make_async_copy(
            blocks.at[spread(spot)],
            held.at[
                pl.ds(pl.multiple_of(r * BLOCK, BLOCK), BLOCK),
                pl.ds(pl.multiple_of(c * BLOCK, BLOCK), BLOCK),
            ],
            sem,
        ).start()
        return carry

    lax.fori_loop(0, rows * cols, one, 0)


def fetched(view, sem):
    pltpu.make_async_copy(view, view, sem).wait()


class Outbox:
    def __init__(self, places, out, stage, sems):
        self.places, self.out, self.stage, self.sems = places, out, stage, sems

    def put(self, turn, values, start, across, row, col, first):
        rows, cols = values.shape[0] // BLOCK, values.shape[1] // BLOCK
        k = turn % RING

        def settle():
            self.settle(k)

        if first is False:
            settle()
        elif first is not True:
            pl.when(jnp.logical_not(first))(settle)
        for r in range(rows):
            for c in range(cols):
                self.stage[k, r * cols + c] = values[
                    r * BLOCK : (r + 1) * BLOCK, c * BLOCK : (c + 1) * BLOCK
                ].astype(jnp.bfloat16)

        def one(i, carry):
            spot = self.places[place_of(start, across, row + i // cols, col + i % cols)]
            pltpu.make_async_copy(self.stage.at[k, i], self.out.at[spot], self.sems.at[k]).start()
            return carry

        lax.fori_loop(0, rows * cols, one, 0)

    def settle(self, k):
        pltpu.make_async_copy(self.stage.at[k], self.stage.at[k], self.sems.at[k]).wait()


def outbox_scratch():
    return [
        pltpu.VMEM((RING, (D // BLOCK) * (TILE // BLOCK), BLOCK, BLOCK), jnp.bfloat16),
        pltpu.SemaphoreType.DMA((RING,)),
    ]


def column_sum(values):
    return jnp.sum(values, axis=0, keepdims=True)


def project_kernel(
    places, blocks, xt_ref, io_ref, bias_ref, mod_ref, cos_ref, sin_ref, h0_ref, at_ref, out_ref, held, a_ref, sems
):
    tiles = 3 * D // TILE
    for j in range(tiles):
        fetch_tile(places, blocks, held, sems.at[j], 0, 3 * D // BLOCK, 0, D // BLOCK, j * TILE // BLOCK, TILE // BLOCK)
    start = dotg(xt_ref[...], io_ref[...], 0, 0) + bias_ref[...]
    h0_ref[...] = start
    hat, _ = layer_norm(start)
    normed = hat * (1 + mod_ref[1:2]) + mod_ref[0:1]
    a_ref[...] = normed.astype(jnp.bfloat16)
    at_ref[...] = normed.T.astype(jnp.bfloat16)
    heads = TILE // HEAD_DIM
    half = HEAD_DIM // 2

    def one(j, carry):
        col = pl.multiple_of(j * TILE, TILE)
        fetched(held.at[:, pl.ds(col, TILE)], sems.at[j])
        r = matmul(a_ref[...], held[:, pl.ds(col, TILE)]).T
        kind, head = j // (D // TILE), j % (D // TILE) * heads

        def turned():
            c, s = cos_ref[...], sin_ref[...]
            for i in range(heads):
                first = r[i * HEAD_DIM : i * HEAD_DIM + half]
                second = r[i * HEAD_DIM + half : (i + 1) * HEAD_DIM]
                out_ref[head + i, kind, 0:half] = (first * c - second * s).astype(jnp.bfloat16)
                out_ref[head + i, kind, half:] = (first * s + second * c).astype(jnp.bfloat16)

        def plain():
            for i in range(heads):
                out_ref[head + i, kind] = r[i * HEAD_DIM : (i + 1) * HEAD_DIM].astype(jnp.bfloat16)

        pl.when(kind < 2)(turned)
        pl.when(kind == 2)(plain)
        return carry

    lax.fori_loop(0, tiles, one, 0)


def project(places, blocks, xt, embed, bias, mod, cos, sin):
    tokens = xt.shape[1]
    vmem = pl.BlockSpec(memory_space=pltpu.VMEM)
    return pl.pallas_call(
        project_kernel,
        in_specs=[pl.BlockSpec(memory_space=pltpu.SMEM), pl.BlockSpec(memory_space=pl.ANY)] + [vmem] * 6,
        out_specs=[vmem] * 3,
        out_shape=[
            jax.ShapeDtypeStruct((tokens, D), jnp.float32),
            jax.ShapeDtypeStruct((D, tokens), jnp.bfloat16),
            jax.ShapeDtypeStruct((HEADS, 3, HEAD_DIM, tokens), jnp.bfloat16),
        ],
        scratch_shapes=[
            pltpu.VMEM((D, 3 * D), jnp.bfloat16),
            pltpu.VMEM((tokens, D), jnp.bfloat16),
            pltpu.SemaphoreType.DMA((3 * D // TILE,)),
        ],
        compiler_params=pltpu.CompilerParams(vmem_limit_bytes=40 * 2**20),
    )(places, blocks, xt, embed, bias, mod, cos, sin)


GELU_A = math.sqrt(2.0 / math.pi)
GELU_B = 0.044715


def middle_kernel(
    places, blocks, olt_ref, h0_ref, mod_ref, head_ref, target_ref, scalars,
    dot_ref, grads_ref, dh1_ref, dhead_ref, dmod_ref, loss_ref,
    wo, wup, wdown, slope, act, bt, dz_ref, db_ref, h1_ref, y_ref, z_ref, stage, stage_sems, sems,
):
    starts, _ = matrix_starts()
    per = TILE // BLOCK
    wide = D // BLOCK
    up_tiles = FFN // TILE
    fetch_tile(places, blocks, wo, sems.at[0], starts[1], wide, 0, wide, 0, wide)
    for j in range(up_tiles):
        fetch_tile(places, blocks, wup, sems.at[1 + j], starts[2], FFN // BLOCK, 0, wide, j * per, per)
    fetched(wo, sems.at[0])
    attended = olt_ref[...].astype(jnp.float32).T.astype(jnp.bfloat16)
    y = matmul(attended, wo[...])
    y_ref[...] = y
    h1 = h0_ref[...] + mod_ref[2:3] * y
    h1_ref[...] = h1
    hat_two, _ = layer_norm(h1)
    b32 = hat_two * (1 + mod_ref[4:5]) + mod_ref[3:4]
    bt[...] = b32.T.astype(jnp.bfloat16)
    b = b32.astype(jnp.bfloat16)
    for j in range(up_tiles):
        fetch_tile(places, blocks, wdown, sems.at[9 + j], starts[3], wide, j * per, per, 0, wide)

    def rise(j, carry):
        col = pl.multiple_of(j * TILE, TILE)
        fetched(wup.at[:, pl.ds(col, TILE)], sems.at[1 + j])
        u = matmul(b, wup[:, pl.ds(col, TILE)])
        square = u * u
        t = jnp.tanh(GELU_A * (u + GELU_B * (square * u)))
        cdf = 0.5 * (1.0 + t)
        act[:, pl.ds(col, TILE)] = (u * cdf).astype(jnp.bfloat16)
        slope[:, pl.ds(col, TILE)] = cdf + (0.5 * GELU_A) * u * (1.0 - t * t) * (
            1.0 + (3.0 * GELU_B) * square
        )
        return carry

    lax.fori_loop(0, up_tiles, rise, 0)
    for j in range(up_tiles):
        fetched(wdown.at[pl.ds(j * TILE, TILE)], sems.at[9 + j])

    def fall(j, carry):
        col = pl.multiple_of(j * 256, 256)
        z_ref[:, pl.ds(col, 256)] = matmul(act[...], wdown[:, pl.ds(col, 256)])
        return carry

    lax.fori_loop(0, D // 256, fall, 0)
    z = z_ref[...]
    h2 = h1_ref[...] + mod_ref[5:6] * z
    hat_three, inv_three = layer_norm(h2)
    c = (hat_three * (1 + mod_ref[7:8]) + mod_ref[6:7]).astype(jnp.bfloat16)
    noised, inv_scale = scalars[0], scalars[1]
    difference = dotg(head_ref[...], c, 1, 1) - target_ref[...]
    loss_ref[...] = jnp.full((1, BLOCK), 1.0, jnp.float32) * (
        jnp.sum(jnp.sum(difference * difference, axis=0, keepdims=True), axis=1, keepdims=True)
        * (noised * inv_scale)
    )
    dpred = (2.0 * inv_scale * noised * difference).astype(jnp.bfloat16)
    dhead_ref[...] = matmul(dpred, c)
    dc = dotg(dpred, head_ref[...], 0, 0)
    dmod_ref[6:7] = column_sum(dc)
    dmod_ref[7:8] = column_sum(dc * hat_three)
    dh2 = norm_back(dc * (1 + mod_ref[7:8]), hat_three, inv_three)
    dmod_ref[5:6] = column_sum(dh2 * z)
    dz = (dh2 * mod_ref[5:6]).astype(jnp.bfloat16)
    dz_ref[...] = dz
    z_ref[...] = dh2
    db_ref[...] = jnp.zeros_like(db_ref)
    outbox = Outbox(places, grads_ref, stage, stage_sems)

    def back(j, carry):
        col = pl.multiple_of(j * TILE, TILE)
        du = (
            slope[:, pl.ds(col, TILE)] * dotg(dz_ref[...], wdown[pl.ds(col, TILE)], 1, 1)
        ).astype(jnp.bfloat16)
        ddown = dotg(act[:, pl.ds(col, TILE)], dz_ref[...], 0, 0)
        outbox.put(2 * (j % 2), ddown, starts[3], wide, j * per, 0, j < 2)
        dup = matmul(bt[...], du)
        outbox.put(2 * (j % 2) + 1, dup, starts[2], FFN // BLOCK, 0, j * per, j < 2)
        db_ref[...] += dotg(du, wup[:, pl.ds(col, TILE)], 1, 1)
        return carry

    lax.fori_loop(0, up_tiles, back, 0)
    hat_two, inv_two = layer_norm(h1_ref[...])
    db = db_ref[...]
    dmod_ref[3:4] = column_sum(db)
    dmod_ref[4:5] = column_sum(db * hat_two)
    dh1 = z_ref[...] + norm_back(db * (1 + mod_ref[4:5]), hat_two, inv_two)
    dh1_ref[...] = dh1
    dmod_ref[2:3] = column_sum(dh1 * y_ref[...])
    dmod_ref[0:2] = jnp.zeros((2, D), jnp.float32)
    dz_ref[...] = (dh1 * mod_ref[2:3]).astype(jnp.bfloat16)
    for j in range(D // TILE):
        rows = pl.ds(j * TILE, TILE)
        dot_ref[rows] = dotg(wo[rows], dz_ref[...], 1, 1).astype(jnp.bfloat16)
    for j in range(D // TILE):
        dout = matmul(olt_ref[...], dz_ref[:, j * TILE : (j + 1) * TILE])
        outbox.put(j, dout, starts[1], wide, 0, j * per, False)
    for k in range(RING):
        outbox.settle(k)


def middle(places, blocks, olt, h0, mod, head, target, scalars):
    tokens = h0.shape[0]
    vmem, smem = pl.BlockSpec(memory_space=pltpu.VMEM), pl.BlockSpec(memory_space=pltpu.SMEM)
    anyspace = pl.BlockSpec(memory_space=pl.ANY)
    f32 = jnp.float32
    return pl.pallas_call(
        middle_kernel,
        in_specs=[smem, anyspace] + [vmem] * 5 + [smem],
        out_specs=[vmem, anyspace] + [vmem] * 4,
        out_shape=[
            jax.ShapeDtypeStruct((D, tokens), jnp.bfloat16),
            jax.ShapeDtypeStruct((matrix_starts()[1], BLOCK, BLOCK), jnp.bfloat16),
            jax.ShapeDtypeStruct((tokens, D), f32),
            jax.ShapeDtypeStruct((PIN, D), f32),
            jax.ShapeDtypeStruct((8, D), f32),
            jax.ShapeDtypeStruct((1, BLOCK), f32),
        ],
        scratch_shapes=[
            pltpu.VMEM((D, D), jnp.bfloat16),
            pltpu.VMEM((D, FFN), jnp.bfloat16),
            pltpu.VMEM((FFN, D), jnp.bfloat16),
            pltpu.VMEM((tokens, FFN), f32),
            pltpu.VMEM((tokens, FFN), jnp.bfloat16),
            pltpu.VMEM((D, tokens), jnp.bfloat16),
            pltpu.VMEM((tokens, D), jnp.bfloat16),
            pltpu.VMEM((tokens, D), f32),
            pltpu.VMEM((tokens, D), f32),
            pltpu.VMEM((tokens, D), f32),
            pltpu.VMEM((tokens, D), f32),
        ]
        + outbox_scratch()
        + [pltpu.SemaphoreType.DMA((17,))],
        compiler_params=pltpu.CompilerParams(vmem_limit_bytes=58 * 2**20),
    )(places, blocks, olt, h0, mod, head, target, scalars)


def final_kernel(
    places, blocks, drt_ref, at_ref, h0_ref, mod_ref, dh1_ref, xt_ref, grads_in,
    grads_ref, dmod_ref, dembed_ref, dbias_ref,
    held, flat, stage, stage_sems, sems,
):
    across = 3 * D // BLOCK
    for j in range(2):
        fetch_tile(places, blocks, held, sems.at[j], 0, across, j * 4, 4, 0, across)
    for kind in range(3):
        for head in range(HEADS):
            row = kind * D + head * HEAD_DIM
            flat[row : row + HEAD_DIM] = drt_ref[head, kind]
    outbox = Outbox(places, grads_ref, stage, stage_sems)
    for j in range(3 * D // TILE):
        dw = dotg(at_ref[...], flat[j * TILE : (j + 1) * TILE], 1, 1)
        outbox.put(j, dw, 0, across, 0, j * TILE // BLOCK, j < RING)
    for j in range(2):
        fetched(held.at[pl.ds(j * TILE, TILE)], sems.at[j])
    da = matmul(held[...], flat[...]).T
    hat, inverse = layer_norm(h0_ref[...])
    dmod_ref[0:1] = column_sum(da)
    dmod_ref[1:2] = column_sum(da * hat)
    dh0 = (dh1_ref[...] + norm_back(da * (1 + mod_ref[1:2]), hat, inverse)).astype(jnp.bfloat16)
    dembed_ref[...] = matmul(xt_ref[...], dh0)
    dbias_ref[...] = column_sum(dh0.astype(jnp.float32))
    for k in range(RING):
        outbox.settle(k)


def final(places, blocks, drt, at, h0, mod, dh1, xt, grads):
    vmem, smem = pl.BlockSpec(memory_space=pltpu.VMEM), pl.BlockSpec(memory_space=pltpu.SMEM)
    anyspace = pl.BlockSpec(memory_space=pl.ANY)
    f32 = jnp.float32
    tokens = h0.shape[0]
    return pl.pallas_call(
        final_kernel,
        in_specs=[smem, anyspace] + [vmem] * 6 + [anyspace],
        out_specs=[anyspace] + [vmem] * 3,
        out_shape=[
            jax.ShapeDtypeStruct(grads.shape, grads.dtype),
            jax.ShapeDtypeStruct((2, D), f32),
            jax.ShapeDtypeStruct((PIN, D), f32),
            jax.ShapeDtypeStruct((1, D), f32),
        ],
        scratch_shapes=[
            pltpu.VMEM((D, 3 * D), jnp.bfloat16),
            pltpu.VMEM((3 * D, tokens), jnp.bfloat16),
        ]
        + outbox_scratch()
        + [pltpu.SemaphoreType.DMA((2,))],
        input_output_aliases={8: 0},
        compiler_params=pltpu.CompilerParams(vmem_limit_bytes=40 * 2**20),
    )(places, blocks, drt, at, h0, mod, dh1, xt, grads)


def matrix_starts():
    starts, total = [], 0
    for rows_in, cols_in in matrix_shapes():
        starts.append(total)
        total += rows_in // BLOCK * (cols_in // BLOCK)
    return starts, total


def spread(place):
    return place + place // NSLOT


def block_places(block_slot):
    owned = block_slot.reshape(32, -1)
    ranks = jnp.sum((owned[:, None, :] < owned[:, :, None]).astype(jnp.int32), axis=2)
    mine = lax.axis_index("frame") * 2 + lax.axis_index("rep")
    own_ranks = lax.dynamic_index_in_dim(ranks, mine, 0, keepdims=False)
    counting = jnp.arange(NSLOT, dtype=jnp.int32)
    perm = jnp.sum(jnp.where(own_ranks[None, :] == counting[:, None], counting[None, :], 0), axis=1)
    spots = (jnp.arange(32, dtype=jnp.int32)[:, None] * NSLOT + ranks).reshape(-1)
    natural = jnp.arange(block_slot.shape[0], dtype=jnp.int32)
    places = jnp.sum(jnp.where(block_slot[None, :] == natural[:, None], spots[None, :], 0), axis=1)
    return own_ranks, perm, places


def rope_columns(frame_ids):
    pairs = HEAD_DIM // 2
    time_pairs = pairs // 4
    row_pairs = (pairs - time_pairs) // 2
    column_pairs = pairs - time_pairs - row_pairs
    shape = (frame_ids.shape[0], pairs, GRID * GRID)
    token = jnp.arange(GRID * GRID, dtype=jnp.int32)
    groups = (
        (time_pairs, frame_ids[:, None, None].astype(jnp.float32)),
        (row_pairs, (token // GRID)[None, None, :].astype(jnp.float32)),
        (column_pairs, (token % GRID)[None, None, :].astype(jnp.float32)),
    )
    angles = jnp.concatenate(
        [
            jnp.broadcast_to(pos * frequencies(n)[None, :, None], (shape[0], n, shape[2]))
            for n, pos in groups
        ],
        axis=1,
    )
    return (jnp.cos(angles), jnp.sin(angles))


def on_grid(
    clean,
    noise,
    levels,
    flags,
    frame_map,
    block_slot,
    step_count,
    mat_weight,
    mat_ema,
    stat_left,
    stat_right,
    root_left,
    root_right,
    mod_table,
    mod_mom,
    mod_var,
    mod_ema,
    io_weight,
    io_mom,
    io_var,
    io_ema,
):
    tok_frame = GRID * GRID
    my_time, my_clip = lax.axis_index("frame"), lax.axis_index("rep")
    level_here = levels[0, 0] * (1 - flags[0, 0])
    noised_here = (1 - flags[0, 0]).astype(jnp.float32)
    fraction = level_here.astype(jnp.float32) / LEVELS
    frames_in = (
        jnp.cos(0.5 * jnp.pi * fraction) * clean[0, 0] + jnp.sin(0.5 * jnp.pi * fraction) * noise[0, 0]
    )
    noise_high = noise[0, 0].astype(jnp.bfloat16)
    noise_low = (noise[0, 0] - noise_high.astype(jnp.float32)).astype(jnp.bfloat16)
    data = jnp.concatenate(
        [
            frames_in.astype(jnp.bfloat16).reshape(-1, BLOCK),
            noise_high.reshape(-1, BLOCK),
            noise_low.reshape(-1, BLOCK),
            jnp.full((16, BLOCK), noised_here.astype(jnp.bfloat16)),
            jnp.full((16, BLOCK), level_here.astype(jnp.bfloat16)),
        ]
    )
    ranks, perm, places = block_places(block_slot)
    gathered = gather_weights(perm, mat_weight, data)
    blocks = gathered.reshape(-1, BLOCK, BLOCK)
    clip_map = lax.dynamic_index_in_dim(frame_map, my_clip, 0, keepdims=False)
    my_slot = jnp.sum(
        jnp.where(clip_map == my_time, jnp.arange(clip_map.shape[0], dtype=jnp.int32), 0)
    )
    my_data = lax.dynamic_index_in_dim(gathered, my_slot * 2 + my_clip, 0, keepdims=False)[DATA]
    noised_total = jnp.maximum(jnp.sum(gathered[:, DATA, 96, 0].astype(jnp.float32)), 1.0)
    noised = my_data[96, 0].astype(jnp.float32)
    level_now = my_data[112, 0].astype(jnp.int32)
    inputs = my_data[:32].reshape(PIN, tok_frame)
    targets = (my_data[32:64].astype(jnp.float32) + my_data[64:96].astype(jnp.float32)).reshape(
        PIN, tok_frame
    )
    modulation = lax.dynamic_index_in_dim(mod_table, level_now, 0, keepdims=False).reshape(8, D)
    io_low = io_weight.astype(jnp.bfloat16)
    cosine, sine = rope_columns(jnp.arange(frame_map.shape[1], dtype=jnp.int32))
    my_cos = lax.dynamic_index_in_dim(cosine, my_time, 0, keepdims=False)
    my_sin = lax.dynamic_index_in_dim(sine, my_time, 0, keepdims=False)
    start, normed, parts = project(
        places, blocks, inputs, io_low[:PIN], io_weight[2 * PIN :], modulation, my_cos, my_sin
    )
    mine = lax.all_to_all(parts, "frame", 0, 0, tiled=True)
    low, full, lse = attend(mine)
    attended = lax.all_to_all(low, "frame", 0, 0, tiled=True).reshape(D, tok_frame)
    inv_scale = 1.0 / (noised_total * tok_frame * PIN)
    grad_heads, grad_blocks, grad_middle, grad_head, grad_mod, loss_part = middle(
        places,
        blocks,
        attended,
        start,
        modulation,
        io_low[PIN : 2 * PIN],
        targets,
        jnp.stack([noised, inv_scale]),
    )
    grad_mine = lax.all_to_all(
        grad_heads.reshape(HEADS, HEAD_DIM, tok_frame), "frame", 0, 0, tiled=True
    )
    back = attend_back(mine, grad_mine, full, lse, cosine, sine)
    grad_proj = lax.all_to_all(back, "frame", 0, 0, tiled=True)
    grad_blocks, grad_mod_one, grad_embed, grad_bias = final(
        places, blocks, grad_proj, normed, start, modulation, grad_middle, inputs, grad_blocks
    )
    row = jnp.concatenate(
        [
            grad_mod_one.reshape(-1, BLOCK),
            grad_mod[2:].reshape(-1, BLOCK),
            jnp.full((4, BLOCK), level_now.astype(jnp.float32)),
            jnp.broadcast_to(loss_part, (4, BLOCK)),
        ]
    )
    grad_io = jnp.concatenate(
        [
            grad_embed,
            grad_head,
            grad_bias,
            jnp.zeros((SMALL_ROWS - 2 * PIN - 1, D), jnp.float32),
        ],
        axis=0,
    )
    owned, rows, grad_io = scatter_grads(
        ranks,
        grad_blocks.reshape(32, -1, BLOCK, BLOCK),
        row,
        grad_io.reshape(SMALL_ROWS, 2, D // 2).swapaxes(0, 1),
    )
    grad_io = grad_io.swapaxes(0, 1).reshape(SMALL_ROWS, D)[: 2 * PIN + 1]
    rows = rows.reshape(32, -1, BLOCK)
    total_loss = jnp.sum(rows[:, 68, 0])
    selector = (
        rows[:, 64, 0].astype(jnp.int32)[None, :] == jnp.arange(LEVELS, dtype=jnp.int32)[:, None]
    ).astype(jnp.float32)
    grad_table = jnp.dot(selector, rows[:, :64].reshape(32, 8 * D), precision=TOP_PRECISION)
    block_limit = CLIP_NORM * BLOCK * NPARAMS ** (-0.5)
    block_norm = jnp.sqrt(jnp.sum(owned * owned, axis=(1, 2), keepdims=True))
    mat_grad = owned * (block_limit / jnp.maximum(block_norm, block_limit))
    grad_norm = jnp.sqrt(jnp.sum(grad_table * grad_table) + jnp.sum(grad_io * grad_io))
    factor = CLIP_NORM / jnp.maximum(grad_norm, CLIP_NORM)
    new_mat_weight, new_stat_left, new_stat_right, new_mat_ema = shampoo(
        mat_grad, mat_weight, mat_ema, stat_left, stat_right, root_left, root_right
    )
    step = step_count[0].astype(jnp.float32)
    new_mod = adamw(grad_table * factor, mod_table, mod_mom, mod_var, mod_ema, step)
    new_io = adamw(grad_io * factor, io_weight, io_mom, io_var, io_ema, step)
    return (
        total_loss * noised_total,
        noised_total,
        grad_norm,
        mat_grad,
        new_mat_weight,
        new_stat_left,
        new_stat_right,
        new_mat_ema,
        new_mod[0],
        new_mod[1],
        new_mod[2],
        new_mod[3],
        new_io[0],
        new_io[1],
        new_io[2],
        new_io[3],
    )


def solution(mesh):
    tuned = dict(mesh.shape) == {"frame": 16, "rep": 2}
    body = on_grid if tuned else on_device
    in_specs = (
        P("rep", "frame", None, None),
        P("rep", "frame", None, None),
        P("rep", "frame"),
        P("rep", "frame"),
        P(),
        P(),
        P(),
        P(("frame", "rep"), None, None),
        P(("frame", "rep"), None, None),
        P(("frame", "rep"), None, None),
        P(("frame", "rep"), None, None),
        P(("frame", "rep"), None, None),
        P(("frame", "rep"), None, None),
        P(),
        P(),
        P(),
        P(),
        P(),
        P(),
        P(),
        P(),
    )
    out_specs = (
        P(),
        P(),
        P(),
        P(("frame", "rep"), None, None),
        P(("frame", "rep"), None, None),
        P(("frame", "rep"), None, None),
        P(("frame", "rep"), None, None),
        P(("frame", "rep"), None, None),
        P(),
        P(),
        P(),
        P(),
        P(),
        P(),
        P(),
        P(),
    )
    return jax.shard_map(
        body, mesh=mesh, in_specs=in_specs, out_specs=out_specs, check_vma=False
    )
```

```python
from functools import partial
import math

import jax
import jax.numpy as jnp
from jax import lax
from jax.experimental import pallas as pl
from jax.experimental.pallas import tpu as pltpu
from jax.sharding import PartitionSpec as P

D = 1024
HEADS = 16
HEAD_DIM = 64
FFN = 4096
PIN = 16
GRID = 16
BLOCK = 128
LEVELS = 32
FR_DEV = 1
NPARAMS = 12878848


LN_EPS = 1e-06
ROPE_BASE = 10000.0
CLIP_NORM = 0.01
BETA_ONE = 0.9
BETA_TWO = 0.999
ADAM_EPS = 1e-08
ADAM_RATE = 0.1
DECAY_RATE = 0.1
STAT_BETA = 0.95
SHAMPOO_RATE = 0.01
EMA_DECAY = 0.9
TOP_PRECISION = lax.Precision.HIGHEST


def matmul(left, right):
    return jnp.dot(left, right, preferred_element_type=jnp.float32)


def layer_norm(hidden):
    centered = hidden - jnp.mean(hidden, axis=-1, keepdims=True)
    inverse = lax.rsqrt(jnp.mean(centered * centered, axis=-1, keepdims=True) + LN_EPS)
    return (centered * inverse, inverse)


def norm_back(grad_hat, normed, inverse):
    return inverse * (
        grad_hat
        - jnp.mean(grad_hat, axis=-1, keepdims=True)
        - normed * jnp.mean(grad_hat * normed, axis=-1, keepdims=True)
    )


def gelu_back(upper, grad_act):
    return jax.vjp(partial(jax.nn.gelu, approximate=True), upper)[1](grad_act)[0]


def frequencies(width):
    return ROPE_BASE ** (-jnp.arange(width, dtype=jnp.float32) / width)


def rope_tables(frame_ids):
    pairs = HEAD_DIM // 2
    time_pairs = pairs // 4
    row_pairs = (pairs - time_pairs) // 2
    column_pairs = pairs - time_pairs - row_pairs
    frames = frame_ids.shape[0]
    tok_frame = GRID * GRID
    token_pos = jnp.arange(tok_frame, dtype=jnp.int32)
    row_pos = (token_pos // GRID).astype(jnp.float32)
    column_pos = (token_pos % GRID).astype(jnp.float32)
    time_angle = (
        frame_ids.astype(jnp.float32)[:, None, None] * frequencies(time_pairs)[None, None, :]
    )
    row_angle = row_pos[None, :, None] * frequencies(row_pairs)[None, None, :]
    column_angle = column_pos[None, :, None] * frequencies(column_pairs)[None, None, :]
    angles = jnp.concatenate(
        [jnp.broadcast_to(time_angle, (frames, tok_frame, time_pairs)), row_angle, column_angle],
        axis=-1,
    )
    angles = angles.reshape(frames * tok_frame, pairs)
    return (jnp.cos(angles), jnp.sin(angles))


def rotate(values, cosine, sine):
    pairs = HEAD_DIM // 2
    first, second = (values[..., :pairs], values[..., pairs:])
    cosine = cosine[:, None, :]
    sine = sine[:, None, :]
    return jnp.concatenate(
        [first * cosine - second * sine, first * sine + second * cosine], axis=-1
    )


def split_heads(flat):
    return flat.reshape(flat.shape[0], HEADS, HEAD_DIM)


def matrix_shapes():
    return ((D, 3 * D), (D, D), (D, FFN), (FFN, D))


def from_blocks(natural):
    matrices = []
    offset = 0
    for rows_in, cols_in in matrix_shapes():
        count_in = rows_in // BLOCK * (cols_in // BLOCK)
        part_blocks = natural[offset : offset + count_in]
        matrices.append(
            part_blocks.reshape(rows_in // BLOCK, cols_in // BLOCK, BLOCK, BLOCK)
            .transpose(0, 2, 1, 3)
            .reshape(rows_in, cols_in)
        )
        offset = offset + count_in
    return matrices


def to_blocks(matrix):
    rows_in, cols_in = matrix.shape
    return (
        matrix.reshape(rows_in // BLOCK, BLOCK, cols_in // BLOCK, BLOCK)
        .transpose(0, 2, 1, 3)
        .reshape(-1, BLOCK, BLOCK)
    )


def score_block(queries, key_block, query_frames, key_frames):
    scores = jnp.einsum(
        "qhd,khd->hqk", queries, key_block, preferred_element_type=jnp.float32
    ) * HEAD_DIM ** (-0.5)
    visible = key_frames[None, None, :] <= query_frames[None, :, None]
    return jnp.where(visible, scores, -jnp.inf)


def stack_keys(key_rows, value_rows, frame_rows):
    total_rows = key_rows.shape[0]
    block_rows = math.gcd(total_rows, 512)
    blocks = total_rows // block_rows
    return (
        (
            key_rows.reshape(blocks, block_rows, HEADS, HEAD_DIM),
            value_rows.reshape(blocks, block_rows, HEADS, HEAD_DIM),
            frame_rows.reshape(blocks, block_rows),
        ),
        block_rows,
    )


def keep_state(previous):
    return previous


def fold_keys(state, shard_rows, queries, query_frames, key_frames_all):
    key_rows, value_rows = shard_rows
    stacks, block_rows = stack_keys(key_rows, value_rows, key_frames_all)
    top_query = jnp.max(query_frames)

    def fold_step_block(carried, block_in):
        key_block, value_block, key_frames = block_in

        def fold_compute(previous):
            running, denominator, accumulated = previous
            scores = score_block(queries, key_block, query_frames, key_frames)
            new_max = jnp.maximum(running, jnp.max(scores, axis=-1))
            weights = jnp.exp(scores - new_max[..., None])
            rescale = jnp.exp(running - new_max)
            contrib = jnp.einsum(
                "hqk,khd->hqd",
                weights.astype(jnp.bfloat16),
                value_block,
                preferred_element_type=jnp.float32,
            )
            return (
                new_max,
                denominator * rescale + jnp.sum(weights, axis=-1),
                accumulated * rescale[..., None] + contrib,
            )

        return (lax.cond(jnp.min(key_frames) <= top_query, fold_compute, keep_state, carried), None)

    state, unused = lax.scan(fold_step_block, state, stacks)
    return state


def grad_parts(
    queries, grad_heads, delta, log_total, query_frames, key_block, value_block, key_frames
):
    probs = jnp.exp(
        score_block(queries, key_block, query_frames, key_frames) - log_total[..., None]
    )
    grad_probs = jnp.einsum(
        "qhd,khd->hqk", grad_heads, value_block, preferred_element_type=jnp.float32
    )
    grad_scores = (probs * (grad_probs - delta[..., None])).astype(jnp.bfloat16)
    return (probs, grad_scores)


def key_value_block(
    queries, grad_heads, delta, log_total, query_frames, key_block, value_block, key_frames
):
    block_rows = key_block.shape[0]
    probs, grad_scores = grad_parts(
        queries, grad_heads, delta, log_total, query_frames, key_block, value_block, key_frames
    )
    key_grad = jnp.einsum(
        "hqk,qhd->khd", grad_scores, queries, preferred_element_type=jnp.float32
    ) * HEAD_DIM ** (-0.5)
    value_grad = jnp.einsum(
        "hqk,qhd->khd", probs.astype(jnp.bfloat16), grad_heads, preferred_element_type=jnp.float32
    )
    return jnp.concatenate(
        [key_grad.reshape(block_rows, D), value_grad.reshape(block_rows, D)], axis=1
    )


def query_grads(
    queries, grad_heads, delta, log_total, query_frames, key_all, value_all, key_frames_all
):
    stacks, block_rows = stack_keys(key_all, value_all, key_frames_all)
    top_query = jnp.max(query_frames)

    def query_step_block(carried, block_in):
        key_block, value_block, key_frames = block_in

        def query_compute(previous):
            probs, grad_scores = grad_parts(
                queries,
                grad_heads,
                delta,
                log_total,
                query_frames,
                key_block,
                value_block,
                key_frames,
            )
            return previous + jnp.einsum(
                "hqk,khd->qhd", grad_scores, key_block, preferred_element_type=jnp.float32
            )

        return (
            lax.cond(jnp.min(key_frames) <= top_query, query_compute, keep_state, carried),
            None,
        )

    initial = jnp.zeros(queries.shape, jnp.float32)
    result, unused = lax.scan(query_step_block, initial, stacks)
    return result * HEAD_DIM ** (-0.5)


def key_terms(
    row_count,
    queries,
    grad_heads,
    delta,
    log_total,
    query_frames,
    key_all,
    value_all,
    key_frames_all,
):
    stacks, block_rows = stack_keys(key_all, value_all, key_frames_all)
    top_query = jnp.max(query_frames)

    def one_block(block_in):
        key_block, value_block, key_frames = block_in

        def one_compute(unused):
            return key_value_block(
                queries,
                grad_heads,
                delta,
                log_total,
                query_frames,
                key_block,
                value_block,
                key_frames,
            )

        def nothing(unused):
            return jnp.zeros((block_rows, 2 * D), jnp.float32)

        return lax.cond(jnp.min(key_frames) <= top_query, one_compute, nothing, 0)

    return lax.map(one_block, stacks).reshape(row_count, 2 * D)


def shampoo(grads, weights, average, left, right, left_root, right_root):
    new_left = STAT_BETA * left + (1 - STAT_BETA) * jnp.einsum(
        "bij,bkj->bik", grads, grads, precision=TOP_PRECISION
    )
    new_right = STAT_BETA * right + (1 - STAT_BETA) * jnp.einsum(
        "bji,bjk->bik", grads, grads, precision=TOP_PRECISION
    )
    direction = jnp.einsum("bij,bjk->bik", left_root, grads, precision=TOP_PRECISION)
    direction = jnp.einsum("bij,bjk->bik", direction, right_root, precision=TOP_PRECISION)
    direction = direction * lax.rsqrt(
        jnp.mean(direction * direction, axis=(1, 2), keepdims=True) + 1e-06
    )
    new_weights = weights - SHAMPOO_RATE * (direction + DECAY_RATE * weights)
    new_average = EMA_DECAY * average + (1 - EMA_DECAY) * new_weights
    return (new_weights, new_left, new_right, new_average)


def adamw(grads, weights, first, second, average, step):
    new_first = BETA_ONE * first + (1 - BETA_ONE) * grads
    new_second = BETA_TWO * second + (1 - BETA_TWO) * grads * grads
    first_hat = new_first / (1 - BETA_ONE**step)
    second_hat = new_second / (1 - BETA_TWO**step)
    new_weights = weights - ADAM_RATE * (
        first_hat / (jnp.sqrt(second_hat) + ADAM_EPS) + DECAY_RATE * weights
    )
    new_average = EMA_DECAY * average + (1 - EMA_DECAY) * new_weights
    return (new_weights, new_first, new_second, new_average)


def on_device(
    clean,
    noise,
    levels,
    flags,
    frame_map,
    block_slot,
    step_count,
    mat_weight,
    mat_ema,
    stat_left,
    stat_right,
    root_left,
    root_right,
    mod_table,
    mod_mom,
    mod_var,
    mod_ema,
    io_weight,
    io_mom,
    io_var,
    io_ema,
):
    tok_frame = GRID * GRID
    local_rows = FR_DEV * tok_frame
    noised = (1 - flags[0]).astype(jnp.float32)
    noised_total = jnp.maximum(lax.psum(jnp.sum(noised), ("frame", "rep")), 1.0)
    gathered = lax.all_gather(mat_weight.astype(jnp.bfloat16), ("frame", "rep"), axis=0, tiled=True)
    natural = jnp.zeros_like(gathered).at[block_slot].set(gathered)
    attn_w, out_w, up_w, down_w = from_blocks(natural)
    clip_map = lax.dynamic_index_in_dim(frame_map, lax.axis_index("rep"), 0, keepdims=False)
    my_frames = lax.dynamic_slice_in_dim(clip_map, lax.axis_index("frame") * FR_DEV, FR_DEV)
    key_frames_all = jnp.repeat(clip_map, tok_frame)
    query_frames = jnp.repeat(my_frames, tok_frame)
    level_now = levels[0] * (1 - flags[0])
    fraction = level_now.astype(jnp.float32) / LEVELS
    keep_coef = jnp.cos(0.5 * jnp.pi * fraction)
    noise_coef = jnp.sin(0.5 * jnp.pi * fraction)
    frames_in = keep_coef[:, None, None] * clean[0] + noise_coef[:, None, None] * noise[0]
    inputs = jnp.swapaxes(frames_in, 1, 2).reshape(local_rows, PIN).astype(jnp.bfloat16)
    targets = jnp.swapaxes(noise[0], 1, 2).reshape(local_rows, PIN)
    selector = (level_now[:, None] == jnp.arange(LEVELS, dtype=jnp.int32)[None, :]).astype(
        jnp.float32
    )
    modulation = jnp.dot(selector, mod_table, precision=TOP_PRECISION).reshape(FR_DEV, 8, 1, D)
    io_low = io_weight.astype(jnp.bfloat16)
    embed = io_low[:PIN]
    head = io_low[PIN : 2 * PIN]
    start = (matmul(inputs, embed) + io_weight[2 * PIN]).reshape(FR_DEV, tok_frame, D)
    hat_one, inv_one = layer_norm(start)
    normed = (
        (hat_one * (1 + modulation[:, 1]) + modulation[:, 0])
        .reshape(local_rows, D)
        .astype(jnp.bfloat16)
    )
    projected = matmul(normed, attn_w)
    cosine, sine = rope_tables(my_frames)
    queries = rotate(split_heads(projected[:, :D]), cosine, sine).astype(jnp.bfloat16)
    key_flat = (
        rotate(split_heads(projected[:, D : 2 * D]), cosine, sine)
        .astype(jnp.bfloat16)
        .reshape(local_rows, D)
    )
    value_flat = projected[:, 2 * D :].astype(jnp.bfloat16)
    initial = (
        jnp.full((HEADS, local_rows), -1e30, jnp.float32),
        jnp.zeros((HEADS, local_rows), jnp.float32),
        jnp.zeros((HEADS, local_rows, HEAD_DIM), jnp.float32),
    )
    running, denominator, accumulated = fold_keys(
        initial,
        (
            lax.all_gather(key_flat, "frame", axis=0, tiled=True),
            lax.all_gather(value_flat, "frame", axis=0, tiled=True),
        ),
        queries,
        query_frames,
        key_frames_all,
    )
    attended = jnp.transpose(accumulated / denominator[..., None], (1, 0, 2)).reshape(local_rows, D)
    log_total = running + jnp.log(denominator)
    attended_low = attended.astype(jnp.bfloat16)
    branch = matmul(attended_low, out_w).reshape(FR_DEV, tok_frame, D)
    middle = start + modulation[:, 2] * branch
    hat_two, inv_two = layer_norm(middle)
    normed_two = (
        (hat_two * (1 + modulation[:, 4]) + modulation[:, 3])
        .reshape(local_rows, D)
        .astype(jnp.bfloat16)
    )
    upper = matmul(normed_two, up_w)
    activated = jax.nn.gelu(upper, approximate=True).astype(jnp.bfloat16)
    lower = matmul(activated, down_w).reshape(FR_DEV, tok_frame, D)
    final = middle + modulation[:, 5] * lower
    hat_three, inv_three = layer_norm(final)
    normed_three = (
        (hat_three * (1 + modulation[:, 7]) + modulation[:, 6])
        .reshape(local_rows, D)
        .astype(jnp.bfloat16)
    )
    predicted = matmul(normed_three, head.T)
    row_weight = jnp.repeat(noised, tok_frame)[:, None]
    inv_scale = 1.0 / (noised_total * tok_frame * PIN)
    difference = predicted - targets
    loss_part = jnp.sum(row_weight * difference * difference) * inv_scale
    grad_pred = (2.0 * inv_scale * row_weight * difference).astype(jnp.bfloat16)
    grad_head = jnp.dot(grad_pred.T, normed_three, preferred_element_type=jnp.float32)
    grad_norm_three = matmul(grad_pred, head).reshape(FR_DEV, tok_frame, D)
    grad_final = norm_back(grad_norm_three * (1 + modulation[:, 7]), hat_three, inv_three)
    grad_lower = (grad_final * modulation[:, 5]).reshape(local_rows, D).astype(jnp.bfloat16)
    grad_down = jnp.dot(activated.T, grad_lower, preferred_element_type=jnp.float32)
    grad_upper = gelu_back(upper, matmul(grad_lower, down_w.T)).astype(jnp.bfloat16)
    grad_up = jnp.dot(normed_two.T, grad_upper, preferred_element_type=jnp.float32)
    grad_norm_two = matmul(grad_upper, up_w.T).reshape(FR_DEV, tok_frame, D)
    grad_middle = grad_final + norm_back(grad_norm_two * (1 + modulation[:, 4]), hat_two, inv_two)
    grad_branch = (grad_middle * modulation[:, 2]).reshape(local_rows, D).astype(jnp.bfloat16)
    grad_out_w = jnp.dot(attended_low.T, grad_branch, preferred_element_type=jnp.float32)
    grad_heads = split_heads(matmul(grad_branch, out_w.T).astype(jnp.bfloat16))
    delta = jnp.sum(grad_heads.astype(jnp.float32) * split_heads(attended), axis=-1).T
    key_all, value_all = (
        lax.all_gather(key_flat, "frame", axis=0, tiled=True),
        lax.all_gather(value_flat, "frame", axis=0, tiled=True),
    )
    grad_query = query_grads(
        queries, grad_heads, delta, log_total, query_frames, key_all, value_all, key_frames_all
    )
    key_value_grad = lax.psum_scatter(
        key_terms(
            lax.axis_size("frame") * local_rows,
            queries,
            grad_heads,
            delta,
            log_total,
            query_frames,
            key_all,
            value_all,
            key_frames_all,
        ),
        "frame",
        scatter_dimension=0,
        tiled=True,
    )
    grad_q = rotate(grad_query, cosine, -sine).reshape(local_rows, D)
    grad_k = rotate(split_heads(key_value_grad[:, :D]), cosine, -sine).reshape(local_rows, D)
    grad_proj = jnp.concatenate([grad_q, grad_k, key_value_grad[:, D:]], axis=1).astype(
        jnp.bfloat16
    )
    grad_attn_w = jnp.dot(normed.T, grad_proj, preferred_element_type=jnp.float32)
    grad_norm_one = matmul(grad_proj, attn_w.T).reshape(FR_DEV, tok_frame, D)
    grad_start = grad_middle + norm_back(grad_norm_one * (1 + modulation[:, 1]), hat_one, inv_one)
    grad_start_low = grad_start.reshape(local_rows, D).astype(jnp.bfloat16)
    grad_embed = jnp.dot(inputs.T, grad_start_low, preferred_element_type=jnp.float32)
    grad_bias = jnp.sum(grad_start_low.astype(jnp.float32), axis=0)
    mod_terms = [
        grad_norm_one,
        grad_norm_one * hat_one,
        grad_middle * branch,
        grad_norm_two,
        grad_norm_two * hat_two,
        grad_final * lower,
        grad_norm_three,
        grad_norm_three * hat_three,
    ]
    mod_grads = jnp.stack([jnp.sum(term, axis=1) for term in mod_terms], axis=1).reshape(
        FR_DEV, 8 * D
    )
    grad_table = jnp.dot(selector.T, mod_grads, precision=TOP_PRECISION)
    grad_io = jnp.concatenate([grad_embed, grad_head, grad_bias[None, :]], axis=0)
    grad_table, grad_io, total_loss = lax.psum((grad_table, grad_io, loss_part), ("frame", "rep"))
    grad_blocks = jnp.concatenate(
        [to_blocks(grad_attn_w), to_blocks(grad_out_w), to_blocks(grad_up), to_blocks(grad_down)], 0
    )
    owned = lax.psum_scatter(
        grad_blocks[block_slot], ("frame", "rep"), scatter_dimension=0, tiled=True
    )
    block_limit = CLIP_NORM * BLOCK * NPARAMS ** (-0.5)
    block_norm = jnp.sqrt(jnp.sum(owned * owned, axis=(1, 2), keepdims=True))
    mat_grad = owned * (block_limit / jnp.maximum(block_norm, block_limit))
    grad_norm = jnp.sqrt(jnp.sum(grad_table * grad_table) + jnp.sum(grad_io * grad_io))
    factor = CLIP_NORM / jnp.maximum(grad_norm, CLIP_NORM)
    new_mat_weight, new_stat_left, new_stat_right, new_mat_ema = shampoo(
        mat_grad, mat_weight, mat_ema, stat_left, stat_right, root_left, root_right
    )
    step = step_count[0].astype(jnp.float32)
    new_mod = adamw(grad_table * factor, mod_table, mod_mom, mod_var, mod_ema, step)
    new_io = adamw(grad_io * factor, io_weight, io_mom, io_var, io_ema, step)
    return (
        total_loss * noised_total,
        noised_total,
        grad_norm,
        mat_grad,
        new_mat_weight,
        new_stat_left,
        new_stat_right,
        new_mat_ema,
        new_mod[0],
        new_mod[1],
        new_mod[2],
        new_mod[3],
        new_io[0],
        new_io[1],
        new_io[2],
        new_io[3],
    )


TOK = GRID * GRID
GROUP = 4


def fold_rows(values, op):
    return op(values.reshape(values.shape[0] // 8, 8, values.shape[1]), axis=0)


def side_by_side(ref, first, count, kind):
    parts = [ref[first + j, kind] for j in range(count)]
    return jnp.concatenate(parts, axis=1) if count > 1 else parts[0]


def attend_frame(t, qkv, scores, full, lse):
    q = qkv[t, 0] * jnp.bfloat16(HEAD_DIM**-0.5)

    def score(k, top):
        s = dotg(qkv[k, 1], q, 0, 0)
        scores[k] = s
        return jnp.maximum(top, fold_rows(s, jnp.max))

    top = lax.fori_loop(
        0, t + 1, score, jnp.full((8, TOK), -1e30, jnp.float32), unroll=min(GROUP, t + 1)
    )
    top = jnp.max(top, axis=0, keepdims=True)
    total = jnp.zeros((8, TOK), jnp.float32)
    acc = jnp.zeros((HEAD_DIM, TOK), jnp.float32)
    for k in range(0, t + 1, GROUP):
        count = min(GROUP, t + 1 - k)
        probs = []
        for j in range(count):
            p = jnp.exp(scores[k + j] - top)
            total = total + fold_rows(p, jnp.sum)
            probs.append(p.astype(jnp.bfloat16))
        acc = acc + dotg(side_by_side(qkv, k, count, 2), jnp.concatenate(probs, axis=0), 1, 0)
    total = jnp.sum(total, axis=0, keepdims=True)
    out = acc / total
    full[t] = out
    lse[t] = top + jnp.log(total)
    return out.astype(jnp.bfloat16)


def turn_back(values, cosine, sine):
    first, second = values[: HEAD_DIM // 2], values[HEAD_DIM // 2 :]
    return jnp.concatenate(
        [first * cosine + second * sine, second * cosine - first * sine], axis=0
    )


def attend_frame_back(t, qkv, do_ref, full, lse, cos, sin, dk_ref, dv_ref):
    q = qkv[t, 0] * jnp.bfloat16(HEAD_DIM**-0.5)
    do = do_ref[t]
    delta = jnp.sum(do.astype(jnp.float32) * full[t], axis=0, keepdims=True)
    dq = jnp.zeros((HEAD_DIM, TOK), jnp.float32)
    for k in range(0, t + 1, GROUP):
        count = min(GROUP, t + 1 - k)
        keys = side_by_side(qkv, k, count, 1)
        p = jnp.exp(dotg(keys, q, 0, 0) - lse[t])
        dp = dotg(side_by_side(qkv, k, count, 2), do, 0, 0)
        ds = (p * (dp - delta)).astype(jnp.bfloat16)
        dq = dq + dotg(keys, ds, 1, 0)
        dk = dotg(q, ds, 1, 1)
        dv = dotg(do, p.astype(jnp.bfloat16), 1, 1)
        for j in range(count):
            dk_ref[k + j] += dk[:, j * TOK : (j + 1) * TOK]
            dv_ref[k + j] += dv[:, j * TOK : (j + 1) * TOK]
    return (
        turn_back(dq * HEAD_DIM**-0.5, cos[t], sin[t]).astype(jnp.bfloat16),
        turn_back(dk_ref[t], cos[t], sin[t]).astype(jnp.bfloat16),
        dv_ref[t].astype(jnp.bfloat16),
    )


def attend_kernel(qkv_ref, low_ref, full_ref, lse_ref, scores):
    for t in range(qkv_ref.shape[0]):
        low_ref[t] = attend_frame(t, qkv_ref, scores, full_ref, lse_ref)


def attend(qkv):
    frames = qkv.shape[0]
    vmem = pl.BlockSpec(memory_space=pltpu.VMEM)
    return pl.pallas_call(
        attend_kernel,
        in_specs=[vmem],
        out_specs=[vmem] * 3,
        out_shape=[
            jax.ShapeDtypeStruct((frames, HEAD_DIM, TOK), jnp.bfloat16),
            jax.ShapeDtypeStruct((frames, HEAD_DIM, TOK), jnp.float32),
            jax.ShapeDtypeStruct((frames, 1, TOK), jnp.float32),
        ],
        scratch_shapes=[pltpu.VMEM((frames, TOK, TOK), jnp.float32)],
        compiler_params=pltpu.CompilerParams(vmem_limit_bytes=32 * 2**20),
    )(qkv)


def attend_back_kernel(qkv_ref, do_ref, full_ref, lse_ref, cos_ref, sin_ref, out_ref, dk, dv):
    dk[...] = jnp.zeros_like(dk)
    dv[...] = jnp.zeros_like(dv)
    for t in reversed(range(qkv_ref.shape[0])):
        parts = attend_frame_back(t, qkv_ref, do_ref, full_ref, lse_ref, cos_ref, sin_ref, dk, dv)
        for i in range(3):
            out_ref[t, i] = parts[i]


def attend_back(qkv, do, full, lse, cos, sin):
    frames = qkv.shape[0]
    vmem = pl.BlockSpec(memory_space=pltpu.VMEM)
    return pl.pallas_call(
        attend_back_kernel,
        in_specs=[vmem] * 6,
        out_specs=vmem,
        out_shape=jax.ShapeDtypeStruct(qkv.shape, jnp.bfloat16),
        scratch_shapes=[pltpu.VMEM((frames, HEAD_DIM, TOK), jnp.float32)] * 2,
        compiler_params=pltpu.CompilerParams(vmem_limit_bytes=32 * 2**20),
    )(qkv, do, full, lse, cos, sin)


MESH = pl.DeviceIdType.MESH
NSLOT = 24
FIRST = 14
LATER = NSLOT - FIRST
DATA = FIRST
SMALL_ROWS = 40
FIRST_GATHER = (
    ("xzy", 0, 3),
    ("xzy", 3, 2),
    ("yzx", 5, 3),
    ("yzx", 8, 2),
    ("zxy", 10, 2),
    ("zyx", 12, 3),
)
FIRST_SCATTER = FIRST_GATHER[:5] + (("zyx", 12, 2),)
LATER_PARTS = (("xzy", 0, 2), ("yzx", 2, 2), ("zxy", 4, 3), ("zyx", 7, 3))
LATER_SCATTER = (("zyx", 0, 3), ("zyx", 3, 3), ("zyx", 6, 4))


def place():
    frame = lax.axis_index("frame")
    return frame // 4, (frame // 2) % 2, frame % 2, lax.axis_index("rep")


def device(z, y, c, x):
    return ((z * 2 + y) * 2 + c, x)


def owner_of(z, y, c, x):
    return ((z * 2 + y) * 2 + c) * 2 + x


def plane_of(z, y, x):
    return (z * 2 + y) * 2 + x


def offsets():
    return [(dx, dy, dz) for dx in (0, 1) for dy in (0, 1) for dz in range(-3, 4)]


def hops(off):
    return off[0] + off[1] + abs(off[2])


def route_keys(parts):
    keys = [(part, off) for part in range(len(parts)) for off in offsets()]
    return sorted(keys, key=lambda k: (hops(k[1]), k[0]))


def onward(order, off):
    moved = dict(zip("xyz", off))
    last = max((order.index(k) for k in order if moved[k]), default=-1)
    links = []
    if last >= 0 and order[last] == "z":
        links.append("u" if off[2] < 0 else "w")
    for k in order[last + 1 :]:
        links.extend("uw" if k == "z" else k)
    return links


def toward(order, off):
    moved = dict(zip("xyz", off))
    last = [k for k in order if moved[k]][-1]
    if last == "z":
        return ("w", "u") if off[2] < 0 else ("u", "w")
    return last, last


def can(link, z):
    return {"u": z < 3, "w": z > 0}.get(link)


def partner(link, z, y, c, x):
    return {
        "x": device(z, y, c, 1 - x),
        "y": device(z, 1 - y, c, x),
        "u": device(z + 1, y, c, x),
        "w": device(z - 1, y, c, x),
        "c": device(z, y, 1 - c, x),
    }[link]


def when(cond, fn):
    if cond is None:
        fn()
    else:
        pl.when(cond)(fn)


def both(a, b):
    return b if a is None else a if b is None else jnp.logical_and(a, b)


def owner_at(off, z, y, x):
    dx, dy, dz = off
    oz = z + dz
    cond = None if dz == 0 else (oz <= 3 if dz > 0 else oz >= 0)
    return oz, (1 - y if dy else y), (1 - x if dx else x), cond


def greet(z, y, c, x, far=()):
    barrier = pltpu.get_barrier_semaphore()
    for link in "xyuwc":
        when(
            can(link, z),
            lambda link=link: pl.semaphore_signal(
                barrier, inc=1, device_id=partner(link, z, y, c, x), device_id_type=MESH
            ),
        )
    for dev in far:
        pl.semaphore_signal(barrier, inc=1, device_id=dev, device_id_type=MESH)
    ends = jnp.logical_or(z == 0, z == 3)
    pl.when(ends)(lambda: pl.semaphore_wait(barrier, 4 + len(far)))
    pl.when(jnp.logical_not(ends))(lambda: pl.semaphore_wait(barrier, 5 + len(far)))


class Gather:
    def __init__(self, parts, src, out, sems, where, shift=0):
        self.parts, self.src, self.out, self.where, self.shift = parts, src, out, where, shift
        self.total = sum(count for _, _, count in parts)
        self.send, self.recv, self.csend, self.crecv = sems
        self.keys = route_keys(parts)
        self.last = {}
        for key in self.keys:
            self.last[key[1]] = key
        self.sent = []

    @staticmethod
    def sems(parts):
        n = len(parts)
        return [
            pltpu.SemaphoreType.DMA((4, n, 16)),
            pltpu.SemaphoreType.DMA((n, 16)),
            pltpu.SemaphoreType.DMA((16,)),
            pltpu.SemaphoreType.DMA((16,)),
        ]

    def held(self, owner):
        return self.out.at[owner, pl.ds(self.shift, self.total)]

    def hop(self, link, part, src, owner, plane):
        _, first, count = self.parts[part]
        return pltpu.make_async_remote_copy(
            src_ref=src.at[pl.ds(first, count)],
            dst_ref=self.out.at[owner, pl.ds(self.shift + first, count)],
            send_sem=self.send.at["xyuw".index(link), part, plane],
            recv_sem=self.recv.at[part, plane],
            device_id=partner(link, *self.where),
            device_id_type=MESH,
        )

    def across(self, src, owner, plane):
        return pltpu.make_async_remote_copy(
            src_ref=src,
            dst_ref=self.held(owner),
            send_sem=self.csend.at[plane],
            recv_sem=self.crecv.at[plane],
            device_id=partner("c", *self.where),
            device_id_type=MESH,
        )

    def step(self, key):
        part, off = key
        z, y, c, x = self.where
        oz, oy, ox, cond = owner_at(off, z, y, x)
        owner, plane = owner_of(oz, oy, c, ox), plane_of(oz, oy, ox)
        own = off == (0, 0, 0)
        src = self.src if own else self.held(owner)
        links = onward(self.parts[part][0], off)

        def act():
            if not own:
                self.hop("x", part, src, owner, plane).wait_recv()
            for link in links:
                when(can(link, z), lambda link=link: self.hop(link, part, src, owner, plane).start())
            if self.last[off] == key:
                self.across(src, owner, plane).start()

        when(cond, act)
        for link in links:
            self.sent.append(
                (both(cond, can(link, z)), lambda link=link: self.hop(link, part, src, owner, plane))
            )
        if self.last[off] == key:
            self.sent.append((cond, lambda: self.across(src, owner, plane)))

    def finish(self):
        for cond, make in self.sent:
            when(cond, lambda make=make: make().wait_send())
        c = self.where[2]
        for plane in range(16):
            owner = owner_of(plane // 4, (plane // 2) % 2, 1 - c, plane % 2)
            self.across(self.held(owner), owner, plane).wait_recv()


def gather_kernel(perm_ref, w_ref, data_ref, out_ref, later_ref, stage, local, *sems):
    where = place()
    z, y, c, x = where

    def take(i, carry):
        stage[i] = w_ref[perm_ref[i]].astype(jnp.bfloat16)
        return carry

    def take_later(i, carry):
        later_ref[i] = w_ref[perm_ref[FIRST + i]].astype(jnp.bfloat16)
        return carry

    lax.fori_loop(0, FIRST, take, 0)
    stage[DATA] = data_ref[...]
    greet(*where)
    own = pltpu.make_async_copy(
        stage, out_ref.at[owner_of(z, y, c, x), pl.ds(0, FIRST + 1)], local.at[0]
    )
    own.start()
    gather = Gather(FIRST_GATHER, stage, out_ref, sems, where)
    for i, key in enumerate(gather.keys):
        gather.step(key)
        if i == len(FIRST_GATHER):
            lax.fori_loop(0, LATER, take_later, 0)
    gather.finish()
    own.wait()


def gather_weights(perm, blocks, data):
    vmem = pl.BlockSpec(memory_space=pltpu.VMEM)
    return pl.pallas_call(
        gather_kernel,
        out_shape=(
            jax.ShapeDtypeStruct((32, NSLOT + 1, BLOCK, BLOCK), jnp.bfloat16),
            jax.ShapeDtypeStruct((LATER, BLOCK, BLOCK), jnp.bfloat16),
        ),
        in_specs=[pl.BlockSpec(memory_space=pltpu.SMEM), vmem, vmem],
        out_specs=(pl.BlockSpec(memory_space=pltpu.HBM), vmem),
        scratch_shapes=[
            pltpu.VMEM((FIRST + 1, BLOCK, BLOCK), jnp.bfloat16),
            pltpu.SemaphoreType.DMA((1,)),
        ]
        + Gather.sems(FIRST_GATHER),
        compiler_params=pltpu.CompilerParams(
            collective_id=1, has_side_effects=True, vmem_limit_bytes=60 * 2**20
        ),
    )(perm, blocks, data)


def inbox_axes(order, link):
    dim = "z" if link in "uw" else link
    axes = order[: order.index(dim)]
    return axes + "z" if dim == "z" else axes


def inbox_starts(parts, link):
    starts, total = [], 0
    for order, _, count in parts:
        starts.append(total)
        size = count
        for d in inbox_axes(order, link):
            size *= 4 if d == "z" else 2
        total += size
    return starts, total


class Scatter:
    def __init__(self, parts, acc, sib, boxes, send, recvs, where, ready, store):
        self.parts, self.acc, self.sib, self.where = parts, acc, sib, where
        self.boxes = dict(zip("xyuw", boxes))
        self.recvs = dict(zip("xyuw", recvs))
        self.send, self.ready, self.store = send, ready, store
        self.keys = list(reversed(route_keys(parts)))
        self.seen = []
        for _, off in self.keys:
            if off not in self.seen:
                self.seen.append(off)
        self.fresh = set()

    @staticmethod
    def boxes_of(parts):
        return [
            pltpu.VMEM((inbox_starts(parts, link)[1], 128, 128), jnp.bfloat16) for link in "xyuw"
        ]

    @staticmethod
    def sems(parts):
        return [pltpu.SemaphoreType.DMA((len(parts), 16))] + [
            pltpu.SemaphoreType.DMA((len(parts), 16)) for _ in "xyuw"
        ]

    def inbox(self, link, part, oz, oy, ox):
        order, _, count = self.parts[part]
        index = 0
        for d in inbox_axes(order, link):
            index = index * (4 if d == "z" else 2) + {"z": oz, "y": oy, "x": ox}[d]
        return inbox_starts(self.parts, link)[0][part] + index * count

    def clear_ends(self):
        z = self.where[0]

        def clear(box):
            def body(i, carry):
                box[i] = jnp.zeros((128, 128), jnp.bfloat16)
                return carry

            lax.fori_loop(0, box.shape[0], body, 0)

        pl.when(z == 3)(lambda: clear(self.boxes["u"]))
        pl.when(z == 0)(lambda: clear(self.boxes["w"]))

    def hop(self, part, off):
        z, y, c, x = self.where
        oz, oy, ox, _ = owner_at(off, z, y, x)
        plane = plane_of(oz, oy, ox)
        order, first, count = self.parts[part]
        link, named = toward(order, off)
        return pltpu.make_async_remote_copy(
            src_ref=self.acc.at[plane, pl.ds(first, count)],
            dst_ref=self.boxes[named].at[pl.ds(self.inbox(named, part, oz, oy, ox), count)],
            send_sem=self.send.at[part, plane],
            recv_sem=self.recvs[named].at[part, plane],
            device_id=partner(link, *self.where),
            device_id_type=MESH,
        )

    def step(self, key):
        part, off = key
        z, y, c, x = self.where
        oz, oy, ox, cond = owner_at(off, z, y, x)
        plane = plane_of(oz, oy, ox)
        order, first, count = self.parts[part]
        new = off not in self.fresh
        self.fresh.add(off)

        def act():
            if new:
                self.ready(oz, oy, ox)
            sources = []
            for link in onward(order, off):
                start = self.inbox(link, part, oz, oy, ox)
                sources.append((self.boxes[link], start))

                def arrive(link=link, start=start):
                    view = self.boxes[link].at[pl.ds(start, count)]
                    pltpu.make_async_remote_copy(
                        src_ref=view,
                        dst_ref=view,
                        send_sem=self.send.at[part, plane],
                        recv_sem=self.recvs[link].at[part, plane],
                        device_id=partner("c", *self.where),
                        device_id_type=MESH,
                    ).wait_recv()

                when(can(link, z), arrive)

            def add(i, carry):
                total = self.acc[plane, first + i].astype(jnp.float32) + self.sib[
                    plane, first + i
                ].astype(jnp.float32)
                for box, start in sources:
                    total = total + box[start + i].astype(jnp.float32)
                if off == (0, 0, 0):
                    self.store(first + i, total)
                else:
                    self.acc[plane, first + i] = total.astype(jnp.bfloat16)
                return carry

            lax.fori_loop(0, count, add, 0)
            if off != (0, 0, 0):
                self.hop(part, off).start()

        when(cond, act)

    def finish(self):
        z, y, c, x = self.where
        for part, off in self.keys:
            if off != (0, 0, 0):
                cond = owner_at(off, z, y, x)[3]
                when(cond, lambda part=part, off=off: self.hop(part, off).wait_send())


class SmallSums:
    def __init__(self, row, io, rows_out, io_out, mine, inbox, sems, where):
        self.row, self.io, self.rows, self.io_out = row, io, rows_out, io_out
        self.mine, self.inbox, self.where = mine, inbox, where
        self.gsend, self.grecv, self.osend, self.orecv, self.bsend, self.brecv, self.local = sems
        self.order = "zyx"
        self.sent = []

    @staticmethod
    def sems():
        dma = pltpu.SemaphoreType.DMA
        return [dma((4, 16)), dma((16,)), dma((6,)), dma((6,)), dma((1,)), dma((1,)), dma((1,))]

    def far(self):
        z, y, c, x = self.where
        return device(z + 2 - 4 * (z // 2), y, c, x)

    def peer(self, turn):
        z, y, c, x = self.where
        if turn == 3:
            return device(z + 1 - 2 * (z % 2), y, c, x)
        if turn == 4:
            return self.far()
        return partner("cxyyyc"[turn], *self.where)

    def swap(self, turn):
        c = self.where[2]
        if turn == 0:
            src, dst = self.io.at[1 - c], self.inbox.at[0]
        elif turn == 5:
            src, dst = self.mine.at[5], self.io_out.at[c]
        else:
            src, dst = self.mine.at[turn], self.inbox.at[turn]
        return pltpu.make_async_remote_copy(
            src_ref=src,
            dst_ref=dst,
            send_sem=self.osend.at[turn],
            recv_sem=self.orecv.at[turn],
            device_id=self.peer(turn),
            device_id_type=MESH,
        )

    def hop(self, link, src, plane):
        return pltpu.make_async_remote_copy(
            src_ref=src,
            dst_ref=self.rows.at[self.where[2], plane],
            send_sem=self.gsend.at["xyuw".index(link), plane],
            recv_sem=self.grecv.at[plane],
            device_id=partner(link, *self.where),
            device_id_type=MESH,
        )

    def bulk(self, core):
        return pltpu.make_async_remote_copy(
            src_ref=self.rows.at[core],
            dst_ref=self.rows.at[core],
            send_sem=self.bsend.at[0],
            recv_sem=self.brecv.at[0],
            device_id=partner("c", *self.where),
            device_id_type=MESH,
        )

    def row_step(self, off):
        z, y, c, x = self.where
        oz, oy, ox, cond = owner_at(off, z, y, x)
        plane = plane_of(oz, oy, ox)
        own = off == (0, 0, 0)
        src = self.row if own else self.rows.at[c, plane]
        links = onward(self.order, off)

        def act():
            if not own:
                self.hop("x", src, plane).wait_recv()
            for link in links:
                when(can(link, z), lambda link=link: self.hop(link, src, plane).start())

        when(cond, act)
        for link in links:
            self.sent.append(
                (both(cond, can(link, z)), lambda link=link: self.hop(link, src, plane))
            )

    def begin(self):
        z, y, c, x = self.where
        self.own = pltpu.make_async_copy(
            self.row, self.rows.at[c, plane_of(z, y, x)], self.local.at[0]
        )
        self.own.start()
        self.swap(0).start()
        self.row_step((0, 0, 0))

    def turn(self, turn):
        c = self.where[2]
        self.swap(turn).wait_recv()
        if turn < 5:
            before = self.io[c] if turn == 0 else self.mine[turn]
            self.mine[turn + 1] = before + self.inbox[turn]
            if turn == 4:
                self.io_out[c] = self.mine[5]
            self.swap(turn + 1).start()

    def tasks(self):
        todo = [
            lambda off=off: self.row_step(off)
            for off in sorted(offsets(), key=hops)
            if off != (0, 0, 0)
        ]
        for turn in range(6):
            todo.insert(5 * turn + 2, lambda turn=turn: self.turn(turn))

        def last():
            self.own.wait()
            self.bulk(self.where[2]).start()

        return todo + [last]

    def finish(self):
        c = self.where[2]
        self.bulk(1 - c).wait_recv()
        self.bulk(c).wait_send()
        for turn in range(6):
            self.swap(turn).wait_send()
        for cond, make in self.sent:
            when(cond, lambda make=make: make().wait_send())


def own_blocks(g_ref, owner, first, count):
    return g_ref.at[owner, pl.ds(first, count)]


class Halves:
    def __init__(self, g_ref, first, count, acc, sib, csend, crecv, local, where):
        self.g_ref, self.first, self.count, self.acc, self.sib = g_ref, first, count, acc, sib
        self.csend, self.crecv, self.local, self.where = csend, crecv, local, where

    def across(self, oz, oy, ox):
        plane = plane_of(oz, oy, ox)
        other = owner_of(oz, oy, 1 - self.where[2], ox)
        return pltpu.make_async_remote_copy(
            src_ref=own_blocks(self.g_ref, other, self.first, self.count),
            dst_ref=self.sib.at[plane],
            send_sem=self.csend.at[plane],
            recv_sem=self.crecv.at[plane],
            device_id=partner("c", *self.where),
            device_id_type=MESH,
        )

    def load(self, oz, oy, ox):
        plane = plane_of(oz, oy, ox)
        same = owner_of(oz, oy, self.where[2], ox)
        return pltpu.make_async_copy(
            own_blocks(self.g_ref, same, self.first, self.count),
            self.acc.at[plane],
            self.local.at[plane],
        )

    def begin(self, offs):
        z, y, c, x = self.where
        for off in offs:
            oz, oy, ox, cond = owner_at(off, z, y, x)

            def start(oz=oz, oy=oy, ox=ox):
                self.across(oz, oy, ox).start()
                self.load(oz, oy, ox).start()

            when(cond, start)

    def ready(self, oz, oy, ox):
        self.across(oz, oy, ox).wait_recv()
        self.load(oz, oy, ox).wait()

    def finish(self):
        for plane in range(16):
            self.across(plane // 4, (plane // 2) % 2, plane % 2).wait_send()


def scatter_kernel(rank_ref, g_ref, row_ref, io_ref, later_ref, out_ref, rows_out, io_out, *refs):
    acc, sib, total = refs[:3]
    boxes, refs = refs[3:7], refs[7:]
    mine, inbox = refs[:2]
    csend, crecv, local, send = refs[2:6]
    recvs, small_sems = refs[6:10], refs[10:]
    where = place()
    z, y, c, x = where
    small = SmallSums(row_ref, io_ref, rows_out, io_out, mine, inbox, small_sems, where)
    greet(*where, far=(small.far(),))
    small.begin()

    halves = Halves(g_ref, 0, FIRST, acc, sib, csend, crecv, local, where)

    def store(row, value):
        total[row] = value

    scatter = Scatter(FIRST_SCATTER, acc, sib, boxes, send, recvs, where, halves.ready, store)
    halves.begin(scatter.seen)
    scatter.clear_ends()
    tasks = small.tasks()
    for i, key in enumerate(scatter.keys):
        scatter.step(key)
        if i % 5 == 4 and tasks:
            tasks.pop(0)()
    for task in tasks:
        task()

    def keep(i, carry):
        total[FIRST + i] = later_ref[i]
        return carry

    lax.fori_loop(0, LATER, keep, 0)

    def put(i, carry):
        out_ref[i] = total[rank_ref[i]]
        return carry

    lax.fori_loop(0, NSLOT, put, 0)
    scatter.finish()
    halves.finish()
    small.finish()


def scatter_grads(ranks, grads, row, io, later):
    vmem = pl.BlockSpec(memory_space=pltpu.VMEM)
    dma = pltpu.SemaphoreType.DMA
    held = pltpu.VMEM((16, FIRST, BLOCK, BLOCK), jnp.bfloat16)
    half = (SMALL_ROWS, D // 2)
    return pl.pallas_call(
        scatter_kernel,
        out_shape=(
            jax.ShapeDtypeStruct((NSLOT, 128, 128), jnp.float32),
            jax.ShapeDtypeStruct((2, 16) + row.shape, jnp.float32),
            jax.ShapeDtypeStruct((2,) + half, jnp.float32),
        ),
        in_specs=[
            pl.BlockSpec(memory_space=pltpu.SMEM),
            pl.BlockSpec(memory_space=pl.ANY),
            vmem,
            vmem,
            vmem,
        ],
        out_specs=(vmem, vmem, vmem),
        scratch_shapes=[held, held, pltpu.VMEM((NSLOT, 128, 128), jnp.float32)]
        + Scatter.boxes_of(FIRST_SCATTER)
        + [pltpu.VMEM((6,) + half, jnp.float32), pltpu.VMEM((6,) + half, jnp.float32)]
        + [dma((16,)), dma((16,)), dma((16,))]
        + Scatter.sems(FIRST_SCATTER)
        + SmallSums.sems(),
        compiler_params=pltpu.CompilerParams(
            collective_id=2, has_side_effects=True, vmem_limit_bytes=58 * 2**20
        ),
    )(ranks, grads, row, io, later)


def clip_peers(frame, fn):
    count = lax.axis_size("frame")

    def body(step, carry):
        peer = lax.rem(frame + step, count)
        fn(step, peer, (peer, lax.axis_index("rep")))
        return carry

    lax.fori_loop(1, count, body, 0)


def greet_clip(frame, where):
    barrier = pltpu.get_barrier_semaphore()
    clip_peers(
        frame,
        lambda step, peer, dev: pl.semaphore_signal(
            barrier, inc=1, device_id=dev, device_id_type=MESH
        ),
    )
    pl.semaphore_signal(barrier, inc=1, device_id=partner("x", *where), device_id_type=MESH)
    pl.semaphore_wait(barrier, lax.axis_size("frame"))


class Exchange:
    def __init__(self, src, dst, send, recv, frame):
        self.src, self.dst, self.send, self.recv, self.frame = src, dst, send, recv, frame

    @staticmethod
    def sems():
        return [pltpu.SemaphoreType.DMA((16,)), pltpu.SemaphoreType.DMA((16,))]

    def copy(self, peer):
        return pltpu.make_async_remote_copy(
            src_ref=self.src.at[peer],
            dst_ref=self.dst.at[self.frame],
            send_sem=self.send.at[peer],
            recv_sem=self.recv.at[self.frame],
            device_id=(peer, lax.axis_index("rep")),
            device_id_type=MESH,
        )

    def own(self):
        self.dst[self.frame] = self.src[self.frame]

    def start_all(self):
        clip_peers(self.frame, lambda step, peer, dev: self.copy(peer).start())
        self.own()

    def start(self, peer):
        pl.when(self.frame != peer)(lambda: self.copy(peer).start())
        pl.when(self.frame == peer)(self.own)

    def arrived(self, peer):
        def wait():
            pltpu.make_async_remote_copy(
                src_ref=self.src.at[peer],
                dst_ref=self.dst.at[peer],
                send_sem=self.send.at[peer],
                recv_sem=self.recv.at[peer],
                device_id=(peer, lax.axis_index("rep")),
                device_id_type=MESH,
            ).wait_recv()

        pl.when(self.frame != peer)(wait)

    def all_arrived(self):
        for peer in range(16):
            self.arrived(peer)

    def finish(self):
        for peer in range(16):
            pl.when(self.frame != peer)(lambda peer=peer: self.copy(peer).wait_send())


def spread_evenly(steps, slots, weights):
    total, taken, acc, runs = sum(weights), 0, 0, []
    for slot in range(slots):
        acc += weights[slot]
        upto = round(len(steps) * acc / total)
        runs.append(steps[taken:upto])
        taken = upto
    return runs


def forward_kernel(
    parts_ref, stage_ref, blocks_in, mine_ref, blocks_ref, olt_ref, full_ref, lse_ref, scores, low, *sems
):
    where = place()
    frame = lax.axis_index("frame")
    qkv = Exchange(parts_ref, mine_ref, sems[0], sems[1], frame)
    back = Exchange(low, olt_ref, sems[2], sems[3], frame)
    local, gather_sems = sems[4], sems[5:]
    greet_clip(frame, where)
    qkv.start_all()
    gather = Gather(LATER_PARTS, stage_ref, blocks_ref, gather_sems, where, FIRST + 1)
    own = pltpu.make_async_copy(stage_ref, gather.held(owner_of(*where)), local.at[0])
    own.start()
    first = len(LATER_PARTS)
    for key in gather.keys[:first]:
        gather.step(key)
    frames = mine_ref.shape[0]
    runs = spread_evenly(gather.keys[first:], frames, FORWARD_WEIGHTS)
    for t in range(frames):
        for key in runs[t]:
            gather.step(key)
        qkv.arrived(t)
        low[t] = attend_frame(t, mine_ref, scores, full_ref, lse_ref)
        back.start(t)
    gather.finish()
    own.wait()
    qkv.finish()
    back.all_arrived()
    back.finish()


FORWARD_WEIGHTS = (50,) + (2,) * 7 + (6,) * 8


def forward_exchange(parts, stage, blocks):
    frames = 16
    vmem = pl.BlockSpec(memory_space=pltpu.VMEM)
    return pl.pallas_call(
        forward_kernel,
        in_specs=[vmem] * 2 + [pl.BlockSpec(memory_space=pltpu.HBM)],
        out_specs=[vmem, pl.BlockSpec(memory_space=pltpu.HBM), vmem, vmem, vmem],
        input_output_aliases={2: 1},
        out_shape=[
            jax.ShapeDtypeStruct((frames,) + parts.shape[1:], jnp.bfloat16),
            jax.ShapeDtypeStruct(blocks.shape, blocks.dtype),
            jax.ShapeDtypeStruct((HEADS, HEAD_DIM, TOK), jnp.bfloat16),
            jax.ShapeDtypeStruct((frames, HEAD_DIM, TOK), jnp.float32),
            jax.ShapeDtypeStruct((frames, 1, TOK), jnp.float32),
        ],
        scratch_shapes=[
            pltpu.VMEM((frames, TOK, TOK), jnp.float32),
            pltpu.VMEM((frames, HEAD_DIM, TOK), jnp.bfloat16),
        ]
        + Exchange.sems()
        + Exchange.sems()
        + [pltpu.SemaphoreType.DMA((1,))]
        + Gather.sems(LATER_PARTS),
        compiler_params=pltpu.CompilerParams(
            collective_id=3, has_side_effects=True, vmem_limit_bytes=56 * 2**20
        ),
    )(parts, stage, blocks)


def backward_kernel(
    heads_ref, mine_ref, full_ref, lse_ref, cos_ref, sin_ref, g_ref, drt_ref, later_ref, *refs
):
    do, grads, dk, dv, acc, sib = refs[:6]
    boxes, sems = refs[6:10], refs[10:]
    where = place()
    frame = lax.axis_index("frame")
    inward = Exchange(heads_ref, do, sems[0], sems[1], frame)
    outward = Exchange(grads, drt_ref, sems[2], sems[3], frame)
    csend, crecv, local, send = sems[4:8]
    halves = Halves(g_ref, FIRST, LATER, acc, sib, csend, crecv, local, where)

    def store(row, value):
        later_ref[row] = value

    scatter = Scatter(LATER_SCATTER, acc, sib, boxes, send, sems[8:12], where, halves.ready, store)
    greet_clip(frame, where)
    inward.start_all()
    halves.begin(scatter.seen)
    scatter.clear_ends()
    dk[...] = jnp.zeros_like(dk)
    dv[...] = jnp.zeros_like(dv)
    frames = mine_ref.shape[0]
    runs = spread_evenly(scatter.keys, frames + 1, BACKWARD_WEIGHTS)
    for i, t in enumerate(reversed(range(frames))):
        for key in runs[i]:
            scatter.step(key)
        inward.arrived(t)
        parts = attend_frame_back(t, mine_ref, do, full_ref, lse_ref, cos_ref, sin_ref, dk, dv)
        for kind in range(3):
            grads[t, kind] = parts[kind]
        outward.start(t)
    for key in runs[frames]:
        scatter.step(key)
    scatter.finish()
    halves.finish()
    inward.finish()
    outward.all_arrived()
    outward.finish()


BACKWARD_WEIGHTS = (16,) + (6,) * 8 + (4,) * 7 + (16,)


def backward_exchange(heads, mine, full, lse, cos, sin, grads):
    frames = mine.shape[0]
    vmem = pl.BlockSpec(memory_space=pltpu.VMEM)
    dma = pltpu.SemaphoreType.DMA
    held = pltpu.VMEM((16, LATER, BLOCK, BLOCK), jnp.bfloat16)
    return pl.pallas_call(
        backward_kernel,
        in_specs=[vmem] * 6 + [pl.BlockSpec(memory_space=pltpu.HBM)],
        out_specs=[vmem, vmem],
        out_shape=[
            jax.ShapeDtypeStruct((HEADS,) + mine.shape[1:], jnp.bfloat16),
            jax.ShapeDtypeStruct((LATER, BLOCK, BLOCK), jnp.float32),
        ],
        scratch_shapes=[
            pltpu.VMEM((frames, HEAD_DIM, TOK), jnp.bfloat16),
            pltpu.VMEM((frames, 3, HEAD_DIM, TOK), jnp.bfloat16),
            pltpu.VMEM((frames, HEAD_DIM, TOK), jnp.float32),
            pltpu.VMEM((frames, HEAD_DIM, TOK), jnp.float32),
            held,
            held,
        ]
        + Scatter.boxes_of(LATER_SCATTER)
        + Exchange.sems()
        + Exchange.sems()
        + [dma((16,)), dma((16,)), dma((16,))]
        + Scatter.sems(LATER_SCATTER),
        compiler_params=pltpu.CompilerParams(
            collective_id=4, has_side_effects=True, vmem_limit_bytes=56 * 2**20
        ),
    )(heads, mine, full, lse, cos, sin, grads)


def late_gather_kernel(stage_ref, blocks_in, blocks_ref, local, *sems):
    where = place()
    greet(*where)
    gather = Gather(LATER_PARTS, stage_ref, blocks_ref, sems, where, FIRST + 1)
    own = pltpu.make_async_copy(stage_ref, gather.held(owner_of(*where)), local.at[0])
    own.start()
    for key in gather.keys:
        gather.step(key)
    gather.finish()
    own.wait()


def late_gather(stage, blocks):
    hbm = pl.BlockSpec(memory_space=pltpu.HBM)
    return pl.pallas_call(
        late_gather_kernel,
        in_specs=[pl.BlockSpec(memory_space=pltpu.VMEM), hbm],
        out_specs=hbm,
        out_shape=jax.ShapeDtypeStruct(blocks.shape, blocks.dtype),
        scratch_shapes=[pltpu.SemaphoreType.DMA((1,))] + Gather.sems(LATER_PARTS),
        input_output_aliases={1: 0},
        compiler_params=pltpu.CompilerParams(
            collective_id=5, has_side_effects=True, vmem_limit_bytes=56 * 2**20
        ),
    )(stage, blocks)


def late_scatter_kernel(g_ref, later_ref, *refs):
    acc, sib, boxes, sems = refs[0], refs[1], refs[2:6], refs[6:]
    where = place()
    halves = Halves(g_ref, FIRST, LATER, acc, sib, sems[0], sems[1], sems[2], where)

    def store(row, value):
        later_ref[row] = value

    scatter = Scatter(LATER_SCATTER, acc, sib, boxes, sems[3], sems[4:8], where, halves.ready, store)
    greet(*where)
    halves.begin(scatter.seen)
    scatter.clear_ends()
    for key in scatter.keys:
        scatter.step(key)
    scatter.finish()
    halves.finish()


def late_scatter(grads):
    dma = pltpu.SemaphoreType.DMA
    held = pltpu.VMEM((16, LATER, BLOCK, BLOCK), jnp.bfloat16)
    return pl.pallas_call(
        late_scatter_kernel,
        in_specs=[pl.BlockSpec(memory_space=pltpu.HBM)],
        out_specs=pl.BlockSpec(memory_space=pltpu.VMEM),
        out_shape=jax.ShapeDtypeStruct((LATER, BLOCK, BLOCK), jnp.float32),
        scratch_shapes=[held, held]
        + Scatter.boxes_of(LATER_SCATTER)
        + [dma((16,)), dma((16,)), dma((16,))]
        + Scatter.sems(LATER_SCATTER),
        compiler_params=pltpu.CompilerParams(
            collective_id=6, has_side_effects=True, vmem_limit_bytes=56 * 2**20
        ),
    )(grads)


TILE = 512
LIMIT = pltpu.CompilerParams(vmem_limit_bytes=60 * 2**20)


def dotg(left, right, left_dim, right_dim):
    return lax.dot_general(
        left, right, (((left_dim,), (right_dim,)), ((), ())), preferred_element_type=jnp.float32
    )


def block_of(held, row, col):
    return held.at[
        pl.ds(pl.multiple_of(row * BLOCK, BLOCK), BLOCK),
        pl.ds(pl.multiple_of(col * BLOCK, BLOCK), BLOCK),
    ]


def move_tile(places, blocks, held, sem, start, across, row, rows, col, cols, outward=False):
    for r in range(rows):
        for c in range(cols):
            slot = blocks.at[places[start + (row + r) * across + col + c]]
            here = block_of(held, row + r, col + c)
            src, dst = (here, slot) if outward else (slot, here)
            pltpu.make_async_copy(src, dst, sem).start()


def settled(view, sem):
    pltpu.make_async_copy(view, view, sem).wait()


def column_sum(values):
    return jnp.sum(values, axis=0, keepdims=True)


def project_kernel(
    source, places, blocks, table_ref, head_ref, bias_ref, cos_ref, sin_ref,
    h0_ref, at_ref, out_ref, mod_ref, target_ref, xt_ref, scalars_ref,
    held, a_ref, data, flags, sems, small_sems,
):
    across = 3 * D // BLOCK
    per = TILE // BLOCK
    tiles = 3 * D // TILE
    mine = pltpu.make_async_copy(blocks.at[source[0] * (NSLOT + 1) + DATA], data, small_sems.at[0])
    mine.start()

    def flag(owner):
        return pltpu.make_async_copy(
            blocks.at[owner * (NSLOT + 1) + DATA, pl.ds(96, 16)], flags.at[owner], small_sems.at[1]
        )

    for owner in range(32):
        flag(owner).start()
    for j in range(tiles):
        move_tile(places, blocks, held, sems.at[j], 0, across, 0, D // BLOCK, j * per, per)
    mine.wait()
    settled(flags, small_sems.at[1])
    xt = data[0:32]
    xt_ref[...] = jnp.concatenate([xt.reshape(PIN, 2, BLOCK)[:, i] for i in range(2)], axis=1)
    noise = data[32:64].astype(jnp.float32) + data[64:96].astype(jnp.float32)
    target_ref[...] = jnp.concatenate([noise.reshape(PIN, 2, BLOCK)[:, i] for i in range(2)], axis=1)
    noised = data[96:97].astype(jnp.float32)
    level = data[112:113].astype(jnp.float32)
    total = flags[0].astype(jnp.float32)
    for owner in range(1, 32):
        total = total + flags[owner].astype(jnp.float32)
    total = jnp.maximum(total[0:1], 1.0)
    scalars_ref[0:1] = noised
    scalars_ref[1:2] = 1.0 / (total * (TOK * PIN))
    scalars_ref[2:3] = total
    scalars_ref[3:4] = level
    scalars_ref[4:8] = jnp.zeros((4, BLOCK), jnp.float32)
    rows = lax.broadcasted_iota(jnp.int32, (LEVELS, D), 0).astype(jnp.float32)
    picked = rows == level[0:1, 0:1]
    for i in range(8):
        mod_ref[i : i + 1] = column_sum(jnp.where(picked, table_ref[:, i * D : (i + 1) * D], 0.0))
    start = dotg(xt_ref[...], head_ref[0:PIN], 0, 0) + bias_ref[...]
    h0_ref[...] = start
    hat, _ = layer_norm(start)
    normed = hat * (1 + mod_ref[1:2]) + mod_ref[0:1]
    a_ref[...] = normed.astype(jnp.bfloat16)
    at_ref[...] = normed.T.astype(jnp.bfloat16)
    heads = TILE // HEAD_DIM
    half = HEAD_DIM // 2
    frame = lax.axis_index("frame")
    c, s = cos_ref[frame], sin_ref[frame]
    for j in range(tiles):
        settled(held.at[:, pl.ds(j * TILE, TILE)], sems.at[j])
        r = matmul(a_ref[...], held[:, j * TILE : (j + 1) * TILE]).T
        kind, head = j // (D // TILE), j % (D // TILE) * heads
        for i in range(heads):
            own = r[i * HEAD_DIM : (i + 1) * HEAD_DIM]
            if kind < 2:
                first, second = own[:half], own[half:]
                own = jnp.concatenate(
                    [first * c - second * s, first * s + second * c], axis=0
                )
            out_ref[head + i, kind] = own.astype(jnp.bfloat16)


def project(source, places, blocks, table, head, bias, cos, sin):
    vmem, smem = pl.BlockSpec(memory_space=pltpu.VMEM), pl.BlockSpec(memory_space=pltpu.SMEM)
    f32, bf16 = jnp.float32, jnp.bfloat16
    return pl.pallas_call(
        project_kernel,
        in_specs=[smem, smem, pl.BlockSpec(memory_space=pltpu.HBM)] + [vmem] * 5,
        out_specs=[vmem] * 7,
        out_shape=[
            jax.ShapeDtypeStruct((TOK, D), f32),
            jax.ShapeDtypeStruct((D, TOK), bf16),
            jax.ShapeDtypeStruct((HEADS, 3, HEAD_DIM, TOK), bf16),
            jax.ShapeDtypeStruct((8, D), f32),
            jax.ShapeDtypeStruct((PIN, TOK), f32),
            jax.ShapeDtypeStruct((PIN, TOK), bf16),
            jax.ShapeDtypeStruct((8, BLOCK), f32),
        ],
        scratch_shapes=[
            pltpu.VMEM((D, 3 * D), bf16),
            pltpu.VMEM((TOK, D), bf16),
            pltpu.VMEM((BLOCK, BLOCK), bf16),
            pltpu.VMEM((32, 16, BLOCK), bf16),
            pltpu.SemaphoreType.DMA((3 * D // TILE,)),
            pltpu.SemaphoreType.DMA((2,)),
        ],
        compiler_params=LIMIT,
    )(source, places, blocks, table, head, bias, cos, sin)


GELU_A = math.sqrt(2.0 / math.pi)
GELU_B = 0.044715


def middle_kernel(
    places, slots, blocks, olt_ref, h0_ref, mod_ref, head_ref, target_ref, scalars_ref,
    dot_ref, grads_ref, dh1_ref, dhead_ref, dmod_ref, loss_ref,
    wo, wup, wdown, gout, gup, gdown, slope, act, bt, dz_ref, db_ref, h1_ref, y_ref, z_ref, sems, out_sems,
):
    starts, _ = matrix_starts()
    per = TILE // BLOCK
    wide = D // BLOCK
    up_tiles = FFN // TILE
    up_across = FFN // BLOCK

    def fetch_up(j):
        move_tile(places, blocks, wup, sems.at[1 + j], starts[2], up_across, 0, wide, j * per, per)

    def fetch_down(j):
        move_tile(places, blocks, wdown, sems.at[9 + j], starts[3], wide, j * per, per, 0, wide)

    move_tile(places, blocks, wo, sems.at[0], starts[1], wide, 0, wide, 0, wide)
    fetch_up(0)
    fetch_up(1)
    attended = olt_ref[...].astype(jnp.float32).T.astype(jnp.bfloat16)
    settled(wo, sems.at[0])
    y = matmul(attended, wo[...])
    y_ref[...] = y
    h1 = h0_ref[...] + mod_ref[2:3] * y
    h1_ref[...] = h1
    hat_two, _ = layer_norm(h1)
    b32 = hat_two * (1 + mod_ref[4:5]) + mod_ref[3:4]
    bt[...] = b32.T.astype(jnp.bfloat16)
    b = b32.astype(jnp.bfloat16)
    dz_ref[...] = b

    def rise(j, carry):
        col = pl.multiple_of(j * TILE, TILE)
        settled(wup.at[:, pl.ds(col, TILE)], sems.at[1 + j])
        fetch_down(j)
        pl.when(j < up_tiles - 2)(lambda: fetch_up(j + 2))
        u = matmul(dz_ref[...], wup[:, pl.ds(col, TILE)])
        square = u * u
        t = jnp.tanh(GELU_A * (u + GELU_B * (square * u)))
        cdf = 0.5 * (1.0 + t)
        act[:, pl.ds(col, TILE)] = (u * cdf).astype(jnp.bfloat16)
        slope[:, pl.ds(col, TILE)] = cdf + (0.5 * GELU_A) * u * (1.0 - t * t) * (
            1.0 + (3.0 * GELU_B) * square
        )
        return carry

    lax.fori_loop(0, up_tiles, rise, 0)
    for j in range(up_tiles):
        settled(wdown.at[pl.ds(j * TILE, TILE)], sems.at[9 + j])

    def fall(j, carry):
        col = pl.multiple_of(j * 256, 256)
        z_ref[:, pl.ds(col, 256)] = matmul(act[...], wdown[:, pl.ds(col, 256)])
        return carry

    lax.fori_loop(0, D // 256, fall, 0)
    z = z_ref[...]
    h2 = h1_ref[...] + mod_ref[5:6] * z
    hat_three, inv_three = layer_norm(h2)
    c = (hat_three * (1 + mod_ref[7:8]) + mod_ref[6:7]).astype(jnp.bfloat16)
    noised, inv_scale = scalars_ref[0:1, 0:1], scalars_ref[1:2, 0:1]
    difference = dotg(head_ref[...], c, 1, 1) - target_ref[...]
    loss_ref[...] = jnp.full((1, BLOCK), 1.0, jnp.float32) * (
        jnp.sum(jnp.sum(difference * difference, axis=0, keepdims=True), axis=1, keepdims=True)
        * (noised * inv_scale)
    )
    dpred = (2.0 * inv_scale * noised * difference).astype(jnp.bfloat16)
    dhead_ref[...] = matmul(dpred, c)
    dc = dotg(dpred, head_ref[...], 0, 0)
    dmod_ref[6:7] = column_sum(dc)
    dmod_ref[7:8] = column_sum(dc * hat_three)
    dh2 = norm_back(dc * (1 + mod_ref[7:8]), hat_three, inv_three)
    dmod_ref[5:6] = column_sum(dh2 * z)
    dz_ref[...] = (dh2 * mod_ref[5:6]).astype(jnp.bfloat16)
    z_ref[...] = dh2
    db_ref[...] = jnp.zeros_like(db_ref)

    def back(j, carry):
        col = pl.multiple_of(j * TILE, TILE)
        du = (
            slope[:, pl.ds(col, TILE)] * dotg(dz_ref[...], wdown[pl.ds(col, TILE)], 1, 1)
        ).astype(jnp.bfloat16)
        gdown[pl.ds(col, TILE)] = dotg(act[:, pl.ds(col, TILE)], dz_ref[...], 0, 0).astype(
            jnp.bfloat16
        )
        move_tile(
            slots, grads_ref, gdown, out_sems.at[0], starts[3], wide, j * per, per, 0, wide, True
        )
        gup[:, pl.ds(col, TILE)] = matmul(bt[...], du).astype(jnp.bfloat16)
        move_tile(
            slots, grads_ref, gup, out_sems.at[1], starts[2], up_across, 0, wide, j * per, per, True
        )
        db_ref[...] += dotg(du, wup[:, pl.ds(col, TILE)], 1, 1)
        return carry

    lax.fori_loop(0, up_tiles, back, 0)
    hat_two, inv_two = layer_norm(h1_ref[...])
    db = db_ref[...]
    dmod_ref[3:4] = column_sum(db)
    dmod_ref[4:5] = column_sum(db * hat_two)
    dh1 = z_ref[...] + norm_back(db * (1 + mod_ref[4:5]), hat_two, inv_two)
    dh1_ref[...] = dh1
    dmod_ref[2:3] = column_sum(dh1 * y_ref[...])
    dmod_ref[0:2] = jnp.zeros((2, D), jnp.float32)
    dz_ref[...] = (dh1 * mod_ref[2:3]).astype(jnp.bfloat16)
    gout[...] = matmul(olt_ref[...], dz_ref[...]).astype(jnp.bfloat16)
    move_tile(slots, grads_ref, gout, out_sems.at[2], starts[1], wide, 0, wide, 0, wide, True)
    for j in range(D // TILE):
        rows = pl.ds(j * TILE, TILE)
        dot_ref[rows] = dotg(wo[rows], dz_ref[...], 1, 1).astype(jnp.bfloat16)
    settled(gdown, out_sems.at[0])
    settled(gup, out_sems.at[1])
    settled(gout, out_sems.at[2])


def middle(places, slots, blocks, olt, h0, mod, head, target, scalars):
    vmem, smem = pl.BlockSpec(memory_space=pltpu.VMEM), pl.BlockSpec(memory_space=pltpu.SMEM)
    hbm = pl.BlockSpec(memory_space=pltpu.HBM)
    f32, bf16 = jnp.float32, jnp.bfloat16
    up, down, square = pltpu.VMEM((D, FFN), bf16), pltpu.VMEM((FFN, D), bf16), pltpu.VMEM((D, D), bf16)
    rows = pltpu.VMEM((TOK, D), f32)
    return pl.pallas_call(
        middle_kernel,
        in_specs=[smem, smem, hbm] + [vmem] * 6,
        out_specs=[vmem, hbm] + [vmem] * 4,
        out_shape=[
            jax.ShapeDtypeStruct((D, TOK), bf16),
            jax.ShapeDtypeStruct((32 * NSLOT, BLOCK, BLOCK), bf16),
            jax.ShapeDtypeStruct((TOK, D), f32),
            jax.ShapeDtypeStruct((PIN, D), f32),
            jax.ShapeDtypeStruct((8, D), f32),
            jax.ShapeDtypeStruct((1, BLOCK), f32),
        ],
        scratch_shapes=[square, up, down, square, up, down]
        + [
            pltpu.VMEM((TOK, FFN), f32),
            pltpu.VMEM((TOK, FFN), bf16),
            pltpu.VMEM((D, TOK), bf16),
            pltpu.VMEM((TOK, D), bf16),
            rows,
            rows,
            rows,
            rows,
            pltpu.SemaphoreType.DMA((17,)),
            pltpu.SemaphoreType.DMA((3,)),
        ],
        compiler_params=LIMIT,
    )(places, slots, blocks, olt, h0, mod, head, target, scalars)


def final_kernel(
    places, slots, blocks, drt_ref, at_ref, h0_ref, mod_ref, dh1_ref, xt_ref, dmod_in, scalars_ref, loss_ref,
    dhead_ref, grads_in, grads_ref, row_ref, io_ref, held, gqkv, flat, sems, out_sem,
):
    across = 3 * D // BLOCK
    per = TILE // BLOCK
    for j in range(2):
        move_tile(places, blocks, held, sems.at[j], 0, across, j * per, per, 0, across)
    for kind in range(3):
        for head in range(HEADS):
            row = kind * D + head * HEAD_DIM
            flat[row : row + HEAD_DIM] = drt_ref[head, kind]
    for j in range(3 * D // TILE):
        cols = slice(j * TILE, (j + 1) * TILE)
        gqkv[:, cols] = dotg(at_ref[...], flat[cols], 1, 1).astype(jnp.bfloat16)
        move_tile(slots, grads_ref, gqkv, out_sem.at[0], 0, across, 0, D // BLOCK, j * per, per, True)
    for j in range(2):
        settled(held.at[pl.ds(j * TILE, TILE)], sems.at[j])
    da = matmul(held[...], flat[...]).T
    hat, inverse = layer_norm(h0_ref[...])

    def put_row(i, values):
        for k in range(D // BLOCK):
            row_ref[i * (D // BLOCK) + k : i * (D // BLOCK) + k + 1] = values[
                :, k * BLOCK : (k + 1) * BLOCK
            ]

    put_row(0, column_sum(da))
    put_row(1, column_sum(da * hat))
    for i in range(2, 8):
        put_row(i, dmod_in[i : i + 1])
    row_ref[64:68] = jnp.broadcast_to(scalars_ref[3:4], (4, BLOCK))
    row_ref[68:72] = jnp.broadcast_to(loss_ref[...], (4, BLOCK))
    dh0 = (dh1_ref[...] + norm_back(da * (1 + mod_ref[1:2]), hat, inverse)).astype(jnp.bfloat16)
    dembed = matmul(xt_ref[...], dh0)
    dbias = column_sum(dh0.astype(jnp.float32))
    for i in range(2):
        cols = slice(i * D // 2, (i + 1) * D // 2)
        io_ref[i, 0:PIN] = dembed[:, cols]
        io_ref[i, PIN : 2 * PIN] = dhead_ref[:, cols]
        io_ref[i, 2 * PIN :] = jnp.zeros((SMALL_ROWS - 2 * PIN, D // 2), jnp.float32)
        io_ref[i, 2 * PIN : 2 * PIN + 1] = dbias[:, cols]
    settled(gqkv, out_sem.at[0])


def final(places, slots, blocks, drt, at, h0, mod, dh1, xt, dmod, scalars, loss, dhead, grads):
    vmem, smem = pl.BlockSpec(memory_space=pltpu.VMEM), pl.BlockSpec(memory_space=pltpu.SMEM)
    hbm = pl.BlockSpec(memory_space=pltpu.HBM)
    f32, bf16 = jnp.float32, jnp.bfloat16
    return pl.pallas_call(
        final_kernel,
        in_specs=[smem, smem, hbm] + [vmem] * 10 + [hbm],
        out_specs=[hbm] + [vmem] * 2,
        out_shape=[
            jax.ShapeDtypeStruct(grads.shape, grads.dtype),
            jax.ShapeDtypeStruct((8 * D // BLOCK + 8, BLOCK), f32),
            jax.ShapeDtypeStruct((2, SMALL_ROWS, D // 2), f32),
        ],
        scratch_shapes=[
            pltpu.VMEM((D, 3 * D), bf16),
            pltpu.VMEM((D, 3 * D), bf16),
            pltpu.VMEM((3 * D, TOK), bf16),
            pltpu.SemaphoreType.DMA((2,)),
            pltpu.SemaphoreType.DMA((1,)),
        ],
        input_output_aliases={13: 0},
        compiler_params=LIMIT,
    )(places, slots, blocks, drt, at, h0, mod, dh1, xt, dmod, scalars, loss, dhead, grads)


def top_dot(left, right, left_dim, right_dim):
    return lax.dot_general(
        left,
        right,
        (((left_dim,), (right_dim,)), ((), ())),
        precision=TOP_PRECISION,
        preferred_element_type=jnp.float32,
    )


SHAMPOO_BLOCKS = 4


def shampoo_kernel(
    g_ref, w_ref, ema_ref, left_ref, right_ref, root_left, root_right,
    grad_out, w_out, left_out, right_out, ema_out,
):
    limit = CLIP_NORM * BLOCK * NPARAMS ** (-0.5)

    def whole(values):
        return jnp.sum(jnp.sum(values, axis=0, keepdims=True), axis=1, keepdims=True)

    for i in range(SHAMPOO_BLOCKS):
        g = g_ref[i]
        g = g * (limit / jnp.maximum(jnp.sqrt(whole(g * g)), limit))
        grad_out[i] = g
        left_out[i] = STAT_BETA * left_ref[i] + (1 - STAT_BETA) * top_dot(g, g, 1, 1)
        right_out[i] = STAT_BETA * right_ref[i] + (1 - STAT_BETA) * top_dot(g, g, 0, 0)
        p = top_dot(top_dot(root_left[i], g, 1, 0), root_right[i], 1, 0)
        p = p * lax.rsqrt(whole(p * p) * (1.0 / (BLOCK * BLOCK)) + 1e-06)
        w = w_ref[i]
        w = w - SHAMPOO_RATE * (p + DECAY_RATE * w)
        w_out[i] = w
        ema_out[i] = EMA_DECAY * ema_ref[i] + (1 - EMA_DECAY) * w


def shampoo_blocks(*arrays):
    spec = pl.BlockSpec((SHAMPOO_BLOCKS, BLOCK, BLOCK), lambda i: (i, 0, 0))
    shape = jax.ShapeDtypeStruct(arrays[0].shape, jnp.float32)
    return pl.pallas_call(
        shampoo_kernel,
        grid=(arrays[0].shape[0] // SHAMPOO_BLOCKS,),
        in_specs=[spec] * 7,
        out_specs=[spec] * 5,
        out_shape=[shape] * 5,
        compiler_params=pltpu.CompilerParams(vmem_limit_bytes=24 * 2**20),
    )(*arrays)


def adam_kernel(
    fade, rows_ref, gio_ref, table, mom, var, ema, io, io_mom, io_var, io_ema,
    table_out, mom_out, var_out, ema_out, io_out, io_mom_out, io_var_out, io_ema_out, sums_out, grad,
):
    levels = lax.broadcasted_iota(jnp.int32, (LEVELS, BLOCK), 0).astype(jnp.float32)
    level = rows_ref[:, 64, :]
    frames = level.shape[0]
    picks = (
        level[:, 0:1] == lax.broadcasted_iota(jnp.int32, (frames, LEVELS), 1).astype(jnp.float32)
    ).astype(jnp.float32)
    square = jnp.zeros((LEVELS, BLOCK), jnp.float32)
    for i in range(8 * D // BLOCK):
        part = top_dot(picks, rows_ref[:, i, :], 0, 0)
        grad[:, i * BLOCK : (i + 1) * BLOCK] = part
        square = square + part * part
    gio = jnp.concatenate([gio_ref[0, 0 : 2 * PIN + 1], gio_ref[1, 0 : 2 * PIN + 1]], axis=1)

    def whole(values):
        return jnp.sum(jnp.sum(values, axis=0, keepdims=True), axis=1, keepdims=True)

    norm = jnp.sqrt(whole(square) + whole(gio * gio))
    factor = CLIP_NORM / jnp.maximum(norm, CLIP_NORM)
    sums_out[0:1] = jnp.full((1, BLOCK), 1.0, jnp.float32) * norm
    sums_out[1:2] = jnp.sum(rows_ref[:, 68, :], axis=0, keepdims=True)
    sums_out[2:8] = jnp.zeros((6, BLOCK), jnp.float32)
    fade_one, fade_two = fade[0], fade[1]

    def update(g, weight, first, second, average):
        new_first = BETA_ONE * first + (1 - BETA_ONE) * g
        new_second = BETA_TWO * second + (1 - BETA_TWO) * g * g
        new = weight - ADAM_RATE * (
            (new_first / fade_one) / (jnp.sqrt(new_second / fade_two) + ADAM_EPS)
            + DECAY_RATE * weight
        )
        return new, new_first, new_second, EMA_DECAY * average + (1 - EMA_DECAY) * new

    outs = (io_out, io_mom_out, io_var_out, io_ema_out)
    for ref, value in zip(outs, update(gio * factor, io[...], io_mom[...], io_var[...], io_ema[...])):
        ref[...] = value
    outs = (table_out, mom_out, var_out, ema_out)

    def one(i, carry):
        cols = pl.ds(pl.multiple_of(i * D, D), D)
        values = update(grad[:, cols] * factor, table[:, cols], mom[:, cols], var[:, cols], ema[:, cols])
        for ref, value in zip(outs, values):
            ref[:, cols] = value
        return carry

    lax.fori_loop(0, 8, one, 0)


def adam(fade, rows, gio, *arrays):
    vmem, smem = pl.BlockSpec(memory_space=pltpu.VMEM), pl.BlockSpec(memory_space=pltpu.SMEM)
    return pl.pallas_call(
        adam_kernel,
        in_specs=[smem] + [vmem] * 10,
        out_specs=[vmem] * 9,
        out_shape=[jax.ShapeDtypeStruct(a.shape, jnp.float32) for a in arrays]
        + [jax.ShapeDtypeStruct((8, BLOCK), jnp.float32)],
        scratch_shapes=[pltpu.VMEM((LEVELS, 8 * D), jnp.float32)],
        compiler_params=pltpu.CompilerParams(vmem_limit_bytes=32 * 2**20),
    )(fade, rows, gio, *arrays)


def matrix_starts():
    starts, total = [], 0
    for rows_in, cols_in in matrix_shapes():
        starts.append(total)
        total += rows_in // BLOCK * (cols_in // BLOCK)
    return starts, total


def block_places(block_slot):
    owned = block_slot.reshape(32, -1)
    ranks = jnp.sum((owned[:, None, :] < owned[:, :, None]).astype(jnp.int32), axis=2)
    mine = lax.axis_index("frame") * 2 + lax.axis_index("rep")
    own_ranks = lax.dynamic_index_in_dim(ranks, mine, 0, keepdims=False)
    counting = jnp.arange(NSLOT, dtype=jnp.int32)
    perm = jnp.sum(jnp.where(own_ranks[None, :] == counting[:, None], counting[None, :], 0), axis=1)
    owners = jnp.arange(32, dtype=jnp.int32)[:, None]
    gathered = owners * (NSLOT + 1) + ranks + (ranks >= FIRST).astype(jnp.int32)
    scattered = owners * NSLOT + ranks
    natural = jnp.arange(block_slot.shape[0], dtype=jnp.int32)
    same = block_slot[None, :] == natural[:, None]
    places = jnp.sum(jnp.where(same, gathered.reshape(1, -1), 0), axis=1)
    slots = jnp.sum(jnp.where(same, scattered.reshape(1, -1), 0), axis=1)
    early = jnp.sum((owned < matrix_starts()[0][1]).astype(jnp.int32), axis=1)
    return own_ranks, perm, places, slots, jnp.max(early) > FIRST


def rope_columns(frame_ids):
    pairs = HEAD_DIM // 2
    time_pairs = pairs // 4
    row_pairs = (pairs - time_pairs) // 2
    column_pairs = pairs - time_pairs - row_pairs
    shape = (frame_ids.shape[0], pairs, GRID * GRID)
    token = jnp.arange(GRID * GRID, dtype=jnp.int32)
    groups = (
        (time_pairs, frame_ids[:, None, None].astype(jnp.float32)),
        (row_pairs, (token // GRID)[None, None, :].astype(jnp.float32)),
        (column_pairs, (token % GRID)[None, None, :].astype(jnp.float32)),
    )
    angles = jnp.concatenate(
        [
            jnp.broadcast_to(pos * frequencies(n)[None, :, None], (shape[0], n, shape[2]))
            for n, pos in groups
        ],
        axis=1,
    )
    return (jnp.cos(angles), jnp.sin(angles))


def on_grid(
    clean,
    noise,
    levels,
    flags,
    frame_map,
    block_slot,
    step_count,
    mat_weight,
    mat_ema,
    stat_left,
    stat_right,
    root_left,
    root_right,
    mod_table,
    mod_mom,
    mod_var,
    mod_ema,
    io_weight,
    io_mom,
    io_var,
    io_ema,
):
    tok_frame = GRID * GRID
    my_time, my_clip = lax.axis_index("frame"), lax.axis_index("rep")
    level_here = levels[0, 0] * (1 - flags[0, 0])
    noised_here = (1 - flags[0, 0]).astype(jnp.float32)
    fraction = level_here.astype(jnp.float32) / LEVELS
    frames_in = (
        jnp.cos(0.5 * jnp.pi * fraction) * clean[0, 0] + jnp.sin(0.5 * jnp.pi * fraction) * noise[0, 0]
    )
    noise_high = noise[0, 0].astype(jnp.bfloat16)
    noise_low = (noise[0, 0] - noise_high.astype(jnp.float32)).astype(jnp.bfloat16)
    data = jnp.concatenate(
        [
            frames_in.astype(jnp.bfloat16).reshape(-1, BLOCK),
            noise_high.reshape(-1, BLOCK),
            noise_low.reshape(-1, BLOCK),
            jnp.full((16, BLOCK), noised_here.astype(jnp.bfloat16)),
            jnp.full((16, BLOCK), level_here.astype(jnp.bfloat16)),
        ]
    )
    ranks, perm, places, slots, spills = block_places(block_slot)
    clip_map = lax.dynamic_index_in_dim(frame_map, my_clip, 0, keepdims=False)
    my_slot = jnp.sum(
        jnp.where(clip_map == my_time, jnp.arange(clip_map.shape[0], dtype=jnp.int32), 0)
    )
    source = (my_slot * 2 + my_clip).reshape(1)
    cosine, sine = rope_columns(jnp.arange(frame_map.shape[1], dtype=jnp.int32))
    io_low = io_weight.astype(jnp.bfloat16)
    gathered, stage = gather_weights(perm, mat_weight, data)
    gathered = lax.cond(spills, lambda: late_gather(stage, gathered), lambda: gathered)
    start, normed, parts, modulation, targets, inputs, scalars = project(
        source,
        places,
        gathered.reshape(-1, BLOCK, BLOCK),
        mod_table,
        io_low[:PIN],
        io_weight[2 * PIN :],
        cosine,
        sine,
    )
    mine, gathered, attended, full, lse = forward_exchange(parts, stage, gathered)
    blocks = gathered.reshape(-1, BLOCK, BLOCK)
    grad_heads, grad_blocks, grad_middle, grad_head, grad_mod, loss_part = middle(
        places,
        slots,
        blocks,
        attended.reshape(D, tok_frame),
        start,
        modulation,
        io_low[PIN : 2 * PIN],
        targets,
        scalars,
    )
    grad_proj, later = backward_exchange(
        grad_heads.reshape(HEADS, HEAD_DIM, tok_frame),
        mine,
        full,
        lse,
        cosine,
        sine,
        grad_blocks.reshape(32, NSLOT, BLOCK, BLOCK),
    )
    grad_blocks, row, grad_io = final(
        places,
        slots,
        blocks,
        grad_proj,
        normed,
        start,
        modulation,
        grad_middle,
        inputs,
        grad_mod,
        scalars,
        loss_part,
        grad_head,
        grad_blocks,
    )
    grad_blocks = grad_blocks.reshape(32, NSLOT, BLOCK, BLOCK)
    later = lax.cond(spills, lambda: late_scatter(grad_blocks), lambda: later)
    owned, rows, grad_io = scatter_grads(ranks, grad_blocks, row, grad_io, later)
    step = step_count[0].astype(jnp.float32)
    new_small = adam(
        jnp.stack([1 - BETA_ONE**step, 1 - BETA_TWO**step]),
        rows.reshape(32, -1, BLOCK),
        grad_io,
        mod_table,
        mod_mom,
        mod_var,
        mod_ema,
        io_weight,
        io_mom,
        io_var,
        io_ema,
    )
    new_mod, new_io, sums = new_small[:4], new_small[4:8], new_small[8]
    mat_grad, new_mat_weight, new_stat_left, new_stat_right, new_mat_ema = shampoo_blocks(
        owned, mat_weight, mat_ema, stat_left, stat_right, root_left, root_right
    )
    noised_total, grad_norm, total_loss = scalars[2, 0], sums[0, 0], sums[1, 0]
    return (
        total_loss * noised_total,
        noised_total,
        grad_norm,
        mat_grad,
        new_mat_weight,
        new_stat_left,
        new_stat_right,
        new_mat_ema,
        new_mod[0],
        new_mod[1],
        new_mod[2],
        new_mod[3],
        new_io[0],
        new_io[1],
        new_io[2],
        new_io[3],
    )


def solution(mesh):
    tuned = dict(mesh.shape) == {"frame": 16, "rep": 2}
    body = on_grid if tuned else on_device
    in_specs = (
        P("rep", "frame", None, None),
        P("rep", "frame", None, None),
        P("rep", "frame"),
        P("rep", "frame"),
        P(),
        P(),
        P(),
        P(("frame", "rep"), None, None),
        P(("frame", "rep"), None, None),
        P(("frame", "rep"), None, None),
        P(("frame", "rep"), None, None),
        P(("frame", "rep"), None, None),
        P(("frame", "rep"), None, None),
        P(),
        P(),
        P(),
        P(),
        P(),
        P(),
        P(),
        P(),
    )
    out_specs = (
        P(),
        P(),
        P(),
        P(("frame", "rep"), None, None),
        P(("frame", "rep"), None, None),
        P(("frame", "rep"), None, None),
        P(("frame", "rep"), None, None),
        P(("frame", "rep"), None, None),
        P(),
        P(),
        P(),
        P(),
        P(),
        P(),
        P(),
        P(),
    )
    return jax.shard_map(
        body, mesh=mesh, in_specs=in_specs, out_specs=out_specs, check_vma=False
    )
```

```python
from functools import partial
import math

import jax
import jax.numpy as jnp
import numpy as np
from jax import lax
from jax.experimental import pallas as pl
from jax.experimental.pallas import tpu as pltpu
from jax.sharding import PartitionSpec as P

D = 1024
HEADS = 16
HEAD_DIM = 64
FFN = 4096
PIN = 16
GRID = 16
BLOCK = 128
LEVELS = 32
FR_DEV = 1
NPARAMS = 12878848


LN_EPS = 1e-06
ROPE_BASE = 10000.0
CLIP_NORM = 0.01
BETA_ONE = 0.9
BETA_TWO = 0.999
ADAM_EPS = 1e-08
ADAM_RATE = 0.1
DECAY_RATE = 0.1
STAT_BETA = 0.95
SHAMPOO_RATE = 0.01
EMA_DECAY = 0.9
TOP_PRECISION = lax.Precision.HIGHEST


def matmul(left, right):
    return jnp.dot(left, right, preferred_element_type=jnp.float32)


def layer_norm(hidden):
    centered = hidden - jnp.mean(hidden, axis=-1, keepdims=True)
    inverse = lax.rsqrt(jnp.mean(centered * centered, axis=-1, keepdims=True) + LN_EPS)
    return (centered * inverse, inverse)


def norm_back(grad_hat, normed, inverse):
    return inverse * (
        grad_hat
        - jnp.mean(grad_hat, axis=-1, keepdims=True)
        - normed * jnp.mean(grad_hat * normed, axis=-1, keepdims=True)
    )


def gelu_back(upper, grad_act):
    return jax.vjp(partial(jax.nn.gelu, approximate=True), upper)[1](grad_act)[0]


def frequencies(width):
    return ROPE_BASE ** (-jnp.arange(width, dtype=jnp.float32) / width)


def rope_tables(frame_ids):
    pairs = HEAD_DIM // 2
    time_pairs = pairs // 4
    row_pairs = (pairs - time_pairs) // 2
    column_pairs = pairs - time_pairs - row_pairs
    frames = frame_ids.shape[0]
    tok_frame = GRID * GRID
    token_pos = jnp.arange(tok_frame, dtype=jnp.int32)
    row_pos = (token_pos // GRID).astype(jnp.float32)
    column_pos = (token_pos % GRID).astype(jnp.float32)
    time_angle = (
        frame_ids.astype(jnp.float32)[:, None, None] * frequencies(time_pairs)[None, None, :]
    )
    row_angle = row_pos[None, :, None] * frequencies(row_pairs)[None, None, :]
    column_angle = column_pos[None, :, None] * frequencies(column_pairs)[None, None, :]
    angles = jnp.concatenate(
        [jnp.broadcast_to(time_angle, (frames, tok_frame, time_pairs)), row_angle, column_angle],
        axis=-1,
    )
    angles = angles.reshape(frames * tok_frame, pairs)
    return (jnp.cos(angles), jnp.sin(angles))


def rotate(values, cosine, sine):
    pairs = HEAD_DIM // 2
    first, second = (values[..., :pairs], values[..., pairs:])
    cosine = cosine[:, None, :]
    sine = sine[:, None, :]
    return jnp.concatenate(
        [first * cosine - second * sine, first * sine + second * cosine], axis=-1
    )


def split_heads(flat):
    return flat.reshape(flat.shape[0], HEADS, HEAD_DIM)


def matrix_shapes():
    return ((D, 3 * D), (D, D), (D, FFN), (FFN, D))


def from_blocks(natural):
    matrices = []
    offset = 0
    for rows_in, cols_in in matrix_shapes():
        count_in = rows_in // BLOCK * (cols_in // BLOCK)
        part_blocks = natural[offset : offset + count_in]
        matrices.append(
            part_blocks.reshape(rows_in // BLOCK, cols_in // BLOCK, BLOCK, BLOCK)
            .transpose(0, 2, 1, 3)
            .reshape(rows_in, cols_in)
        )
        offset = offset + count_in
    return matrices


def to_blocks(matrix):
    rows_in, cols_in = matrix.shape
    return (
        matrix.reshape(rows_in // BLOCK, BLOCK, cols_in // BLOCK, BLOCK)
        .transpose(0, 2, 1, 3)
        .reshape(-1, BLOCK, BLOCK)
    )


def score_block(queries, key_block, query_frames, key_frames):
    scores = jnp.einsum(
        "qhd,khd->hqk", queries, key_block, preferred_element_type=jnp.float32
    ) * HEAD_DIM ** (-0.5)
    visible = key_frames[None, None, :] <= query_frames[None, :, None]
    return jnp.where(visible, scores, -jnp.inf)


def stack_keys(key_rows, value_rows, frame_rows):
    total_rows = key_rows.shape[0]
    block_rows = math.gcd(total_rows, 512)
    blocks = total_rows // block_rows
    return (
        (
            key_rows.reshape(blocks, block_rows, HEADS, HEAD_DIM),
            value_rows.reshape(blocks, block_rows, HEADS, HEAD_DIM),
            frame_rows.reshape(blocks, block_rows),
        ),
        block_rows,
    )


def keep_state(previous):
    return previous


def fold_keys(state, shard_rows, queries, query_frames, key_frames_all):
    key_rows, value_rows = shard_rows
    stacks, block_rows = stack_keys(key_rows, value_rows, key_frames_all)
    top_query = jnp.max(query_frames)

    def fold_step_block(carried, block_in):
        key_block, value_block, key_frames = block_in

        def fold_compute(previous):
            running, denominator, accumulated = previous
            scores = score_block(queries, key_block, query_frames, key_frames)
            new_max = jnp.maximum(running, jnp.max(scores, axis=-1))
            weights = jnp.exp(scores - new_max[..., None])
            rescale = jnp.exp(running - new_max)
            contrib = jnp.einsum(
                "hqk,khd->hqd",
                weights.astype(jnp.bfloat16),
                value_block,
                preferred_element_type=jnp.float32,
            )
            return (
                new_max,
                denominator * rescale + jnp.sum(weights, axis=-1),
                accumulated * rescale[..., None] + contrib,
            )

        return (lax.cond(jnp.min(key_frames) <= top_query, fold_compute, keep_state, carried), None)

    state, unused = lax.scan(fold_step_block, state, stacks)
    return state


def grad_parts(
    queries, grad_heads, delta, log_total, query_frames, key_block, value_block, key_frames
):
    probs = jnp.exp(
        score_block(queries, key_block, query_frames, key_frames) - log_total[..., None]
    )
    grad_probs = jnp.einsum(
        "qhd,khd->hqk", grad_heads, value_block, preferred_element_type=jnp.float32
    )
    grad_scores = (probs * (grad_probs - delta[..., None])).astype(jnp.bfloat16)
    return (probs, grad_scores)


def key_value_block(
    queries, grad_heads, delta, log_total, query_frames, key_block, value_block, key_frames
):
    block_rows = key_block.shape[0]
    probs, grad_scores = grad_parts(
        queries, grad_heads, delta, log_total, query_frames, key_block, value_block, key_frames
    )
    key_grad = jnp.einsum(
        "hqk,qhd->khd", grad_scores, queries, preferred_element_type=jnp.float32
    ) * HEAD_DIM ** (-0.5)
    value_grad = jnp.einsum(
        "hqk,qhd->khd", probs.astype(jnp.bfloat16), grad_heads, preferred_element_type=jnp.float32
    )
    return jnp.concatenate(
        [key_grad.reshape(block_rows, D), value_grad.reshape(block_rows, D)], axis=1
    )


def query_grads(
    queries, grad_heads, delta, log_total, query_frames, key_all, value_all, key_frames_all
):
    stacks, block_rows = stack_keys(key_all, value_all, key_frames_all)
    top_query = jnp.max(query_frames)

    def query_step_block(carried, block_in):
        key_block, value_block, key_frames = block_in

        def query_compute(previous):
            probs, grad_scores = grad_parts(
                queries,
                grad_heads,
                delta,
                log_total,
                query_frames,
                key_block,
                value_block,
                key_frames,
            )
            return previous + jnp.einsum(
                "hqk,khd->qhd", grad_scores, key_block, preferred_element_type=jnp.float32
            )

        return (
            lax.cond(jnp.min(key_frames) <= top_query, query_compute, keep_state, carried),
            None,
        )

    initial = jnp.zeros(queries.shape, jnp.float32)
    result, unused = lax.scan(query_step_block, initial, stacks)
    return result * HEAD_DIM ** (-0.5)


def key_terms(
    row_count,
    queries,
    grad_heads,
    delta,
    log_total,
    query_frames,
    key_all,
    value_all,
    key_frames_all,
):
    stacks, block_rows = stack_keys(key_all, value_all, key_frames_all)
    top_query = jnp.max(query_frames)

    def one_block(block_in):
        key_block, value_block, key_frames = block_in

        def one_compute(unused):
            return key_value_block(
                queries,
                grad_heads,
                delta,
                log_total,
                query_frames,
                key_block,
                value_block,
                key_frames,
            )

        def nothing(unused):
            return jnp.zeros((block_rows, 2 * D), jnp.float32)

        return lax.cond(jnp.min(key_frames) <= top_query, one_compute, nothing, 0)

    return lax.map(one_block, stacks).reshape(row_count, 2 * D)


def shampoo(grads, weights, average, left, right, left_root, right_root):
    new_left = STAT_BETA * left + (1 - STAT_BETA) * jnp.einsum(
        "bij,bkj->bik", grads, grads, precision=TOP_PRECISION
    )
    new_right = STAT_BETA * right + (1 - STAT_BETA) * jnp.einsum(
        "bji,bjk->bik", grads, grads, precision=TOP_PRECISION
    )
    direction = jnp.einsum("bij,bjk->bik", left_root, grads, precision=TOP_PRECISION)
    direction = jnp.einsum("bij,bjk->bik", direction, right_root, precision=TOP_PRECISION)
    direction = direction * lax.rsqrt(
        jnp.mean(direction * direction, axis=(1, 2), keepdims=True) + 1e-06
    )
    new_weights = weights - SHAMPOO_RATE * (direction + DECAY_RATE * weights)
    new_average = EMA_DECAY * average + (1 - EMA_DECAY) * new_weights
    return (new_weights, new_left, new_right, new_average)


def adamw(grads, weights, first, second, average, step):
    new_first = BETA_ONE * first + (1 - BETA_ONE) * grads
    new_second = BETA_TWO * second + (1 - BETA_TWO) * grads * grads
    first_hat = new_first / (1 - BETA_ONE**step)
    second_hat = new_second / (1 - BETA_TWO**step)
    new_weights = weights - ADAM_RATE * (
        first_hat / (jnp.sqrt(second_hat) + ADAM_EPS) + DECAY_RATE * weights
    )
    new_average = EMA_DECAY * average + (1 - EMA_DECAY) * new_weights
    return (new_weights, new_first, new_second, new_average)


def on_device(
    clean,
    noise,
    levels,
    flags,
    frame_map,
    block_slot,
    step_count,
    mat_weight,
    mat_ema,
    stat_left,
    stat_right,
    root_left,
    root_right,
    mod_table,
    mod_mom,
    mod_var,
    mod_ema,
    io_weight,
    io_mom,
    io_var,
    io_ema,
):
    tok_frame = GRID * GRID
    local_rows = FR_DEV * tok_frame
    noised = (1 - flags[0]).astype(jnp.float32)
    noised_total = jnp.maximum(lax.psum(jnp.sum(noised), ("frame", "rep")), 1.0)
    gathered = lax.all_gather(mat_weight.astype(jnp.bfloat16), ("frame", "rep"), axis=0, tiled=True)
    natural = jnp.zeros_like(gathered).at[block_slot].set(gathered)
    attn_w, out_w, up_w, down_w = from_blocks(natural)
    clip_map = lax.dynamic_index_in_dim(frame_map, lax.axis_index("rep"), 0, keepdims=False)
    my_frames = lax.dynamic_slice_in_dim(clip_map, lax.axis_index("frame") * FR_DEV, FR_DEV)
    key_frames_all = jnp.repeat(clip_map, tok_frame)
    query_frames = jnp.repeat(my_frames, tok_frame)
    level_now = levels[0] * (1 - flags[0])
    fraction = level_now.astype(jnp.float32) / LEVELS
    keep_coef = jnp.cos(0.5 * jnp.pi * fraction)
    noise_coef = jnp.sin(0.5 * jnp.pi * fraction)
    frames_in = keep_coef[:, None, None] * clean[0] + noise_coef[:, None, None] * noise[0]
    inputs = jnp.swapaxes(frames_in, 1, 2).reshape(local_rows, PIN).astype(jnp.bfloat16)
    targets = jnp.swapaxes(noise[0], 1, 2).reshape(local_rows, PIN)
    selector = (level_now[:, None] == jnp.arange(LEVELS, dtype=jnp.int32)[None, :]).astype(
        jnp.float32
    )
    modulation = jnp.dot(selector, mod_table, precision=TOP_PRECISION).reshape(FR_DEV, 8, 1, D)
    io_low = io_weight.astype(jnp.bfloat16)
    embed = io_low[:PIN]
    head = io_low[PIN : 2 * PIN]
    start = (matmul(inputs, embed) + io_weight[2 * PIN]).reshape(FR_DEV, tok_frame, D)
    hat_one, inv_one = layer_norm(start)
    normed = (
        (hat_one * (1 + modulation[:, 1]) + modulation[:, 0])
        .reshape(local_rows, D)
        .astype(jnp.bfloat16)
    )
    projected = matmul(normed, attn_w)
    cosine, sine = rope_tables(my_frames)
    queries = rotate(split_heads(projected[:, :D]), cosine, sine).astype(jnp.bfloat16)
    key_flat = (
        rotate(split_heads(projected[:, D : 2 * D]), cosine, sine)
        .astype(jnp.bfloat16)
        .reshape(local_rows, D)
    )
    value_flat = projected[:, 2 * D :].astype(jnp.bfloat16)
    initial = (
        jnp.full((HEADS, local_rows), -1e30, jnp.float32),
        jnp.zeros((HEADS, local_rows), jnp.float32),
        jnp.zeros((HEADS, local_rows, HEAD_DIM), jnp.float32),
    )
    running, denominator, accumulated = fold_keys(
        initial,
        (
            lax.all_gather(key_flat, "frame", axis=0, tiled=True),
            lax.all_gather(value_flat, "frame", axis=0, tiled=True),
        ),
        queries,
        query_frames,
        key_frames_all,
    )
    attended = jnp.transpose(accumulated / denominator[..., None], (1, 0, 2)).reshape(local_rows, D)
    log_total = running + jnp.log(denominator)
    attended_low = attended.astype(jnp.bfloat16)
    branch = matmul(attended_low, out_w).reshape(FR_DEV, tok_frame, D)
    middle = start + modulation[:, 2] * branch
    hat_two, inv_two = layer_norm(middle)
    normed_two = (
        (hat_two * (1 + modulation[:, 4]) + modulation[:, 3])
        .reshape(local_rows, D)
        .astype(jnp.bfloat16)
    )
    upper = matmul(normed_two, up_w)
    activated = jax.nn.gelu(upper, approximate=True).astype(jnp.bfloat16)
    lower = matmul(activated, down_w).reshape(FR_DEV, tok_frame, D)
    final = middle + modulation[:, 5] * lower
    hat_three, inv_three = layer_norm(final)
    normed_three = (
        (hat_three * (1 + modulation[:, 7]) + modulation[:, 6])
        .reshape(local_rows, D)
        .astype(jnp.bfloat16)
    )
    predicted = matmul(normed_three, head.T)
    row_weight = jnp.repeat(noised, tok_frame)[:, None]
    inv_scale = 1.0 / (noised_total * tok_frame * PIN)
    difference = predicted - targets
    loss_part = jnp.sum(row_weight * difference * difference) * inv_scale
    grad_pred = (2.0 * inv_scale * row_weight * difference).astype(jnp.bfloat16)
    grad_head = jnp.dot(grad_pred.T, normed_three, preferred_element_type=jnp.float32)
    grad_norm_three = matmul(grad_pred, head).reshape(FR_DEV, tok_frame, D)
    grad_final = norm_back(grad_norm_three * (1 + modulation[:, 7]), hat_three, inv_three)
    grad_lower = (grad_final * modulation[:, 5]).reshape(local_rows, D).astype(jnp.bfloat16)
    grad_down = jnp.dot(activated.T, grad_lower, preferred_element_type=jnp.float32)
    grad_upper = gelu_back(upper, matmul(grad_lower, down_w.T)).astype(jnp.bfloat16)
    grad_up = jnp.dot(normed_two.T, grad_upper, preferred_element_type=jnp.float32)
    grad_norm_two = matmul(grad_upper, up_w.T).reshape(FR_DEV, tok_frame, D)
    grad_middle = grad_final + norm_back(grad_norm_two * (1 + modulation[:, 4]), hat_two, inv_two)
    grad_branch = (grad_middle * modulation[:, 2]).reshape(local_rows, D).astype(jnp.bfloat16)
    grad_out_w = jnp.dot(attended_low.T, grad_branch, preferred_element_type=jnp.float32)
    grad_heads = split_heads(matmul(grad_branch, out_w.T).astype(jnp.bfloat16))
    delta = jnp.sum(grad_heads.astype(jnp.float32) * split_heads(attended), axis=-1).T
    key_all, value_all = (
        lax.all_gather(key_flat, "frame", axis=0, tiled=True),
        lax.all_gather(value_flat, "frame", axis=0, tiled=True),
    )
    grad_query = query_grads(
        queries, grad_heads, delta, log_total, query_frames, key_all, value_all, key_frames_all
    )
    key_value_grad = lax.psum_scatter(
        key_terms(
            lax.axis_size("frame") * local_rows,
            queries,
            grad_heads,
            delta,
            log_total,
            query_frames,
            key_all,
            value_all,
            key_frames_all,
        ),
        "frame",
        scatter_dimension=0,
        tiled=True,
    )
    grad_q = rotate(grad_query, cosine, -sine).reshape(local_rows, D)
    grad_k = rotate(split_heads(key_value_grad[:, :D]), cosine, -sine).reshape(local_rows, D)
    grad_proj = jnp.concatenate([grad_q, grad_k, key_value_grad[:, D:]], axis=1).astype(
        jnp.bfloat16
    )
    grad_attn_w = jnp.dot(normed.T, grad_proj, preferred_element_type=jnp.float32)
    grad_norm_one = matmul(grad_proj, attn_w.T).reshape(FR_DEV, tok_frame, D)
    grad_start = grad_middle + norm_back(grad_norm_one * (1 + modulation[:, 1]), hat_one, inv_one)
    grad_start_low = grad_start.reshape(local_rows, D).astype(jnp.bfloat16)
    grad_embed = jnp.dot(inputs.T, grad_start_low, preferred_element_type=jnp.float32)
    grad_bias = jnp.sum(grad_start_low.astype(jnp.float32), axis=0)
    mod_terms = [
        grad_norm_one,
        grad_norm_one * hat_one,
        grad_middle * branch,
        grad_norm_two,
        grad_norm_two * hat_two,
        grad_final * lower,
        grad_norm_three,
        grad_norm_three * hat_three,
    ]
    mod_grads = jnp.stack([jnp.sum(term, axis=1) for term in mod_terms], axis=1).reshape(
        FR_DEV, 8 * D
    )
    grad_table = jnp.dot(selector.T, mod_grads, precision=TOP_PRECISION)
    grad_io = jnp.concatenate([grad_embed, grad_head, grad_bias[None, :]], axis=0)
    grad_table, grad_io, total_loss = lax.psum((grad_table, grad_io, loss_part), ("frame", "rep"))
    grad_blocks = jnp.concatenate(
        [to_blocks(grad_attn_w), to_blocks(grad_out_w), to_blocks(grad_up), to_blocks(grad_down)], 0
    )
    owned = lax.psum_scatter(
        grad_blocks[block_slot], ("frame", "rep"), scatter_dimension=0, tiled=True
    )
    block_limit = CLIP_NORM * BLOCK * NPARAMS ** (-0.5)
    block_norm = jnp.sqrt(jnp.sum(owned * owned, axis=(1, 2), keepdims=True))
    mat_grad = owned * (block_limit / jnp.maximum(block_norm, block_limit))
    grad_norm = jnp.sqrt(jnp.sum(grad_table * grad_table) + jnp.sum(grad_io * grad_io))
    factor = CLIP_NORM / jnp.maximum(grad_norm, CLIP_NORM)
    new_mat_weight, new_stat_left, new_stat_right, new_mat_ema = shampoo(
        mat_grad, mat_weight, mat_ema, stat_left, stat_right, root_left, root_right
    )
    step = step_count[0].astype(jnp.float32)
    new_mod = adamw(grad_table * factor, mod_table, mod_mom, mod_var, mod_ema, step)
    new_io = adamw(grad_io * factor, io_weight, io_mom, io_var, io_ema, step)
    return (
        total_loss * noised_total,
        noised_total,
        grad_norm,
        mat_grad,
        new_mat_weight,
        new_stat_left,
        new_stat_right,
        new_mat_ema,
        new_mod[0],
        new_mod[1],
        new_mod[2],
        new_mod[3],
        new_io[0],
        new_io[1],
        new_io[2],
        new_io[3],
    )


TOK = GRID * GRID
GROUP = 4


def fold_rows(values, op):
    return op(values.reshape(values.shape[0] // 8, 8, values.shape[1]), axis=0)


def side_by_side(ref, first, count, kind):
    parts = [ref[first + j, kind] for j in range(count)]
    return jnp.concatenate(parts, axis=1) if count > 1 else parts[0]


def attend_frame(t, qkv, scores, full, lse):
    q = qkv[t, 0] * jnp.bfloat16(HEAD_DIM**-0.5)

    def score(k, top):
        s = dotg(qkv[k, 1], q, 0, 0)
        scores[k] = s
        return jnp.maximum(top, fold_rows(s, jnp.max))

    top = lax.fori_loop(
        0, t + 1, score, jnp.full((8, TOK), -1e30, jnp.float32), unroll=min(GROUP, t + 1)
    )
    top = jnp.max(top, axis=0, keepdims=True)
    total = jnp.zeros((8, TOK), jnp.float32)
    acc = jnp.zeros((HEAD_DIM, TOK), jnp.float32)
    for k in range(0, t + 1, GROUP):
        count = min(GROUP, t + 1 - k)
        probs = []
        for j in range(count):
            p = jnp.exp(scores[k + j] - top)
            total = total + fold_rows(p, jnp.sum)
            probs.append(p.astype(jnp.bfloat16))
        acc = acc + dotg(side_by_side(qkv, k, count, 2), jnp.concatenate(probs, axis=0), 1, 0)
    total = jnp.sum(total, axis=0, keepdims=True)
    out = acc / total
    full[t] = out
    lse[t] = top + jnp.log(total)
    return out.astype(jnp.bfloat16)


def turn_back(values, cosine, sine):
    first, second = values[: HEAD_DIM // 2], values[HEAD_DIM // 2 :]
    return jnp.concatenate(
        [first * cosine + second * sine, second * cosine - first * sine], axis=0
    )


def attend_frame_back(t, qkv, do_ref, full, lse, cos, sin, dk_ref, dv_ref):
    q = qkv[t, 0] * jnp.bfloat16(HEAD_DIM**-0.5)
    do = do_ref[t]
    delta = jnp.sum(do.astype(jnp.float32) * full[t], axis=0, keepdims=True)
    dq = jnp.zeros((HEAD_DIM, TOK), jnp.float32)
    for k in range(0, t + 1, GROUP):
        count = min(GROUP, t + 1 - k)
        keys = side_by_side(qkv, k, count, 1)
        p = jnp.exp(dotg(keys, q, 0, 0) - lse[t])
        dp = dotg(side_by_side(qkv, k, count, 2), do, 0, 0)
        ds = (p * (dp - delta)).astype(jnp.bfloat16)
        dq = dq + dotg(keys, ds, 1, 0)
        dk = dotg(q, ds, 1, 1)
        dv = dotg(do, p.astype(jnp.bfloat16), 1, 1)
        for j in range(count):
            dk_ref[k + j] += dk[:, j * TOK : (j + 1) * TOK]
            dv_ref[k + j] += dv[:, j * TOK : (j + 1) * TOK]
    return (
        turn_back(dq * HEAD_DIM**-0.5, cos[t], sin[t]).astype(jnp.bfloat16),
        turn_back(dk_ref[t], cos[t], sin[t]).astype(jnp.bfloat16),
        dv_ref[t].astype(jnp.bfloat16),
    )


def attend_kernel(qkv_ref, low_ref, full_ref, lse_ref, scores):
    for t in range(qkv_ref.shape[0]):
        low_ref[t] = attend_frame(t, qkv_ref, scores, full_ref, lse_ref)


def attend(qkv):
    frames = qkv.shape[0]
    vmem = pl.BlockSpec(memory_space=pltpu.VMEM)
    return pl.pallas_call(
        attend_kernel,
        in_specs=[vmem],
        out_specs=[vmem] * 3,
        out_shape=[
            jax.ShapeDtypeStruct((frames, HEAD_DIM, TOK), jnp.bfloat16),
            jax.ShapeDtypeStruct((frames, HEAD_DIM, TOK), jnp.float32),
            jax.ShapeDtypeStruct((frames, 1, TOK), jnp.float32),
        ],
        scratch_shapes=[pltpu.VMEM((frames, TOK, TOK), jnp.float32)],
        compiler_params=pltpu.CompilerParams(vmem_limit_bytes=32 * 2**20),
    )(qkv)


def attend_back_kernel(qkv_ref, do_ref, full_ref, lse_ref, cos_ref, sin_ref, out_ref, dk, dv):
    dk[...] = jnp.zeros_like(dk)
    dv[...] = jnp.zeros_like(dv)
    for t in reversed(range(qkv_ref.shape[0])):
        parts = attend_frame_back(t, qkv_ref, do_ref, full_ref, lse_ref, cos_ref, sin_ref, dk, dv)
        for i in range(3):
            out_ref[t, i] = parts[i]


def attend_back(qkv, do, full, lse, cos, sin):
    frames = qkv.shape[0]
    vmem = pl.BlockSpec(memory_space=pltpu.VMEM)
    return pl.pallas_call(
        attend_back_kernel,
        in_specs=[vmem] * 6,
        out_specs=vmem,
        out_shape=jax.ShapeDtypeStruct(qkv.shape, jnp.bfloat16),
        scratch_shapes=[pltpu.VMEM((frames, HEAD_DIM, TOK), jnp.float32)] * 2,
        compiler_params=pltpu.CompilerParams(vmem_limit_bytes=32 * 2**20),
    )(qkv, do, full, lse, cos, sin)


MESH = pl.DeviceIdType.MESH
NSLOT = 24
FIRST = 14
LATER = NSLOT - FIRST
DATA = FIRST
SMALL_ROWS = 40
FIRST_GATHER = (
    ("xzy", 0, 2),
    ("yzx", 2, 2),
    ("zxy", 4, 3),
    ("zyx", 7, 3),
    ("zxy", 10, 2),
    ("zyx", 12, 3),
)
FIRST_SCATTER = FIRST_GATHER[:5] + (("zyx", 12, 2),)
LATER_PARTS = (("zyx", 0, 5), ("zyx", 5, 5))


def place():
    frame = lax.axis_index("frame")
    return frame // 4, (frame // 2) % 2, frame % 2, lax.axis_index("rep")


def device(z, y, c, x):
    return ((z * 2 + y) * 2 + c, x)


def owner_of(z, y, c, x):
    return ((z * 2 + y) * 2 + c) * 2 + x


def plane_of(z, y, x):
    return (z * 2 + y) * 2 + x


def offsets():
    return [(dx, dy, dz) for dx in (0, 1) for dy in (0, 1) for dz in range(-3, 4)]


def hops(off):
    return off[0] + off[1] + abs(off[2])


def route_keys(parts):
    keys = [(part, off) for part in range(len(parts)) for off in offsets()]
    return sorted(keys, key=lambda k: (hops(k[1]), k[0]))


def onward(order, off):
    moved = dict(zip("xyz", off))
    last = max((order.index(k) for k in order if moved[k]), default=-1)
    links = []
    if last >= 0 and order[last] == "z":
        links.append("u" if off[2] < 0 else "w")
    for k in order[last + 1 :]:
        links.extend("uw" if k == "z" else k)
    return links


def toward(order, off):
    moved = dict(zip("xyz", off))
    last = [k for k in order if moved[k]][-1]
    if last == "z":
        return ("w", "u") if off[2] < 0 else ("u", "w")
    return last, last


def can(link, z):
    return {"u": z < 3, "w": z > 0}.get(link)


def partner(link, z, y, c, x):
    return {
        "x": device(z, y, c, 1 - x),
        "y": device(z, 1 - y, c, x),
        "u": device(z + 1, y, c, x),
        "w": device(z - 1, y, c, x),
        "c": device(z, y, 1 - c, x),
    }[link]


def when(cond, fn):
    if cond is None:
        fn()
    else:
        pl.when(cond)(fn)


def both(a, b):
    return b if a is None else a if b is None else jnp.logical_and(a, b)


def owner_at(off, z, y, x):
    dx, dy, dz = off
    oz = z + dz
    cond = None if dz == 0 else (oz <= 3 if dz > 0 else oz >= 0)
    return oz, (1 - y if dy else y), (1 - x if dx else x), cond


def greet(z, y, c, x, far=()):
    barrier = pltpu.get_barrier_semaphore()
    for link in "xyuwc":
        when(
            can(link, z),
            lambda link=link: pl.semaphore_signal(
                barrier, inc=1, device_id=partner(link, z, y, c, x), device_id_type=MESH
            ),
        )
    for dev in far:
        pl.semaphore_signal(barrier, inc=1, device_id=dev, device_id_type=MESH)
    ends = jnp.logical_or(z == 0, z == 3)
    pl.when(ends)(lambda: pl.semaphore_wait(barrier, 4 + len(far)))
    pl.when(jnp.logical_not(ends))(lambda: pl.semaphore_wait(barrier, 5 + len(far)))


class Gather:
    def __init__(self, parts, src, out, sems, where, shift=0, axes="xyz"):
        self.parts, self.src, self.out, self.where, self.shift = parts, src, out, where, shift
        self.axes = axes
        self.total = sum(count for _, _, count in parts)
        self.send, self.recv, self.csend, self.crecv = sems
        self.keys = [k for k in route_keys(parts) if "x" in axes or k[1][:2] == (0, 0)]
        self.last = {}
        for key in self.keys if "x" in axes else ():
            self.last[key[1]] = key
        self.sent = []

    @staticmethod
    def sems(parts):
        n = len(parts)
        return [
            pltpu.SemaphoreType.DMA((4, n, 16)),
            pltpu.SemaphoreType.DMA((n, 16)),
            pltpu.SemaphoreType.DMA((16,)),
            pltpu.SemaphoreType.DMA((16,)),
        ]

    def held(self, owner):
        return self.out.at[owner, pl.ds(self.shift, self.total)]

    def hop(self, link, part, src, owner, plane):
        _, first, count = self.parts[part]
        return pltpu.make_async_remote_copy(
            src_ref=src.at[pl.ds(first, count)],
            dst_ref=self.out.at[owner, pl.ds(self.shift + first, count)],
            send_sem=self.send.at["xyuw".index(link), part, plane],
            recv_sem=self.recv.at[part, plane],
            device_id=partner(link, *self.where),
            device_id_type=MESH,
        )

    def across(self, src, owner, plane):
        return pltpu.make_async_remote_copy(
            src_ref=src,
            dst_ref=self.held(owner),
            send_sem=self.csend.at[plane],
            recv_sem=self.crecv.at[plane],
            device_id=partner("c", *self.where),
            device_id_type=MESH,
        )

    def step(self, key):
        part, off = key
        z, y, c, x = self.where
        oz, oy, ox, cond = owner_at(off, z, y, x)
        owner, plane = owner_of(oz, oy, c, ox), plane_of(oz, oy, ox)
        own = off == (0, 0, 0)
        here = own or (self.axes == "xy" and off[:2] == (0, 0))
        src = self.src if own and self.axes != "xy" else self.held(owner)
        links = [k for k in onward(self.parts[part][0], off) if ("z" if k in "uw" else k) in self.axes]

        def act():
            if not here:
                self.hop("x", part, src, owner, plane).wait_recv()
            for link in links:
                when(can(link, z), lambda link=link: self.hop(link, part, src, owner, plane).start())
            if self.last.get(off) == key:
                self.across(src, owner, plane).start()

        when(cond, act)
        for link in links:
            self.sent.append(
                (both(cond, can(link, z)), lambda link=link: self.hop(link, part, src, owner, plane))
            )
        if self.last.get(off) == key:
            self.sent.append((cond, lambda: self.across(src, owner, plane)))

    def finish(self):
        for cond, make in self.sent:
            when(cond, lambda make=make: make().wait_send())
        c = self.where[2]
        for plane in range(16) if self.last else ():
            owner = owner_of(plane // 4, (plane // 2) % 2, 1 - c, plane % 2)
            self.across(self.held(owner), owner, plane).wait_recv()


def gather_kernel(perm_ref, w_ref, data_ref, out_ref, stage, later, local, *sems):
    where = place()
    owner = owner_of(*where)
    count = len(Gather.sems(FIRST_GATHER))

    def take(i, carry):
        stage[i] = w_ref[perm_ref[i]].astype(jnp.bfloat16)
        return carry

    def take_later(i, carry):
        later[i] = w_ref[perm_ref[FIRST + i]].astype(jnp.bfloat16)
        return carry

    lax.fori_loop(0, FIRST, take, 0)
    stage[DATA] = data_ref[...]
    greet(*where)
    gather = Gather(FIRST_GATHER, stage, out_ref, sems[:count], where)
    along = Gather(LATER_PARTS, later, out_ref, sems[count:], where, FIRST + 1, "z")
    own = [
        pltpu.make_async_copy(stage, gather.held(owner), local.at[0]),
        pltpu.make_async_copy(later, along.held(owner), local.at[1]),
    ]
    own[0].start()
    begun = len(FIRST_GATHER)
    for key in gather.keys[:begun]:
        gather.step(key)
    lax.fori_loop(0, LATER, take_later, 0)
    own[1].start()
    steps = [(hops(key[1]), 0, i, gather, key) for i, key in enumerate(gather.keys[begun:])]
    steps += [(hops(key[1]) + 1.5, 1, i, along, key) for i, key in enumerate(along.keys)]
    for step in sorted(steps, key=lambda step: step[:3]):
        step[3].step(step[4])
    gather.finish()
    along.finish()
    for copy in own:
        copy.wait()


def gather_weights(perm, blocks, data):
    vmem = pl.BlockSpec(memory_space=pltpu.VMEM)
    return pl.pallas_call(
        gather_kernel,
        out_shape=jax.ShapeDtypeStruct((32, NSLOT + 1, BLOCK, BLOCK), jnp.bfloat16),
        in_specs=[pl.BlockSpec(memory_space=pltpu.SMEM), vmem, vmem],
        out_specs=pl.BlockSpec(memory_space=pltpu.HBM),
        scratch_shapes=[
            pltpu.VMEM((FIRST + 1, BLOCK, BLOCK), jnp.bfloat16),
            pltpu.VMEM((LATER, BLOCK, BLOCK), jnp.bfloat16),
            pltpu.SemaphoreType.DMA((2,)),
        ]
        + Gather.sems(FIRST_GATHER)
        + Gather.sems(LATER_PARTS),
        compiler_params=pltpu.CompilerParams(
            collective_id=1, has_side_effects=True, vmem_limit_bytes=60 * 2**20
        ),
    )(perm, blocks, data)


def inbox_axes(order, link):
    dim = "z" if link in "uw" else link
    axes = order[: order.index(dim)]
    return axes + "z" if dim == "z" else axes


def inbox_starts(parts, link):
    starts, total = [], 0
    for order, _, count in parts:
        starts.append(total)
        size = count
        for d in inbox_axes(order, link):
            size *= 4 if d == "z" else 2
        total += size
    return starts, total


class Scatter:
    def __init__(self, parts, acc, sib, boxes, send, recvs, where, ready, store, axes="xyz"):
        self.parts, self.acc, self.sib, self.where, self.axes = parts, acc, sib, where, axes
        links = self.links_of(axes)
        self.boxes = dict(zip(links, boxes))
        self.recvs = dict(zip(links, recvs))
        self.send, self.ready, self.store = send, ready, store
        self.keys = [
            k for k in reversed(route_keys(parts)) if "x" in axes or k[1][:2] == (0, 0)
        ]
        self.seen = []
        for _, off in self.keys:
            if off not in self.seen:
                self.seen.append(off)
        self.fresh = set()

    @staticmethod
    def links_of(axes):
        return ("xy" if "x" in axes else "") + ("uw" if "z" in axes else "")

    @classmethod
    def boxes_of(cls, parts, axes="xyz"):
        return [
            pltpu.VMEM((inbox_starts(parts, link)[1], 128, 128), jnp.bfloat16)
            for link in cls.links_of(axes)
        ]

    @classmethod
    def sems(cls, parts, axes="xyz"):
        return [pltpu.SemaphoreType.DMA((len(parts), 16))] + [
            pltpu.SemaphoreType.DMA((len(parts), 16)) for _ in cls.links_of(axes)
        ]

    def row(self, oz, oy, ox):
        return oz if self.axes == "z" else plane_of(oz, oy, ox)

    def inbox(self, link, part, oz, oy, ox):
        order, _, count = self.parts[part]
        index = 0
        for d in inbox_axes(order, link):
            index = index * (4 if d == "z" else 2) + {"z": oz, "y": oy, "x": ox}[d]
        return inbox_starts(self.parts, link)[0][part] + index * count

    def clear_ends(self):
        z = self.where[0]

        def clear(box):
            def body(i, carry):
                box[i] = jnp.zeros((128, 128), jnp.bfloat16)
                return carry

            lax.fori_loop(0, box.shape[0], body, 0)

        pl.when(z == 3)(lambda: clear(self.boxes["u"]))
        pl.when(z == 0)(lambda: clear(self.boxes["w"]))

    def hop(self, part, off):
        z, y, c, x = self.where
        oz, oy, ox, _ = owner_at(off, z, y, x)
        plane = plane_of(oz, oy, ox)
        order, first, count = self.parts[part]
        link, named = toward(order, off)
        return pltpu.make_async_remote_copy(
            src_ref=self.acc.at[self.row(oz, oy, ox), pl.ds(first, count)],
            dst_ref=self.boxes[named].at[pl.ds(self.inbox(named, part, oz, oy, ox), count)],
            send_sem=self.send.at[part, plane],
            recv_sem=self.recvs[named].at[part, plane],
            device_id=partner(link, *self.where),
            device_id_type=MESH,
        )

    def step(self, key):
        part, off = key
        z, y, c, x = self.where
        oz, oy, ox, cond = owner_at(off, z, y, x)
        plane = plane_of(oz, oy, ox)
        order, first, count = self.parts[part]
        new = off not in self.fresh
        self.fresh.add(off)
        row = self.row(oz, oy, ox)
        ends = off[:2] == (0, 0) if self.axes == "xy" else off == (0, 0, 0)

        def act():
            if new:
                self.ready(oz, oy, ox)
            sources = []
            for link in [k for k in onward(order, off) if k in self.boxes]:
                start = self.inbox(link, part, oz, oy, ox)
                sources.append((self.boxes[link], start))

                def arrive(link=link, start=start):
                    view = self.boxes[link].at[pl.ds(start, count)]
                    pltpu.make_async_remote_copy(
                        src_ref=view,
                        dst_ref=view,
                        send_sem=self.send.at[part, plane],
                        recv_sem=self.recvs[link].at[part, plane],
                        device_id=partner("c", *self.where),
                        device_id_type=MESH,
                    ).wait_recv()

                when(can(link, z), arrive)

            def add(i, carry):
                total = self.acc[row, first + i].astype(jnp.float32)
                if self.sib is not None:
                    total = total + self.sib[row, first + i].astype(jnp.float32)
                for box, start in sources:
                    total = total + box[start + i].astype(jnp.float32)
                if ends:
                    self.store(oz, first + i, total)
                else:
                    self.acc[row, first + i] = total.astype(jnp.bfloat16)
                return carry

            lax.fori_loop(0, count, add, 0)
            if not ends:
                self.hop(part, off).start()

        when(cond, act)

    def finish(self):
        z, y, c, x = self.where
        for part, off in self.keys:
            if off[:2] != (0, 0) or (off[2] != 0 and self.axes != "xy"):
                cond = owner_at(off, z, y, x)[3]
                when(cond, lambda part=part, off=off: self.hop(part, off).wait_send())


class SmallSums:
    def __init__(self, row, io, rows_out, io_out, mine, inbox, sems, where):
        self.row, self.io, self.rows, self.io_out = row, io, rows_out, io_out
        self.mine, self.inbox, self.where = mine, inbox, where
        self.gsend, self.grecv, self.osend, self.orecv, self.bsend, self.brecv, self.local = sems
        self.order = "zyx"
        self.sent = []

    @staticmethod
    def sems():
        dma = pltpu.SemaphoreType.DMA
        return [dma((4, 16)), dma((16,)), dma((6,)), dma((6,)), dma((1,)), dma((1,)), dma((1,))]

    def far(self):
        z, y, c, x = self.where
        return device(z + 2 - 4 * (z // 2), y, c, x)

    def peer(self, turn):
        z, y, c, x = self.where
        if turn == 3:
            return device(z + 1 - 2 * (z % 2), y, c, x)
        if turn == 4:
            return self.far()
        return partner("cxyyyc"[turn], *self.where)

    def swap(self, turn):
        c = self.where[2]
        if turn == 0:
            src, dst = self.io.at[1 - c], self.inbox.at[0]
        elif turn == 5:
            src, dst = self.mine.at[5], self.io_out.at[c]
        else:
            src, dst = self.mine.at[turn], self.inbox.at[turn]
        return pltpu.make_async_remote_copy(
            src_ref=src,
            dst_ref=dst,
            send_sem=self.osend.at[turn],
            recv_sem=self.orecv.at[turn],
            device_id=self.peer(turn),
            device_id_type=MESH,
        )

    def hop(self, link, src, plane):
        return pltpu.make_async_remote_copy(
            src_ref=src,
            dst_ref=self.rows.at[self.where[2], plane],
            send_sem=self.gsend.at["xyuw".index(link), plane],
            recv_sem=self.grecv.at[plane],
            device_id=partner(link, *self.where),
            device_id_type=MESH,
        )

    def bulk(self, core):
        return pltpu.make_async_remote_copy(
            src_ref=self.rows.at[core],
            dst_ref=self.rows.at[core],
            send_sem=self.bsend.at[0],
            recv_sem=self.brecv.at[0],
            device_id=partner("c", *self.where),
            device_id_type=MESH,
        )

    def row_step(self, off):
        z, y, c, x = self.where
        oz, oy, ox, cond = owner_at(off, z, y, x)
        plane = plane_of(oz, oy, ox)
        own = off == (0, 0, 0)
        src = self.row if own else self.rows.at[c, plane]
        links = onward(self.order, off)

        def act():
            if not own:
                self.hop("x", src, plane).wait_recv()
            for link in links:
                when(can(link, z), lambda link=link: self.hop(link, src, plane).start())

        when(cond, act)
        for link in links:
            self.sent.append(
                (both(cond, can(link, z)), lambda link=link: self.hop(link, src, plane))
            )

    def begin(self):
        z, y, c, x = self.where
        self.own = pltpu.make_async_copy(
            self.row, self.rows.at[c, plane_of(z, y, x)], self.local.at[0]
        )
        self.own.start()
        self.swap(0).start()
        self.row_step((0, 0, 0))

    def turn(self, turn):
        c = self.where[2]
        self.swap(turn).wait_recv()
        if turn < 5:
            before = self.io[c] if turn == 0 else self.mine[turn]
            self.mine[turn + 1] = before + self.inbox[turn]
            if turn == 4:
                self.io_out[c] = self.mine[5]
            self.swap(turn + 1).start()

    def tasks(self):
        todo = [
            lambda off=off: self.row_step(off)
            for off in sorted(offsets(), key=hops)
            if off != (0, 0, 0)
        ]
        for turn in range(6):
            todo.insert(5 * turn + 2, lambda turn=turn: self.turn(turn))

        def last():
            self.own.wait()
            self.bulk(self.where[2]).start()

        return todo + [last]

    def finish(self):
        c = self.where[2]
        self.bulk(1 - c).wait_recv()
        self.bulk(c).wait_send()
        for turn in range(6):
            self.swap(turn).wait_send()
        for cond, make in self.sent:
            when(cond, lambda make=make: make().wait_send())


def own_blocks(g_ref, owner, first, count):
    return g_ref.at[owner, pl.ds(first, count)]


class Halves:
    def __init__(self, g_ref, first, count, acc, sib, csend, crecv, local, where):
        self.g_ref, self.first, self.count, self.acc, self.sib = g_ref, first, count, acc, sib
        self.csend, self.crecv, self.local, self.where = csend, crecv, local, where

    def across(self, oz, oy, ox):
        plane = plane_of(oz, oy, ox)
        other = owner_of(oz, oy, 1 - self.where[2], ox)
        return pltpu.make_async_remote_copy(
            src_ref=own_blocks(self.g_ref, other, self.first, self.count),
            dst_ref=self.sib.at[plane],
            send_sem=self.csend.at[plane],
            recv_sem=self.crecv.at[plane],
            device_id=partner("c", *self.where),
            device_id_type=MESH,
        )

    def load(self, oz, oy, ox):
        plane = plane_of(oz, oy, ox)
        same = owner_of(oz, oy, self.where[2], ox)
        return pltpu.make_async_copy(
            own_blocks(self.g_ref, same, self.first, self.count),
            self.acc.at[plane],
            self.local.at[plane],
        )

    def begin(self, offs):
        z, y, c, x = self.where
        for off in offs:
            oz, oy, ox, cond = owner_at(off, z, y, x)

            def start(oz=oz, oy=oy, ox=ox):
                self.across(oz, oy, ox).start()
                self.load(oz, oy, ox).start()

            when(cond, start)

    def ready(self, oz, oy, ox):
        self.across(oz, oy, ox).wait_recv()
        self.load(oz, oy, ox).wait()

    def finish(self):
        for plane in range(16):
            self.across(plane // 4, (plane // 2) % 2, plane % 2).wait_send()


def scatter_kernel(rank_ref, g_ref, row_ref, io_ref, later_ref, out_ref, rows_out, io_out, *refs):
    acc, sib, along, total = refs[:4]
    boxes, refs = refs[4:8], refs[8:]
    later_boxes, refs = refs[:2], refs[2:]
    mine, inbox = refs[:2]
    csend, crecv, local, later_local, send = refs[2:7]
    recvs, later_send, later_recvs, small_sems = refs[7:11], refs[11], refs[12:14], refs[14:]
    where = place()
    small = SmallSums(row_ref, io_ref, rows_out, io_out, mine, inbox, small_sems, where)
    whole = pltpu.make_async_copy(later_ref, along, later_local.at[0])
    whole.start()
    greet(*where, far=(small.far(),))
    small.begin()
    halves = Halves(g_ref, 0, FIRST, acc, sib, csend, crecv, local, where)

    def store(oz, row, value):
        total[row] = value

    def store_later(oz, row, value):
        total[FIRST + row] = value

    scatter = Scatter(FIRST_SCATTER, acc, sib, boxes, send, recvs, where, halves.ready, store)
    later = Scatter(
        LATER_PARTS, along, None, later_boxes, later_send, later_recvs, where,
        lambda *place: None, store_later, "z",
    )
    halves.begin(scatter.seen)
    scatter.clear_ends()
    later.clear_ends()
    whole.wait()
    tasks = small.tasks()
    steps = [(-hops(key[1]), 1, i, scatter, key) for i, key in enumerate(scatter.keys)]
    steps += [(-hops(key[1]) - 1.5, 0, i, later, key) for i, key in enumerate(later.keys)]
    for i, step in enumerate(sorted(steps, key=lambda step: step[:3])):
        step[3].step(step[4])
        if i % 5 == 4 and tasks:
            tasks.pop(0)()
    for task in tasks:
        task()

    def put(i, carry):
        out_ref[i] = total[rank_ref[i]]
        return carry

    lax.fori_loop(0, NSLOT, put, 0)
    scatter.finish()
    later.finish()
    halves.finish()
    small.finish()


def scatter_grads(ranks, grads, row, io, later):
    vmem = pl.BlockSpec(memory_space=pltpu.VMEM)
    dma = pltpu.SemaphoreType.DMA
    held = pltpu.VMEM((16, FIRST, BLOCK, BLOCK), jnp.bfloat16)
    half = (SMALL_ROWS, D // 2)
    return pl.pallas_call(
        scatter_kernel,
        out_shape=(
            jax.ShapeDtypeStruct((NSLOT, BLOCK, BLOCK), jnp.float32),
            jax.ShapeDtypeStruct((2, 16) + row.shape, jnp.float32),
            jax.ShapeDtypeStruct((2,) + half, jnp.float32),
        ),
        in_specs=[
            pl.BlockSpec(memory_space=pltpu.SMEM),
            pl.BlockSpec(memory_space=pl.ANY),
            vmem,
            vmem,
            pl.BlockSpec(memory_space=pl.ANY),
        ],
        out_specs=(vmem, vmem, vmem),
        scratch_shapes=[
            held,
            held,
            pltpu.VMEM(later.shape, later.dtype),
            pltpu.VMEM((NSLOT, BLOCK, BLOCK), jnp.float32),
        ]
        + Scatter.boxes_of(FIRST_SCATTER)
        + Scatter.boxes_of(LATER_PARTS, "z")
        + [pltpu.VMEM((6,) + half, jnp.float32), pltpu.VMEM((6,) + half, jnp.float32)]
        + [dma((16,)), dma((16,)), dma((16,)), dma((1,))]
        + Scatter.sems(FIRST_SCATTER)
        + Scatter.sems(LATER_PARTS, "z")
        + SmallSums.sems(),
        compiler_params=pltpu.CompilerParams(
            collective_id=2, has_side_effects=True, vmem_limit_bytes=58 * 2**20
        ),
    )(ranks, grads, row, io, later)


def clip_peers(frame, fn):
    count = lax.axis_size("frame")

    def body(step, carry):
        peer = lax.rem(frame + step, count)
        fn(step, peer, (peer, lax.axis_index("rep")))
        return carry

    lax.fori_loop(1, count, body, 0)


def greet_clip(frame, where):
    barrier = pltpu.get_barrier_semaphore()
    clip_peers(
        frame,
        lambda step, peer, dev: pl.semaphore_signal(
            barrier, inc=1, device_id=dev, device_id_type=MESH
        ),
    )
    pl.semaphore_signal(barrier, inc=1, device_id=partner("x", *where), device_id_type=MESH)
    pl.semaphore_wait(barrier, lax.axis_size("frame"))


class Exchange:
    def __init__(self, src, dst, send, recv, frame):
        self.src, self.dst, self.send, self.recv, self.frame = src, dst, send, recv, frame

    @staticmethod
    def sems():
        return [pltpu.SemaphoreType.DMA((16,)), pltpu.SemaphoreType.DMA((16,))]

    def copy(self, peer):
        return pltpu.make_async_remote_copy(
            src_ref=self.src.at[peer],
            dst_ref=self.dst.at[self.frame],
            send_sem=self.send.at[peer],
            recv_sem=self.recv.at[self.frame],
            device_id=(peer, lax.axis_index("rep")),
            device_id_type=MESH,
        )

    def own(self):
        self.dst[self.frame] = self.src[self.frame]

    def start_all(self):
        clip_peers(self.frame, lambda step, peer, dev: self.copy(peer).start())
        self.own()

    def start(self, peer):
        pl.when(self.frame != peer)(lambda: self.copy(peer).start())
        pl.when(self.frame == peer)(self.own)

    def arrived(self, peer):
        def wait():
            pltpu.make_async_remote_copy(
                src_ref=self.src.at[peer],
                dst_ref=self.dst.at[peer],
                send_sem=self.send.at[peer],
                recv_sem=self.recv.at[peer],
                device_id=(peer, lax.axis_index("rep")),
                device_id_type=MESH,
            ).wait_recv()

        pl.when(self.frame != peer)(wait)

    def all_arrived(self):
        for peer in range(16):
            self.arrived(peer)

    def finish(self):
        for peer in range(16):
            pl.when(self.frame != peer)(lambda peer=peer: self.copy(peer).wait_send())


def spread_evenly(steps, slots, weights):
    total, taken, acc, runs = sum(weights), 0, 0, []
    for slot in range(slots):
        acc += weights[slot]
        upto = round(len(steps) * acc / total)
        runs.append(steps[taken:upto])
        taken = upto
    return runs


def forward_kernel(
    parts_ref, blocks_in, mine_ref, blocks_ref, olt_ref, full_ref, lse_ref, scores, low, *sems
):
    where = place()
    frame = lax.axis_index("frame")
    qkv = Exchange(parts_ref, mine_ref, sems[0], sems[1], frame)
    back = Exchange(low, olt_ref, sems[2], sems[3], frame)
    gather_sems = sems[4:]
    greet_clip(frame, where)
    qkv.start_all()
    gather = Gather(LATER_PARTS, None, blocks_ref, gather_sems, where, FIRST + 1, "xy")
    ready = [key for key in gather.keys if key[1][:2] == (0, 0)]
    steps = [key for key in gather.keys if key not in ready]
    for key in ready:
        gather.step(key)
    frames = mine_ref.shape[0]
    runs = spread_evenly(steps, frames, FORWARD_WEIGHTS)
    for t in range(frames):
        for key in runs[t]:
            gather.step(key)
        qkv.arrived(t)
        low[t] = attend_frame(t, mine_ref, scores, full_ref, lse_ref)
        back.start(t)
    gather.finish()
    qkv.finish()
    back.all_arrived()
    back.finish()


FORWARD_WEIGHTS = (50,) + (2,) * 7 + (6,) * 8


def forward_exchange(parts, blocks):
    frames = 16
    vmem = pl.BlockSpec(memory_space=pltpu.VMEM)
    return pl.pallas_call(
        forward_kernel,
        in_specs=[vmem, pl.BlockSpec(memory_space=pltpu.HBM)],
        out_specs=[vmem, pl.BlockSpec(memory_space=pltpu.HBM), vmem, vmem, vmem],
        input_output_aliases={1: 1},
        out_shape=[
            jax.ShapeDtypeStruct((frames,) + parts.shape[1:], jnp.bfloat16),
            jax.ShapeDtypeStruct(blocks.shape, blocks.dtype),
            jax.ShapeDtypeStruct((HEADS, HEAD_DIM, TOK), jnp.bfloat16),
            jax.ShapeDtypeStruct((frames, HEAD_DIM, TOK), jnp.float32),
            jax.ShapeDtypeStruct((frames, 1, TOK), jnp.float32),
        ],
        scratch_shapes=[
            pltpu.VMEM((frames, TOK, TOK), jnp.float32),
            pltpu.VMEM((frames, HEAD_DIM, TOK), jnp.bfloat16),
        ]
        + Exchange.sems()
        + Exchange.sems()
        + Gather.sems(LATER_PARTS),
        compiler_params=pltpu.CompilerParams(
            collective_id=3, has_side_effects=True, vmem_limit_bytes=56 * 2**20
        ),
    )(parts, blocks)


def backward_kernel(
    heads_ref, mine_ref, full_ref, lse_ref, cos_ref, sin_ref, g_ref, drt_ref, later_ref, *refs
):
    do, grads, dk, dv, acc, sib = refs[:6]
    boxes, sems = refs[6:8], refs[8:]
    where = place()
    frame = lax.axis_index("frame")
    inward = Exchange(heads_ref, do, sems[0], sems[1], frame)
    outward = Exchange(grads, drt_ref, sems[2], sems[3], frame)
    csend, crecv, local, send = sems[4:8]
    halves = Halves(g_ref, FIRST, LATER, acc, sib, csend, crecv, local, where)

    def store(oz, row, value):
        later_ref[oz, row] = value.astype(jnp.bfloat16)

    scatter = Scatter(
        LATER_PARTS, acc, sib, boxes, send, sems[8:10], where, halves.ready, store, "xy"
    )
    greet_clip(frame, where)
    inward.start_all()
    halves.begin(scatter.seen)
    dk[...] = jnp.zeros_like(dk)
    dv[...] = jnp.zeros_like(dv)
    frames = mine_ref.shape[0]
    runs = spread_evenly(scatter.keys, frames + 1, BACKWARD_WEIGHTS)
    for i, t in enumerate(reversed(range(frames))):
        for key in runs[i]:
            scatter.step(key)
        inward.arrived(t)
        parts = attend_frame_back(t, mine_ref, do, full_ref, lse_ref, cos_ref, sin_ref, dk, dv)
        for kind in range(3):
            grads[t, kind] = parts[kind]
        outward.start(t)
    for key in runs[frames]:
        scatter.step(key)
    scatter.finish()
    halves.finish()
    inward.finish()
    outward.all_arrived()
    outward.finish()


BACKWARD_WEIGHTS = (16,) + (6,) * 8 + (4,) * 7 + (16,)


def backward_exchange(heads, mine, full, lse, cos, sin, grads):
    frames = mine.shape[0]
    vmem = pl.BlockSpec(memory_space=pltpu.VMEM)
    dma = pltpu.SemaphoreType.DMA
    held = pltpu.VMEM((16, LATER, BLOCK, BLOCK), jnp.bfloat16)
    return pl.pallas_call(
        backward_kernel,
        in_specs=[vmem] * 6 + [pl.BlockSpec(memory_space=pltpu.HBM)],
        out_specs=[vmem, vmem],
        out_shape=[
            jax.ShapeDtypeStruct((HEADS,) + mine.shape[1:], jnp.bfloat16),
            jax.ShapeDtypeStruct((4, LATER, BLOCK, BLOCK), jnp.bfloat16),
        ],
        scratch_shapes=[
            pltpu.VMEM((frames, HEAD_DIM, TOK), jnp.bfloat16),
            pltpu.VMEM((frames, 3, HEAD_DIM, TOK), jnp.bfloat16),
            pltpu.VMEM((frames, HEAD_DIM, TOK), jnp.float32),
            pltpu.VMEM((frames, HEAD_DIM, TOK), jnp.float32),
            held,
            held,
        ]
        + Scatter.boxes_of(LATER_PARTS, "xy")
        + Exchange.sems()
        + Exchange.sems()
        + [dma((16,)), dma((16,)), dma((16,))]
        + Scatter.sems(LATER_PARTS, "xy"),
        compiler_params=pltpu.CompilerParams(
            collective_id=4, has_side_effects=True, vmem_limit_bytes=56 * 2**20
        ),
    )(heads, mine, full, lse, cos, sin, grads)


def late_gather_kernel(blocks_in, blocks_ref, *sems):
    where = place()
    greet(*where)
    gather = Gather(LATER_PARTS, None, blocks_ref, sems, where, FIRST + 1, "xy")
    for key in gather.keys:
        gather.step(key)
    gather.finish()


def late_gather(blocks):
    hbm = pl.BlockSpec(memory_space=pltpu.HBM)
    return pl.pallas_call(
        late_gather_kernel,
        in_specs=[hbm],
        out_specs=hbm,
        out_shape=jax.ShapeDtypeStruct(blocks.shape, blocks.dtype),
        scratch_shapes=Gather.sems(LATER_PARTS),
        input_output_aliases={0: 0},
        compiler_params=pltpu.CompilerParams(
            collective_id=5, has_side_effects=True, vmem_limit_bytes=56 * 2**20
        ),
    )(blocks)


def late_scatter_kernel(g_ref, later_ref, *refs):
    acc, sib, boxes, sems = refs[0], refs[1], refs[2:4], refs[4:]
    where = place()
    halves = Halves(g_ref, FIRST, LATER, acc, sib, sems[0], sems[1], sems[2], where)

    def store(oz, row, value):
        later_ref[oz, row] = value.astype(jnp.bfloat16)

    scatter = Scatter(
        LATER_PARTS, acc, sib, boxes, sems[3], sems[4:6], where, halves.ready, store, "xy"
    )
    greet(*where)
    halves.begin(scatter.seen)
    for key in scatter.keys:
        scatter.step(key)
    scatter.finish()
    halves.finish()


def late_scatter(grads):
    dma = pltpu.SemaphoreType.DMA
    held = pltpu.VMEM((16, LATER, BLOCK, BLOCK), jnp.bfloat16)
    return pl.pallas_call(
        late_scatter_kernel,
        in_specs=[pl.BlockSpec(memory_space=pltpu.HBM)],
        out_specs=pl.BlockSpec(memory_space=pltpu.VMEM),
        out_shape=jax.ShapeDtypeStruct((4, LATER, BLOCK, BLOCK), jnp.bfloat16),
        scratch_shapes=[held, held]
        + Scatter.boxes_of(LATER_PARTS, "xy")
        + [dma((16,)), dma((16,)), dma((16,))]
        + Scatter.sems(LATER_PARTS, "xy"),
        compiler_params=pltpu.CompilerParams(
            collective_id=6, has_side_effects=True, vmem_limit_bytes=56 * 2**20
        ),
    )(grads)


TILE = 512
LIMIT = pltpu.CompilerParams(vmem_limit_bytes=60 * 2**20)


def dotg(left, right, left_dim, right_dim):
    return lax.dot_general(
        left, right, (((left_dim,), (right_dim,)), ((), ())), preferred_element_type=jnp.float32
    )


def block_of(held, row, col):
    return held.at[
        pl.ds(pl.multiple_of(row * BLOCK, BLOCK), BLOCK),
        pl.ds(pl.multiple_of(col * BLOCK, BLOCK), BLOCK),
    ]


def move_tile(places, blocks, held, sem, start, across, row, rows, col, cols, outward=False):
    for r in range(rows):
        for c in range(cols):
            slot = blocks.at[places[start + (row + r) * across + col + c]]
            here = block_of(held, row + r, col + c)
            src, dst = (here, slot) if outward else (slot, here)
            pltpu.make_async_copy(src, dst, sem).start()


def settled(view, sem):
    pltpu.make_async_copy(view, view, sem).wait()


def column_sum(values):
    return jnp.sum(values, axis=0, keepdims=True)


def project_kernel(
    source, places, blocks, table_ref, io_ref, cos_ref, sin_ref,
    h0_ref, at_ref, out_ref, mod_ref, target_ref, xt_ref, scalars_ref,
    held, a_ref, data, flags, sems, small_sems,
):
    across = 3 * D // BLOCK
    per = TILE // BLOCK
    tiles = 3 * D // TILE
    mine = pltpu.make_async_copy(blocks.at[source[0] * (NSLOT + 1) + DATA], data, small_sems.at[0])
    mine.start()

    def flag(owner):
        return pltpu.make_async_copy(
            blocks.at[owner * (NSLOT + 1) + DATA, pl.ds(96, 16)], flags.at[owner], small_sems.at[1]
        )

    for owner in range(32):
        flag(owner).start()
    for j in range(tiles):
        move_tile(places, blocks, held, sems.at[j], 0, across, 0, D // BLOCK, j * per, per)
    mine.wait()
    settled(flags, small_sems.at[1])
    xt = data[0:32]
    xt_ref[...] = jnp.concatenate([xt.reshape(PIN, 2, BLOCK)[:, i] for i in range(2)], axis=1)
    noise = data[32:64].astype(jnp.float32) + data[64:96].astype(jnp.float32)
    target_ref[...] = jnp.concatenate([noise.reshape(PIN, 2, BLOCK)[:, i] for i in range(2)], axis=1)
    noised = data[96:97].astype(jnp.float32)
    level = data[112:113].astype(jnp.float32)
    total = flags[0].astype(jnp.float32)
    for owner in range(1, 32):
        total = total + flags[owner].astype(jnp.float32)
    total = jnp.maximum(total[0:1], 1.0)
    scalars_ref[0:1] = noised
    scalars_ref[1:2] = 1.0 / (total * (TOK * PIN))
    scalars_ref[2:3] = total
    scalars_ref[3:4] = level
    scalars_ref[4:8] = jnp.zeros((4, BLOCK), jnp.float32)
    rows = lax.broadcasted_iota(jnp.int32, (LEVELS, D), 0).astype(jnp.float32)
    picked = rows == level[0:1, 0:1]
    for i in range(8):
        mod_ref[i : i + 1] = column_sum(jnp.where(picked, table_ref[:, i * D : (i + 1) * D], 0.0))
    start = dotg(xt_ref[...], io_ref[0:PIN].astype(jnp.bfloat16), 0, 0) + io_ref[2 * PIN :]
    h0_ref[...] = start
    hat, _ = layer_norm(start)
    normed = hat * (1 + mod_ref[1:2]) + mod_ref[0:1]
    a_ref[...] = normed.astype(jnp.bfloat16)
    at_ref[...] = normed.T.astype(jnp.bfloat16)
    heads = TILE // HEAD_DIM
    half = HEAD_DIM // 2
    frame = lax.axis_index("frame")
    c, s = cos_ref[frame], sin_ref[frame]
    for j in range(tiles):
        settled(held.at[:, pl.ds(j * TILE, TILE)], sems.at[j])
        r = matmul(a_ref[...], held[:, j * TILE : (j + 1) * TILE]).T
        kind, head = j // (D // TILE), j % (D // TILE) * heads
        for i in range(heads):
            own = r[i * HEAD_DIM : (i + 1) * HEAD_DIM]
            if kind < 2:
                first, second = own[:half], own[half:]
                own = jnp.concatenate(
                    [first * c - second * s, first * s + second * c], axis=0
                )
            out_ref[head + i, kind] = own.astype(jnp.bfloat16)


def project(source, places, blocks, table, io, cos, sin):
    vmem, smem = pl.BlockSpec(memory_space=pltpu.VMEM), pl.BlockSpec(memory_space=pltpu.SMEM)
    f32, bf16 = jnp.float32, jnp.bfloat16
    return pl.pallas_call(
        project_kernel,
        in_specs=[smem, smem, pl.BlockSpec(memory_space=pltpu.HBM)] + [vmem] * 4,
        out_specs=[vmem] * 7,
        out_shape=[
            jax.ShapeDtypeStruct((TOK, D), f32),
            jax.ShapeDtypeStruct((D, TOK), bf16),
            jax.ShapeDtypeStruct((HEADS, 3, HEAD_DIM, TOK), bf16),
            jax.ShapeDtypeStruct((8, D), f32),
            jax.ShapeDtypeStruct((PIN, TOK), f32),
            jax.ShapeDtypeStruct((PIN, TOK), bf16),
            jax.ShapeDtypeStruct((8, BLOCK), f32),
        ],
        scratch_shapes=[
            pltpu.VMEM((D, 3 * D), bf16),
            pltpu.VMEM((TOK, D), bf16),
            pltpu.VMEM((BLOCK, BLOCK), bf16),
            pltpu.VMEM((32, 16, BLOCK), bf16),
            pltpu.SemaphoreType.DMA((3 * D // TILE,)),
            pltpu.SemaphoreType.DMA((2,)),
        ],
        compiler_params=LIMIT,
    )(source, places, blocks, table, io, cos, sin)


GELU_A = math.sqrt(2.0 / math.pi)
GELU_B = 0.044715


def middle_kernel(
    places, slots, blocks, olt_ref, h0_ref, mod_ref, io_ref, target_ref, scalars_ref,
    dot_ref, grads_ref, dh1_ref, dhead_ref, dmod_ref, loss_ref,
    wo, wup, wdown, gout, gup, gdown, slope, act, bt, dz_ref, db_ref, h1_ref, y_ref, z_ref, sems, out_sems,
):
    starts, _ = matrix_starts()
    per = TILE // BLOCK
    wide = D // BLOCK
    up_tiles = FFN // TILE
    up_across = FFN // BLOCK

    def fetch_up(j):
        move_tile(places, blocks, wup, sems.at[1 + j], starts[2], up_across, 0, wide, j * per, per)

    def fetch_down(j):
        move_tile(places, blocks, wdown, sems.at[9 + j], starts[3], wide, j * per, per, 0, wide)

    move_tile(places, blocks, wo, sems.at[0], starts[1], wide, 0, wide, 0, wide)
    fetch_up(0)
    fetch_up(1)
    attended = olt_ref[...].astype(jnp.float32).T.astype(jnp.bfloat16)
    settled(wo, sems.at[0])
    y = matmul(attended, wo[...])
    y_ref[...] = y
    h1 = h0_ref[...] + mod_ref[2:3] * y
    h1_ref[...] = h1
    hat_two, _ = layer_norm(h1)
    b32 = hat_two * (1 + mod_ref[4:5]) + mod_ref[3:4]
    bt[...] = b32.T.astype(jnp.bfloat16)
    b = b32.astype(jnp.bfloat16)
    dz_ref[...] = b

    def rise(j, carry):
        col = pl.multiple_of(j * TILE, TILE)
        settled(wup.at[:, pl.ds(col, TILE)], sems.at[1 + j])
        fetch_down(j)
        pl.when(j < up_tiles - 2)(lambda: fetch_up(j + 2))
        u = matmul(dz_ref[...], wup[:, pl.ds(col, TILE)])
        square = u * u
        t = jnp.tanh(GELU_A * (u + GELU_B * (square * u)))
        cdf = 0.5 * (1.0 + t)
        act[:, pl.ds(col, TILE)] = (u * cdf).astype(jnp.bfloat16)
        slope[:, pl.ds(col, TILE)] = cdf + (0.5 * GELU_A) * u * (1.0 - t * t) * (
            1.0 + (3.0 * GELU_B) * square
        )
        return carry

    lax.fori_loop(0, up_tiles, rise, 0)
    for j in range(up_tiles):
        settled(wdown.at[pl.ds(j * TILE, TILE)], sems.at[9 + j])

    def fall(j, carry):
        col = pl.multiple_of(j * 256, 256)
        z_ref[:, pl.ds(col, 256)] = matmul(act[...], wdown[:, pl.ds(col, 256)])
        return carry

    lax.fori_loop(0, D // 256, fall, 0)
    z = z_ref[...]
    h2 = h1_ref[...] + mod_ref[5:6] * z
    hat_three, inv_three = layer_norm(h2)
    c = (hat_three * (1 + mod_ref[7:8]) + mod_ref[6:7]).astype(jnp.bfloat16)
    noised, inv_scale = scalars_ref[0:1, 0:1], scalars_ref[1:2, 0:1]
    head = io_ref[PIN : 2 * PIN].astype(jnp.bfloat16)
    difference = dotg(head, c, 1, 1) - target_ref[...]
    loss_ref[...] = jnp.full((1, BLOCK), 1.0, jnp.float32) * (
        jnp.sum(jnp.sum(difference * difference, axis=0, keepdims=True), axis=1, keepdims=True)
        * (noised * inv_scale)
    )
    dpred = (2.0 * inv_scale * noised * difference).astype(jnp.bfloat16)
    dhead_ref[...] = matmul(dpred, c)
    dc = dotg(dpred, head, 0, 0)
    dmod_ref[6:7] = column_sum(dc)
    dmod_ref[7:8] = column_sum(dc * hat_three)
    dh2 = norm_back(dc * (1 + mod_ref[7:8]), hat_three, inv_three)
    dmod_ref[5:6] = column_sum(dh2 * z)
    dz_ref[...] = (dh2 * mod_ref[5:6]).astype(jnp.bfloat16)
    z_ref[...] = dh2
    db_ref[...] = jnp.zeros_like(db_ref)

    def back(j, carry):
        col = pl.multiple_of(j * TILE, TILE)
        du = (
            slope[:, pl.ds(col, TILE)] * dotg(dz_ref[...], wdown[pl.ds(col, TILE)], 1, 1)
        ).astype(jnp.bfloat16)
        gdown[pl.ds(col, TILE)] = dotg(act[:, pl.ds(col, TILE)], dz_ref[...], 0, 0).astype(
            jnp.bfloat16
        )
        move_tile(
            slots, grads_ref, gdown, out_sems.at[0], starts[3], wide, j * per, per, 0, wide, True
        )
        gup[:, pl.ds(col, TILE)] = matmul(bt[...], du).astype(jnp.bfloat16)
        move_tile(
            slots, grads_ref, gup, out_sems.at[1], starts[2], up_across, 0, wide, j * per, per, True
        )
        db_ref[...] += dotg(du, wup[:, pl.ds(col, TILE)], 1, 1)
        return carry

    lax.fori_loop(0, up_tiles, back, 0)
    hat_two, inv_two = layer_norm(h1_ref[...])
    db = db_ref[...]
    dmod_ref[3:4] = column_sum(db)
    dmod_ref[4:5] = column_sum(db * hat_two)
    dh1 = z_ref[...] + norm_back(db * (1 + mod_ref[4:5]), hat_two, inv_two)
    dh1_ref[...] = dh1
    dmod_ref[2:3] = column_sum(dh1 * y_ref[...])
    dmod_ref[0:2] = jnp.zeros((2, D), jnp.float32)
    dz_ref[...] = (dh1 * mod_ref[2:3]).astype(jnp.bfloat16)
    gout[...] = matmul(olt_ref[...], dz_ref[...]).astype(jnp.bfloat16)
    move_tile(slots, grads_ref, gout, out_sems.at[2], starts[1], wide, 0, wide, 0, wide, True)
    for j in range(D // TILE):
        rows = pl.ds(j * TILE, TILE)
        dot_ref[rows] = dotg(wo[rows], dz_ref[...], 1, 1).astype(jnp.bfloat16)
    settled(gdown, out_sems.at[0])
    settled(gup, out_sems.at[1])
    settled(gout, out_sems.at[2])


def middle(places, slots, blocks, olt, h0, mod, io, target, scalars):
    vmem, smem = pl.BlockSpec(memory_space=pltpu.VMEM), pl.BlockSpec(memory_space=pltpu.SMEM)
    hbm = pl.BlockSpec(memory_space=pltpu.HBM)
    f32, bf16 = jnp.float32, jnp.bfloat16
    up, down, square = pltpu.VMEM((D, FFN), bf16), pltpu.VMEM((FFN, D), bf16), pltpu.VMEM((D, D), bf16)
    rows = pltpu.VMEM((TOK, D), f32)
    return pl.pallas_call(
        middle_kernel,
        in_specs=[smem, smem, hbm] + [vmem] * 6,
        out_specs=[vmem, hbm] + [vmem] * 4,
        out_shape=[
            jax.ShapeDtypeStruct((D, TOK), bf16),
            jax.ShapeDtypeStruct((32 * NSLOT, BLOCK, BLOCK), bf16),
            jax.ShapeDtypeStruct((TOK, D), f32),
            jax.ShapeDtypeStruct((PIN, D), f32),
            jax.ShapeDtypeStruct((8, D), f32),
            jax.ShapeDtypeStruct((1, BLOCK), f32),
        ],
        scratch_shapes=[square, up, down, square, up, down]
        + [
            pltpu.VMEM((TOK, FFN), f32),
            pltpu.VMEM((TOK, FFN), bf16),
            pltpu.VMEM((D, TOK), bf16),
            pltpu.VMEM((TOK, D), bf16),
            rows,
            rows,
            rows,
            rows,
            pltpu.SemaphoreType.DMA((17,)),
            pltpu.SemaphoreType.DMA((3,)),
        ],
        compiler_params=LIMIT,
    )(places, slots, blocks, olt, h0, mod, io, target, scalars)


def final_kernel(
    places, slots, blocks, drt_ref, at_ref, h0_ref, mod_ref, dh1_ref, xt_ref, dmod_in, scalars_ref, loss_ref,
    dhead_ref, grads_in, grads_ref, row_ref, io_ref, held, gqkv, flat, sems, out_sem,
):
    across = 3 * D // BLOCK
    per = TILE // BLOCK
    for j in range(2):
        move_tile(places, blocks, held, sems.at[j], 0, across, j * per, per, 0, across)
    for kind in range(3):
        for head in range(HEADS):
            row = kind * D + head * HEAD_DIM
            flat[row : row + HEAD_DIM] = drt_ref[head, kind]
    for j in range(3 * D // TILE):
        cols = slice(j * TILE, (j + 1) * TILE)
        gqkv[:, cols] = dotg(at_ref[...], flat[cols], 1, 1).astype(jnp.bfloat16)
        move_tile(slots, grads_ref, gqkv, out_sem.at[0], 0, across, 0, D // BLOCK, j * per, per, True)
    for j in range(2):
        settled(held.at[pl.ds(j * TILE, TILE)], sems.at[j])
    da = matmul(held[...], flat[...]).T
    hat, inverse = layer_norm(h0_ref[...])

    def put_row(i, values):
        for k in range(D // BLOCK):
            row_ref[i * (D // BLOCK) + k : i * (D // BLOCK) + k + 1] = values[
                :, k * BLOCK : (k + 1) * BLOCK
            ]

    put_row(0, column_sum(da))
    put_row(1, column_sum(da * hat))
    for i in range(2, 8):
        put_row(i, dmod_in[i : i + 1])
    row_ref[64:68] = jnp.broadcast_to(scalars_ref[3:4], (4, BLOCK))
    row_ref[68:72] = jnp.broadcast_to(loss_ref[...], (4, BLOCK))
    dh0 = (dh1_ref[...] + norm_back(da * (1 + mod_ref[1:2]), hat, inverse)).astype(jnp.bfloat16)
    dembed = matmul(xt_ref[...], dh0)
    dbias = column_sum(dh0.astype(jnp.float32))
    for i in range(2):
        cols = slice(i * D // 2, (i + 1) * D // 2)
        io_ref[i, 0:PIN] = dembed[:, cols]
        io_ref[i, PIN : 2 * PIN] = dhead_ref[:, cols]
        io_ref[i, 2 * PIN :] = jnp.zeros((SMALL_ROWS - 2 * PIN, D // 2), jnp.float32)
        io_ref[i, 2 * PIN : 2 * PIN + 1] = dbias[:, cols]
    settled(gqkv, out_sem.at[0])


def final(places, slots, blocks, drt, at, h0, mod, dh1, xt, dmod, scalars, loss, dhead, grads):
    vmem, smem = pl.BlockSpec(memory_space=pltpu.VMEM), pl.BlockSpec(memory_space=pltpu.SMEM)
    hbm = pl.BlockSpec(memory_space=pltpu.HBM)
    f32, bf16 = jnp.float32, jnp.bfloat16
    return pl.pallas_call(
        final_kernel,
        in_specs=[smem, smem, hbm] + [vmem] * 10 + [hbm],
        out_specs=[hbm] + [vmem] * 2,
        out_shape=[
            jax.ShapeDtypeStruct(grads.shape, grads.dtype),
            jax.ShapeDtypeStruct((8 * D // BLOCK + 8, BLOCK), f32),
            jax.ShapeDtypeStruct((2, SMALL_ROWS, D // 2), f32),
        ],
        scratch_shapes=[
            pltpu.VMEM((D, 3 * D), bf16),
            pltpu.VMEM((D, 3 * D), bf16),
            pltpu.VMEM((3 * D, TOK), bf16),
            pltpu.SemaphoreType.DMA((2,)),
            pltpu.SemaphoreType.DMA((1,)),
        ],
        input_output_aliases={13: 0},
        compiler_params=LIMIT,
    )(places, slots, blocks, drt, at, h0, mod, dh1, xt, dmod, scalars, loss, dhead, grads)


def top_dot(left, right, left_dim, right_dim):
    return lax.dot_general(
        left,
        right,
        (((left_dim,), (right_dim,)), ((), ())),
        precision=TOP_PRECISION,
        preferred_element_type=jnp.float32,
    )


SHAMPOO_BLOCKS = 4


def halves_of(values):
    high = values.astype(jnp.bfloat16)
    return high, (values - high.astype(jnp.float32)).astype(jnp.bfloat16)


def fine_dot(left, right):
    (lh, ll), (rh, rl) = left, right
    return (
        matmul(jnp.concatenate([lh, ll], axis=1), jnp.concatenate([rh, rh], axis=0))
        + matmul(lh, rl)
    )


def shampoo_kernel(
    g_ref, w_ref, ema_ref, left_ref, right_ref, root_left, root_right,
    grad_out, w_out, left_out, right_out, ema_out,
):
    limit = CLIP_NORM * BLOCK * NPARAMS ** (-0.5)

    def whole(values):
        return jnp.sum(jnp.sum(values, axis=0, keepdims=True), axis=1, keepdims=True)

    for i in range(SHAMPOO_BLOCKS):
        g = g_ref[i]
        g = g * (limit / jnp.maximum(jnp.sqrt(whole(g * g)), limit))
        grad_out[i] = g
        mine, turned = halves_of(g), halves_of(g.T)
        left_out[i] = STAT_BETA * left_ref[i] + (1 - STAT_BETA) * fine_dot(mine, turned)
        right_out[i] = STAT_BETA * right_ref[i] + (1 - STAT_BETA) * fine_dot(turned, mine)
        p = fine_dot(halves_of(root_left[i]), mine)
        p = fine_dot(halves_of(p), halves_of(root_right[i]))
        p = p * lax.rsqrt(whole(p * p) * (1.0 / (BLOCK * BLOCK)) + 1e-06)
        w = w_ref[i]
        w = w - SHAMPOO_RATE * (p + DECAY_RATE * w)
        w_out[i] = w
        ema_out[i] = EMA_DECAY * ema_ref[i] + (1 - EMA_DECAY) * w


def shampoo_blocks(*arrays):
    spec = pl.BlockSpec((SHAMPOO_BLOCKS, BLOCK, BLOCK), lambda i: (i, 0, 0))
    shape = jax.ShapeDtypeStruct(arrays[0].shape, jnp.float32)
    return pl.pallas_call(
        shampoo_kernel,
        grid=(arrays[0].shape[0] // SHAMPOO_BLOCKS,),
        in_specs=[spec] * 7,
        out_specs=[spec] * 5,
        out_shape=[shape] * 5,
        compiler_params=LIMIT,
    )(*arrays)


def adam_kernel(
    fade, rows_ref, gio_ref, scalars_ref, table_in, mom_in, var_in, ema_in, io, io_mom, io_var, io_ema,
    table_out, mom_out, var_out, ema_out, io_out, io_mom_out, io_var_out, io_ema_out, norm_out, loss_out, count_out,
    grad, flat, table, mom, var, ema, sems,
):
    loads = [
        pltpu.make_async_copy(src, dst, sems.at[i])
        for i, (src, dst) in enumerate(
            ((table_in, table), (mom_in, mom), (var_in, var), (ema_in, ema))
        )
    ]
    for load in loads:
        load.start()
    level = rows_ref[:, 64, :]
    frames = level.shape[0]
    picks = (
        level[:, 0:1] == lax.broadcasted_iota(jnp.int32, (frames, LEVELS), 1).astype(jnp.float32)
    ).astype(jnp.float32)
    for i in range(8 * D // BLOCK):
        flat[:, i * BLOCK : (i + 1) * BLOCK] = rows_ref[:, i, :]
    square = jnp.zeros((LEVELS, D), jnp.float32)
    for i in range(8):
        part = top_dot(picks, flat[:, i * D : (i + 1) * D], 0, 0)
        grad[:, i * D : (i + 1) * D] = part
        square = square + part * part
    gio = jnp.concatenate([gio_ref[0, 0 : 2 * PIN + 1], gio_ref[1, 0 : 2 * PIN + 1]], axis=1)

    def whole(values):
        return jnp.sum(jnp.sum(values, axis=0, keepdims=True), axis=1, keepdims=True)

    norm = jnp.sqrt(whole(square) + whole(gio * gio))
    factor = CLIP_NORM / jnp.maximum(norm, CLIP_NORM)
    count = scalars_ref[2:3, 0:1]
    norm_out[...] = norm
    loss_out[...] = jnp.sum(rows_ref[:, 68, :], axis=0, keepdims=True)[:, 0:1] * count
    count_out[...] = count
    fade_one, fade_two = fade[0], fade[1]

    def update(g, weight, first, second, average):
        new_first = BETA_ONE * first + (1 - BETA_ONE) * g
        new_second = BETA_TWO * second + (1 - BETA_TWO) * g * g
        new = weight - ADAM_RATE * (
            (new_first / fade_one) / (jnp.sqrt(new_second / fade_two) + ADAM_EPS)
            + DECAY_RATE * weight
        )
        return new, new_first, new_second, EMA_DECAY * average + (1 - EMA_DECAY) * new

    outs = (io_out, io_mom_out, io_var_out, io_ema_out)
    for ref, value in zip(outs, update(gio * factor, io[...], io_mom[...], io_var[...], io_ema[...])):
        ref[...] = value
    outs = (table_out, mom_out, var_out, ema_out)
    for load in loads:
        load.wait()

    def one(i, carry):
        cols = pl.ds(pl.multiple_of(i * D, D), D)
        values = update(grad[:, cols] * factor, table[:, cols], mom[:, cols], var[:, cols], ema[:, cols])
        for ref, value in zip(outs, values):
            ref[:, cols] = value
        return carry

    lax.fori_loop(0, 8, one, 0)


def adam(fade, rows, gio, scalars, *arrays):
    vmem, smem = pl.BlockSpec(memory_space=pltpu.VMEM), pl.BlockSpec(memory_space=pltpu.SMEM)
    return pl.pallas_call(
        adam_kernel,
        in_specs=[smem] + [vmem] * 3 + [pl.BlockSpec(memory_space=pl.ANY)] * 4 + [vmem] * 4,
        out_specs=[vmem] * 11,
        out_shape=[jax.ShapeDtypeStruct(a.shape, jnp.float32) for a in arrays]
        + [jax.ShapeDtypeStruct((1, 1), jnp.float32)] * 3,
        scratch_shapes=[
            pltpu.VMEM((LEVELS, 8 * D), jnp.float32),
            pltpu.VMEM((rows.shape[0], 8 * D), jnp.float32),
        ]
        + [pltpu.VMEM((LEVELS, 8 * D), jnp.float32)] * 4
        + [pltpu.SemaphoreType.DMA((4,))],
        compiler_params=pltpu.CompilerParams(vmem_limit_bytes=32 * 2**20),
    )(fade, rows, gio, scalars, *arrays)


def matrix_starts():
    starts, total = [], 0
    for rows_in, cols_in in matrix_shapes():
        starts.append(total)
        total += rows_in // BLOCK * (cols_in // BLOCK)
    return starts, total


def block_places(block_slot):
    owned = block_slot.reshape(32, -1)
    ranks = jnp.sum((owned[:, None, :] < owned[:, :, None]).astype(jnp.int32), axis=2)
    mine = lax.axis_index("frame") * 2 + lax.axis_index("rep")
    own_ranks = lax.dynamic_index_in_dim(ranks, mine, 0, keepdims=False)
    counting = jnp.arange(NSLOT, dtype=jnp.int32)
    perm = jnp.sum(jnp.where(own_ranks[None, :] == counting[:, None], counting[None, :], 0), axis=1)
    owners = jnp.arange(32, dtype=jnp.int32)[:, None]
    gathered = owners * (NSLOT + 1) + ranks + (ranks >= FIRST).astype(jnp.int32)
    scattered = owners * NSLOT + ranks
    natural = jnp.arange(block_slot.shape[0], dtype=jnp.int32)
    same = block_slot[None, :] == natural[:, None]
    places = jnp.sum(jnp.where(same, gathered.reshape(1, -1), 0), axis=1)
    slots = jnp.sum(jnp.where(same, scattered.reshape(1, -1), 0), axis=1)
    early = jnp.sum((owned < matrix_starts()[0][1]).astype(jnp.int32), axis=1)
    return own_ranks, perm, places, slots, jnp.max(early) > FIRST


def rope_columns(frames):
    pairs = HEAD_DIM // 2
    time_pairs = pairs // 4
    row_pairs = (pairs - time_pairs) // 2
    column_pairs = pairs - time_pairs - row_pairs
    token = np.arange(GRID * GRID)
    groups = (
        (time_pairs, np.arange(frames)[:, None, None]),
        (row_pairs, (token // GRID)[None, None, :]),
        (column_pairs, (token % GRID)[None, None, :]),
    )
    angles = [
        np.broadcast_to(
            pos * (ROPE_BASE ** (-np.arange(n) / n))[None, :, None], (frames, n, GRID * GRID)
        )
        for n, pos in groups
    ]
    angles = np.concatenate(angles, axis=1)
    return np.cos(angles).astype(np.float32), np.sin(angles).astype(np.float32)


def on_grid(
    clean,
    noise,
    levels,
    flags,
    frame_map,
    block_slot,
    step_count,
    mat_weight,
    mat_ema,
    stat_left,
    stat_right,
    root_left,
    root_right,
    mod_table,
    mod_mom,
    mod_var,
    mod_ema,
    io_weight,
    io_mom,
    io_var,
    io_ema,
):
    tok_frame = GRID * GRID
    my_time, my_clip = lax.axis_index("frame"), lax.axis_index("rep")
    level_here = levels[0, 0] * (1 - flags[0, 0])
    noised_here = (1 - flags[0, 0]).astype(jnp.float32)
    fraction = level_here.astype(jnp.float32) / LEVELS
    frames_in = (
        jnp.cos(0.5 * jnp.pi * fraction) * clean[0, 0] + jnp.sin(0.5 * jnp.pi * fraction) * noise[0, 0]
    )
    noise_high = noise[0, 0].astype(jnp.bfloat16)
    noise_low = (noise[0, 0] - noise_high.astype(jnp.float32)).astype(jnp.bfloat16)
    data = jnp.concatenate(
        [
            frames_in.astype(jnp.bfloat16).reshape(-1, BLOCK),
            noise_high.reshape(-1, BLOCK),
            noise_low.reshape(-1, BLOCK),
            jnp.full((16, BLOCK), noised_here.astype(jnp.bfloat16)),
            jnp.full((16, BLOCK), level_here.astype(jnp.bfloat16)),
        ]
    )
    ranks, perm, places, slots, spills = block_places(block_slot)
    clip_map = lax.dynamic_index_in_dim(frame_map, my_clip, 0, keepdims=False)
    my_slot = jnp.sum(
        jnp.where(clip_map == my_time, jnp.arange(clip_map.shape[0], dtype=jnp.int32), 0)
    )
    source = (my_slot * 2 + my_clip).reshape(1)
    cosine, sine = rope_columns(frame_map.shape[1])
    gathered = gather_weights(perm, mat_weight, data)
    gathered = lax.cond(spills, lambda: late_gather(gathered), lambda: gathered)
    start, normed, parts, modulation, targets, inputs, scalars = project(
        source,
        places,
        gathered.reshape(-1, BLOCK, BLOCK),
        mod_table,
        io_weight,
        cosine,
        sine,
    )
    mine, gathered, attended, full, lse = forward_exchange(parts, gathered)
    blocks = gathered.reshape(-1, BLOCK, BLOCK)
    grad_heads, grad_blocks, grad_middle, grad_head, grad_mod, loss_part = middle(
        places,
        slots,
        blocks,
        attended.reshape(D, tok_frame),
        start,
        modulation,
        io_weight,
        targets,
        scalars,
    )
    grad_proj, later = backward_exchange(
        grad_heads.reshape(HEADS, HEAD_DIM, tok_frame),
        mine,
        full,
        lse,
        cosine,
        sine,
        grad_blocks.reshape(32, NSLOT, BLOCK, BLOCK),
    )
    grad_blocks, row, grad_io = final(
        places,
        slots,
        blocks,
        grad_proj,
        normed,
        start,
        modulation,
        grad_middle,
        inputs,
        grad_mod,
        scalars,
        loss_part,
        grad_head,
        grad_blocks,
    )
    grad_blocks = grad_blocks.reshape(32, NSLOT, BLOCK, BLOCK)
    later = lax.cond(spills, lambda: late_scatter(grad_blocks), lambda: later)
    owned, rows, grad_io = scatter_grads(ranks, grad_blocks, row, grad_io, later)
    step = step_count[0].astype(jnp.float32)
    new_small = adam(
        jnp.stack([1 - BETA_ONE**step, 1 - BETA_TWO**step]),
        rows.reshape(32, -1, BLOCK),
        grad_io,
        scalars,
        mod_table,
        mod_mom,
        mod_var,
        mod_ema,
        io_weight,
        io_mom,
        io_var,
        io_ema,
    )
    new_mod, new_io = new_small[:4], new_small[4:8]
    grad_norm, loss_sum, noised_total = (value.reshape(()) for value in new_small[8:])
    mat_grad, new_mat_weight, new_stat_left, new_stat_right, new_mat_ema = shampoo_blocks(
        owned, mat_weight, mat_ema, stat_left, stat_right, root_left, root_right
    )
    return (
        loss_sum,
        noised_total,
        grad_norm,
        mat_grad,
        new_mat_weight,
        new_stat_left,
        new_stat_right,
        new_mat_ema,
        new_mod[0],
        new_mod[1],
        new_mod[2],
        new_mod[3],
        new_io[0],
        new_io[1],
        new_io[2],
        new_io[3],
    )


def solution(mesh):
    tuned = dict(mesh.shape) == {"frame": 16, "rep": 2}
    body = on_grid if tuned else on_device
    in_specs = (
        P("rep", "frame", None, None),
        P("rep", "frame", None, None),
        P("rep", "frame"),
        P("rep", "frame"),
        P(),
        P(),
        P(),
        P(("frame", "rep"), None, None),
        P(("frame", "rep"), None, None),
        P(("frame", "rep"), None, None),
        P(("frame", "rep"), None, None),
        P(("frame", "rep"), None, None),
        P(("frame", "rep"), None, None),
        P(),
        P(),
        P(),
        P(),
        P(),
        P(),
        P(),
        P(),
    )
    out_specs = (
        P(),
        P(),
        P(),
        P(("frame", "rep"), None, None),
        P(("frame", "rep"), None, None),
        P(("frame", "rep"), None, None),
        P(("frame", "rep"), None, None),
        P(("frame", "rep"), None, None),
        P(),
        P(),
        P(),
        P(),
        P(),
        P(),
        P(),
        P(),
    )
    return jax.shard_map(
        body, mesh=mesh, in_specs=in_specs, out_specs=out_specs, check_vma=False
    )
```

```python
from functools import partial
import math

import jax
import jax.numpy as jnp
import numpy as np
from jax import lax
from jax.experimental import pallas as pl
from jax.experimental.pallas import tpu as pltpu
from jax.sharding import PartitionSpec as P

D = 1024
HEADS = 16
HEAD_DIM = 64
FFN = 4096
PIN = 16
GRID = 16
BLOCK = 128
LEVELS = 32
FR_DEV = 1
NPARAMS = 12878848


LN_EPS = 1e-06
ROPE_BASE = 10000.0
CLIP_NORM = 0.01
BETA_ONE = 0.9
BETA_TWO = 0.999
ADAM_EPS = 1e-08
ADAM_RATE = 0.1
DECAY_RATE = 0.1
STAT_BETA = 0.95
SHAMPOO_RATE = 0.01
EMA_DECAY = 0.9
TOP_PRECISION = lax.Precision.HIGHEST


def matmul(left, right):
    return jnp.dot(left, right, preferred_element_type=jnp.float32)


def layer_norm(hidden):
    centered = hidden - jnp.mean(hidden, axis=-1, keepdims=True)
    inverse = lax.rsqrt(jnp.mean(centered * centered, axis=-1, keepdims=True) + LN_EPS)
    return (centered * inverse, inverse)


def norm_back(grad_hat, normed, inverse):
    return inverse * (
        grad_hat
        - jnp.mean(grad_hat, axis=-1, keepdims=True)
        - normed * jnp.mean(grad_hat * normed, axis=-1, keepdims=True)
    )


def gelu_back(upper, grad_act):
    return jax.vjp(partial(jax.nn.gelu, approximate=True), upper)[1](grad_act)[0]


def frequencies(width):
    return ROPE_BASE ** (-jnp.arange(width, dtype=jnp.float32) / width)


def rope_tables(frame_ids):
    pairs = HEAD_DIM // 2
    time_pairs = pairs // 4
    row_pairs = (pairs - time_pairs) // 2
    column_pairs = pairs - time_pairs - row_pairs
    frames = frame_ids.shape[0]
    tok_frame = GRID * GRID
    token_pos = jnp.arange(tok_frame, dtype=jnp.int32)
    row_pos = (token_pos // GRID).astype(jnp.float32)
    column_pos = (token_pos % GRID).astype(jnp.float32)
    time_angle = (
        frame_ids.astype(jnp.float32)[:, None, None] * frequencies(time_pairs)[None, None, :]
    )
    row_angle = row_pos[None, :, None] * frequencies(row_pairs)[None, None, :]
    column_angle = column_pos[None, :, None] * frequencies(column_pairs)[None, None, :]
    angles = jnp.concatenate(
        [jnp.broadcast_to(time_angle, (frames, tok_frame, time_pairs)), row_angle, column_angle],
        axis=-1,
    )
    angles = angles.reshape(frames * tok_frame, pairs)
    return (jnp.cos(angles), jnp.sin(angles))


def rotate(values, cosine, sine):
    pairs = HEAD_DIM // 2
    first, second = (values[..., :pairs], values[..., pairs:])
    cosine = cosine[:, None, :]
    sine = sine[:, None, :]
    return jnp.concatenate(
        [first * cosine - second * sine, first * sine + second * cosine], axis=-1
    )


def split_heads(flat):
    return flat.reshape(flat.shape[0], HEADS, HEAD_DIM)


def matrix_shapes():
    return ((D, 3 * D), (D, D), (D, FFN), (FFN, D))


def from_blocks(natural):
    matrices = []
    offset = 0
    for rows_in, cols_in in matrix_shapes():
        count_in = rows_in // BLOCK * (cols_in // BLOCK)
        part_blocks = natural[offset : offset + count_in]
        matrices.append(
            part_blocks.reshape(rows_in // BLOCK, cols_in // BLOCK, BLOCK, BLOCK)
            .transpose(0, 2, 1, 3)
            .reshape(rows_in, cols_in)
        )
        offset = offset + count_in
    return matrices


def to_blocks(matrix):
    rows_in, cols_in = matrix.shape
    return (
        matrix.reshape(rows_in // BLOCK, BLOCK, cols_in // BLOCK, BLOCK)
        .transpose(0, 2, 1, 3)
        .reshape(-1, BLOCK, BLOCK)
    )


def score_block(queries, key_block, query_frames, key_frames):
    scores = jnp.einsum(
        "qhd,khd->hqk", queries, key_block, preferred_element_type=jnp.float32
    ) * HEAD_DIM ** (-0.5)
    visible = key_frames[None, None, :] <= query_frames[None, :, None]
    return jnp.where(visible, scores, -jnp.inf)


def stack_keys(key_rows, value_rows, frame_rows):
    total_rows = key_rows.shape[0]
    block_rows = math.gcd(total_rows, 512)
    blocks = total_rows // block_rows
    return (
        (
            key_rows.reshape(blocks, block_rows, HEADS, HEAD_DIM),
            value_rows.reshape(blocks, block_rows, HEADS, HEAD_DIM),
            frame_rows.reshape(blocks, block_rows),
        ),
        block_rows,
    )


def keep_state(previous):
    return previous


def fold_keys(state, shard_rows, queries, query_frames, key_frames_all):
    key_rows, value_rows = shard_rows
    stacks, block_rows = stack_keys(key_rows, value_rows, key_frames_all)
    top_query = jnp.max(query_frames)

    def fold_step_block(carried, block_in):
        key_block, value_block, key_frames = block_in

        def fold_compute(previous):
            running, denominator, accumulated = previous
            scores = score_block(queries, key_block, query_frames, key_frames)
            new_max = jnp.maximum(running, jnp.max(scores, axis=-1))
            weights = jnp.exp(scores - new_max[..., None])
            rescale = jnp.exp(running - new_max)
            contrib = jnp.einsum(
                "hqk,khd->hqd",
                weights.astype(jnp.bfloat16),
                value_block,
                preferred_element_type=jnp.float32,
            )
            return (
                new_max,
                denominator * rescale + jnp.sum(weights, axis=-1),
                accumulated * rescale[..., None] + contrib,
            )

        return (lax.cond(jnp.min(key_frames) <= top_query, fold_compute, keep_state, carried), None)

    state, unused = lax.scan(fold_step_block, state, stacks)
    return state


def grad_parts(
    queries, grad_heads, delta, log_total, query_frames, key_block, value_block, key_frames
):
    probs = jnp.exp(
        score_block(queries, key_block, query_frames, key_frames) - log_total[..., None]
    )
    grad_probs = jnp.einsum(
        "qhd,khd->hqk", grad_heads, value_block, preferred_element_type=jnp.float32
    )
    grad_scores = (probs * (grad_probs - delta[..., None])).astype(jnp.bfloat16)
    return (probs, grad_scores)


def key_value_block(
    queries, grad_heads, delta, log_total, query_frames, key_block, value_block, key_frames
):
    block_rows = key_block.shape[0]
    probs, grad_scores = grad_parts(
        queries, grad_heads, delta, log_total, query_frames, key_block, value_block, key_frames
    )
    key_grad = jnp.einsum(
        "hqk,qhd->khd", grad_scores, queries, preferred_element_type=jnp.float32
    ) * HEAD_DIM ** (-0.5)
    value_grad = jnp.einsum(
        "hqk,qhd->khd", probs.astype(jnp.bfloat16), grad_heads, preferred_element_type=jnp.float32
    )
    return jnp.concatenate(
        [key_grad.reshape(block_rows, D), value_grad.reshape(block_rows, D)], axis=1
    )


def query_grads(
    queries, grad_heads, delta, log_total, query_frames, key_all, value_all, key_frames_all
):
    stacks, block_rows = stack_keys(key_all, value_all, key_frames_all)
    top_query = jnp.max(query_frames)

    def query_step_block(carried, block_in):
        key_block, value_block, key_frames = block_in

        def query_compute(previous):
            probs, grad_scores = grad_parts(
                queries,
                grad_heads,
                delta,
                log_total,
                query_frames,
                key_block,
                value_block,
                key_frames,
            )
            return previous + jnp.einsum(
                "hqk,khd->qhd", grad_scores, key_block, preferred_element_type=jnp.float32
            )

        return (
            lax.cond(jnp.min(key_frames) <= top_query, query_compute, keep_state, carried),
            None,
        )

    initial = jnp.zeros(queries.shape, jnp.float32)
    result, unused = lax.scan(query_step_block, initial, stacks)
    return result * HEAD_DIM ** (-0.5)


def key_terms(
    row_count,
    queries,
    grad_heads,
    delta,
    log_total,
    query_frames,
    key_all,
    value_all,
    key_frames_all,
):
    stacks, block_rows = stack_keys(key_all, value_all, key_frames_all)
    top_query = jnp.max(query_frames)

    def one_block(block_in):
        key_block, value_block, key_frames = block_in

        def one_compute(unused):
            return key_value_block(
                queries,
                grad_heads,
                delta,
                log_total,
                query_frames,
                key_block,
                value_block,
                key_frames,
            )

        def nothing(unused):
            return jnp.zeros((block_rows, 2 * D), jnp.float32)

        return lax.cond(jnp.min(key_frames) <= top_query, one_compute, nothing, 0)

    return lax.map(one_block, stacks).reshape(row_count, 2 * D)


def shampoo(grads, weights, average, left, right, left_root, right_root):
    new_left = STAT_BETA * left + (1 - STAT_BETA) * jnp.einsum(
        "bij,bkj->bik", grads, grads, precision=TOP_PRECISION
    )
    new_right = STAT_BETA * right + (1 - STAT_BETA) * jnp.einsum(
        "bji,bjk->bik", grads, grads, precision=TOP_PRECISION
    )
    direction = jnp.einsum("bij,bjk->bik", left_root, grads, precision=TOP_PRECISION)
    direction = jnp.einsum("bij,bjk->bik", direction, right_root, precision=TOP_PRECISION)
    direction = direction * lax.rsqrt(
        jnp.mean(direction * direction, axis=(1, 2), keepdims=True) + 1e-06
    )
    new_weights = weights - SHAMPOO_RATE * (direction + DECAY_RATE * weights)
    new_average = EMA_DECAY * average + (1 - EMA_DECAY) * new_weights
    return (new_weights, new_left, new_right, new_average)


def adamw(grads, weights, first, second, average, step):
    new_first = BETA_ONE * first + (1 - BETA_ONE) * grads
    new_second = BETA_TWO * second + (1 - BETA_TWO) * grads * grads
    first_hat = new_first / (1 - BETA_ONE**step)
    second_hat = new_second / (1 - BETA_TWO**step)
    new_weights = weights - ADAM_RATE * (
        first_hat / (jnp.sqrt(second_hat) + ADAM_EPS) + DECAY_RATE * weights
    )
    new_average = EMA_DECAY * average + (1 - EMA_DECAY) * new_weights
    return (new_weights, new_first, new_second, new_average)


def on_device(
    clean,
    noise,
    levels,
    flags,
    frame_map,
    block_slot,
    step_count,
    mat_weight,
    mat_ema,
    stat_left,
    stat_right,
    root_left,
    root_right,
    mod_table,
    mod_mom,
    mod_var,
    mod_ema,
    io_weight,
    io_mom,
    io_var,
    io_ema,
):
    tok_frame = GRID * GRID
    local_rows = FR_DEV * tok_frame
    noised = (1 - flags[0]).astype(jnp.float32)
    noised_total = jnp.maximum(lax.psum(jnp.sum(noised), ("frame", "rep")), 1.0)
    gathered = lax.all_gather(mat_weight.astype(jnp.bfloat16), ("frame", "rep"), axis=0, tiled=True)
    natural = jnp.zeros_like(gathered).at[block_slot].set(gathered)
    attn_w, out_w, up_w, down_w = from_blocks(natural)
    clip_map = lax.dynamic_index_in_dim(frame_map, lax.axis_index("rep"), 0, keepdims=False)
    my_frames = lax.dynamic_slice_in_dim(clip_map, lax.axis_index("frame") * FR_DEV, FR_DEV)
    key_frames_all = jnp.repeat(clip_map, tok_frame)
    query_frames = jnp.repeat(my_frames, tok_frame)
    level_now = levels[0] * (1 - flags[0])
    fraction = level_now.astype(jnp.float32) / LEVELS
    keep_coef = jnp.cos(0.5 * jnp.pi * fraction)
    noise_coef = jnp.sin(0.5 * jnp.pi * fraction)
    frames_in = keep_coef[:, None, None] * clean[0] + noise_coef[:, None, None] * noise[0]
    inputs = jnp.swapaxes(frames_in, 1, 2).reshape(local_rows, PIN).astype(jnp.bfloat16)
    targets = jnp.swapaxes(noise[0], 1, 2).reshape(local_rows, PIN)
    selector = (level_now[:, None] == jnp.arange(LEVELS, dtype=jnp.int32)[None, :]).astype(
        jnp.float32
    )
    modulation = jnp.dot(selector, mod_table, precision=TOP_PRECISION).reshape(FR_DEV, 8, 1, D)
    io_low = io_weight.astype(jnp.bfloat16)
    embed = io_low[:PIN]
    head = io_low[PIN : 2 * PIN]
    start = (matmul(inputs, embed) + io_weight[2 * PIN]).reshape(FR_DEV, tok_frame, D)
    hat_one, inv_one = layer_norm(start)
    normed = (
        (hat_one * (1 + modulation[:, 1]) + modulation[:, 0])
        .reshape(local_rows, D)
        .astype(jnp.bfloat16)
    )
    projected = matmul(normed, attn_w)
    cosine, sine = rope_tables(my_frames)
    queries = rotate(split_heads(projected[:, :D]), cosine, sine).astype(jnp.bfloat16)
    key_flat = (
        rotate(split_heads(projected[:, D : 2 * D]), cosine, sine)
        .astype(jnp.bfloat16)
        .reshape(local_rows, D)
    )
    value_flat = projected[:, 2 * D :].astype(jnp.bfloat16)
    initial = (
        jnp.full((HEADS, local_rows), -1e30, jnp.float32),
        jnp.zeros((HEADS, local_rows), jnp.float32),
        jnp.zeros((HEADS, local_rows, HEAD_DIM), jnp.float32),
    )
    running, denominator, accumulated = fold_keys(
        initial,
        (
            lax.all_gather(key_flat, "frame", axis=0, tiled=True),
            lax.all_gather(value_flat, "frame", axis=0, tiled=True),
        ),
        queries,
        query_frames,
        key_frames_all,
    )
    attended = jnp.transpose(accumulated / denominator[..., None], (1, 0, 2)).reshape(local_rows, D)
    log_total = running + jnp.log(denominator)
    attended_low = attended.astype(jnp.bfloat16)
    branch = matmul(attended_low, out_w).reshape(FR_DEV, tok_frame, D)
    middle = start + modulation[:, 2] * branch
    hat_two, inv_two = layer_norm(middle)
    normed_two = (
        (hat_two * (1 + modulation[:, 4]) + modulation[:, 3])
        .reshape(local_rows, D)
        .astype(jnp.bfloat16)
    )
    upper = matmul(normed_two, up_w)
    activated = jax.nn.gelu(upper, approximate=True).astype(jnp.bfloat16)
    lower = matmul(activated, down_w).reshape(FR_DEV, tok_frame, D)
    final = middle + modulation[:, 5] * lower
    hat_three, inv_three = layer_norm(final)
    normed_three = (
        (hat_three * (1 + modulation[:, 7]) + modulation[:, 6])
        .reshape(local_rows, D)
        .astype(jnp.bfloat16)
    )
    predicted = matmul(normed_three, head.T)
    row_weight = jnp.repeat(noised, tok_frame)[:, None]
    inv_scale = 1.0 / (noised_total * tok_frame * PIN)
    difference = predicted - targets
    loss_part = jnp.sum(row_weight * difference * difference) * inv_scale
    grad_pred = (2.0 * inv_scale * row_weight * difference).astype(jnp.bfloat16)
    grad_head = jnp.dot(grad_pred.T, normed_three, preferred_element_type=jnp.float32)
    grad_norm_three = matmul(grad_pred, head).reshape(FR_DEV, tok_frame, D)
    grad_final = norm_back(grad_norm_three * (1 + modulation[:, 7]), hat_three, inv_three)
    grad_lower = (grad_final * modulation[:, 5]).reshape(local_rows, D).astype(jnp.bfloat16)
    grad_down = jnp.dot(activated.T, grad_lower, preferred_element_type=jnp.float32)
    grad_upper = gelu_back(upper, matmul(grad_lower, down_w.T)).astype(jnp.bfloat16)
    grad_up = jnp.dot(normed_two.T, grad_upper, preferred_element_type=jnp.float32)
    grad_norm_two = matmul(grad_upper, up_w.T).reshape(FR_DEV, tok_frame, D)
    grad_middle = grad_final + norm_back(grad_norm_two * (1 + modulation[:, 4]), hat_two, inv_two)
    grad_branch = (grad_middle * modulation[:, 2]).reshape(local_rows, D).astype(jnp.bfloat16)
    grad_out_w = jnp.dot(attended_low.T, grad_branch, preferred_element_type=jnp.float32)
    grad_heads = split_heads(matmul(grad_branch, out_w.T).astype(jnp.bfloat16))
    delta = jnp.sum(grad_heads.astype(jnp.float32) * split_heads(attended), axis=-1).T
    key_all, value_all = (
        lax.all_gather(key_flat, "frame", axis=0, tiled=True),
        lax.all_gather(value_flat, "frame", axis=0, tiled=True),
    )
    grad_query = query_grads(
        queries, grad_heads, delta, log_total, query_frames, key_all, value_all, key_frames_all
    )
    key_value_grad = lax.psum_scatter(
        key_terms(
            lax.axis_size("frame") * local_rows,
            queries,
            grad_heads,
            delta,
            log_total,
            query_frames,
            key_all,
            value_all,
            key_frames_all,
        ),
        "frame",
        scatter_dimension=0,
        tiled=True,
    )
    grad_q = rotate(grad_query, cosine, -sine).reshape(local_rows, D)
    grad_k = rotate(split_heads(key_value_grad[:, :D]), cosine, -sine).reshape(local_rows, D)
    grad_proj = jnp.concatenate([grad_q, grad_k, key_value_grad[:, D:]], axis=1).astype(
        jnp.bfloat16
    )
    grad_attn_w = jnp.dot(normed.T, grad_proj, preferred_element_type=jnp.float32)
    grad_norm_one = matmul(grad_proj, attn_w.T).reshape(FR_DEV, tok_frame, D)
    grad_start = grad_middle + norm_back(grad_norm_one * (1 + modulation[:, 1]), hat_one, inv_one)
    grad_start_low = grad_start.reshape(local_rows, D).astype(jnp.bfloat16)
    grad_embed = jnp.dot(inputs.T, grad_start_low, preferred_element_type=jnp.float32)
    grad_bias = jnp.sum(grad_start_low.astype(jnp.float32), axis=0)
    mod_terms = [
        grad_norm_one,
        grad_norm_one * hat_one,
        grad_middle * branch,
        grad_norm_two,
        grad_norm_two * hat_two,
        grad_final * lower,
        grad_norm_three,
        grad_norm_three * hat_three,
    ]
    mod_grads = jnp.stack([jnp.sum(term, axis=1) for term in mod_terms], axis=1).reshape(
        FR_DEV, 8 * D
    )
    grad_table = jnp.dot(selector.T, mod_grads, precision=TOP_PRECISION)
    grad_io = jnp.concatenate([grad_embed, grad_head, grad_bias[None, :]], axis=0)
    grad_table, grad_io, total_loss = lax.psum((grad_table, grad_io, loss_part), ("frame", "rep"))
    grad_blocks = jnp.concatenate(
        [to_blocks(grad_attn_w), to_blocks(grad_out_w), to_blocks(grad_up), to_blocks(grad_down)], 0
    )
    owned = lax.psum_scatter(
        grad_blocks[block_slot], ("frame", "rep"), scatter_dimension=0, tiled=True
    )
    block_limit = CLIP_NORM * BLOCK * NPARAMS ** (-0.5)
    block_norm = jnp.sqrt(jnp.sum(owned * owned, axis=(1, 2), keepdims=True))
    mat_grad = owned * (block_limit / jnp.maximum(block_norm, block_limit))
    grad_norm = jnp.sqrt(jnp.sum(grad_table * grad_table) + jnp.sum(grad_io * grad_io))
    factor = CLIP_NORM / jnp.maximum(grad_norm, CLIP_NORM)
    new_mat_weight, new_stat_left, new_stat_right, new_mat_ema = shampoo(
        mat_grad, mat_weight, mat_ema, stat_left, stat_right, root_left, root_right
    )
    step = step_count[0].astype(jnp.float32)
    new_mod = adamw(grad_table * factor, mod_table, mod_mom, mod_var, mod_ema, step)
    new_io = adamw(grad_io * factor, io_weight, io_mom, io_var, io_ema, step)
    return (
        total_loss * noised_total,
        noised_total,
        grad_norm,
        mat_grad,
        new_mat_weight,
        new_stat_left,
        new_stat_right,
        new_mat_ema,
        new_mod[0],
        new_mod[1],
        new_mod[2],
        new_mod[3],
        new_io[0],
        new_io[1],
        new_io[2],
        new_io[3],
    )


TOK = GRID * GRID
GROUP = 4


def fold_rows(values, op):
    return op(values.reshape(values.shape[0] // 8, 8, values.shape[1]), axis=0)


def side_by_side(ref, first, count, kind):
    parts = [ref[first + j, kind] for j in range(count)]
    return jnp.concatenate(parts, axis=1) if count > 1 else parts[0]


def attend_frame(t, qkv, scores, full, lse):
    q = qkv[t, 0] * jnp.bfloat16(HEAD_DIM**-0.5)

    def score(k, top):
        s = dotg(qkv[k, 1], q, 0, 0)
        scores[k] = s
        return jnp.maximum(top, fold_rows(s, jnp.max))

    top = lax.fori_loop(
        0, t + 1, score, jnp.full((8, TOK), -1e30, jnp.float32), unroll=min(GROUP, t + 1)
    )
    top = jnp.max(top, axis=0, keepdims=True)
    total = jnp.zeros((8, TOK), jnp.float32)
    acc = jnp.zeros((HEAD_DIM, TOK), jnp.float32)
    for k in range(0, t + 1, GROUP):
        count = min(GROUP, t + 1 - k)
        probs = []
        for j in range(count):
            p = jnp.exp(scores[k + j] - top)
            total = total + fold_rows(p, jnp.sum)
            probs.append(p.astype(jnp.bfloat16))
        acc = acc + dotg(side_by_side(qkv, k, count, 2), jnp.concatenate(probs, axis=0), 1, 0)
    total = jnp.sum(total, axis=0, keepdims=True)
    out = acc / total
    full[t] = out
    lse[t] = top + jnp.log(total)
    return out.astype(jnp.bfloat16)


def turn_back(values, cosine, sine):
    first, second = values[: HEAD_DIM // 2], values[HEAD_DIM // 2 :]
    return jnp.concatenate(
        [first * cosine + second * sine, second * cosine - first * sine], axis=0
    )


def attend_frame_back(t, qkv, do_ref, full, lse, cos, sin, dk_ref, dv_ref):
    q = qkv[t, 0] * jnp.bfloat16(HEAD_DIM**-0.5)
    do = do_ref[t]
    delta = jnp.sum(do.astype(jnp.float32) * full[t], axis=0, keepdims=True)
    dq = jnp.zeros((HEAD_DIM, TOK), jnp.float32)
    for k in range(0, t + 1, GROUP):
        count = min(GROUP, t + 1 - k)
        keys = side_by_side(qkv, k, count, 1)
        p = jnp.exp(dotg(keys, q, 0, 0) - lse[t])
        dp = dotg(side_by_side(qkv, k, count, 2), do, 0, 0)
        ds = (p * (dp - delta)).astype(jnp.bfloat16)
        dq = dq + dotg(keys, ds, 1, 0)
        dk = dotg(q, ds, 1, 1)
        dv = dotg(do, p.astype(jnp.bfloat16), 1, 1)
        for j in range(count):
            dk_ref[k + j] += dk[:, j * TOK : (j + 1) * TOK]
            dv_ref[k + j] += dv[:, j * TOK : (j + 1) * TOK]
    return (
        turn_back(dq * HEAD_DIM**-0.5, cos[t], sin[t]).astype(jnp.bfloat16),
        turn_back(dk_ref[t], cos[t], sin[t]).astype(jnp.bfloat16),
        dv_ref[t].astype(jnp.bfloat16),
    )


def attend_kernel(qkv_ref, low_ref, full_ref, lse_ref, scores):
    for t in range(qkv_ref.shape[0]):
        low_ref[t] = attend_frame(t, qkv_ref, scores, full_ref, lse_ref)


def attend(qkv):
    frames = qkv.shape[0]
    vmem = pl.BlockSpec(memory_space=pltpu.VMEM)
    return pl.pallas_call(
        attend_kernel,
        in_specs=[vmem],
        out_specs=[vmem] * 3,
        out_shape=[
            jax.ShapeDtypeStruct((frames, HEAD_DIM, TOK), jnp.bfloat16),
            jax.ShapeDtypeStruct((frames, HEAD_DIM, TOK), jnp.float32),
            jax.ShapeDtypeStruct((frames, 1, TOK), jnp.float32),
        ],
        scratch_shapes=[pltpu.VMEM((frames, TOK, TOK), jnp.float32)],
        compiler_params=pltpu.CompilerParams(vmem_limit_bytes=32 * 2**20),
    )(qkv)


def attend_back_kernel(qkv_ref, do_ref, full_ref, lse_ref, cos_ref, sin_ref, out_ref, dk, dv):
    dk[...] = jnp.zeros_like(dk)
    dv[...] = jnp.zeros_like(dv)
    for t in reversed(range(qkv_ref.shape[0])):
        parts = attend_frame_back(t, qkv_ref, do_ref, full_ref, lse_ref, cos_ref, sin_ref, dk, dv)
        for i in range(3):
            out_ref[t, i] = parts[i]


def attend_back(qkv, do, full, lse, cos, sin):
    frames = qkv.shape[0]
    vmem = pl.BlockSpec(memory_space=pltpu.VMEM)
    return pl.pallas_call(
        attend_back_kernel,
        in_specs=[vmem] * 6,
        out_specs=vmem,
        out_shape=jax.ShapeDtypeStruct(qkv.shape, jnp.bfloat16),
        scratch_shapes=[pltpu.VMEM((frames, HEAD_DIM, TOK), jnp.float32)] * 2,
        compiler_params=pltpu.CompilerParams(vmem_limit_bytes=32 * 2**20),
    )(qkv, do, full, lse, cos, sin)


MESH = pl.DeviceIdType.MESH
NSLOT = 24
FIRST = 14
LATER = NSLOT - FIRST
DATA = FIRST
SMALL_ROWS = 40
FIRST_GATHER = (
    ("xzy", 0, 2),
    ("yzx", 2, 2),
    ("zxy", 4, 3),
    ("zyx", 7, 3),
    ("zxy", 10, 2),
    ("zyx", 12, 3),
)
FIRST_SCATTER = FIRST_GATHER[:5] + (("zyx", 12, 2),)
LATER_PARTS = (("zyx", 0, 5), ("zyx", 5, 5))


def place():
    frame = lax.axis_index("frame")
    return frame // 4, (frame // 2) % 2, frame % 2, lax.axis_index("rep")


def device(z, y, c, x):
    return ((z * 2 + y) * 2 + c, x)


def owner_of(z, y, c, x):
    return ((z * 2 + y) * 2 + c) * 2 + x


def plane_of(z, y, x):
    return (z * 2 + y) * 2 + x


def offsets():
    return [(dx, dy, dz) for dx in (0, 1) for dy in (0, 1) for dz in range(-3, 4)]


def hops(off):
    return off[0] + off[1] + abs(off[2])


def route_keys(parts):
    keys = [(part, off) for part in range(len(parts)) for off in offsets()]
    return sorted(keys, key=lambda k: (hops(k[1]), k[0]))


def onward(order, off):
    moved = dict(zip("xyz", off))
    last = max((order.index(k) for k in order if moved[k]), default=-1)
    links = []
    if last >= 0 and order[last] == "z":
        links.append("u" if off[2] < 0 else "w")
    for k in order[last + 1 :]:
        links.extend("uw" if k == "z" else k)
    return links


def toward(order, off):
    moved = dict(zip("xyz", off))
    last = [k for k in order if moved[k]][-1]
    if last == "z":
        return ("w", "u") if off[2] < 0 else ("u", "w")
    return last, last


def can(link, z):
    return {"u": z < 3, "w": z > 0}.get(link)


def partner(link, z, y, c, x):
    return {
        "x": device(z, y, c, 1 - x),
        "y": device(z, 1 - y, c, x),
        "u": device(z + 1, y, c, x),
        "w": device(z - 1, y, c, x),
        "c": device(z, y, 1 - c, x),
    }[link]


def when(cond, fn):
    if cond is None:
        fn()
    else:
        pl.when(cond)(fn)


def both(a, b):
    return b if a is None else a if b is None else jnp.logical_and(a, b)


def owner_at(off, z, y, x):
    dx, dy, dz = off
    oz = z + dz
    cond = None if dz == 0 else (oz <= 3 if dz > 0 else oz >= 0)
    return oz, (1 - y if dy else y), (1 - x if dx else x), cond


def greet(z, y, c, x, far=()):
    barrier = pltpu.get_barrier_semaphore()
    for link in "xyuwc":
        when(
            can(link, z),
            lambda link=link: pl.semaphore_signal(
                barrier, inc=1, device_id=partner(link, z, y, c, x), device_id_type=MESH
            ),
        )
    for dev in far:
        pl.semaphore_signal(barrier, inc=1, device_id=dev, device_id_type=MESH)
    ends = jnp.logical_or(z == 0, z == 3)
    pl.when(ends)(lambda: pl.semaphore_wait(barrier, 4 + len(far)))
    pl.when(jnp.logical_not(ends))(lambda: pl.semaphore_wait(barrier, 5 + len(far)))


class Gather:
    def __init__(self, parts, src, out, sems, where, shift=0, axes="xyz"):
        self.parts, self.src, self.out, self.where, self.shift = parts, src, out, where, shift
        self.axes = axes
        self.total = sum(count for _, _, count in parts)
        self.send, self.recv, self.csend, self.crecv = sems
        self.keys = [k for k in route_keys(parts) if "x" in axes or k[1][:2] == (0, 0)]
        self.last = {}
        for key in self.keys if "x" in axes else ():
            self.last[key[1]] = key
        self.sent = []

    @staticmethod
    def sems(parts):
        n = len(parts)
        return [
            pltpu.SemaphoreType.DMA((4, n, 16)),
            pltpu.SemaphoreType.DMA((n, 16)),
            pltpu.SemaphoreType.DMA((16,)),
            pltpu.SemaphoreType.DMA((16,)),
        ]

    def held(self, owner):
        return self.out.at[owner, pl.ds(self.shift, self.total)]

    def hop(self, link, part, src, owner, plane):
        _, first, count = self.parts[part]
        return pltpu.make_async_remote_copy(
            src_ref=src.at[pl.ds(first, count)],
            dst_ref=self.out.at[owner, pl.ds(self.shift + first, count)],
            send_sem=self.send.at["xyuw".index(link), part, plane],
            recv_sem=self.recv.at[part, plane],
            device_id=partner(link, *self.where),
            device_id_type=MESH,
        )

    def across(self, src, owner, plane):
        return pltpu.make_async_remote_copy(
            src_ref=src,
            dst_ref=self.held(owner),
            send_sem=self.csend.at[plane],
            recv_sem=self.crecv.at[plane],
            device_id=partner("c", *self.where),
            device_id_type=MESH,
        )

    def step(self, key):
        part, off = key
        z, y, c, x = self.where
        oz, oy, ox, cond = owner_at(off, z, y, x)
        owner, plane = owner_of(oz, oy, c, ox), plane_of(oz, oy, ox)
        own = off == (0, 0, 0)
        here = own or (self.axes == "xy" and off[:2] == (0, 0))
        src = self.src if own and self.axes != "xy" else self.held(owner)
        links = [k for k in onward(self.parts[part][0], off) if ("z" if k in "uw" else k) in self.axes]

        def act():
            if not here:
                self.hop("x", part, src, owner, plane).wait_recv()
            for link in links:
                when(can(link, z), lambda link=link: self.hop(link, part, src, owner, plane).start())
            if self.last.get(off) == key:
                self.across(src, owner, plane).start()

        when(cond, act)
        for link in links:
            self.sent.append(
                (both(cond, can(link, z)), lambda link=link: self.hop(link, part, src, owner, plane))
            )
        if self.last.get(off) == key:
            self.sent.append((cond, lambda: self.across(src, owner, plane)))

    def finish(self):
        for cond, make in self.sent:
            when(cond, lambda make=make: make().wait_send())
        c = self.where[2]
        for plane in range(16) if self.last else ():
            owner = owner_of(plane // 4, (plane // 2) % 2, 1 - c, plane % 2)
            self.across(self.held(owner), owner, plane).wait_recv()


def gather_kernel(perm_ref, w_ref, data_ref, out_ref, stage, later, local, *sems):
    where = place()
    owner = owner_of(*where)
    count = len(Gather.sems(FIRST_GATHER))

    def take(i, carry):
        stage[i] = w_ref[perm_ref[i]].astype(jnp.bfloat16)
        return carry

    def take_later(i, carry):
        later[i] = w_ref[perm_ref[FIRST + i]].astype(jnp.bfloat16)
        return carry

    lax.fori_loop(0, FIRST, take, 0)
    stage[DATA] = data_ref[...]
    greet(*where)
    gather = Gather(FIRST_GATHER, stage, out_ref, sems[:count], where)
    along = Gather(LATER_PARTS, later, out_ref, sems[count:], where, FIRST + 1, "z")
    own = [
        pltpu.make_async_copy(stage, gather.held(owner), local.at[0]),
        pltpu.make_async_copy(later, along.held(owner), local.at[1]),
    ]
    own[0].start()
    begun = len(FIRST_GATHER)
    for key in gather.keys[:begun]:
        gather.step(key)
    lax.fori_loop(0, LATER, take_later, 0)
    own[1].start()
    steps = [(hops(key[1]), 0, i, gather, key) for i, key in enumerate(gather.keys[begun:])]
    steps += [(hops(key[1]) + 1.5, 1, i, along, key) for i, key in enumerate(along.keys)]
    for step in sorted(steps, key=lambda step: step[:3]):
        step[3].step(step[4])
    gather.finish()
    along.finish()
    for copy in own:
        copy.wait()


def gather_weights(perm, blocks, data):
    vmem = pl.BlockSpec(memory_space=pltpu.VMEM)
    return pl.pallas_call(
        gather_kernel,
        out_shape=jax.ShapeDtypeStruct((32, NSLOT + 1, BLOCK, BLOCK), jnp.bfloat16),
        in_specs=[pl.BlockSpec(memory_space=pltpu.SMEM), vmem, vmem],
        out_specs=pl.BlockSpec(memory_space=pltpu.HBM),
        scratch_shapes=[
            pltpu.VMEM((FIRST + 1, BLOCK, BLOCK), jnp.bfloat16),
            pltpu.VMEM((LATER, BLOCK, BLOCK), jnp.bfloat16),
            pltpu.SemaphoreType.DMA((2,)),
        ]
        + Gather.sems(FIRST_GATHER)
        + Gather.sems(LATER_PARTS),
        compiler_params=pltpu.CompilerParams(
            collective_id=1, has_side_effects=True, vmem_limit_bytes=60 * 2**20
        ),
    )(perm, blocks, data)


def inbox_axes(order, link):
    dim = "z" if link in "uw" else link
    axes = order[: order.index(dim)]
    return axes + "z" if dim == "z" else axes


def inbox_starts(parts, link):
    starts, total = [], 0
    for order, _, count in parts:
        starts.append(total)
        size = count
        for d in inbox_axes(order, link):
            size *= 4 if d == "z" else 2
        total += size
    return starts, total


class Scatter:
    def __init__(self, parts, acc, sib, boxes, send, recvs, where, ready, store, axes="xyz"):
        self.parts, self.acc, self.sib, self.where, self.axes = parts, acc, sib, where, axes
        links = self.links_of(axes)
        self.boxes = dict(zip(links, boxes))
        self.recvs = dict(zip(links, recvs))
        self.send, self.ready, self.store = send, ready, store
        self.keys = [
            k for k in reversed(route_keys(parts)) if "x" in axes or k[1][:2] == (0, 0)
        ]
        self.seen = []
        for _, off in self.keys:
            if off not in self.seen:
                self.seen.append(off)
        self.fresh = set()

    @staticmethod
    def links_of(axes):
        return ("xy" if "x" in axes else "") + ("uw" if "z" in axes else "")

    @classmethod
    def boxes_of(cls, parts, axes="xyz"):
        return [
            pltpu.VMEM((inbox_starts(parts, link)[1], 128, 128), jnp.bfloat16)
            for link in cls.links_of(axes)
        ]

    @classmethod
    def sems(cls, parts, axes="xyz"):
        return [pltpu.SemaphoreType.DMA((len(parts), 16))] + [
            pltpu.SemaphoreType.DMA((len(parts), 16)) for _ in cls.links_of(axes)
        ]

    def row(self, oz, oy, ox):
        return oz if self.axes == "z" else plane_of(oz, oy, ox)

    def inbox(self, link, part, oz, oy, ox):
        order, _, count = self.parts[part]
        index = 0
        for d in inbox_axes(order, link):
            index = index * (4 if d == "z" else 2) + {"z": oz, "y": oy, "x": ox}[d]
        return inbox_starts(self.parts, link)[0][part] + index * count

    def clear_ends(self):
        z = self.where[0]

        def clear(box):
            def body(i, carry):
                box[i] = jnp.zeros((128, 128), jnp.bfloat16)
                return carry

            lax.fori_loop(0, box.shape[0], body, 0)

        pl.when(z == 3)(lambda: clear(self.boxes["u"]))
        pl.when(z == 0)(lambda: clear(self.boxes["w"]))

    def hop(self, part, off):
        z, y, c, x = self.where
        oz, oy, ox, _ = owner_at(off, z, y, x)
        plane = plane_of(oz, oy, ox)
        order, first, count = self.parts[part]
        link, named = toward(order, off)
        return pltpu.make_async_remote_copy(
            src_ref=self.acc.at[self.row(oz, oy, ox), pl.ds(first, count)],
            dst_ref=self.boxes[named].at[pl.ds(self.inbox(named, part, oz, oy, ox), count)],
            send_sem=self.send.at[part, plane],
            recv_sem=self.recvs[named].at[part, plane],
            device_id=partner(link, *self.where),
            device_id_type=MESH,
        )

    def step(self, key):
        part, off = key
        z, y, c, x = self.where
        oz, oy, ox, cond = owner_at(off, z, y, x)
        plane = plane_of(oz, oy, ox)
        order, first, count = self.parts[part]
        new = off not in self.fresh
        self.fresh.add(off)
        row = self.row(oz, oy, ox)
        ends = off[:2] == (0, 0) if self.axes == "xy" else off == (0, 0, 0)

        def act():
            if new:
                self.ready(oz, oy, ox)
            sources = []
            for link in [k for k in onward(order, off) if k in self.boxes]:
                start = self.inbox(link, part, oz, oy, ox)
                sources.append((self.boxes[link], start))

                def arrive(link=link, start=start):
                    view = self.boxes[link].at[pl.ds(start, count)]
                    pltpu.make_async_remote_copy(
                        src_ref=view,
                        dst_ref=view,
                        send_sem=self.send.at[part, plane],
                        recv_sem=self.recvs[link].at[part, plane],
                        device_id=partner("c", *self.where),
                        device_id_type=MESH,
                    ).wait_recv()

                when(can(link, z), arrive)

            def add(i, carry):
                total = self.acc[row, first + i].astype(jnp.float32)
                if self.sib is not None:
                    total = total + self.sib[row, first + i].astype(jnp.float32)
                for box, start in sources:
                    total = total + box[start + i].astype(jnp.float32)
                if ends:
                    self.store(oz, first + i, total)
                else:
                    self.acc[row, first + i] = total.astype(jnp.bfloat16)
                return carry

            lax.fori_loop(0, count, add, 0)
            if not ends:
                self.hop(part, off).start()

        when(cond, act)

    def finish(self):
        z, y, c, x = self.where
        for part, off in self.keys:
            if off[:2] != (0, 0) or (off[2] != 0 and self.axes != "xy"):
                cond = owner_at(off, z, y, x)[3]
                when(cond, lambda part=part, off=off: self.hop(part, off).wait_send())


class SmallSums:
    def __init__(self, row, io, rows_out, io_out, mine, inbox, sems, where):
        self.row, self.io, self.rows, self.io_out = row, io, rows_out, io_out
        self.mine, self.inbox, self.where = mine, inbox, where
        self.gsend, self.grecv, self.osend, self.orecv, self.bsend, self.brecv, self.local = sems
        self.order = "zyx"
        self.sent = []

    @staticmethod
    def sems():
        dma = pltpu.SemaphoreType.DMA
        return [dma((4, 16)), dma((16,)), dma((6,)), dma((6,)), dma((1,)), dma((1,)), dma((1,))]

    def far(self):
        z, y, c, x = self.where
        return device(z + 2 - 4 * (z // 2), y, c, x)

    def peer(self, turn):
        z, y, c, x = self.where
        if turn == 3:
            return device(z + 1 - 2 * (z % 2), y, c, x)
        if turn == 4:
            return self.far()
        return partner("cxyyyc"[turn], *self.where)

    def swap(self, turn):
        c = self.where[2]
        if turn == 0:
            src, dst = self.io.at[1 - c], self.inbox.at[0]
        elif turn == 5:
            src, dst = self.mine.at[5], self.io_out.at[c]
        else:
            src, dst = self.mine.at[turn], self.inbox.at[turn]
        return pltpu.make_async_remote_copy(
            src_ref=src,
            dst_ref=dst,
            send_sem=self.osend.at[turn],
            recv_sem=self.orecv.at[turn],
            device_id=self.peer(turn),
            device_id_type=MESH,
        )

    def hop(self, link, src, plane):
        return pltpu.make_async_remote_copy(
            src_ref=src,
            dst_ref=self.rows.at[self.where[2], plane],
            send_sem=self.gsend.at["xyuw".index(link), plane],
            recv_sem=self.grecv.at[plane],
            device_id=partner(link, *self.where),
            device_id_type=MESH,
        )

    def bulk(self, core):
        return pltpu.make_async_remote_copy(
            src_ref=self.rows.at[core],
            dst_ref=self.rows.at[core],
            send_sem=self.bsend.at[0],
            recv_sem=self.brecv.at[0],
            device_id=partner("c", *self.where),
            device_id_type=MESH,
        )

    def row_step(self, off):
        z, y, c, x = self.where
        oz, oy, ox, cond = owner_at(off, z, y, x)
        plane = plane_of(oz, oy, ox)
        own = off == (0, 0, 0)
        src = self.row if own else self.rows.at[c, plane]
        links = onward(self.order, off)

        def act():
            if not own:
                self.hop("x", src, plane).wait_recv()
            for link in links:
                when(can(link, z), lambda link=link: self.hop(link, src, plane).start())

        when(cond, act)
        for link in links:
            self.sent.append(
                (both(cond, can(link, z)), lambda link=link: self.hop(link, src, plane))
            )

    def begin(self):
        z, y, c, x = self.where
        self.own = pltpu.make_async_copy(
            self.row, self.rows.at[c, plane_of(z, y, x)], self.local.at[0]
        )
        self.own.start()
        self.swap(0).start()
        self.row_step((0, 0, 0))

    def turn(self, turn):
        c = self.where[2]
        self.swap(turn).wait_recv()
        if turn < 5:
            before = self.io[c] if turn == 0 else self.mine[turn]
            self.mine[turn + 1] = before + self.inbox[turn]
            if turn == 4:
                self.io_out[c] = self.mine[5]
            self.swap(turn + 1).start()

    def tasks(self):
        todo = [
            lambda off=off: self.row_step(off)
            for off in sorted(offsets(), key=hops)
            if off != (0, 0, 0)
        ]
        for turn in range(6):
            todo.insert(5 * turn + 2, lambda turn=turn: self.turn(turn))

        def last():
            self.own.wait()
            self.bulk(self.where[2]).start()

        return todo + [last]

    def finish(self):
        c = self.where[2]
        self.bulk(1 - c).wait_recv()
        self.bulk(c).wait_send()
        for turn in range(6):
            self.swap(turn).wait_send()
        for cond, make in self.sent:
            when(cond, lambda make=make: make().wait_send())


def own_blocks(g_ref, owner, first, count):
    return g_ref.at[owner, pl.ds(first, count)]


class Halves:
    def __init__(self, g_ref, first, count, acc, sib, csend, crecv, local, where):
        self.g_ref, self.first, self.count, self.acc, self.sib = g_ref, first, count, acc, sib
        self.csend, self.crecv, self.local, self.where = csend, crecv, local, where

    def across(self, oz, oy, ox):
        plane = plane_of(oz, oy, ox)
        other = owner_of(oz, oy, 1 - self.where[2], ox)
        return pltpu.make_async_remote_copy(
            src_ref=own_blocks(self.g_ref, other, self.first, self.count),
            dst_ref=self.sib.at[plane],
            send_sem=self.csend.at[plane],
            recv_sem=self.crecv.at[plane],
            device_id=partner("c", *self.where),
            device_id_type=MESH,
        )

    def load(self, oz, oy, ox):
        plane = plane_of(oz, oy, ox)
        same = owner_of(oz, oy, self.where[2], ox)
        return pltpu.make_async_copy(
            own_blocks(self.g_ref, same, self.first, self.count),
            self.acc.at[plane],
            self.local.at[plane],
        )

    def begin(self, offs):
        z, y, c, x = self.where
        for off in offs:
            oz, oy, ox, cond = owner_at(off, z, y, x)

            def start(oz=oz, oy=oy, ox=ox):
                self.across(oz, oy, ox).start()
                self.load(oz, oy, ox).start()

            when(cond, start)

    def ready(self, oz, oy, ox):
        self.across(oz, oy, ox).wait_recv()
        self.load(oz, oy, ox).wait()

    def finish(self):
        for plane in range(16):
            self.across(plane // 4, (plane // 2) % 2, plane % 2).wait_send()


def scatter_kernel(rank_ref, g_ref, row_ref, io_ref, later_ref, out_ref, rows_out, io_out, *refs):
    acc, sib, along, total = refs[:4]
    boxes, refs = refs[4:8], refs[8:]
    later_boxes, refs = refs[:2], refs[2:]
    mine, inbox = refs[:2]
    csend, crecv, local, later_local, send = refs[2:7]
    recvs, later_send, later_recvs, small_sems = refs[7:11], refs[11], refs[12:14], refs[14:]
    where = place()
    small = SmallSums(row_ref, io_ref, rows_out, io_out, mine, inbox, small_sems, where)
    whole = pltpu.make_async_copy(later_ref, along, later_local.at[0])
    whole.start()
    greet(*where, far=(small.far(),))
    small.begin()
    halves = Halves(g_ref, 0, FIRST, acc, sib, csend, crecv, local, where)

    def store(oz, row, value):
        total[row] = value

    def store_later(oz, row, value):
        total[FIRST + row] = value

    scatter = Scatter(FIRST_SCATTER, acc, sib, boxes, send, recvs, where, halves.ready, store)
    later = Scatter(
        LATER_PARTS, along, None, later_boxes, later_send, later_recvs, where,
        lambda *place: None, store_later, "z",
    )
    halves.begin(scatter.seen)
    scatter.clear_ends()
    later.clear_ends()
    whole.wait()
    tasks = small.tasks()
    steps = [(-hops(key[1]), 1, i, scatter, key) for i, key in enumerate(scatter.keys)]
    steps += [(-hops(key[1]) - 1.5, 0, i, later, key) for i, key in enumerate(later.keys)]
    for i, step in enumerate(sorted(steps, key=lambda step: step[:3])):
        step[3].step(step[4])
        if i % 5 == 4 and tasks:
            tasks.pop(0)()
    for task in tasks:
        task()

    def put(i, carry):
        out_ref[i] = total[rank_ref[i]]
        return carry

    lax.fori_loop(0, NSLOT, put, 0)
    scatter.finish()
    later.finish()
    halves.finish()
    small.finish()


def scatter_grads(ranks, grads, row, io, later):
    vmem = pl.BlockSpec(memory_space=pltpu.VMEM)
    dma = pltpu.SemaphoreType.DMA
    held = pltpu.VMEM((16, FIRST, BLOCK, BLOCK), jnp.bfloat16)
    half = (SMALL_ROWS, D // 2)
    return pl.pallas_call(
        scatter_kernel,
        out_shape=(
            jax.ShapeDtypeStruct((NSLOT, BLOCK, BLOCK), jnp.float32),
            jax.ShapeDtypeStruct((2, 16) + row.shape, jnp.float32),
            jax.ShapeDtypeStruct((2,) + half, jnp.float32),
        ),
        in_specs=[
            pl.BlockSpec(memory_space=pltpu.SMEM),
            pl.BlockSpec(memory_space=pl.ANY),
            vmem,
            vmem,
            pl.BlockSpec(memory_space=pl.ANY),
        ],
        out_specs=(vmem, vmem, vmem),
        scratch_shapes=[
            held,
            held,
            pltpu.VMEM(later.shape, later.dtype),
            pltpu.VMEM((NSLOT, BLOCK, BLOCK), jnp.float32),
        ]
        + Scatter.boxes_of(FIRST_SCATTER)
        + Scatter.boxes_of(LATER_PARTS, "z")
        + [pltpu.VMEM((6,) + half, jnp.float32), pltpu.VMEM((6,) + half, jnp.float32)]
        + [dma((16,)), dma((16,)), dma((16,)), dma((1,))]
        + Scatter.sems(FIRST_SCATTER)
        + Scatter.sems(LATER_PARTS, "z")
        + SmallSums.sems(),
        compiler_params=pltpu.CompilerParams(
            collective_id=2, has_side_effects=True, vmem_limit_bytes=58 * 2**20
        ),
    )(ranks, grads, row, io, later)


def swapped(index):
    return lax.rem(index, 4) * 4 + lax.div(index, 4)


def clip_peers(frame, fn):
    count = lax.axis_size("frame")

    def body(step, carry):
        peer = lax.rem(frame + step, count)
        fn(step, peer, (swapped(peer), lax.axis_index("rep")))
        return carry

    lax.fori_loop(1, count, body, 0)


def greet_clip(frame, where):
    barrier = pltpu.get_barrier_semaphore()
    clip_peers(
        frame,
        lambda step, peer, dev: pl.semaphore_signal(
            barrier, inc=1, device_id=dev, device_id_type=MESH
        ),
    )
    pl.semaphore_signal(barrier, inc=1, device_id=partner("x", *where), device_id_type=MESH)
    pl.semaphore_wait(barrier, lax.axis_size("frame"))


class Exchange:
    def __init__(self, src, dst, send, recv, frame):
        self.src, self.dst, self.send, self.recv, self.frame = src, dst, send, recv, frame

    @staticmethod
    def sems():
        return [pltpu.SemaphoreType.DMA((16,)), pltpu.SemaphoreType.DMA((16,))]

    def copy(self, peer):
        return pltpu.make_async_remote_copy(
            src_ref=self.src.at[peer],
            dst_ref=self.dst.at[self.frame],
            send_sem=self.send.at[peer],
            recv_sem=self.recv.at[self.frame],
            device_id=(swapped(jnp.int32(peer)), lax.axis_index("rep")),
            device_id_type=MESH,
        )

    def own(self):
        self.dst[self.frame] = self.src[self.frame]

    def start_all(self):
        clip_peers(self.frame, lambda step, peer, dev: self.copy(peer).start())
        self.own()

    def start(self, peer):
        pl.when(self.frame != peer)(lambda: self.copy(peer).start())
        pl.when(self.frame == peer)(self.own)

    def arrived(self, peer):
        def wait():
            pltpu.make_async_remote_copy(
                src_ref=self.src.at[peer],
                dst_ref=self.dst.at[peer],
                send_sem=self.send.at[peer],
                recv_sem=self.recv.at[peer],
                device_id=(swapped(jnp.int32(peer)), lax.axis_index("rep")),
                device_id_type=MESH,
            ).wait_recv()

        pl.when(self.frame != peer)(wait)

    def all_arrived(self):
        for peer in range(16):
            self.arrived(peer)

    def finish(self):
        for peer in range(16):
            pl.when(self.frame != peer)(lambda peer=peer: self.copy(peer).wait_send())


def spread_evenly(steps, slots, weights):
    total, taken, acc, runs = sum(weights), 0, 0, []
    for slot in range(slots):
        acc += weights[slot]
        upto = round(len(steps) * acc / total)
        runs.append(steps[taken:upto])
        taken = upto
    return runs


def forward_kernel(
    parts_ref, blocks_in, mine_ref, blocks_ref, olt_ref, full_ref, lse_ref, scores, low, *sems
):
    where = place()
    frame = swapped(lax.axis_index("frame"))
    qkv = Exchange(parts_ref, mine_ref, sems[0], sems[1], frame)
    back = Exchange(low, olt_ref, sems[2], sems[3], frame)
    gather_sems = sems[4:]
    greet_clip(frame, where)
    qkv.start_all()
    gather = Gather(LATER_PARTS, None, blocks_ref, gather_sems, where, FIRST + 1, "xy")
    ready = [key for key in gather.keys if key[1][:2] == (0, 0)]
    steps = [key for key in gather.keys if key not in ready]
    for key in ready:
        gather.step(key)
    frames = mine_ref.shape[0]
    runs = spread_evenly(steps, frames, FORWARD_WEIGHTS)
    for t in range(frames):
        for key in runs[t]:
            gather.step(key)
        qkv.arrived(t)
        low[t] = attend_frame(t, mine_ref, scores, full_ref, lse_ref)
        back.start(t)
    gather.finish()
    qkv.finish()
    back.all_arrived()
    back.finish()


FORWARD_WEIGHTS = (20,) + (5,) * 15


def forward_exchange(parts, blocks):
    frames = 16
    vmem = pl.BlockSpec(memory_space=pltpu.VMEM)
    return pl.pallas_call(
        forward_kernel,
        in_specs=[vmem, pl.BlockSpec(memory_space=pltpu.HBM)],
        out_specs=[vmem, pl.BlockSpec(memory_space=pltpu.HBM), vmem, vmem, vmem],
        input_output_aliases={1: 1},
        out_shape=[
            jax.ShapeDtypeStruct((frames,) + parts.shape[1:], jnp.bfloat16),
            jax.ShapeDtypeStruct(blocks.shape, blocks.dtype),
            jax.ShapeDtypeStruct((HEADS, HEAD_DIM, TOK), jnp.bfloat16),
            jax.ShapeDtypeStruct((frames, HEAD_DIM, TOK), jnp.float32),
            jax.ShapeDtypeStruct((frames, 1, TOK), jnp.float32),
        ],
        scratch_shapes=[
            pltpu.VMEM((frames, TOK, TOK), jnp.float32),
            pltpu.VMEM((frames, HEAD_DIM, TOK), jnp.bfloat16),
        ]
        + Exchange.sems()
        + Exchange.sems()
        + Gather.sems(LATER_PARTS),
        compiler_params=pltpu.CompilerParams(
            collective_id=3, has_side_effects=True, vmem_limit_bytes=56 * 2**20
        ),
    )(parts, blocks)


def backward_kernel(
    heads_ref, mine_ref, full_ref, lse_ref, cos_ref, sin_ref, g_ref, drt_ref, later_ref, *refs
):
    do, grads, dk, dv, acc, sib = refs[:6]
    boxes, sems = refs[6:8], refs[8:]
    where = place()
    frame = swapped(lax.axis_index("frame"))
    inward = Exchange(heads_ref, do, sems[0], sems[1], frame)
    outward = Exchange(grads, drt_ref, sems[2], sems[3], frame)
    csend, crecv, local, send = sems[4:8]
    halves = Halves(g_ref, FIRST, LATER, acc, sib, csend, crecv, local, where)

    def store(oz, row, value):
        later_ref[oz, row] = value.astype(jnp.bfloat16)

    scatter = Scatter(
        LATER_PARTS, acc, sib, boxes, send, sems[8:10], where, halves.ready, store, "xy"
    )
    greet_clip(frame, where)
    inward.start_all()
    halves.begin(scatter.seen)
    dk[...] = jnp.zeros_like(dk)
    dv[...] = jnp.zeros_like(dv)
    frames = mine_ref.shape[0]
    runs = spread_evenly(scatter.keys, frames + 1, BACKWARD_WEIGHTS)
    for i, t in enumerate(reversed(range(frames))):
        for key in runs[i]:
            scatter.step(key)
        inward.arrived(t)
        parts = attend_frame_back(t, mine_ref, do, full_ref, lse_ref, cos_ref, sin_ref, dk, dv)
        for kind in range(3):
            grads[t, kind] = parts[kind]
        outward.start(t)
    for key in runs[frames]:
        scatter.step(key)
    scatter.finish()
    halves.finish()
    inward.finish()
    outward.all_arrived()
    outward.finish()


BACKWARD_WEIGHTS = (40,) + (5,) * 15 + (10,)


def backward_exchange(heads, mine, full, lse, cos, sin, grads):
    frames = mine.shape[0]
    vmem = pl.BlockSpec(memory_space=pltpu.VMEM)
    dma = pltpu.SemaphoreType.DMA
    held = pltpu.VMEM((16, LATER, BLOCK, BLOCK), jnp.bfloat16)
    return pl.pallas_call(
        backward_kernel,
        in_specs=[vmem] * 6 + [pl.BlockSpec(memory_space=pltpu.HBM)],
        out_specs=[vmem, vmem],
        out_shape=[
            jax.ShapeDtypeStruct((HEADS,) + mine.shape[1:], jnp.bfloat16),
            jax.ShapeDtypeStruct((4, LATER, BLOCK, BLOCK), jnp.bfloat16),
        ],
        scratch_shapes=[
            pltpu.VMEM((frames, HEAD_DIM, TOK), jnp.bfloat16),
            pltpu.VMEM((frames, 3, HEAD_DIM, TOK), jnp.bfloat16),
            pltpu.VMEM((frames, HEAD_DIM, TOK), jnp.float32),
            pltpu.VMEM((frames, HEAD_DIM, TOK), jnp.float32),
            held,
            held,
        ]
        + Scatter.boxes_of(LATER_PARTS, "xy")
        + Exchange.sems()
        + Exchange.sems()
        + [dma((16,)), dma((16,)), dma((16,))]
        + Scatter.sems(LATER_PARTS, "xy"),
        compiler_params=pltpu.CompilerParams(
            collective_id=4, has_side_effects=True, vmem_limit_bytes=56 * 2**20
        ),
    )(heads, mine, full, lse, cos, sin, grads)


def late_gather_kernel(blocks_in, blocks_ref, *sems):
    where = place()
    greet(*where)
    gather = Gather(LATER_PARTS, None, blocks_ref, sems, where, FIRST + 1, "xy")
    for key in gather.keys:
        gather.step(key)
    gather.finish()


def late_gather(blocks):
    hbm = pl.BlockSpec(memory_space=pltpu.HBM)
    return pl.pallas_call(
        late_gather_kernel,
        in_specs=[hbm],
        out_specs=hbm,
        out_shape=jax.ShapeDtypeStruct(blocks.shape, blocks.dtype),
        scratch_shapes=Gather.sems(LATER_PARTS),
        input_output_aliases={0: 0},
        compiler_params=pltpu.CompilerParams(
            collective_id=5, has_side_effects=True, vmem_limit_bytes=56 * 2**20
        ),
    )(blocks)


def late_scatter_kernel(g_ref, later_ref, *refs):
    acc, sib, boxes, sems = refs[0], refs[1], refs[2:4], refs[4:]
    where = place()
    halves = Halves(g_ref, FIRST, LATER, acc, sib, sems[0], sems[1], sems[2], where)

    def store(oz, row, value):
        later_ref[oz, row] = value.astype(jnp.bfloat16)

    scatter = Scatter(
        LATER_PARTS, acc, sib, boxes, sems[3], sems[4:6], where, halves.ready, store, "xy"
    )
    greet(*where)
    halves.begin(scatter.seen)
    for key in scatter.keys:
        scatter.step(key)
    scatter.finish()
    halves.finish()


def late_scatter(grads):
    dma = pltpu.SemaphoreType.DMA
    held = pltpu.VMEM((16, LATER, BLOCK, BLOCK), jnp.bfloat16)
    return pl.pallas_call(
        late_scatter_kernel,
        in_specs=[pl.BlockSpec(memory_space=pltpu.HBM)],
        out_specs=pl.BlockSpec(memory_space=pltpu.VMEM),
        out_shape=jax.ShapeDtypeStruct((4, LATER, BLOCK, BLOCK), jnp.bfloat16),
        scratch_shapes=[held, held]
        + Scatter.boxes_of(LATER_PARTS, "xy")
        + [dma((16,)), dma((16,)), dma((16,))]
        + Scatter.sems(LATER_PARTS, "xy"),
        compiler_params=pltpu.CompilerParams(
            collective_id=6, has_side_effects=True, vmem_limit_bytes=56 * 2**20
        ),
    )(grads)


TILE = 512
LIMIT = pltpu.CompilerParams(vmem_limit_bytes=60 * 2**20)


def dotg(left, right, left_dim, right_dim):
    return lax.dot_general(
        left, right, (((left_dim,), (right_dim,)), ((), ())), preferred_element_type=jnp.float32
    )


def block_of(held, row, col):
    return held.at[
        pl.ds(pl.multiple_of(row * BLOCK, BLOCK), BLOCK),
        pl.ds(pl.multiple_of(col * BLOCK, BLOCK), BLOCK),
    ]


def move_tile(places, blocks, held, sem, start, across, row, rows, col, cols, outward=False):
    for r in range(rows):
        for c in range(cols):
            slot = blocks.at[places[start + (row + r) * across + col + c]]
            here = block_of(held, row + r, col + c)
            src, dst = (here, slot) if outward else (slot, here)
            pltpu.make_async_copy(src, dst, sem).start()


def settled(view, sem):
    pltpu.make_async_copy(view, view, sem).wait()


def column_sum(values):
    return jnp.sum(values, axis=0, keepdims=True)


def project_kernel(
    source, places, blocks, table_ref, io_ref, cos_ref, sin_ref,
    h0_ref, at_ref, out_ref, mod_ref, target_ref, xt_ref, scalars_ref,
    held, a_ref, data, flags, sems, small_sems,
):
    across = 3 * D // BLOCK
    per = TILE // BLOCK
    tiles = 3 * D // TILE
    mine = pltpu.make_async_copy(blocks.at[source[0] * (NSLOT + 1) + DATA], data, small_sems.at[0])
    mine.start()

    def flag(owner):
        return pltpu.make_async_copy(
            blocks.at[owner * (NSLOT + 1) + DATA, pl.ds(96, 16)], flags.at[owner], small_sems.at[1]
        )

    for owner in range(32):
        flag(owner).start()
    for j in range(tiles):
        move_tile(places, blocks, held, sems.at[j], 0, across, 0, D // BLOCK, j * per, per)
    mine.wait()
    settled(flags, small_sems.at[1])
    xt = data[0:32]
    xt_ref[...] = jnp.concatenate([xt.reshape(PIN, 2, BLOCK)[:, i] for i in range(2)], axis=1)
    noise = data[32:64].astype(jnp.float32) + data[64:96].astype(jnp.float32)
    target_ref[...] = jnp.concatenate([noise.reshape(PIN, 2, BLOCK)[:, i] for i in range(2)], axis=1)
    noised = data[96:97].astype(jnp.float32)
    level = data[112:113].astype(jnp.float32)
    total = flags[0].astype(jnp.float32)
    for owner in range(1, 32):
        total = total + flags[owner].astype(jnp.float32)
    total = jnp.maximum(total[0:1], 1.0)
    scalars_ref[0:1] = noised
    scalars_ref[1:2] = 1.0 / (total * (TOK * PIN))
    scalars_ref[2:3] = total
    scalars_ref[3:4] = level
    scalars_ref[4:8] = jnp.zeros((4, BLOCK), jnp.float32)
    rows = lax.broadcasted_iota(jnp.int32, (LEVELS, D), 0).astype(jnp.float32)
    picked = rows == level[0:1, 0:1]
    for i in range(8):
        mod_ref[i : i + 1] = column_sum(jnp.where(picked, table_ref[:, i * D : (i + 1) * D], 0.0))
    start = dotg(xt_ref[...], io_ref[0:PIN].astype(jnp.bfloat16), 0, 0) + io_ref[2 * PIN :]
    h0_ref[...] = start
    hat, _ = layer_norm(start)
    normed = hat * (1 + mod_ref[1:2]) + mod_ref[0:1]
    a_ref[...] = normed.astype(jnp.bfloat16)
    at_ref[...] = normed.T.astype(jnp.bfloat16)
    heads = TILE // HEAD_DIM
    half = HEAD_DIM // 2
    frame = swapped(lax.axis_index("frame"))
    c, s = cos_ref[frame], sin_ref[frame]
    for j in range(tiles):
        settled(held.at[:, pl.ds(j * TILE, TILE)], sems.at[j])
        r = matmul(a_ref[...], held[:, j * TILE : (j + 1) * TILE]).T
        kind, head = j // (D // TILE), j % (D // TILE) * heads
        for i in range(heads):
            own = r[i * HEAD_DIM : (i + 1) * HEAD_DIM]
            if kind < 2:
                first, second = own[:half], own[half:]
                own = jnp.concatenate(
                    [first * c - second * s, first * s + second * c], axis=0
                )
            out_ref[head + i, kind] = own.astype(jnp.bfloat16)


def project(source, places, blocks, table, io, cos, sin):
    vmem, smem = pl.BlockSpec(memory_space=pltpu.VMEM), pl.BlockSpec(memory_space=pltpu.SMEM)
    f32, bf16 = jnp.float32, jnp.bfloat16
    return pl.pallas_call(
        project_kernel,
        in_specs=[smem, smem, pl.BlockSpec(memory_space=pltpu.HBM)] + [vmem] * 4,
        out_specs=[vmem] * 7,
        out_shape=[
            jax.ShapeDtypeStruct((TOK, D), f32),
            jax.ShapeDtypeStruct((D, TOK), bf16),
            jax.ShapeDtypeStruct((HEADS, 3, HEAD_DIM, TOK), bf16),
            jax.ShapeDtypeStruct((8, D), f32),
            jax.ShapeDtypeStruct((PIN, TOK), f32),
            jax.ShapeDtypeStruct((PIN, TOK), bf16),
            jax.ShapeDtypeStruct((8, BLOCK), f32),
        ],
        scratch_shapes=[
            pltpu.VMEM((D, 3 * D), bf16),
            pltpu.VMEM((TOK, D), bf16),
            pltpu.VMEM((BLOCK, BLOCK), bf16),
            pltpu.VMEM((32, 16, BLOCK), bf16),
            pltpu.SemaphoreType.DMA((3 * D // TILE,)),
            pltpu.SemaphoreType.DMA((2,)),
        ],
        compiler_params=LIMIT,
    )(source, places, blocks, table, io, cos, sin)


GELU_A = math.sqrt(2.0 / math.pi)
GELU_B = 0.044715


def middle_kernel(
    places, slots, blocks, olt_ref, h0_ref, mod_ref, io_ref, target_ref, scalars_ref,
    dot_ref, grads_ref, dh1_ref, dhead_ref, dmod_ref, loss_ref,
    wo, wup, wdown, gout, gup, gdown, slope, act, bt, dz_ref, db_ref, h1_ref, y_ref, z_ref, sems, out_sems,
):
    starts, _ = matrix_starts()
    per = TILE // BLOCK
    wide = D // BLOCK
    up_tiles = FFN // TILE
    up_across = FFN // BLOCK

    def fetch_up(j):
        move_tile(places, blocks, wup, sems.at[1 + j], starts[2], up_across, 0, wide, j * per, per)

    def fetch_down(j):
        move_tile(places, blocks, wdown, sems.at[9 + j], starts[3], wide, j * per, per, 0, wide)

    move_tile(places, blocks, wo, sems.at[0], starts[1], wide, 0, wide, 0, wide)
    fetch_up(0)
    fetch_up(1)
    attended = olt_ref[...].astype(jnp.float32).T.astype(jnp.bfloat16)
    settled(wo, sems.at[0])
    y = matmul(attended, wo[...])
    y_ref[...] = y
    h1 = h0_ref[...] + mod_ref[2:3] * y
    h1_ref[...] = h1
    hat_two, _ = layer_norm(h1)
    b32 = hat_two * (1 + mod_ref[4:5]) + mod_ref[3:4]
    bt[...] = b32.T.astype(jnp.bfloat16)
    b = b32.astype(jnp.bfloat16)
    dz_ref[...] = b

    def rise(j, carry):
        col = pl.multiple_of(j * TILE, TILE)
        settled(wup.at[:, pl.ds(col, TILE)], sems.at[1 + j])
        fetch_down(j)
        pl.when(j < up_tiles - 2)(lambda: fetch_up(j + 2))
        u = matmul(dz_ref[...], wup[:, pl.ds(col, TILE)])
        square = u * u
        t = jnp.tanh(GELU_A * (u + GELU_B * (square * u)))
        cdf = 0.5 * (1.0 + t)
        act[:, pl.ds(col, TILE)] = (u * cdf).astype(jnp.bfloat16)
        slope[:, pl.ds(col, TILE)] = cdf + (0.5 * GELU_A) * u * (1.0 - t * t) * (
            1.0 + (3.0 * GELU_B) * square
        )
        return carry

    lax.fori_loop(0, up_tiles, rise, 0)
    for j in range(up_tiles):
        settled(wdown.at[pl.ds(j * TILE, TILE)], sems.at[9 + j])

    def fall(j, carry):
        col = pl.multiple_of(j * 256, 256)
        z_ref[:, pl.ds(col, 256)] = matmul(act[...], wdown[:, pl.ds(col, 256)])
        return carry

    lax.fori_loop(0, D // 256, fall, 0)
    z = z_ref[...]
    h2 = h1_ref[...] + mod_ref[5:6] * z
    hat_three, inv_three = layer_norm(h2)
    c = (hat_three * (1 + mod_ref[7:8]) + mod_ref[6:7]).astype(jnp.bfloat16)
    noised, inv_scale = scalars_ref[0:1, 0:1], scalars_ref[1:2, 0:1]
    head = io_ref[PIN : 2 * PIN].astype(jnp.bfloat16)
    difference = dotg(head, c, 1, 1) - target_ref[...]
    loss_ref[...] = jnp.full((1, BLOCK), 1.0, jnp.float32) * (
        jnp.sum(jnp.sum(difference * difference, axis=0, keepdims=True), axis=1, keepdims=True)
        * (noised * inv_scale)
    )
    dpred = (2.0 * inv_scale * noised * difference).astype(jnp.bfloat16)
    dhead_ref[...] = matmul(dpred, c)
    dc = dotg(dpred, head, 0, 0)
    dmod_ref[6:7] = column_sum(dc)
    dmod_ref[7:8] = column_sum(dc * hat_three)
    dh2 = norm_back(dc * (1 + mod_ref[7:8]), hat_three, inv_three)
    dmod_ref[5:6] = column_sum(dh2 * z)
    dz_ref[...] = (dh2 * mod_ref[5:6]).astype(jnp.bfloat16)
    z_ref[...] = dh2
    db_ref[...] = jnp.zeros_like(db_ref)

    def back(j, carry):
        col = pl.multiple_of(j * TILE, TILE)
        du = (
            slope[:, pl.ds(col, TILE)] * dotg(dz_ref[...], wdown[pl.ds(col, TILE)], 1, 1)
        ).astype(jnp.bfloat16)
        gdown[pl.ds(col, TILE)] = dotg(act[:, pl.ds(col, TILE)], dz_ref[...], 0, 0).astype(
            jnp.bfloat16
        )
        move_tile(
            slots, grads_ref, gdown, out_sems.at[0], starts[3], wide, j * per, per, 0, wide, True
        )
        gup[:, pl.ds(col, TILE)] = matmul(bt[...], du).astype(jnp.bfloat16)
        move_tile(
            slots, grads_ref, gup, out_sems.at[1], starts[2], up_across, 0, wide, j * per, per, True
        )
        db_ref[...] += dotg(du, wup[:, pl.ds(col, TILE)], 1, 1)
        return carry

    lax.fori_loop(0, up_tiles, back, 0)
    hat_two, inv_two = layer_norm(h1_ref[...])
    db = db_ref[...]
    dmod_ref[3:4] = column_sum(db)
    dmod_ref[4:5] = column_sum(db * hat_two)
    dh1 = z_ref[...] + norm_back(db * (1 + mod_ref[4:5]), hat_two, inv_two)
    dh1_ref[...] = dh1
    dmod_ref[2:3] = column_sum(dh1 * y_ref[...])
    dmod_ref[0:2] = jnp.zeros((2, D), jnp.float32)
    dz_ref[...] = (dh1 * mod_ref[2:3]).astype(jnp.bfloat16)
    gout[...] = matmul(olt_ref[...], dz_ref[...]).astype(jnp.bfloat16)
    move_tile(slots, grads_ref, gout, out_sems.at[2], starts[1], wide, 0, wide, 0, wide, True)
    for j in range(D // TILE):
        rows = pl.ds(j * TILE, TILE)
        dot_ref[rows] = dotg(wo[rows], dz_ref[...], 1, 1).astype(jnp.bfloat16)
    settled(gdown, out_sems.at[0])
    settled(gup, out_sems.at[1])
    settled(gout, out_sems.at[2])


def middle(places, slots, blocks, olt, h0, mod, io, target, scalars):
    vmem, smem = pl.BlockSpec(memory_space=pltpu.VMEM), pl.BlockSpec(memory_space=pltpu.SMEM)
    hbm = pl.BlockSpec(memory_space=pltpu.HBM)
    f32, bf16 = jnp.float32, jnp.bfloat16
    up, down, square = pltpu.VMEM((D, FFN), bf16), pltpu.VMEM((FFN, D), bf16), pltpu.VMEM((D, D), bf16)
    rows = pltpu.VMEM((TOK, D), f32)
    return pl.pallas_call(
        middle_kernel,
        in_specs=[smem, smem, hbm] + [vmem] * 6,
        out_specs=[vmem, hbm] + [vmem] * 4,
        out_shape=[
            jax.ShapeDtypeStruct((D, TOK), bf16),
            jax.ShapeDtypeStruct((32 * NSLOT, BLOCK, BLOCK), bf16),
            jax.ShapeDtypeStruct((TOK, D), f32),
            jax.ShapeDtypeStruct((PIN, D), f32),
            jax.ShapeDtypeStruct((8, D), f32),
            jax.ShapeDtypeStruct((1, BLOCK), f32),
        ],
        scratch_shapes=[square, up, down, square, up, down]
        + [
            pltpu.VMEM((TOK, FFN), f32),
            pltpu.VMEM((TOK, FFN), bf16),
            pltpu.VMEM((D, TOK), bf16),
            pltpu.VMEM((TOK, D), bf16),
            rows,
            rows,
            rows,
            rows,
            pltpu.SemaphoreType.DMA((17,)),
            pltpu.SemaphoreType.DMA((3,)),
        ],
        compiler_params=LIMIT,
    )(places, slots, blocks, olt, h0, mod, io, target, scalars)


def final_kernel(
    places, slots, blocks, drt_ref, at_ref, h0_ref, mod_ref, dh1_ref, xt_ref, dmod_in, scalars_ref, loss_ref,
    dhead_ref, grads_in, grads_ref, row_ref, io_ref, held, gqkv, flat, sems, out_sem,
):
    across = 3 * D // BLOCK
    per = TILE // BLOCK
    for j in range(2):
        move_tile(places, blocks, held, sems.at[j], 0, across, j * per, per, 0, across)
    for kind in range(3):
        for head in range(HEADS):
            row = kind * D + head * HEAD_DIM
            flat[row : row + HEAD_DIM] = drt_ref[head, kind]
    for j in range(3 * D // TILE):
        cols = slice(j * TILE, (j + 1) * TILE)
        gqkv[:, cols] = dotg(at_ref[...], flat[cols], 1, 1).astype(jnp.bfloat16)
        move_tile(slots, grads_ref, gqkv, out_sem.at[0], 0, across, 0, D // BLOCK, j * per, per, True)
    for j in range(2):
        settled(held.at[pl.ds(j * TILE, TILE)], sems.at[j])
    da = matmul(held[...], flat[...]).T
    hat, inverse = layer_norm(h0_ref[...])

    def put_row(i, values):
        for k in range(D // BLOCK):
            row_ref[i * (D // BLOCK) + k : i * (D // BLOCK) + k + 1] = values[
                :, k * BLOCK : (k + 1) * BLOCK
            ]

    put_row(0, column_sum(da))
    put_row(1, column_sum(da * hat))
    for i in range(2, 8):
        put_row(i, dmod_in[i : i + 1])
    row_ref[64:68] = jnp.broadcast_to(scalars_ref[3:4], (4, BLOCK))
    row_ref[68:72] = jnp.broadcast_to(loss_ref[...], (4, BLOCK))
    dh0 = (dh1_ref[...] + norm_back(da * (1 + mod_ref[1:2]), hat, inverse)).astype(jnp.bfloat16)
    dembed = matmul(xt_ref[...], dh0)
    dbias = column_sum(dh0.astype(jnp.float32))
    for i in range(2):
        cols = slice(i * D // 2, (i + 1) * D // 2)
        io_ref[i, 0:PIN] = dembed[:, cols]
        io_ref[i, PIN : 2 * PIN] = dhead_ref[:, cols]
        io_ref[i, 2 * PIN :] = jnp.zeros((SMALL_ROWS - 2 * PIN, D // 2), jnp.float32)
        io_ref[i, 2 * PIN : 2 * PIN + 1] = dbias[:, cols]
    settled(gqkv, out_sem.at[0])


def final(places, slots, blocks, drt, at, h0, mod, dh1, xt, dmod, scalars, loss, dhead, grads):
    vmem, smem = pl.BlockSpec(memory_space=pltpu.VMEM), pl.BlockSpec(memory_space=pltpu.SMEM)
    hbm = pl.BlockSpec(memory_space=pltpu.HBM)
    f32, bf16 = jnp.float32, jnp.bfloat16
    return pl.pallas_call(
        final_kernel,
        in_specs=[smem, smem, hbm] + [vmem] * 10 + [hbm],
        out_specs=[hbm] + [vmem] * 2,
        out_shape=[
            jax.ShapeDtypeStruct(grads.shape, grads.dtype),
            jax.ShapeDtypeStruct((8 * D // BLOCK + 8, BLOCK), f32),
            jax.ShapeDtypeStruct((2, SMALL_ROWS, D // 2), f32),
        ],
        scratch_shapes=[
            pltpu.VMEM((D, 3 * D), bf16),
            pltpu.VMEM((D, 3 * D), bf16),
            pltpu.VMEM((3 * D, TOK), bf16),
            pltpu.SemaphoreType.DMA((2,)),
            pltpu.SemaphoreType.DMA((1,)),
        ],
        input_output_aliases={13: 0},
        compiler_params=LIMIT,
    )(places, slots, blocks, drt, at, h0, mod, dh1, xt, dmod, scalars, loss, dhead, grads)


def top_dot(left, right, left_dim, right_dim):
    return lax.dot_general(
        left,
        right,
        (((left_dim,), (right_dim,)), ((), ())),
        precision=TOP_PRECISION,
        preferred_element_type=jnp.float32,
    )


SHAMPOO_BLOCKS = 4


def halves_of(values):
    high = values.astype(jnp.bfloat16)
    return high, (values - high.astype(jnp.float32)).astype(jnp.bfloat16)


def fine_dot(left, right):
    (lh, ll), (rh, rl) = left, right
    return (
        matmul(jnp.concatenate([lh, ll], axis=1), jnp.concatenate([rh, rh], axis=0))
        + matmul(lh, rl)
    )


def shampoo_kernel(
    g_ref, w_ref, ema_ref, left_ref, right_ref, root_left, root_right,
    grad_out, w_out, left_out, right_out, ema_out,
):
    limit = CLIP_NORM * BLOCK * NPARAMS ** (-0.5)

    def whole(values):
        return jnp.sum(jnp.sum(values, axis=0, keepdims=True), axis=1, keepdims=True)

    for i in range(SHAMPOO_BLOCKS):
        g = g_ref[i]
        g = g * (limit / jnp.maximum(jnp.sqrt(whole(g * g)), limit))
        grad_out[i] = g
        mine, turned = halves_of(g), halves_of(g.T)
        left_out[i] = STAT_BETA * left_ref[i] + (1 - STAT_BETA) * fine_dot(mine, turned)
        right_out[i] = STAT_BETA * right_ref[i] + (1 - STAT_BETA) * fine_dot(turned, mine)
        p = fine_dot(halves_of(root_left[i]), mine)
        p = fine_dot(halves_of(p), halves_of(root_right[i]))
        p = p * lax.rsqrt(whole(p * p) * (1.0 / (BLOCK * BLOCK)) + 1e-06)
        w = w_ref[i]
        w = w - SHAMPOO_RATE * (p + DECAY_RATE * w)
        w_out[i] = w
        ema_out[i] = EMA_DECAY * ema_ref[i] + (1 - EMA_DECAY) * w


def shampoo_blocks(*arrays):
    spec = pl.BlockSpec((SHAMPOO_BLOCKS, BLOCK, BLOCK), lambda i: (i, 0, 0))
    shape = jax.ShapeDtypeStruct(arrays[0].shape, jnp.float32)
    return pl.pallas_call(
        shampoo_kernel,
        grid=(arrays[0].shape[0] // SHAMPOO_BLOCKS,),
        in_specs=[spec] * 7,
        out_specs=[spec] * 5,
        out_shape=[shape] * 5,
        compiler_params=LIMIT,
    )(*arrays)


def adam_kernel(
    fade, rows_in, gio_in, scalars_ref, table_in, mom_in, var_in, ema_in, io, io_mom, io_var, io_ema,
    table_out, mom_out, var_out, ema_out, io_out, io_mom_out, io_var_out, io_ema_out, norm_out, loss_out, count_out,
    grad, flat, rows_ref, gio_ref, table, mom, var, ema, sems,
):
    loads = [
        pltpu.make_async_copy(src, dst, sems.at[i])
        for i, (src, dst) in enumerate(
            (
                (rows_in, rows_ref),
                (gio_in, gio_ref),
                (table_in, table),
                (mom_in, mom),
                (var_in, var),
                (ema_in, ema),
            )
        )
    ]
    for load in loads:
        load.start()
    for load in loads[:2]:
        load.wait()
    level = rows_ref[:, 64, :]
    frames = level.shape[0]
    picks = (
        level[:, 0:1] == lax.broadcasted_iota(jnp.int32, (frames, LEVELS), 1).astype(jnp.float32)
    ).astype(jnp.float32)
    for i in range(8 * D // BLOCK):
        flat[:, i * BLOCK : (i + 1) * BLOCK] = rows_ref[:, i, :]
    square = jnp.zeros((LEVELS, D), jnp.float32)
    for i in range(8):
        part = top_dot(picks, flat[:, i * D : (i + 1) * D], 0, 0)
        grad[:, i * D : (i + 1) * D] = part
        square = square + part * part
    gio = jnp.concatenate([gio_ref[0, 0 : 2 * PIN + 1], gio_ref[1, 0 : 2 * PIN + 1]], axis=1)

    def whole(values):
        return jnp.sum(jnp.sum(values, axis=0, keepdims=True), axis=1, keepdims=True)

    norm = jnp.sqrt(whole(square) + whole(gio * gio))
    factor = CLIP_NORM / jnp.maximum(norm, CLIP_NORM)
    count = scalars_ref[2:3, 0:1]
    norm_out[...] = norm
    loss_out[...] = jnp.sum(rows_ref[:, 68, :], axis=0, keepdims=True)[:, 0:1] * count
    count_out[...] = count
    fade_one, fade_two = fade[0], fade[1]

    def update(g, weight, first, second, average):
        new_first = BETA_ONE * first + (1 - BETA_ONE) * g
        new_second = BETA_TWO * second + (1 - BETA_TWO) * g * g
        new = weight - ADAM_RATE * (
            (new_first / fade_one) / (jnp.sqrt(new_second / fade_two) + ADAM_EPS)
            + DECAY_RATE * weight
        )
        return new, new_first, new_second, EMA_DECAY * average + (1 - EMA_DECAY) * new

    outs = (io_out, io_mom_out, io_var_out, io_ema_out)
    for ref, value in zip(outs, update(gio * factor, io[...], io_mom[...], io_var[...], io_ema[...])):
        ref[...] = value
    outs = (table_out, mom_out, var_out, ema_out)
    for load in loads[2:]:
        load.wait()

    def one(i, carry):
        cols = pl.ds(pl.multiple_of(i * D, D), D)
        values = update(grad[:, cols] * factor, table[:, cols], mom[:, cols], var[:, cols], ema[:, cols])
        for ref, value in zip(outs, values):
            ref[:, cols] = value
        return carry

    lax.fori_loop(0, 8, one, 0)


def adam(fade, rows, gio, scalars, *arrays):
    vmem, smem = pl.BlockSpec(memory_space=pltpu.VMEM), pl.BlockSpec(memory_space=pltpu.SMEM)
    return pl.pallas_call(
        adam_kernel,
        in_specs=[smem]
        + [pl.BlockSpec(memory_space=pl.ANY)] * 2
        + [vmem]
        + [pl.BlockSpec(memory_space=pl.ANY)] * 4
        + [vmem] * 4,
        out_specs=[vmem] * 11,
        out_shape=[jax.ShapeDtypeStruct(a.shape, jnp.float32) for a in arrays]
        + [jax.ShapeDtypeStruct((1, 1), jnp.float32)] * 3,
        scratch_shapes=[
            pltpu.VMEM((LEVELS, 8 * D), jnp.float32),
            pltpu.VMEM((rows.shape[0], 8 * D), jnp.float32),
            pltpu.VMEM(rows.shape, jnp.float32),
            pltpu.VMEM(gio.shape, jnp.float32),
        ]
        + [pltpu.VMEM((LEVELS, 8 * D), jnp.float32)] * 4
        + [pltpu.SemaphoreType.DMA((6,))],
        compiler_params=pltpu.CompilerParams(vmem_limit_bytes=56 * 2**20),
    )(fade, rows, gio, scalars, *arrays)


def matrix_starts():
    starts, total = [], 0
    for rows_in, cols_in in matrix_shapes():
        starts.append(total)
        total += rows_in // BLOCK * (cols_in // BLOCK)
    return starts, total


def block_places(block_slot):
    owned = block_slot.reshape(32, -1)
    ranks = jnp.sum((owned[:, None, :] < owned[:, :, None]).astype(jnp.int32), axis=2)
    mine = lax.axis_index("frame") * 2 + lax.axis_index("rep")
    own_ranks = lax.dynamic_index_in_dim(ranks, mine, 0, keepdims=False)
    counting = jnp.arange(NSLOT, dtype=jnp.int32)
    perm = jnp.sum(jnp.where(own_ranks[None, :] == counting[:, None], counting[None, :], 0), axis=1)
    owners = jnp.arange(32, dtype=jnp.int32)[:, None]
    gathered = owners * (NSLOT + 1) + ranks + (ranks >= FIRST).astype(jnp.int32)
    scattered = owners * NSLOT + ranks
    natural = jnp.arange(block_slot.shape[0], dtype=jnp.int32)
    same = block_slot[None, :] == natural[:, None]
    places = jnp.sum(jnp.where(same, gathered.reshape(1, -1), 0), axis=1)
    slots = jnp.sum(jnp.where(same, scattered.reshape(1, -1), 0), axis=1)
    early = jnp.sum((owned < matrix_starts()[0][1]).astype(jnp.int32), axis=1)
    return own_ranks, perm, places, slots, jnp.max(early) > FIRST


def rope_columns(frames):
    pairs = HEAD_DIM // 2
    time_pairs = pairs // 4
    row_pairs = (pairs - time_pairs) // 2
    column_pairs = pairs - time_pairs - row_pairs
    token = np.arange(GRID * GRID)
    groups = (
        (time_pairs, np.arange(frames)[:, None, None]),
        (row_pairs, (token // GRID)[None, None, :]),
        (column_pairs, (token % GRID)[None, None, :]),
    )
    angles = [
        np.broadcast_to(
            pos * (ROPE_BASE ** (-np.arange(n) / n))[None, :, None], (frames, n, GRID * GRID)
        )
        for n, pos in groups
    ]
    angles = np.concatenate(angles, axis=1)
    return np.cos(angles).astype(np.float32), np.sin(angles).astype(np.float32)


def on_grid(
    clean,
    noise,
    levels,
    flags,
    frame_map,
    block_slot,
    step_count,
    mat_weight,
    mat_ema,
    stat_left,
    stat_right,
    root_left,
    root_right,
    mod_table,
    mod_mom,
    mod_var,
    mod_ema,
    io_weight,
    io_mom,
    io_var,
    io_ema,
):
    tok_frame = GRID * GRID
    my_time, my_clip = swapped(lax.axis_index("frame")), lax.axis_index("rep")
    level_here = levels[0, 0] * (1 - flags[0, 0])
    noised_here = (1 - flags[0, 0]).astype(jnp.float32)
    fraction = level_here.astype(jnp.float32) / LEVELS
    frames_in = (
        jnp.cos(0.5 * jnp.pi * fraction) * clean[0, 0] + jnp.sin(0.5 * jnp.pi * fraction) * noise[0, 0]
    )
    noise_high = noise[0, 0].astype(jnp.bfloat16)
    noise_low = (noise[0, 0] - noise_high.astype(jnp.float32)).astype(jnp.bfloat16)
    data = jnp.concatenate(
        [
            frames_in.astype(jnp.bfloat16).reshape(-1, BLOCK),
            noise_high.reshape(-1, BLOCK),
            noise_low.reshape(-1, BLOCK),
            jnp.full((16, BLOCK), noised_here.astype(jnp.bfloat16)),
            jnp.full((16, BLOCK), level_here.astype(jnp.bfloat16)),
        ]
    )
    ranks, perm, places, slots, spills = block_places(block_slot)
    clip_map = lax.dynamic_index_in_dim(frame_map, my_clip, 0, keepdims=False)
    my_slot = jnp.sum(
        jnp.where(clip_map == my_time, jnp.arange(clip_map.shape[0], dtype=jnp.int32), 0)
    )
    source = (my_slot * 2 + my_clip).reshape(1)
    cosine, sine = rope_columns(frame_map.shape[1])
    gathered = gather_weights(perm, mat_weight, data)
    gathered = lax.cond(spills, lambda: late_gather(gathered), lambda: gathered)
    start, normed, parts, modulation, targets, inputs, scalars = project(
        source,
        places,
        gathered.reshape(-1, BLOCK, BLOCK),
        mod_table,
        io_weight,
        cosine,
        sine,
    )
    mine, gathered, attended, full, lse = forward_exchange(parts, gathered)
    blocks = gathered.reshape(-1, BLOCK, BLOCK)
    grad_heads, grad_blocks, grad_middle, grad_head, grad_mod, loss_part = middle(
        places,
        slots,
        blocks,
        attended.reshape(D, tok_frame),
        start,
        modulation,
        io_weight,
        targets,
        scalars,
    )
    grad_proj, later = backward_exchange(
        grad_heads.reshape(HEADS, HEAD_DIM, tok_frame),
        mine,
        full,
        lse,
        cosine,
        sine,
        grad_blocks.reshape(32, NSLOT, BLOCK, BLOCK),
    )
    grad_blocks, row, grad_io = final(
        places,
        slots,
        blocks,
        grad_proj,
        normed,
        start,
        modulation,
        grad_middle,
        inputs,
        grad_mod,
        scalars,
        loss_part,
        grad_head,
        grad_blocks,
    )
    grad_blocks = grad_blocks.reshape(32, NSLOT, BLOCK, BLOCK)
    later = lax.cond(spills, lambda: late_scatter(grad_blocks), lambda: later)
    owned, rows, grad_io = scatter_grads(ranks, grad_blocks, row, grad_io, later)
    step = step_count[0].astype(jnp.float32)
    new_small = adam(
        jnp.stack([1 - BETA_ONE**step, 1 - BETA_TWO**step]),
        rows.reshape(32, -1, BLOCK),
        grad_io,
        scalars,
        mod_table,
        mod_mom,
        mod_var,
        mod_ema,
        io_weight,
        io_mom,
        io_var,
        io_ema,
    )
    new_mod, new_io = new_small[:4], new_small[4:8]
    grad_norm, loss_sum, noised_total = (value.reshape(()) for value in new_small[8:])
    mat_grad, new_mat_weight, new_stat_left, new_stat_right, new_mat_ema = shampoo_blocks(
        owned, mat_weight, mat_ema, stat_left, stat_right, root_left, root_right
    )
    return (
        loss_sum,
        noised_total,
        grad_norm,
        mat_grad,
        new_mat_weight,
        new_stat_left,
        new_stat_right,
        new_mat_ema,
        new_mod[0],
        new_mod[1],
        new_mod[2],
        new_mod[3],
        new_io[0],
        new_io[1],
        new_io[2],
        new_io[3],
    )


def solution(mesh):
    tuned = dict(mesh.shape) == {"frame": 16, "rep": 2}
    body = on_grid if tuned else on_device
    in_specs = (
        P("rep", "frame", None, None),
        P("rep", "frame", None, None),
        P("rep", "frame"),
        P("rep", "frame"),
        P(),
        P(),
        P(),
        P(("frame", "rep"), None, None),
        P(("frame", "rep"), None, None),
        P(("frame", "rep"), None, None),
        P(("frame", "rep"), None, None),
        P(("frame", "rep"), None, None),
        P(("frame", "rep"), None, None),
        P(),
        P(),
        P(),
        P(),
        P(),
        P(),
        P(),
        P(),
    )
    out_specs = (
        P(),
        P(),
        P(),
        P(("frame", "rep"), None, None),
        P(("frame", "rep"), None, None),
        P(("frame", "rep"), None, None),
        P(("frame", "rep"), None, None),
        P(("frame", "rep"), None, None),
        P(),
        P(),
        P(),
        P(),
        P(),
        P(),
        P(),
        P(),
    )
    return jax.shard_map(
        body, mesh=mesh, in_specs=in_specs, out_specs=out_specs, check_vma=False
    )
```

```python
from functools import partial
import math

import jax
import jax.numpy as jnp
import numpy as np
from jax import lax
from jax.experimental import pallas as pl
from jax.experimental.pallas import tpu as pltpu
from jax.sharding import PartitionSpec as P

D = 1024
HEADS = 16
HEAD_DIM = 64
FFN = 4096
PIN = 16
GRID = 16
BLOCK = 128
LEVELS = 32
FR_DEV = 1
NPARAMS = 12878848


LN_EPS = 1e-06
ROPE_BASE = 10000.0
CLIP_NORM = 0.01
BETA_ONE = 0.9
BETA_TWO = 0.999
ADAM_EPS = 1e-08
ADAM_RATE = 0.1
DECAY_RATE = 0.1
STAT_BETA = 0.95
SHAMPOO_RATE = 0.01
EMA_DECAY = 0.9
TOP_PRECISION = lax.Precision.HIGHEST


def matmul(left, right):
    return jnp.dot(left, right, preferred_element_type=jnp.float32)


def layer_norm(hidden):
    centered = hidden - jnp.mean(hidden, axis=-1, keepdims=True)
    inverse = lax.rsqrt(jnp.mean(centered * centered, axis=-1, keepdims=True) + LN_EPS)
    return (centered * inverse, inverse)


def norm_back(grad_hat, normed, inverse):
    return inverse * (
        grad_hat
        - jnp.mean(grad_hat, axis=-1, keepdims=True)
        - normed * jnp.mean(grad_hat * normed, axis=-1, keepdims=True)
    )


def gelu_back(upper, grad_act):
    return jax.vjp(partial(jax.nn.gelu, approximate=True), upper)[1](grad_act)[0]


def frequencies(width):
    return ROPE_BASE ** (-jnp.arange(width, dtype=jnp.float32) / width)


def rope_tables(frame_ids):
    pairs = HEAD_DIM // 2
    time_pairs = pairs // 4
    row_pairs = (pairs - time_pairs) // 2
    column_pairs = pairs - time_pairs - row_pairs
    frames = frame_ids.shape[0]
    tok_frame = GRID * GRID
    token_pos = jnp.arange(tok_frame, dtype=jnp.int32)
    row_pos = (token_pos // GRID).astype(jnp.float32)
    column_pos = (token_pos % GRID).astype(jnp.float32)
    time_angle = (
        frame_ids.astype(jnp.float32)[:, None, None] * frequencies(time_pairs)[None, None, :]
    )
    row_angle = row_pos[None, :, None] * frequencies(row_pairs)[None, None, :]
    column_angle = column_pos[None, :, None] * frequencies(column_pairs)[None, None, :]
    angles = jnp.concatenate(
        [jnp.broadcast_to(time_angle, (frames, tok_frame, time_pairs)), row_angle, column_angle],
        axis=-1,
    )
    angles = angles.reshape(frames * tok_frame, pairs)
    return (jnp.cos(angles), jnp.sin(angles))


def rotate(values, cosine, sine):
    pairs = HEAD_DIM // 2
    first, second = (values[..., :pairs], values[..., pairs:])
    cosine = cosine[:, None, :]
    sine = sine[:, None, :]
    return jnp.concatenate(
        [first * cosine - second * sine, first * sine + second * cosine], axis=-1
    )


def split_heads(flat):
    return flat.reshape(flat.shape[0], HEADS, HEAD_DIM)


def matrix_shapes():
    return ((D, 3 * D), (D, D), (D, FFN), (FFN, D))


def from_blocks(natural):
    matrices = []
    offset = 0
    for rows_in, cols_in in matrix_shapes():
        count_in = rows_in // BLOCK * (cols_in // BLOCK)
        part_blocks = natural[offset : offset + count_in]
        matrices.append(
            part_blocks.reshape(rows_in // BLOCK, cols_in // BLOCK, BLOCK, BLOCK)
            .transpose(0, 2, 1, 3)
            .reshape(rows_in, cols_in)
        )
        offset = offset + count_in
    return matrices


def to_blocks(matrix):
    rows_in, cols_in = matrix.shape
    return (
        matrix.reshape(rows_in // BLOCK, BLOCK, cols_in // BLOCK, BLOCK)
        .transpose(0, 2, 1, 3)
        .reshape(-1, BLOCK, BLOCK)
    )


def score_block(queries, key_block, query_frames, key_frames):
    scores = jnp.einsum(
        "qhd,khd->hqk", queries, key_block, preferred_element_type=jnp.float32
    ) * HEAD_DIM ** (-0.5)
    visible = key_frames[None, None, :] <= query_frames[None, :, None]
    return jnp.where(visible, scores, -jnp.inf)


def stack_keys(key_rows, value_rows, frame_rows):
    total_rows = key_rows.shape[0]
    block_rows = math.gcd(total_rows, 512)
    blocks = total_rows // block_rows
    return (
        (
            key_rows.reshape(blocks, block_rows, HEADS, HEAD_DIM),
            value_rows.reshape(blocks, block_rows, HEADS, HEAD_DIM),
            frame_rows.reshape(blocks, block_rows),
        ),
        block_rows,
    )


def keep_state(previous):
    return previous


def fold_keys(state, shard_rows, queries, query_frames, key_frames_all):
    key_rows, value_rows = shard_rows
    stacks, block_rows = stack_keys(key_rows, value_rows, key_frames_all)
    top_query = jnp.max(query_frames)

    def fold_step_block(carried, block_in):
        key_block, value_block, key_frames = block_in

        def fold_compute(previous):
            running, denominator, accumulated = previous
            scores = score_block(queries, key_block, query_frames, key_frames)
            new_max = jnp.maximum(running, jnp.max(scores, axis=-1))
            weights = jnp.exp(scores - new_max[..., None])
            rescale = jnp.exp(running - new_max)
            contrib = jnp.einsum(
                "hqk,khd->hqd",
                weights.astype(jnp.bfloat16),
                value_block,
                preferred_element_type=jnp.float32,
            )
            return (
                new_max,
                denominator * rescale + jnp.sum(weights, axis=-1),
                accumulated * rescale[..., None] + contrib,
            )

        return (lax.cond(jnp.min(key_frames) <= top_query, fold_compute, keep_state, carried), None)

    state, unused = lax.scan(fold_step_block, state, stacks)
    return state


def grad_parts(
    queries, grad_heads, delta, log_total, query_frames, key_block, value_block, key_frames
):
    probs = jnp.exp(
        score_block(queries, key_block, query_frames, key_frames) - log_total[..., None]
    )
    grad_probs = jnp.einsum(
        "qhd,khd->hqk", grad_heads, value_block, preferred_element_type=jnp.float32
    )
    grad_scores = (probs * (grad_probs - delta[..., None])).astype(jnp.bfloat16)
    return (probs, grad_scores)


def key_value_block(
    queries, grad_heads, delta, log_total, query_frames, key_block, value_block, key_frames
):
    block_rows = key_block.shape[0]
    probs, grad_scores = grad_parts(
        queries, grad_heads, delta, log_total, query_frames, key_block, value_block, key_frames
    )
    key_grad = jnp.einsum(
        "hqk,qhd->khd", grad_scores, queries, preferred_element_type=jnp.float32
    ) * HEAD_DIM ** (-0.5)
    value_grad = jnp.einsum(
        "hqk,qhd->khd", probs.astype(jnp.bfloat16), grad_heads, preferred_element_type=jnp.float32
    )
    return jnp.concatenate(
        [key_grad.reshape(block_rows, D), value_grad.reshape(block_rows, D)], axis=1
    )


def query_grads(
    queries, grad_heads, delta, log_total, query_frames, key_all, value_all, key_frames_all
):
    stacks, block_rows = stack_keys(key_all, value_all, key_frames_all)
    top_query = jnp.max(query_frames)

    def query_step_block(carried, block_in):
        key_block, value_block, key_frames = block_in

        def query_compute(previous):
            probs, grad_scores = grad_parts(
                queries,
                grad_heads,
                delta,
                log_total,
                query_frames,
                key_block,
                value_block,
                key_frames,
            )
            return previous + jnp.einsum(
                "hqk,khd->qhd", grad_scores, key_block, preferred_element_type=jnp.float32
            )

        return (
            lax.cond(jnp.min(key_frames) <= top_query, query_compute, keep_state, carried),
            None,
        )

    initial = jnp.zeros(queries.shape, jnp.float32)
    result, unused = lax.scan(query_step_block, initial, stacks)
    return result * HEAD_DIM ** (-0.5)


def key_terms(
    row_count,
    queries,
    grad_heads,
    delta,
    log_total,
    query_frames,
    key_all,
    value_all,
    key_frames_all,
):
    stacks, block_rows = stack_keys(key_all, value_all, key_frames_all)
    top_query = jnp.max(query_frames)

    def one_block(block_in):
        key_block, value_block, key_frames = block_in

        def one_compute(unused):
            return key_value_block(
                queries,
                grad_heads,
                delta,
                log_total,
                query_frames,
                key_block,
                value_block,
                key_frames,
            )

        def nothing(unused):
            return jnp.zeros((block_rows, 2 * D), jnp.float32)

        return lax.cond(jnp.min(key_frames) <= top_query, one_compute, nothing, 0)

    return lax.map(one_block, stacks).reshape(row_count, 2 * D)


def shampoo(grads, weights, average, left, right, left_root, right_root):
    new_left = STAT_BETA * left + (1 - STAT_BETA) * jnp.einsum(
        "bij,bkj->bik", grads, grads, precision=TOP_PRECISION
    )
    new_right = STAT_BETA * right + (1 - STAT_BETA) * jnp.einsum(
        "bji,bjk->bik", grads, grads, precision=TOP_PRECISION
    )
    direction = jnp.einsum("bij,bjk->bik", left_root, grads, precision=TOP_PRECISION)
    direction = jnp.einsum("bij,bjk->bik", direction, right_root, precision=TOP_PRECISION)
    direction = direction * lax.rsqrt(
        jnp.mean(direction * direction, axis=(1, 2), keepdims=True) + 1e-06
    )
    new_weights = weights - SHAMPOO_RATE * (direction + DECAY_RATE * weights)
    new_average = EMA_DECAY * average + (1 - EMA_DECAY) * new_weights
    return (new_weights, new_left, new_right, new_average)


def adamw(grads, weights, first, second, average, step):
    new_first = BETA_ONE * first + (1 - BETA_ONE) * grads
    new_second = BETA_TWO * second + (1 - BETA_TWO) * grads * grads
    first_hat = new_first / (1 - BETA_ONE**step)
    second_hat = new_second / (1 - BETA_TWO**step)
    new_weights = weights - ADAM_RATE * (
        first_hat / (jnp.sqrt(second_hat) + ADAM_EPS) + DECAY_RATE * weights
    )
    new_average = EMA_DECAY * average + (1 - EMA_DECAY) * new_weights
    return (new_weights, new_first, new_second, new_average)


def on_device(
    clean,
    noise,
    levels,
    flags,
    frame_map,
    block_slot,
    step_count,
    mat_weight,
    mat_ema,
    stat_left,
    stat_right,
    root_left,
    root_right,
    mod_table,
    mod_mom,
    mod_var,
    mod_ema,
    io_weight,
    io_mom,
    io_var,
    io_ema,
):
    tok_frame = GRID * GRID
    local_rows = FR_DEV * tok_frame
    noised = (1 - flags[0]).astype(jnp.float32)
    noised_total = jnp.maximum(lax.psum(jnp.sum(noised), ("frame", "rep")), 1.0)
    gathered = lax.all_gather(mat_weight.astype(jnp.bfloat16), ("frame", "rep"), axis=0, tiled=True)
    natural = jnp.zeros_like(gathered).at[block_slot].set(gathered)
    attn_w, out_w, up_w, down_w = from_blocks(natural)
    clip_map = lax.dynamic_index_in_dim(frame_map, lax.axis_index("rep"), 0, keepdims=False)
    my_frames = lax.dynamic_slice_in_dim(clip_map, lax.axis_index("frame") * FR_DEV, FR_DEV)
    key_frames_all = jnp.repeat(clip_map, tok_frame)
    query_frames = jnp.repeat(my_frames, tok_frame)
    level_now = levels[0] * (1 - flags[0])
    fraction = level_now.astype(jnp.float32) / LEVELS
    keep_coef = jnp.cos(0.5 * jnp.pi * fraction)
    noise_coef = jnp.sin(0.5 * jnp.pi * fraction)
    frames_in = keep_coef[:, None, None] * clean[0] + noise_coef[:, None, None] * noise[0]
    inputs = jnp.swapaxes(frames_in, 1, 2).reshape(local_rows, PIN).astype(jnp.bfloat16)
    targets = jnp.swapaxes(noise[0], 1, 2).reshape(local_rows, PIN)
    selector = (level_now[:, None] == jnp.arange(LEVELS, dtype=jnp.int32)[None, :]).astype(
        jnp.float32
    )
    modulation = jnp.dot(selector, mod_table, precision=TOP_PRECISION).reshape(FR_DEV, 8, 1, D)
    io_low = io_weight.astype(jnp.bfloat16)
    embed = io_low[:PIN]
    head = io_low[PIN : 2 * PIN]
    start = (matmul(inputs, embed) + io_weight[2 * PIN]).reshape(FR_DEV, tok_frame, D)
    hat_one, inv_one = layer_norm(start)
    normed = (
        (hat_one * (1 + modulation[:, 1]) + modulation[:, 0])
        .reshape(local_rows, D)
        .astype(jnp.bfloat16)
    )
    projected = matmul(normed, attn_w)
    cosine, sine = rope_tables(my_frames)
    queries = rotate(split_heads(projected[:, :D]), cosine, sine).astype(jnp.bfloat16)
    key_flat = (
        rotate(split_heads(projected[:, D : 2 * D]), cosine, sine)
        .astype(jnp.bfloat16)
        .reshape(local_rows, D)
    )
    value_flat = projected[:, 2 * D :].astype(jnp.bfloat16)
    initial = (
        jnp.full((HEADS, local_rows), -1e30, jnp.float32),
        jnp.zeros((HEADS, local_rows), jnp.float32),
        jnp.zeros((HEADS, local_rows, HEAD_DIM), jnp.float32),
    )
    running, denominator, accumulated = fold_keys(
        initial,
        (
            lax.all_gather(key_flat, "frame", axis=0, tiled=True),
            lax.all_gather(value_flat, "frame", axis=0, tiled=True),
        ),
        queries,
        query_frames,
        key_frames_all,
    )
    attended = jnp.transpose(accumulated / denominator[..., None], (1, 0, 2)).reshape(local_rows, D)
    log_total = running + jnp.log(denominator)
    attended_low = attended.astype(jnp.bfloat16)
    branch = matmul(attended_low, out_w).reshape(FR_DEV, tok_frame, D)
    middle = start + modulation[:, 2] * branch
    hat_two, inv_two = layer_norm(middle)
    normed_two = (
        (hat_two * (1 + modulation[:, 4]) + modulation[:, 3])
        .reshape(local_rows, D)
        .astype(jnp.bfloat16)
    )
    upper = matmul(normed_two, up_w)
    activated = jax.nn.gelu(upper, approximate=True).astype(jnp.bfloat16)
    lower = matmul(activated, down_w).reshape(FR_DEV, tok_frame, D)
    final = middle + modulation[:, 5] * lower
    hat_three, inv_three = layer_norm(final)
    normed_three = (
        (hat_three * (1 + modulation[:, 7]) + modulation[:, 6])
        .reshape(local_rows, D)
        .astype(jnp.bfloat16)
    )
    predicted = matmul(normed_three, head.T)
    row_weight = jnp.repeat(noised, tok_frame)[:, None]
    inv_scale = 1.0 / (noised_total * tok_frame * PIN)
    difference = predicted - targets
    loss_part = jnp.sum(row_weight * difference * difference) * inv_scale
    grad_pred = (2.0 * inv_scale * row_weight * difference).astype(jnp.bfloat16)
    grad_head = jnp.dot(grad_pred.T, normed_three, preferred_element_type=jnp.float32)
    grad_norm_three = matmul(grad_pred, head).reshape(FR_DEV, tok_frame, D)
    grad_final = norm_back(grad_norm_three * (1 + modulation[:, 7]), hat_three, inv_three)
    grad_lower = (grad_final * modulation[:, 5]).reshape(local_rows, D).astype(jnp.bfloat16)
    grad_down = jnp.dot(activated.T, grad_lower, preferred_element_type=jnp.float32)
    grad_upper = gelu_back(upper, matmul(grad_lower, down_w.T)).astype(jnp.bfloat16)
    grad_up = jnp.dot(normed_two.T, grad_upper, preferred_element_type=jnp.float32)
    grad_norm_two = matmul(grad_upper, up_w.T).reshape(FR_DEV, tok_frame, D)
    grad_middle = grad_final + norm_back(grad_norm_two * (1 + modulation[:, 4]), hat_two, inv_two)
    grad_branch = (grad_middle * modulation[:, 2]).reshape(local_rows, D).astype(jnp.bfloat16)
    grad_out_w = jnp.dot(attended_low.T, grad_branch, preferred_element_type=jnp.float32)
    grad_heads = split_heads(matmul(grad_branch, out_w.T).astype(jnp.bfloat16))
    delta = jnp.sum(grad_heads.astype(jnp.float32) * split_heads(attended), axis=-1).T
    key_all, value_all = (
        lax.all_gather(key_flat, "frame", axis=0, tiled=True),
        lax.all_gather(value_flat, "frame", axis=0, tiled=True),
    )
    grad_query = query_grads(
        queries, grad_heads, delta, log_total, query_frames, key_all, value_all, key_frames_all
    )
    key_value_grad = lax.psum_scatter(
        key_terms(
            lax.axis_size("frame") * local_rows,
            queries,
            grad_heads,
            delta,
            log_total,
            query_frames,
            key_all,
            value_all,
            key_frames_all,
        ),
        "frame",
        scatter_dimension=0,
        tiled=True,
    )
    grad_q = rotate(grad_query, cosine, -sine).reshape(local_rows, D)
    grad_k = rotate(split_heads(key_value_grad[:, :D]), cosine, -sine).reshape(local_rows, D)
    grad_proj = jnp.concatenate([grad_q, grad_k, key_value_grad[:, D:]], axis=1).astype(
        jnp.bfloat16
    )
    grad_attn_w = jnp.dot(normed.T, grad_proj, preferred_element_type=jnp.float32)
    grad_norm_one = matmul(grad_proj, attn_w.T).reshape(FR_DEV, tok_frame, D)
    grad_start = grad_middle + norm_back(grad_norm_one * (1 + modulation[:, 1]), hat_one, inv_one)
    grad_start_low = grad_start.reshape(local_rows, D).astype(jnp.bfloat16)
    grad_embed = jnp.dot(inputs.T, grad_start_low, preferred_element_type=jnp.float32)
    grad_bias = jnp.sum(grad_start_low.astype(jnp.float32), axis=0)
    mod_terms = [
        grad_norm_one,
        grad_norm_one * hat_one,
        grad_middle * branch,
        grad_norm_two,
        grad_norm_two * hat_two,
        grad_final * lower,
        grad_norm_three,
        grad_norm_three * hat_three,
    ]
    mod_grads = jnp.stack([jnp.sum(term, axis=1) for term in mod_terms], axis=1).reshape(
        FR_DEV, 8 * D
    )
    grad_table = jnp.dot(selector.T, mod_grads, precision=TOP_PRECISION)
    grad_io = jnp.concatenate([grad_embed, grad_head, grad_bias[None, :]], axis=0)
    grad_table, grad_io, total_loss = lax.psum((grad_table, grad_io, loss_part), ("frame", "rep"))
    grad_blocks = jnp.concatenate(
        [to_blocks(grad_attn_w), to_blocks(grad_out_w), to_blocks(grad_up), to_blocks(grad_down)], 0
    )
    owned = lax.psum_scatter(
        grad_blocks[block_slot], ("frame", "rep"), scatter_dimension=0, tiled=True
    )
    block_limit = CLIP_NORM * BLOCK * NPARAMS ** (-0.5)
    block_norm = jnp.sqrt(jnp.sum(owned * owned, axis=(1, 2), keepdims=True))
    mat_grad = owned * (block_limit / jnp.maximum(block_norm, block_limit))
    grad_norm = jnp.sqrt(jnp.sum(grad_table * grad_table) + jnp.sum(grad_io * grad_io))
    factor = CLIP_NORM / jnp.maximum(grad_norm, CLIP_NORM)
    new_mat_weight, new_stat_left, new_stat_right, new_mat_ema = shampoo(
        mat_grad, mat_weight, mat_ema, stat_left, stat_right, root_left, root_right
    )
    step = step_count[0].astype(jnp.float32)
    new_mod = adamw(grad_table * factor, mod_table, mod_mom, mod_var, mod_ema, step)
    new_io = adamw(grad_io * factor, io_weight, io_mom, io_var, io_ema, step)
    return (
        total_loss * noised_total,
        noised_total,
        grad_norm,
        mat_grad,
        new_mat_weight,
        new_stat_left,
        new_stat_right,
        new_mat_ema,
        new_mod[0],
        new_mod[1],
        new_mod[2],
        new_mod[3],
        new_io[0],
        new_io[1],
        new_io[2],
        new_io[3],
    )


TOK = GRID * GRID
GROUP = 4


def fold_rows(values, op):
    return op(values.reshape(values.shape[0] // 8, 8, values.shape[1]), axis=0)


def side_by_side(ref, first, count, kind):
    parts = [ref[first + j, kind] for j in range(count)]
    return jnp.concatenate(parts, axis=1) if count > 1 else parts[0]


def attend_frame(t, qkv, scores, full, lse):
    q = qkv[t, 0] * jnp.bfloat16(HEAD_DIM**-0.5)

    def score(k, top):
        s = dotg(qkv[k, 1], q, 0, 0)
        scores[k] = s
        return jnp.maximum(top, fold_rows(s, jnp.max))

    top = lax.fori_loop(
        0, t + 1, score, jnp.full((8, TOK), -1e30, jnp.float32), unroll=min(GROUP, t + 1)
    )
    top = jnp.max(top, axis=0, keepdims=True)
    total = jnp.zeros((8, TOK), jnp.float32)
    acc = jnp.zeros((HEAD_DIM, TOK), jnp.float32)
    for k in range(0, t + 1, GROUP):
        count = min(GROUP, t + 1 - k)
        probs = []
        for j in range(count):
            p = jnp.exp(scores[k + j] - top)
            total = total + fold_rows(p, jnp.sum)
            probs.append(p.astype(jnp.bfloat16))
        acc = acc + dotg(side_by_side(qkv, k, count, 2), jnp.concatenate(probs, axis=0), 1, 0)
    total = jnp.sum(total, axis=0, keepdims=True)
    out = acc / total
    full[t] = out
    lse[t] = top + jnp.log(total)
    return out.astype(jnp.bfloat16)


def turn_back(values, cosine, sine):
    first, second = values[: HEAD_DIM // 2], values[HEAD_DIM // 2 :]
    return jnp.concatenate(
        [first * cosine + second * sine, second * cosine - first * sine], axis=0
    )


def attend_frame_back(t, qkv, do_ref, full, lse, cos, sin, dk_ref, dv_ref):
    q = qkv[t, 0] * jnp.bfloat16(HEAD_DIM**-0.5)
    do = do_ref[t]
    delta = jnp.sum(do.astype(jnp.float32) * full[t], axis=0, keepdims=True)
    dq = jnp.zeros((HEAD_DIM, TOK), jnp.float32)
    for k in range(0, t + 1, GROUP):
        count = min(GROUP, t + 1 - k)
        keys = side_by_side(qkv, k, count, 1)
        p = jnp.exp(dotg(keys, q, 0, 0) - lse[t])
        dp = dotg(side_by_side(qkv, k, count, 2), do, 0, 0)
        ds = (p * (dp - delta)).astype(jnp.bfloat16)
        dq = dq + dotg(keys, ds, 1, 0)
        dk = dotg(q, ds, 1, 1)
        dv = dotg(do, p.astype(jnp.bfloat16), 1, 1)
        for j in range(count):
            dk_ref[k + j] += dk[:, j * TOK : (j + 1) * TOK]
            dv_ref[k + j] += dv[:, j * TOK : (j + 1) * TOK]
    return (
        turn_back(dq * HEAD_DIM**-0.5, cos[t], sin[t]).astype(jnp.bfloat16),
        turn_back(dk_ref[t], cos[t], sin[t]).astype(jnp.bfloat16),
        dv_ref[t].astype(jnp.bfloat16),
    )


def attend_kernel(qkv_ref, low_ref, full_ref, lse_ref, scores):
    for t in range(qkv_ref.shape[0]):
        low_ref[t] = attend_frame(t, qkv_ref, scores, full_ref, lse_ref)


def attend(qkv):
    frames = qkv.shape[0]
    vmem = pl.BlockSpec(memory_space=pltpu.VMEM)
    return pl.pallas_call(
        attend_kernel,
        in_specs=[vmem],
        out_specs=[vmem] * 3,
        out_shape=[
            jax.ShapeDtypeStruct((frames, HEAD_DIM, TOK), jnp.bfloat16),
            jax.ShapeDtypeStruct((frames, HEAD_DIM, TOK), jnp.float32),
            jax.ShapeDtypeStruct((frames, 1, TOK), jnp.float32),
        ],
        scratch_shapes=[pltpu.VMEM((frames, TOK, TOK), jnp.float32)],
        compiler_params=pltpu.CompilerParams(vmem_limit_bytes=32 * 2**20),
    )(qkv)


def attend_back_kernel(qkv_ref, do_ref, full_ref, lse_ref, cos_ref, sin_ref, out_ref, dk, dv):
    dk[...] = jnp.zeros_like(dk)
    dv[...] = jnp.zeros_like(dv)
    for t in reversed(range(qkv_ref.shape[0])):
        parts = attend_frame_back(t, qkv_ref, do_ref, full_ref, lse_ref, cos_ref, sin_ref, dk, dv)
        for i in range(3):
            out_ref[t, i] = parts[i]


def attend_back(qkv, do, full, lse, cos, sin):
    frames = qkv.shape[0]
    vmem = pl.BlockSpec(memory_space=pltpu.VMEM)
    return pl.pallas_call(
        attend_back_kernel,
        in_specs=[vmem] * 6,
        out_specs=vmem,
        out_shape=jax.ShapeDtypeStruct(qkv.shape, jnp.bfloat16),
        scratch_shapes=[pltpu.VMEM((frames, HEAD_DIM, TOK), jnp.float32)] * 2,
        compiler_params=pltpu.CompilerParams(vmem_limit_bytes=32 * 2**20),
    )(qkv, do, full, lse, cos, sin)


MESH = pl.DeviceIdType.MESH
NSLOT = 24
FIRST = 14
LATER = NSLOT - FIRST
DATA = FIRST
SMALL_ROWS = 40
FIRST_GATHER = (
    ("xzy", 0, 2),
    ("yzx", 2, 2),
    ("zxy", 4, 3),
    ("zyx", 7, 3),
    ("zxy", 10, 2),
    ("zyx", 12, 3),
)
FIRST_SCATTER = (("xzy", 0, 2), ("yzx", 2, 2), ("zxy", 4, 5), ("zyx", 9, 5))
LATER_PARTS = (("zyx", 0, 5), ("zyx", 5, 5))


def place():
    frame = lax.axis_index("frame")
    return frame // 4, (frame // 2) % 2, frame % 2, lax.axis_index("rep")


def device(z, y, c, x):
    return ((z * 2 + y) * 2 + c, x)


def owner_of(z, y, c, x):
    return ((z * 2 + y) * 2 + c) * 2 + x


def plane_of(z, y, x):
    return (z * 2 + y) * 2 + x


def offsets():
    return [(dx, dy, dz) for dx in (0, 1) for dy in (0, 1) for dz in range(-3, 4)]


def hops(off):
    return off[0] + off[1] + abs(off[2])


def route_keys(parts):
    keys = [(part, off) for part in range(len(parts)) for off in offsets()]
    return sorted(keys, key=lambda k: (hops(k[1]), k[0]))


def onward(order, off):
    moved = dict(zip("xyz", off))
    last = max((order.index(k) for k in order if moved[k]), default=-1)
    links = []
    if last >= 0 and order[last] == "z":
        links.append("u" if off[2] < 0 else "w")
    for k in order[last + 1 :]:
        links.extend("uw" if k == "z" else k)
    return links


def toward(order, off):
    moved = dict(zip("xyz", off))
    last = [k for k in order if moved[k]][-1]
    if last == "z":
        return ("w", "u") if off[2] < 0 else ("u", "w")
    return last, last


def can(link, z):
    return {"u": z < 3, "w": z > 0}.get(link)


def partner(link, z, y, c, x):
    return {
        "x": device(z, y, c, 1 - x),
        "y": device(z, 1 - y, c, x),
        "u": device(z + 1, y, c, x),
        "w": device(z - 1, y, c, x),
        "c": device(z, y, 1 - c, x),
    }[link]


def when(cond, fn):
    if cond is None:
        fn()
    else:
        pl.when(cond)(fn)


def both(a, b):
    return b if a is None else a if b is None else jnp.logical_and(a, b)


def owner_at(off, z, y, x):
    dx, dy, dz = off
    oz = z + dz
    cond = None if dz == 0 else (oz <= 3 if dz > 0 else oz >= 0)
    return oz, (1 - y if dy else y), (1 - x if dx else x), cond


def greet(z, y, c, x, far=()):
    barrier = pltpu.get_barrier_semaphore()
    for link in "xyuwc":
        when(
            can(link, z),
            lambda link=link: pl.semaphore_signal(
                barrier, inc=1, device_id=partner(link, z, y, c, x), device_id_type=MESH
            ),
        )
    for dev in far:
        pl.semaphore_signal(barrier, inc=1, device_id=dev, device_id_type=MESH)
    ends = jnp.logical_or(z == 0, z == 3)
    pl.when(ends)(lambda: pl.semaphore_wait(barrier, 4 + len(far)))
    pl.when(jnp.logical_not(ends))(lambda: pl.semaphore_wait(barrier, 5 + len(far)))


class Gather:
    def __init__(self, parts, src, out, sems, where, shift=0, axes="xyz"):
        self.parts, self.src, self.out, self.where, self.shift = parts, src, out, where, shift
        self.axes = axes
        self.total = sum(count for _, _, count in parts)
        self.send, self.recv, self.csend, self.crecv = sems
        self.keys = [k for k in route_keys(parts) if "x" in axes or k[1][:2] == (0, 0)]
        self.last = {}
        for key in self.keys if "x" in axes else ():
            self.last[key[1]] = key
        self.sent = []

    @staticmethod
    def sems(parts):
        n = len(parts)
        return [
            pltpu.SemaphoreType.DMA((4, n, 16)),
            pltpu.SemaphoreType.DMA((n, 16)),
            pltpu.SemaphoreType.DMA((16,)),
            pltpu.SemaphoreType.DMA((16,)),
        ]

    def held(self, owner):
        return self.out.at[owner, pl.ds(self.shift, self.total)]

    def hop(self, link, part, src, owner, plane):
        _, first, count = self.parts[part]
        return pltpu.make_async_remote_copy(
            src_ref=src.at[pl.ds(first, count)],
            dst_ref=self.out.at[owner, pl.ds(self.shift + first, count)],
            send_sem=self.send.at["xyuw".index(link), part, plane],
            recv_sem=self.recv.at[part, plane],
            device_id=partner(link, *self.where),
            device_id_type=MESH,
        )

    def across(self, src, owner, plane):
        return pltpu.make_async_remote_copy(
            src_ref=src,
            dst_ref=self.held(owner),
            send_sem=self.csend.at[plane],
            recv_sem=self.crecv.at[plane],
            device_id=partner("c", *self.where),
            device_id_type=MESH,
        )

    def step(self, key):
        part, off = key
        z, y, c, x = self.where
        oz, oy, ox, cond = owner_at(off, z, y, x)
        owner, plane = owner_of(oz, oy, c, ox), plane_of(oz, oy, ox)
        own = off == (0, 0, 0)
        here = own or (self.axes == "xy" and off[:2] == (0, 0))
        src = self.src if own and self.axes != "xy" else self.held(owner)
        links = [k for k in onward(self.parts[part][0], off) if ("z" if k in "uw" else k) in self.axes]

        def act():
            if not here:
                self.hop("x", part, src, owner, plane).wait_recv()
            for link in links:
                when(can(link, z), lambda link=link: self.hop(link, part, src, owner, plane).start())
            if self.last.get(off) == key:
                self.across(src, owner, plane).start()

        when(cond, act)
        for link in links:
            self.sent.append(
                (both(cond, can(link, z)), lambda link=link: self.hop(link, part, src, owner, plane))
            )
        if self.last.get(off) == key:
            self.sent.append((cond, lambda: self.across(src, owner, plane)))

    def finish(self):
        for cond, make in self.sent:
            when(cond, lambda make=make: make().wait_send())
        c = self.where[2]
        for plane in range(16) if self.last else ():
            owner = owner_of(plane // 4, (plane // 2) % 2, 1 - c, plane % 2)
            self.across(self.held(owner), owner, plane).wait_recv()


def gather_kernel(perm_ref, w_ref, data_ref, out_ref, stage, later, local, *sems):
    where = place()
    owner = owner_of(*where)
    count = len(Gather.sems(FIRST_GATHER))

    def take(i, carry):
        stage[i] = w_ref[perm_ref[i]].astype(jnp.bfloat16)
        return carry

    def take_later(i, carry):
        later[i] = w_ref[perm_ref[FIRST + i]].astype(jnp.bfloat16)
        return carry

    lax.fori_loop(0, FIRST, take, 0)
    stage[DATA] = data_ref[...]
    greet(*where)
    gather = Gather(FIRST_GATHER, stage, out_ref, sems[:count], where)
    along = Gather(LATER_PARTS, later, out_ref, sems[count:], where, FIRST + 1, "z")
    own = [
        pltpu.make_async_copy(stage, gather.held(owner), local.at[0]),
        pltpu.make_async_copy(later, along.held(owner), local.at[1]),
    ]
    own[0].start()
    begun = len(FIRST_GATHER)
    for key in gather.keys[:begun]:
        gather.step(key)
    lax.fori_loop(0, LATER, take_later, 0)
    own[1].start()
    steps = [(hops(key[1]), 0, i, gather, key) for i, key in enumerate(gather.keys[begun:])]
    steps += [(hops(key[1]) + 1.5, 1, i, along, key) for i, key in enumerate(along.keys)]
    for step in sorted(steps, key=lambda step: step[:3]):
        step[3].step(step[4])
    gather.finish()
    along.finish()
    for copy in own:
        copy.wait()


def gather_weights(perm, blocks, data):
    vmem = pl.BlockSpec(memory_space=pltpu.VMEM)
    return pl.pallas_call(
        gather_kernel,
        out_shape=jax.ShapeDtypeStruct((32, NSLOT + 1, BLOCK, BLOCK), jnp.bfloat16),
        in_specs=[pl.BlockSpec(memory_space=pltpu.SMEM), vmem, vmem],
        out_specs=pl.BlockSpec(memory_space=pltpu.HBM),
        scratch_shapes=[
            pltpu.VMEM((FIRST + 1, BLOCK, BLOCK), jnp.bfloat16),
            pltpu.VMEM((LATER, BLOCK, BLOCK), jnp.bfloat16),
            pltpu.SemaphoreType.DMA((2,)),
        ]
        + Gather.sems(FIRST_GATHER)
        + Gather.sems(LATER_PARTS),
        compiler_params=pltpu.CompilerParams(
            collective_id=1, has_side_effects=True, vmem_limit_bytes=60 * 2**20
        ),
    )(perm, blocks, data)


def inbox_axes(order, link):
    dim = "z" if link in "uw" else link
    axes = order[: order.index(dim)]
    return axes + "z" if dim == "z" else axes


def inbox_starts(parts, link):
    starts, total = [], 0
    for order, _, count in parts:
        starts.append(total)
        size = count
        for d in inbox_axes(order, link):
            size *= 4 if d == "z" else 2
        total += size
    return starts, total


class Scatter:
    def __init__(self, parts, acc, sib, boxes, send, recvs, where, ready, store, axes="xyz"):
        self.parts, self.acc, self.sib, self.where, self.axes = parts, acc, sib, where, axes
        links = self.links_of(axes)
        self.boxes = dict(zip(links, boxes))
        self.recvs = dict(zip(links, recvs))
        self.send, self.ready, self.store = send, ready, store
        self.keys = [
            k for k in reversed(route_keys(parts)) if "x" in axes or k[1][:2] == (0, 0)
        ]
        self.seen = []
        for _, off in self.keys:
            if off not in self.seen:
                self.seen.append(off)
        self.fresh = set()

    @staticmethod
    def links_of(axes):
        return ("xy" if "x" in axes else "") + ("uw" if "z" in axes else "")

    @classmethod
    def boxes_of(cls, parts, axes="xyz"):
        return [
            pltpu.VMEM((inbox_starts(parts, link)[1], 128, 128), jnp.bfloat16)
            for link in cls.links_of(axes)
        ]

    @classmethod
    def sems(cls, parts, axes="xyz"):
        return [pltpu.SemaphoreType.DMA((len(parts), 16))] + [
            pltpu.SemaphoreType.DMA((len(parts), 16)) for _ in cls.links_of(axes)
        ]

    def row(self, oz, oy, ox):
        return oz if self.axes == "z" else plane_of(oz, oy, ox)

    def inbox(self, link, part, oz, oy, ox):
        order, _, count = self.parts[part]
        index = 0
        for d in inbox_axes(order, link):
            index = index * (4 if d == "z" else 2) + {"z": oz, "y": oy, "x": ox}[d]
        return inbox_starts(self.parts, link)[0][part] + index * count

    def clear_ends(self):
        z = self.where[0]

        def clear(box):
            def body(i, carry):
                box[i] = jnp.zeros((128, 128), jnp.bfloat16)
                return carry

            lax.fori_loop(0, box.shape[0], body, 0)

        pl.when(z == 3)(lambda: clear(self.boxes["u"]))
        pl.when(z == 0)(lambda: clear(self.boxes["w"]))

    def hop(self, part, off):
        z, y, c, x = self.where
        oz, oy, ox, _ = owner_at(off, z, y, x)
        plane = plane_of(oz, oy, ox)
        order, first, count = self.parts[part]
        link, named = toward(order, off)
        return pltpu.make_async_remote_copy(
            src_ref=self.acc.at[self.row(oz, oy, ox), pl.ds(first, count)],
            dst_ref=self.boxes[named].at[pl.ds(self.inbox(named, part, oz, oy, ox), count)],
            send_sem=self.send.at[part, plane],
            recv_sem=self.recvs[named].at[part, plane],
            device_id=partner(link, *self.where),
            device_id_type=MESH,
        )

    def step(self, key):
        part, off = key
        z, y, c, x = self.where
        oz, oy, ox, cond = owner_at(off, z, y, x)
        plane = plane_of(oz, oy, ox)
        order, first, count = self.parts[part]
        new = off not in self.fresh
        self.fresh.add(off)
        row = self.row(oz, oy, ox)
        ends = off[:2] == (0, 0) if self.axes == "xy" else off == (0, 0, 0)

        def act():
            if new:
                self.ready(oz, oy, ox)
            sources = []
            for link in [k for k in onward(order, off) if k in self.boxes]:
                start = self.inbox(link, part, oz, oy, ox)
                sources.append((self.boxes[link], start))

                def arrive(link=link, start=start):
                    view = self.boxes[link].at[pl.ds(start, count)]
                    pltpu.make_async_remote_copy(
                        src_ref=view,
                        dst_ref=view,
                        send_sem=self.send.at[part, plane],
                        recv_sem=self.recvs[link].at[part, plane],
                        device_id=partner("c", *self.where),
                        device_id_type=MESH,
                    ).wait_recv()

                when(can(link, z), arrive)

            def add(i, carry):
                total = self.acc[row, first + i].astype(jnp.float32)
                if self.sib is not None:
                    total = total + self.sib[row, first + i].astype(jnp.float32)
                for box, start in sources:
                    total = total + box[start + i].astype(jnp.float32)
                if ends:
                    self.store(oz, first + i, total)
                else:
                    self.acc[row, first + i] = total.astype(jnp.bfloat16)
                return carry

            lax.fori_loop(0, count, add, 0)
            if not ends:
                self.hop(part, off).start()

        when(cond, act)

    def finish(self):
        z, y, c, x = self.where
        for part, off in self.keys:
            if off[:2] != (0, 0) or (off[2] != 0 and self.axes != "xy"):
                cond = owner_at(off, z, y, x)[3]
                when(cond, lambda part=part, off=off: self.hop(part, off).wait_send())


class SmallSums:
    def __init__(self, row, io, rows_out, io_out, mine, inbox, sems, where):
        self.row, self.io, self.rows, self.io_out = row, io, rows_out, io_out
        self.mine, self.inbox, self.where = mine, inbox, where
        self.gsend, self.grecv, self.osend, self.orecv, self.bsend, self.brecv, self.local = sems
        self.order = "zyx"
        self.sent = []

    @staticmethod
    def sems():
        dma = pltpu.SemaphoreType.DMA
        return [dma((4, 16)), dma((16,)), dma((6,)), dma((6,)), dma((1,)), dma((1,)), dma((1,))]

    def far(self):
        z, y, c, x = self.where
        return device(z + 2 - 4 * (z // 2), y, c, x)

    def peer(self, turn):
        z, y, c, x = self.where
        if turn == 3:
            return device(z + 1 - 2 * (z % 2), y, c, x)
        if turn == 4:
            return self.far()
        return partner("cxyyyc"[turn], *self.where)

    def swap(self, turn):
        c = self.where[2]
        if turn == 0:
            src, dst = self.io.at[1 - c], self.inbox.at[0]
        elif turn == 5:
            src, dst = self.mine.at[5], self.io_out.at[c]
        else:
            src, dst = self.mine.at[turn], self.inbox.at[turn]
        return pltpu.make_async_remote_copy(
            src_ref=src,
            dst_ref=dst,
            send_sem=self.osend.at[turn],
            recv_sem=self.orecv.at[turn],
            device_id=self.peer(turn),
            device_id_type=MESH,
        )

    def hop(self, link, src, plane):
        return pltpu.make_async_remote_copy(
            src_ref=src,
            dst_ref=self.rows.at[self.where[2], plane],
            send_sem=self.gsend.at["xyuw".index(link), plane],
            recv_sem=self.grecv.at[plane],
            device_id=partner(link, *self.where),
            device_id_type=MESH,
        )

    def bulk(self, core):
        return pltpu.make_async_remote_copy(
            src_ref=self.rows.at[core],
            dst_ref=self.rows.at[core],
            send_sem=self.bsend.at[0],
            recv_sem=self.brecv.at[0],
            device_id=partner("c", *self.where),
            device_id_type=MESH,
        )

    def row_step(self, off):
        z, y, c, x = self.where
        oz, oy, ox, cond = owner_at(off, z, y, x)
        plane = plane_of(oz, oy, ox)
        own = off == (0, 0, 0)
        src = self.row if own else self.rows.at[c, plane]
        links = onward(self.order, off)

        def act():
            if not own:
                self.hop("x", src, plane).wait_recv()
            for link in links:
                when(can(link, z), lambda link=link: self.hop(link, src, plane).start())

        when(cond, act)
        for link in links:
            self.sent.append(
                (both(cond, can(link, z)), lambda link=link: self.hop(link, src, plane))
            )

    def begin(self):
        z, y, c, x = self.where
        self.own = pltpu.make_async_copy(
            self.row, self.rows.at[c, plane_of(z, y, x)], self.local.at[0]
        )
        self.own.start()
        self.swap(0).start()
        self.row_step((0, 0, 0))

    def turn(self, turn):
        c = self.where[2]
        self.swap(turn).wait_recv()
        if turn < 5:
            before = self.io[c] if turn == 0 else self.mine[turn]
            self.mine[turn + 1] = before + self.inbox[turn]
            if turn == 4:
                self.io_out[c] = self.mine[5]
            self.swap(turn + 1).start()

    def tasks(self):
        todo = [
            lambda off=off: self.row_step(off)
            for off in sorted(offsets(), key=hops)
            if off != (0, 0, 0)
        ]
        for turn in range(6):
            todo.insert(5 * turn + 2, lambda turn=turn: self.turn(turn))

        def last():
            self.own.wait()
            self.bulk(self.where[2]).start()

        return todo + [last]

    def finish(self):
        c = self.where[2]
        self.bulk(1 - c).wait_recv()
        self.bulk(c).wait_send()
        for turn in range(6):
            self.swap(turn).wait_send()
        for cond, make in self.sent:
            when(cond, lambda make=make: make().wait_send())


def own_blocks(g_ref, owner, first, count):
    return g_ref.at[owner, pl.ds(first, count)]


class Halves:
    def __init__(self, g_ref, first, count, acc, sib, csend, crecv, local, where):
        self.g_ref, self.first, self.count, self.acc, self.sib = g_ref, first, count, acc, sib
        self.csend, self.crecv, self.local, self.where = csend, crecv, local, where

    def across(self, oz, oy, ox):
        plane = plane_of(oz, oy, ox)
        other = owner_of(oz, oy, 1 - self.where[2], ox)
        return pltpu.make_async_remote_copy(
            src_ref=own_blocks(self.g_ref, other, self.first, self.count),
            dst_ref=self.sib.at[plane],
            send_sem=self.csend.at[plane],
            recv_sem=self.crecv.at[plane],
            device_id=partner("c", *self.where),
            device_id_type=MESH,
        )

    def load(self, oz, oy, ox):
        plane = plane_of(oz, oy, ox)
        same = owner_of(oz, oy, self.where[2], ox)
        return pltpu.make_async_copy(
            own_blocks(self.g_ref, same, self.first, self.count),
            self.acc.at[plane],
            self.local.at[plane],
        )

    def begin(self, offs):
        z, y, c, x = self.where
        for off in offs:
            oz, oy, ox, cond = owner_at(off, z, y, x)

            def start(oz=oz, oy=oy, ox=ox):
                self.across(oz, oy, ox).start()
                self.load(oz, oy, ox).start()

            when(cond, start)

    def ready(self, oz, oy, ox):
        self.across(oz, oy, ox).wait_recv()
        self.load(oz, oy, ox).wait()

    def finish(self):
        for plane in range(16):
            self.across(plane // 4, (plane // 2) % 2, plane % 2).wait_send()


def scatter_kernel(rank_ref, g_ref, row_ref, io_ref, later_ref, out_ref, rows_out, io_out, *refs):
    acc, sib, along, total = refs[:4]
    boxes, refs = refs[4:8], refs[8:]
    later_boxes, refs = refs[:2], refs[2:]
    mine, inbox = refs[:2]
    csend, crecv, local, later_local, send = refs[2:7]
    recvs, later_send, later_recvs, small_sems = refs[7:11], refs[11], refs[12:14], refs[14:]
    where = place()
    small = SmallSums(row_ref, io_ref, rows_out, io_out, mine, inbox, small_sems, where)
    whole = pltpu.make_async_copy(later_ref, along, later_local.at[0])
    whole.start()
    greet(*where, far=(small.far(),))
    small.begin()
    halves = Halves(g_ref, 0, FIRST, acc, sib, csend, crecv, local, where)

    def store(oz, row, value):
        total[row] = value

    def store_later(oz, row, value):
        total[FIRST + row] = value

    scatter = Scatter(FIRST_SCATTER, acc, sib, boxes, send, recvs, where, halves.ready, store)
    later = Scatter(
        LATER_PARTS, along, None, later_boxes, later_send, later_recvs, where,
        lambda *place: None, store_later, "z",
    )
    halves.begin(scatter.seen)
    scatter.clear_ends()
    later.clear_ends()
    whole.wait()
    tasks = small.tasks()
    steps = [(-hops(key[1]), 1, i, scatter, key) for i, key in enumerate(scatter.keys)]
    steps += [(-hops(key[1]) - 1.5, 0, i, later, key) for i, key in enumerate(later.keys)]
    for i, step in enumerate(sorted(steps, key=lambda step: step[:3])):
        step[3].step(step[4])
        if i % 5 == 4 and tasks:
            tasks.pop(0)()
    for task in tasks:
        task()

    def put(i, carry):
        out_ref[i] = total[rank_ref[i]]
        return carry

    lax.fori_loop(0, NSLOT, put, 0)
    scatter.finish()
    later.finish()
    halves.finish()
    small.finish()


def scatter_grads(ranks, grads, row, io, later):
    vmem = pl.BlockSpec(memory_space=pltpu.VMEM)
    dma = pltpu.SemaphoreType.DMA
    held = pltpu.VMEM((16, FIRST, BLOCK, BLOCK), jnp.bfloat16)
    half = (SMALL_ROWS, D // 2)
    return pl.pallas_call(
        scatter_kernel,
        out_shape=(
            jax.ShapeDtypeStruct((NSLOT, BLOCK, BLOCK), jnp.float32),
            jax.ShapeDtypeStruct((2, 16) + row.shape, jnp.float32),
            jax.ShapeDtypeStruct((2,) + half, jnp.float32),
        ),
        in_specs=[
            pl.BlockSpec(memory_space=pltpu.SMEM),
            pl.BlockSpec(memory_space=pl.ANY),
            vmem,
            vmem,
            pl.BlockSpec(memory_space=pl.ANY),
        ],
        out_specs=(vmem, vmem, vmem),
        scratch_shapes=[
            held,
            held,
            pltpu.VMEM(later.shape, later.dtype),
            pltpu.VMEM((NSLOT, BLOCK, BLOCK), jnp.float32),
        ]
        + Scatter.boxes_of(FIRST_SCATTER)
        + Scatter.boxes_of(LATER_PARTS, "z")
        + [pltpu.VMEM((6,) + half, jnp.float32), pltpu.VMEM((6,) + half, jnp.float32)]
        + [dma((16,)), dma((16,)), dma((16,)), dma((1,))]
        + Scatter.sems(FIRST_SCATTER)
        + Scatter.sems(LATER_PARTS, "z")
        + SmallSums.sems(),
        compiler_params=pltpu.CompilerParams(
            collective_id=2, has_side_effects=True, vmem_limit_bytes=58 * 2**20
        ),
    )(ranks, grads, row, io, later)


def swapped(index):
    return lax.rem(index, 4) * 4 + lax.div(index, 4)


def clip_peers(frame, fn):
    count = lax.axis_size("frame")

    def body(step, carry):
        peer = lax.rem(frame + step, count)
        fn(step, peer, (swapped(peer), lax.axis_index("rep")))
        return carry

    lax.fori_loop(1, count, body, 0)


def greet_clip(frame, where):
    barrier = pltpu.get_barrier_semaphore()
    clip_peers(
        frame,
        lambda step, peer, dev: pl.semaphore_signal(
            barrier, inc=1, device_id=dev, device_id_type=MESH
        ),
    )
    pl.semaphore_signal(barrier, inc=1, device_id=partner("x", *where), device_id_type=MESH)
    pl.semaphore_wait(barrier, lax.axis_size("frame"))


class Exchange:
    def __init__(self, src, dst, send, recv, frame):
        self.src, self.dst, self.send, self.recv, self.frame = src, dst, send, recv, frame

    @staticmethod
    def sems():
        return [pltpu.SemaphoreType.DMA((16,)), pltpu.SemaphoreType.DMA((16,))]

    def copy(self, peer):
        return pltpu.make_async_remote_copy(
            src_ref=self.src.at[peer],
            dst_ref=self.dst.at[self.frame],
            send_sem=self.send.at[peer],
            recv_sem=self.recv.at[self.frame],
            device_id=(swapped(jnp.int32(peer)), lax.axis_index("rep")),
            device_id_type=MESH,
        )

    def own(self):
        self.dst[self.frame] = self.src[self.frame]

    def start_all(self):
        clip_peers(self.frame, lambda step, peer, dev: self.copy(peer).start())
        self.own()

    def start(self, peer):
        pl.when(self.frame != peer)(lambda: self.copy(peer).start())
        pl.when(self.frame == peer)(self.own)

    def arrived(self, peer):
        def wait():
            pltpu.make_async_remote_copy(
                src_ref=self.src.at[peer],
                dst_ref=self.dst.at[peer],
                send_sem=self.send.at[peer],
                recv_sem=self.recv.at[peer],
                device_id=(swapped(jnp.int32(peer)), lax.axis_index("rep")),
                device_id_type=MESH,
            ).wait_recv()

        pl.when(self.frame != peer)(wait)

    def all_arrived(self):
        for peer in range(16):
            self.arrived(peer)

    def finish(self):
        for peer in range(16):
            pl.when(self.frame != peer)(lambda peer=peer: self.copy(peer).wait_send())


def spread_evenly(steps, slots, weights):
    total, taken, acc, runs = sum(weights), 0, 0, []
    for slot in range(slots):
        acc += weights[slot]
        upto = round(len(steps) * acc / total)
        runs.append(steps[taken:upto])
        taken = upto
    return runs


def forward_kernel(
    parts_ref, blocks_in, mine_ref, blocks_ref, olt_ref, full_ref, lse_ref, scores, low, *sems
):
    where = place()
    frame = swapped(lax.axis_index("frame"))
    qkv = Exchange(parts_ref, mine_ref, sems[0], sems[1], frame)
    back = Exchange(low, olt_ref, sems[2], sems[3], frame)
    gather_sems = sems[4:]
    greet_clip(frame, where)
    qkv.start_all()
    gather = Gather(LATER_PARTS, None, blocks_ref, gather_sems, where, FIRST + 1, "xy")
    ready = [key for key in gather.keys if key[1][:2] == (0, 0)]
    steps = [key for key in gather.keys if key not in ready]
    for key in ready:
        gather.step(key)
    frames = mine_ref.shape[0]
    runs = spread_evenly(steps, frames, FORWARD_WEIGHTS)
    for t in range(frames):
        for key in runs[t]:
            gather.step(key)
        qkv.arrived(t)
        low[t] = attend_frame(t, mine_ref, scores, full_ref, lse_ref)
        back.start(t)
    gather.finish()
    qkv.finish()
    back.all_arrived()
    back.finish()


FORWARD_WEIGHTS = (20,) + (5,) * 15


def forward_exchange(parts, blocks):
    frames = 16
    vmem = pl.BlockSpec(memory_space=pltpu.VMEM)
    return pl.pallas_call(
        forward_kernel,
        in_specs=[vmem, pl.BlockSpec(memory_space=pltpu.HBM)],
        out_specs=[vmem, pl.BlockSpec(memory_space=pltpu.HBM), vmem, vmem, vmem],
        input_output_aliases={1: 1},
        out_shape=[
            jax.ShapeDtypeStruct((frames,) + parts.shape[1:], jnp.bfloat16),
            jax.ShapeDtypeStruct(blocks.shape, blocks.dtype),
            jax.ShapeDtypeStruct((HEADS, HEAD_DIM, TOK), jnp.bfloat16),
            jax.ShapeDtypeStruct((frames, HEAD_DIM, TOK), jnp.float32),
            jax.ShapeDtypeStruct((frames, 1, TOK), jnp.float32),
        ],
        scratch_shapes=[
            pltpu.VMEM((frames, TOK, TOK), jnp.float32),
            pltpu.VMEM((frames, HEAD_DIM, TOK), jnp.bfloat16),
        ]
        + Exchange.sems()
        + Exchange.sems()
        + Gather.sems(LATER_PARTS),
        compiler_params=pltpu.CompilerParams(
            collective_id=3, has_side_effects=True, vmem_limit_bytes=56 * 2**20
        ),
    )(parts, blocks)


def backward_kernel(
    heads_ref, mine_ref, full_ref, lse_ref, cos_ref, sin_ref, g_ref, drt_ref, later_ref, *refs
):
    do, grads, dk, dv, acc, sib = refs[:6]
    boxes, sems = refs[6:8], refs[8:]
    where = place()
    frame = swapped(lax.axis_index("frame"))
    inward = Exchange(heads_ref, do, sems[0], sems[1], frame)
    outward = Exchange(grads, drt_ref, sems[2], sems[3], frame)
    csend, crecv, local, send = sems[4:8]
    halves = Halves(g_ref, FIRST, LATER, acc, sib, csend, crecv, local, where)

    def store(oz, row, value):
        later_ref[oz, row] = value.astype(jnp.bfloat16)

    scatter = Scatter(
        LATER_PARTS, acc, sib, boxes, send, sems[8:10], where, halves.ready, store, "xy"
    )
    greet_clip(frame, where)
    inward.start_all()
    halves.begin(scatter.seen)
    dk[...] = jnp.zeros_like(dk)
    dv[...] = jnp.zeros_like(dv)
    frames = mine_ref.shape[0]
    runs = spread_evenly(scatter.keys, frames + 1, BACKWARD_WEIGHTS)
    for i, t in enumerate(reversed(range(frames))):
        for key in runs[i]:
            scatter.step(key)
        inward.arrived(t)
        parts = attend_frame_back(t, mine_ref, do, full_ref, lse_ref, cos_ref, sin_ref, dk, dv)
        for kind in range(3):
            grads[t, kind] = parts[kind]
        outward.start(t)
    for key in runs[frames]:
        scatter.step(key)
    scatter.finish()
    halves.finish()
    inward.finish()
    outward.all_arrived()
    outward.finish()


BACKWARD_WEIGHTS = (40,) + (5,) * 15 + (10,)


def backward_exchange(heads, mine, full, lse, cos, sin, grads):
    frames = mine.shape[0]
    vmem = pl.BlockSpec(memory_space=pltpu.VMEM)
    dma = pltpu.SemaphoreType.DMA
    held = pltpu.VMEM((16, LATER, BLOCK, BLOCK), jnp.bfloat16)
    return pl.pallas_call(
        backward_kernel,
        in_specs=[vmem] * 6 + [pl.BlockSpec(memory_space=pltpu.HBM)],
        out_specs=[vmem, vmem],
        out_shape=[
            jax.ShapeDtypeStruct((HEADS,) + mine.shape[1:], jnp.bfloat16),
            jax.ShapeDtypeStruct((4, LATER, BLOCK, BLOCK), jnp.bfloat16),
        ],
        scratch_shapes=[
            pltpu.VMEM((frames, HEAD_DIM, TOK), jnp.bfloat16),
            pltpu.VMEM((frames, 3, HEAD_DIM, TOK), jnp.bfloat16),
            pltpu.VMEM((frames, HEAD_DIM, TOK), jnp.float32),
            pltpu.VMEM((frames, HEAD_DIM, TOK), jnp.float32),
            held,
            held,
        ]
        + Scatter.boxes_of(LATER_PARTS, "xy")
        + Exchange.sems()
        + Exchange.sems()
        + [dma((16,)), dma((16,)), dma((16,))]
        + Scatter.sems(LATER_PARTS, "xy"),
        compiler_params=pltpu.CompilerParams(
            collective_id=4, has_side_effects=True, vmem_limit_bytes=56 * 2**20
        ),
    )(heads, mine, full, lse, cos, sin, grads)


def late_gather_kernel(blocks_in, blocks_ref, *sems):
    where = place()
    greet(*where)
    gather = Gather(LATER_PARTS, None, blocks_ref, sems, where, FIRST + 1, "xy")
    for key in gather.keys:
        gather.step(key)
    gather.finish()


def late_gather(blocks):
    hbm = pl.BlockSpec(memory_space=pltpu.HBM)
    return pl.pallas_call(
        late_gather_kernel,
        in_specs=[hbm],
        out_specs=hbm,
        out_shape=jax.ShapeDtypeStruct(blocks.shape, blocks.dtype),
        scratch_shapes=Gather.sems(LATER_PARTS),
        input_output_aliases={0: 0},
        compiler_params=pltpu.CompilerParams(
            collective_id=5, has_side_effects=True, vmem_limit_bytes=56 * 2**20
        ),
    )(blocks)


def late_scatter_kernel(g_ref, later_ref, *refs):
    acc, sib, boxes, sems = refs[0], refs[1], refs[2:4], refs[4:]
    where = place()
    halves = Halves(g_ref, FIRST, LATER, acc, sib, sems[0], sems[1], sems[2], where)

    def store(oz, row, value):
        later_ref[oz, row] = value.astype(jnp.bfloat16)

    scatter = Scatter(
        LATER_PARTS, acc, sib, boxes, sems[3], sems[4:6], where, halves.ready, store, "xy"
    )
    greet(*where)
    halves.begin(scatter.seen)
    for key in scatter.keys:
        scatter.step(key)
    scatter.finish()
    halves.finish()


def late_scatter(grads):
    dma = pltpu.SemaphoreType.DMA
    held = pltpu.VMEM((16, LATER, BLOCK, BLOCK), jnp.bfloat16)
    return pl.pallas_call(
        late_scatter_kernel,
        in_specs=[pl.BlockSpec(memory_space=pltpu.HBM)],
        out_specs=pl.BlockSpec(memory_space=pltpu.VMEM),
        out_shape=jax.ShapeDtypeStruct((4, LATER, BLOCK, BLOCK), jnp.bfloat16),
        scratch_shapes=[held, held]
        + Scatter.boxes_of(LATER_PARTS, "xy")
        + [dma((16,)), dma((16,)), dma((16,))]
        + Scatter.sems(LATER_PARTS, "xy"),
        compiler_params=pltpu.CompilerParams(
            collective_id=6, has_side_effects=True, vmem_limit_bytes=56 * 2**20
        ),
    )(grads)


TILE = 512
LIMIT = pltpu.CompilerParams(vmem_limit_bytes=60 * 2**20)


def dotg(left, right, left_dim, right_dim):
    return lax.dot_general(
        left, right, (((left_dim,), (right_dim,)), ((), ())), preferred_element_type=jnp.float32
    )


def block_of(held, row, col):
    return held.at[
        pl.ds(pl.multiple_of(row * BLOCK, BLOCK), BLOCK),
        pl.ds(pl.multiple_of(col * BLOCK, BLOCK), BLOCK),
    ]


def move_tile(places, blocks, held, sem, start, across, row, rows, col, cols, outward=False):
    for r in range(rows):
        for c in range(cols):
            slot = blocks.at[places[start + (row + r) * across + col + c]]
            here = block_of(held, row + r, col + c)
            src, dst = (here, slot) if outward else (slot, here)
            pltpu.make_async_copy(src, dst, sem).start()


def settled(view, sem):
    pltpu.make_async_copy(view, view, sem).wait()


def column_sum(values):
    return jnp.sum(values, axis=0, keepdims=True)


def project_kernel(
    source, places, blocks, table_ref, io_ref, cos_ref, sin_ref,
    h0_ref, at_ref, out_ref, mod_ref, target_ref, xt_ref, scalars_ref,
    held, a_ref, data, flags, sems, small_sems,
):
    across = 3 * D // BLOCK
    per = TILE // BLOCK
    tiles = 3 * D // TILE
    mine = pltpu.make_async_copy(blocks.at[source[0] * (NSLOT + 1) + DATA], data, small_sems.at[0])
    mine.start()

    def flag(owner):
        return pltpu.make_async_copy(
            blocks.at[owner * (NSLOT + 1) + DATA, pl.ds(96, 16)], flags.at[owner], small_sems.at[1]
        )

    for owner in range(32):
        flag(owner).start()
    for j in range(tiles):
        move_tile(places, blocks, held, sems.at[j], 0, across, 0, D // BLOCK, j * per, per)
    mine.wait()
    settled(flags, small_sems.at[1])
    xt = data[0:32]
    xt_ref[...] = jnp.concatenate([xt.reshape(PIN, 2, BLOCK)[:, i] for i in range(2)], axis=1)
    noise = data[32:64].astype(jnp.float32) + data[64:96].astype(jnp.float32)
    target_ref[...] = jnp.concatenate([noise.reshape(PIN, 2, BLOCK)[:, i] for i in range(2)], axis=1)
    noised = data[96:97].astype(jnp.float32)
    level = data[112:113].astype(jnp.float32)
    total = flags[0].astype(jnp.float32)
    for owner in range(1, 32):
        total = total + flags[owner].astype(jnp.float32)
    total = jnp.maximum(total[0:1], 1.0)
    scalars_ref[0:1] = noised
    scalars_ref[1:2] = 1.0 / (total * (TOK * PIN))
    scalars_ref[2:3] = total
    scalars_ref[3:4] = level
    scalars_ref[4:8] = jnp.zeros((4, BLOCK), jnp.float32)
    rows = lax.broadcasted_iota(jnp.int32, (LEVELS, D), 0).astype(jnp.float32)
    picked = rows == level[0:1, 0:1]
    for i in range(8):
        mod_ref[i : i + 1] = column_sum(jnp.where(picked, table_ref[:, i * D : (i + 1) * D], 0.0))
    start = dotg(xt_ref[...], io_ref[0:PIN].astype(jnp.bfloat16), 0, 0) + io_ref[2 * PIN :]
    h0_ref[...] = start
    hat, _ = layer_norm(start)
    normed = hat * (1 + mod_ref[1:2]) + mod_ref[0:1]
    a_ref[...] = normed.astype(jnp.bfloat16)
    at_ref[...] = normed.T.astype(jnp.bfloat16)
    heads = TILE // HEAD_DIM
    half = HEAD_DIM // 2
    frame = swapped(lax.axis_index("frame"))
    c, s = cos_ref[frame], sin_ref[frame]
    for j in range(tiles):
        settled(held.at[:, pl.ds(j * TILE, TILE)], sems.at[j])
        r = matmul(a_ref[...], held[:, j * TILE : (j + 1) * TILE]).T
        kind, head = j // (D // TILE), j % (D // TILE) * heads
        for i in range(heads):
            own = r[i * HEAD_DIM : (i + 1) * HEAD_DIM]
            if kind < 2:
                first, second = own[:half], own[half:]
                own = jnp.concatenate(
                    [first * c - second * s, first * s + second * c], axis=0
                )
            out_ref[head + i, kind] = own.astype(jnp.bfloat16)


def project(source, places, blocks, table, io, cos, sin):
    vmem, smem = pl.BlockSpec(memory_space=pltpu.VMEM), pl.BlockSpec(memory_space=pltpu.SMEM)
    f32, bf16 = jnp.float32, jnp.bfloat16
    return pl.pallas_call(
        project_kernel,
        in_specs=[smem, smem, pl.BlockSpec(memory_space=pltpu.HBM)] + [vmem] * 4,
        out_specs=[vmem] * 7,
        out_shape=[
            jax.ShapeDtypeStruct((TOK, D), f32),
            jax.ShapeDtypeStruct((D, TOK), bf16),
            jax.ShapeDtypeStruct((HEADS, 3, HEAD_DIM, TOK), bf16),
            jax.ShapeDtypeStruct((8, D), f32),
            jax.ShapeDtypeStruct((PIN, TOK), f32),
            jax.ShapeDtypeStruct((PIN, TOK), bf16),
            jax.ShapeDtypeStruct((8, BLOCK), f32),
        ],
        scratch_shapes=[
            pltpu.VMEM((D, 3 * D), bf16),
            pltpu.VMEM((TOK, D), bf16),
            pltpu.VMEM((BLOCK, BLOCK), bf16),
            pltpu.VMEM((32, 16, BLOCK), bf16),
            pltpu.SemaphoreType.DMA((3 * D // TILE,)),
            pltpu.SemaphoreType.DMA((2,)),
        ],
        compiler_params=LIMIT,
    )(source, places, blocks, table, io, cos, sin)


GELU_A = math.sqrt(2.0 / math.pi)
GELU_B = 0.044715


def middle_kernel(
    places, slots, blocks, olt_ref, h0_ref, mod_ref, io_ref, target_ref, scalars_ref,
    dot_ref, grads_ref, dh1_ref, dhead_ref, dmod_ref, loss_ref,
    wo, wup, wdown, gout, gup, gdown, slope, act, bt, dz_ref, db_ref, h1_ref, y_ref, z_ref, sems, out_sems,
):
    starts, _ = matrix_starts()
    per = TILE // BLOCK
    wide = D // BLOCK
    up_tiles = FFN // TILE
    up_across = FFN // BLOCK

    def fetch_up(j):
        move_tile(places, blocks, wup, sems.at[1 + j], starts[2], up_across, 0, wide, j * per, per)

    def fetch_down(j):
        move_tile(places, blocks, wdown, sems.at[9 + j], starts[3], wide, j * per, per, 0, wide)

    move_tile(places, blocks, wo, sems.at[0], starts[1], wide, 0, wide, 0, wide)
    fetch_up(0)
    fetch_up(1)
    attended = olt_ref[...].astype(jnp.float32).T.astype(jnp.bfloat16)
    settled(wo, sems.at[0])
    y = matmul(attended, wo[...])
    y_ref[...] = y
    h1 = h0_ref[...] + mod_ref[2:3] * y
    h1_ref[...] = h1
    hat_two, _ = layer_norm(h1)
    b32 = hat_two * (1 + mod_ref[4:5]) + mod_ref[3:4]
    bt[...] = b32.T.astype(jnp.bfloat16)
    b = b32.astype(jnp.bfloat16)
    dz_ref[...] = b

    def rise(j, carry):
        col = pl.multiple_of(j * TILE, TILE)
        settled(wup.at[:, pl.ds(col, TILE)], sems.at[1 + j])
        fetch_down(j)
        pl.when(j < up_tiles - 2)(lambda: fetch_up(j + 2))
        u = matmul(dz_ref[...], wup[:, pl.ds(col, TILE)])
        square = u * u
        t = jnp.tanh(GELU_A * (u + GELU_B * (square * u)))
        cdf = 0.5 * (1.0 + t)
        act[:, pl.ds(col, TILE)] = (u * cdf).astype(jnp.bfloat16)
        slope[:, pl.ds(col, TILE)] = cdf + (0.5 * GELU_A) * u * (1.0 - t * t) * (
            1.0 + (3.0 * GELU_B) * square
        )
        return carry

    lax.fori_loop(0, up_tiles, rise, 0)
    for j in range(up_tiles):
        settled(wdown.at[pl.ds(j * TILE, TILE)], sems.at[9 + j])

    def fall(j, carry):
        col = pl.multiple_of(j * 256, 256)
        z_ref[:, pl.ds(col, 256)] = matmul(act[...], wdown[:, pl.ds(col, 256)])
        return carry

    lax.fori_loop(0, D // 256, fall, 0)
    z = z_ref[...]
    h2 = h1_ref[...] + mod_ref[5:6] * z
    hat_three, inv_three = layer_norm(h2)
    c = (hat_three * (1 + mod_ref[7:8]) + mod_ref[6:7]).astype(jnp.bfloat16)
    noised, inv_scale = scalars_ref[0:1, 0:1], scalars_ref[1:2, 0:1]
    head = io_ref[PIN : 2 * PIN].astype(jnp.bfloat16)
    difference = dotg(head, c, 1, 1) - target_ref[...]
    loss_ref[...] = jnp.full((1, BLOCK), 1.0, jnp.float32) * (
        jnp.sum(jnp.sum(difference * difference, axis=0, keepdims=True), axis=1, keepdims=True)
        * (noised * inv_scale)
    )
    dpred = (2.0 * inv_scale * noised * difference).astype(jnp.bfloat16)
    dhead_ref[...] = matmul(dpred, c)
    dc = dotg(dpred, head, 0, 0)
    dmod_ref[6:7] = column_sum(dc)
    dmod_ref[7:8] = column_sum(dc * hat_three)
    dh2 = norm_back(dc * (1 + mod_ref[7:8]), hat_three, inv_three)
    dmod_ref[5:6] = column_sum(dh2 * z)
    dz_ref[...] = (dh2 * mod_ref[5:6]).astype(jnp.bfloat16)
    z_ref[...] = dh2
    db_ref[...] = jnp.zeros_like(db_ref)

    def back(j, carry):
        col = pl.multiple_of(j * TILE, TILE)
        du = (
            slope[:, pl.ds(col, TILE)] * dotg(dz_ref[...], wdown[pl.ds(col, TILE)], 1, 1)
        ).astype(jnp.bfloat16)
        gdown[pl.ds(col, TILE)] = dotg(act[:, pl.ds(col, TILE)], dz_ref[...], 0, 0).astype(
            jnp.bfloat16
        )
        move_tile(
            slots, grads_ref, gdown, out_sems.at[0], starts[3], wide, j * per, per, 0, wide, True
        )
        gup[:, pl.ds(col, TILE)] = matmul(bt[...], du).astype(jnp.bfloat16)
        move_tile(
            slots, grads_ref, gup, out_sems.at[1], starts[2], up_across, 0, wide, j * per, per, True
        )
        db_ref[...] += dotg(du, wup[:, pl.ds(col, TILE)], 1, 1)
        return carry

    lax.fori_loop(0, up_tiles, back, 0)
    hat_two, inv_two = layer_norm(h1_ref[...])
    db = db_ref[...]
    dmod_ref[3:4] = column_sum(db)
    dmod_ref[4:5] = column_sum(db * hat_two)
    dh1 = z_ref[...] + norm_back(db * (1 + mod_ref[4:5]), hat_two, inv_two)
    dh1_ref[...] = dh1
    dmod_ref[2:3] = column_sum(dh1 * y_ref[...])
    dmod_ref[0:2] = jnp.zeros((2, D), jnp.float32)
    dz_ref[...] = (dh1 * mod_ref[2:3]).astype(jnp.bfloat16)
    gout[...] = matmul(olt_ref[...], dz_ref[...]).astype(jnp.bfloat16)
    move_tile(slots, grads_ref, gout, out_sems.at[2], starts[1], wide, 0, wide, 0, wide, True)
    for j in range(D // TILE):
        rows = pl.ds(j * TILE, TILE)
        dot_ref[rows] = dotg(wo[rows], dz_ref[...], 1, 1).astype(jnp.bfloat16)
    settled(gdown, out_sems.at[0])
    settled(gup, out_sems.at[1])
    settled(gout, out_sems.at[2])


def middle(places, slots, blocks, olt, h0, mod, io, target, scalars):
    vmem, smem = pl.BlockSpec(memory_space=pltpu.VMEM), pl.BlockSpec(memory_space=pltpu.SMEM)
    hbm = pl.BlockSpec(memory_space=pltpu.HBM)
    f32, bf16 = jnp.float32, jnp.bfloat16
    up, down, square = pltpu.VMEM((D, FFN), bf16), pltpu.VMEM((FFN, D), bf16), pltpu.VMEM((D, D), bf16)
    rows = pltpu.VMEM((TOK, D), f32)
    return pl.pallas_call(
        middle_kernel,
        in_specs=[smem, smem, hbm] + [vmem] * 6,
        out_specs=[vmem, hbm] + [vmem] * 4,
        out_shape=[
            jax.ShapeDtypeStruct((D, TOK), bf16),
            jax.ShapeDtypeStruct((32 * NSLOT, BLOCK, BLOCK), bf16),
            jax.ShapeDtypeStruct((TOK, D), f32),
            jax.ShapeDtypeStruct((PIN, D), f32),
            jax.ShapeDtypeStruct((8, D), f32),
            jax.ShapeDtypeStruct((1, BLOCK), f32),
        ],
        scratch_shapes=[square, up, down, square, up, down]
        + [
            pltpu.VMEM((TOK, FFN), f32),
            pltpu.VMEM((TOK, FFN), bf16),
            pltpu.VMEM((D, TOK), bf16),
            pltpu.VMEM((TOK, D), bf16),
            rows,
            rows,
            rows,
            rows,
            pltpu.SemaphoreType.DMA((17,)),
            pltpu.SemaphoreType.DMA((3,)),
        ],
        compiler_params=LIMIT,
    )(places, slots, blocks, olt, h0, mod, io, target, scalars)


def final_kernel(
    places, slots, blocks, drt_ref, at_ref, h0_ref, mod_ref, dh1_ref, xt_ref, dmod_in, scalars_ref, loss_ref,
    dhead_ref, grads_in, grads_ref, row_ref, io_ref, held, gqkv, flat, sems, out_sem,
):
    across = 3 * D // BLOCK
    per = TILE // BLOCK
    for j in range(2):
        move_tile(places, blocks, held, sems.at[j], 0, across, j * per, per, 0, across)
    for kind in range(3):
        for head in range(HEADS):
            row = kind * D + head * HEAD_DIM
            flat[row : row + HEAD_DIM] = drt_ref[head, kind]
    for j in range(3 * D // TILE):
        cols = slice(j * TILE, (j + 1) * TILE)
        gqkv[:, cols] = dotg(at_ref[...], flat[cols], 1, 1).astype(jnp.bfloat16)
        move_tile(slots, grads_ref, gqkv, out_sem.at[0], 0, across, 0, D // BLOCK, j * per, per, True)
    for j in range(2):
        settled(held.at[pl.ds(j * TILE, TILE)], sems.at[j])
    da = matmul(held[...], flat[...]).T
    hat, inverse = layer_norm(h0_ref[...])

    def put_row(i, values):
        for k in range(D // BLOCK):
            row_ref[i * (D // BLOCK) + k : i * (D // BLOCK) + k + 1] = values[
                :, k * BLOCK : (k + 1) * BLOCK
            ]

    put_row(0, column_sum(da))
    put_row(1, column_sum(da * hat))
    for i in range(2, 8):
        put_row(i, dmod_in[i : i + 1])
    row_ref[64:68] = jnp.broadcast_to(scalars_ref[3:4], (4, BLOCK))
    row_ref[68:72] = jnp.broadcast_to(loss_ref[...], (4, BLOCK))
    dh0 = (dh1_ref[...] + norm_back(da * (1 + mod_ref[1:2]), hat, inverse)).astype(jnp.bfloat16)
    dembed = matmul(xt_ref[...], dh0)
    dbias = column_sum(dh0.astype(jnp.float32))
    for i in range(2):
        cols = slice(i * D // 2, (i + 1) * D // 2)
        io_ref[i, 0:PIN] = dembed[:, cols]
        io_ref[i, PIN : 2 * PIN] = dhead_ref[:, cols]
        io_ref[i, 2 * PIN :] = jnp.zeros((SMALL_ROWS - 2 * PIN, D // 2), jnp.float32)
        io_ref[i, 2 * PIN : 2 * PIN + 1] = dbias[:, cols]
    settled(gqkv, out_sem.at[0])


def final(places, slots, blocks, drt, at, h0, mod, dh1, xt, dmod, scalars, loss, dhead, grads):
    vmem, smem = pl.BlockSpec(memory_space=pltpu.VMEM), pl.BlockSpec(memory_space=pltpu.SMEM)
    hbm = pl.BlockSpec(memory_space=pltpu.HBM)
    f32, bf16 = jnp.float32, jnp.bfloat16
    return pl.pallas_call(
        final_kernel,
        in_specs=[smem, smem, hbm] + [vmem] * 10 + [hbm],
        out_specs=[hbm] + [vmem] * 2,
        out_shape=[
            jax.ShapeDtypeStruct(grads.shape, grads.dtype),
            jax.ShapeDtypeStruct((8 * D // BLOCK + 8, BLOCK), f32),
            jax.ShapeDtypeStruct((2, SMALL_ROWS, D // 2), f32),
        ],
        scratch_shapes=[
            pltpu.VMEM((D, 3 * D), bf16),
            pltpu.VMEM((D, 3 * D), bf16),
            pltpu.VMEM((3 * D, TOK), bf16),
            pltpu.SemaphoreType.DMA((2,)),
            pltpu.SemaphoreType.DMA((1,)),
        ],
        input_output_aliases={13: 0},
        compiler_params=LIMIT,
    )(places, slots, blocks, drt, at, h0, mod, dh1, xt, dmod, scalars, loss, dhead, grads)


def top_dot(left, right, left_dim, right_dim):
    return lax.dot_general(
        left,
        right,
        (((left_dim,), (right_dim,)), ((), ())),
        precision=TOP_PRECISION,
        preferred_element_type=jnp.float32,
    )


SHAMPOO_BLOCKS = 4


def halves_of(values):
    high = values.astype(jnp.bfloat16)
    return high, (values - high.astype(jnp.float32)).astype(jnp.bfloat16)


def fine_dot(left, right):
    (lh, ll), (rh, rl) = left, right
    return (
        matmul(jnp.concatenate([lh, ll], axis=1), jnp.concatenate([rh, rh], axis=0))
        + matmul(lh, rl)
    )


def shampoo_kernel(
    g_ref, w_ref, ema_ref, left_ref, right_ref, root_left, root_right,
    grad_out, w_out, left_out, right_out, ema_out,
):
    limit = CLIP_NORM * BLOCK * NPARAMS ** (-0.5)

    def whole(values):
        return jnp.sum(jnp.sum(values, axis=0, keepdims=True), axis=1, keepdims=True)

    for i in range(SHAMPOO_BLOCKS):
        g = g_ref[i]
        g = g * (limit / jnp.maximum(jnp.sqrt(whole(g * g)), limit))
        grad_out[i] = g
        mine, turned = halves_of(g), halves_of(g.T)
        left_out[i] = STAT_BETA * left_ref[i] + (1 - STAT_BETA) * fine_dot(mine, turned)
        right_out[i] = STAT_BETA * right_ref[i] + (1 - STAT_BETA) * fine_dot(turned, mine)
        p = fine_dot(halves_of(root_left[i]), mine)
        p = fine_dot(halves_of(p), halves_of(root_right[i]))
        p = p * lax.rsqrt(whole(p * p) * (1.0 / (BLOCK * BLOCK)) + 1e-06)
        w = w_ref[i]
        w = w - SHAMPOO_RATE * (p + DECAY_RATE * w)
        w_out[i] = w
        ema_out[i] = EMA_DECAY * ema_ref[i] + (1 - EMA_DECAY) * w


def shampoo_blocks(*arrays):
    spec = pl.BlockSpec((SHAMPOO_BLOCKS, BLOCK, BLOCK), lambda i: (i, 0, 0))
    shape = jax.ShapeDtypeStruct(arrays[0].shape, jnp.float32)
    return pl.pallas_call(
        shampoo_kernel,
        grid=(arrays[0].shape[0] // SHAMPOO_BLOCKS,),
        in_specs=[spec] * 7,
        out_specs=[spec] * 5,
        out_shape=[shape] * 5,
        compiler_params=LIMIT,
    )(*arrays)


def adam_kernel(
    fade, rows_in, gio_in, scalars_ref, table_in, mom_in, var_in, ema_in, io, io_mom, io_var, io_ema,
    table_out, mom_out, var_out, ema_out, io_out, io_mom_out, io_var_out, io_ema_out, norm_out, loss_out, count_out,
    grad, flat, rows_ref, gio_ref, table, mom, var, ema, sems,
):
    loads = [
        pltpu.make_async_copy(src, dst, sems.at[i])
        for i, (src, dst) in enumerate(
            (
                (rows_in, rows_ref),
                (gio_in, gio_ref),
                (table_in, table),
                (mom_in, mom),
                (var_in, var),
                (ema_in, ema),
            )
        )
    ]
    for load in loads:
        load.start()
    for load in loads[:2]:
        load.wait()
    level = rows_ref[:, 64, :]
    frames = level.shape[0]
    picks = (
        level[:, 0:1] == lax.broadcasted_iota(jnp.int32, (frames, LEVELS), 1).astype(jnp.float32)
    ).astype(jnp.float32)
    for i in range(8 * D // BLOCK):
        flat[:, i * BLOCK : (i + 1) * BLOCK] = rows_ref[:, i, :]
    square = jnp.zeros((LEVELS, D), jnp.float32)
    for i in range(8):
        part = top_dot(picks, flat[:, i * D : (i + 1) * D], 0, 0)
        grad[:, i * D : (i + 1) * D] = part
        square = square + part * part
    gio = jnp.concatenate([gio_ref[0, 0 : 2 * PIN + 1], gio_ref[1, 0 : 2 * PIN + 1]], axis=1)

    def whole(values):
        return jnp.sum(jnp.sum(values, axis=0, keepdims=True), axis=1, keepdims=True)

    norm = jnp.sqrt(whole(square) + whole(gio * gio))
    factor = CLIP_NORM / jnp.maximum(norm, CLIP_NORM)
    count = scalars_ref[2:3, 0:1]
    norm_out[...] = norm
    loss_out[...] = jnp.sum(rows_ref[:, 68, :], axis=0, keepdims=True)[:, 0:1] * count
    count_out[...] = count
    fade_one, fade_two = fade[0], fade[1]

    def update(g, weight, first, second, average):
        new_first = BETA_ONE * first + (1 - BETA_ONE) * g
        new_second = BETA_TWO * second + (1 - BETA_TWO) * g * g
        new = weight - ADAM_RATE * (
            (new_first / fade_one) / (jnp.sqrt(new_second / fade_two) + ADAM_EPS)
            + DECAY_RATE * weight
        )
        return new, new_first, new_second, EMA_DECAY * average + (1 - EMA_DECAY) * new

    outs = (io_out, io_mom_out, io_var_out, io_ema_out)
    for ref, value in zip(outs, update(gio * factor, io[...], io_mom[...], io_var[...], io_ema[...])):
        ref[...] = value
    outs = (table_out, mom_out, var_out, ema_out)
    for load in loads[2:]:
        load.wait()

    def one(i, carry):
        cols = pl.ds(pl.multiple_of(i * D, D), D)
        values = update(grad[:, cols] * factor, table[:, cols], mom[:, cols], var[:, cols], ema[:, cols])
        for ref, value in zip(outs, values):
            ref[:, cols] = value
        return carry

    lax.fori_loop(0, 8, one, 0)


def adam(fade, rows, gio, scalars, *arrays):
    vmem, smem = pl.BlockSpec(memory_space=pltpu.VMEM), pl.BlockSpec(memory_space=pltpu.SMEM)
    return pl.pallas_call(
        adam_kernel,
        in_specs=[smem]
        + [pl.BlockSpec(memory_space=pl.ANY)] * 2
        + [vmem]
        + [pl.BlockSpec(memory_space=pl.ANY)] * 4
        + [vmem] * 4,
        out_specs=[vmem] * 11,
        out_shape=[jax.ShapeDtypeStruct(a.shape, jnp.float32) for a in arrays]
        + [jax.ShapeDtypeStruct((1, 1), jnp.float32)] * 3,
        scratch_shapes=[
            pltpu.VMEM((LEVELS, 8 * D), jnp.float32),
            pltpu.VMEM((rows.shape[0], 8 * D), jnp.float32),
            pltpu.VMEM(rows.shape, jnp.float32),
            pltpu.VMEM(gio.shape, jnp.float32),
        ]
        + [pltpu.VMEM((LEVELS, 8 * D), jnp.float32)] * 4
        + [pltpu.SemaphoreType.DMA((6,))],
        compiler_params=pltpu.CompilerParams(vmem_limit_bytes=56 * 2**20),
    )(fade, rows, gio, scalars, *arrays)


def matrix_starts():
    starts, total = [], 0
    for rows_in, cols_in in matrix_shapes():
        starts.append(total)
        total += rows_in // BLOCK * (cols_in // BLOCK)
    return starts, total


def block_places(block_slot):
    owned = block_slot.reshape(32, -1)
    ranks = jnp.sum((owned[:, None, :] < owned[:, :, None]).astype(jnp.int32), axis=2)
    mine = lax.axis_index("frame") * 2 + lax.axis_index("rep")
    own_ranks = lax.dynamic_index_in_dim(ranks, mine, 0, keepdims=False)
    counting = jnp.arange(NSLOT, dtype=jnp.int32)
    perm = jnp.sum(jnp.where(own_ranks[None, :] == counting[:, None], counting[None, :], 0), axis=1)
    owners = jnp.arange(32, dtype=jnp.int32)[:, None]
    gathered = owners * (NSLOT + 1) + ranks + (ranks >= FIRST).astype(jnp.int32)
    scattered = owners * NSLOT + ranks
    natural = jnp.arange(block_slot.shape[0], dtype=jnp.int32)
    same = block_slot[None, :] == natural[:, None]
    places = jnp.sum(jnp.where(same, gathered.reshape(1, -1), 0), axis=1)
    slots = jnp.sum(jnp.where(same, scattered.reshape(1, -1), 0), axis=1)
    early = jnp.sum((owned < matrix_starts()[0][1]).astype(jnp.int32), axis=1)
    return own_ranks, perm, places, slots, jnp.max(early) > FIRST


def rope_columns(frames):
    pairs = HEAD_DIM // 2
    time_pairs = pairs // 4
    row_pairs = (pairs - time_pairs) // 2
    column_pairs = pairs - time_pairs - row_pairs
    token = np.arange(GRID * GRID)
    groups = (
        (time_pairs, np.arange(frames)[:, None, None]),
        (row_pairs, (token // GRID)[None, None, :]),
        (column_pairs, (token % GRID)[None, None, :]),
    )
    angles = [
        np.broadcast_to(
            pos * (ROPE_BASE ** (-np.arange(n) / n))[None, :, None], (frames, n, GRID * GRID)
        )
        for n, pos in groups
    ]
    angles = np.concatenate(angles, axis=1)
    return np.cos(angles).astype(np.float32), np.sin(angles).astype(np.float32)


def on_grid(
    clean,
    noise,
    levels,
    flags,
    frame_map,
    block_slot,
    step_count,
    mat_weight,
    mat_ema,
    stat_left,
    stat_right,
    root_left,
    root_right,
    mod_table,
    mod_mom,
    mod_var,
    mod_ema,
    io_weight,
    io_mom,
    io_var,
    io_ema,
):
    tok_frame = GRID * GRID
    my_time, my_clip = swapped(lax.axis_index("frame")), lax.axis_index("rep")
    level_here = levels[0, 0] * (1 - flags[0, 0])
    noised_here = (1 - flags[0, 0]).astype(jnp.float32)
    fraction = level_here.astype(jnp.float32) / LEVELS
    frames_in = (
        jnp.cos(0.5 * jnp.pi * fraction) * clean[0, 0] + jnp.sin(0.5 * jnp.pi * fraction) * noise[0, 0]
    )
    noise_high = noise[0, 0].astype(jnp.bfloat16)
    noise_low = (noise[0, 0] - noise_high.astype(jnp.float32)).astype(jnp.bfloat16)
    data = jnp.concatenate(
        [
            frames_in.astype(jnp.bfloat16).reshape(-1, BLOCK),
            noise_high.reshape(-1, BLOCK),
            noise_low.reshape(-1, BLOCK),
            jnp.full((16, BLOCK), noised_here.astype(jnp.bfloat16)),
            jnp.full((16, BLOCK), level_here.astype(jnp.bfloat16)),
        ]
    )
    ranks, perm, places, slots, spills = block_places(block_slot)
    clip_map = lax.dynamic_index_in_dim(frame_map, my_clip, 0, keepdims=False)
    my_slot = jnp.sum(
        jnp.where(clip_map == my_time, jnp.arange(clip_map.shape[0], dtype=jnp.int32), 0)
    )
    source = (my_slot * 2 + my_clip).reshape(1)
    cosine, sine = rope_columns(frame_map.shape[1])
    gathered = gather_weights(perm, mat_weight, data)
    gathered = lax.cond(spills, lambda: late_gather(gathered), lambda: gathered)
    start, normed, parts, modulation, targets, inputs, scalars = project(
        source,
        places,
        gathered.reshape(-1, BLOCK, BLOCK),
        mod_table,
        io_weight,
        cosine,
        sine,
    )
    mine, gathered, attended, full, lse = forward_exchange(parts, gathered)
    blocks = gathered.reshape(-1, BLOCK, BLOCK)
    grad_heads, grad_blocks, grad_middle, grad_head, grad_mod, loss_part = middle(
        places,
        slots,
        blocks,
        attended.reshape(D, tok_frame),
        start,
        modulation,
        io_weight,
        targets,
        scalars,
    )
    grad_proj, later = backward_exchange(
        grad_heads.reshape(HEADS, HEAD_DIM, tok_frame),
        mine,
        full,
        lse,
        cosine,
        sine,
        grad_blocks.reshape(32, NSLOT, BLOCK, BLOCK),
    )
    grad_blocks, row, grad_io = final(
        places,
        slots,
        blocks,
        grad_proj,
        normed,
        start,
        modulation,
        grad_middle,
        inputs,
        grad_mod,
        scalars,
        loss_part,
        grad_head,
        grad_blocks,
    )
    grad_blocks = grad_blocks.reshape(32, NSLOT, BLOCK, BLOCK)
    later = lax.cond(spills, lambda: late_scatter(grad_blocks), lambda: later)
    owned, rows, grad_io = scatter_grads(ranks, grad_blocks, row, grad_io, later)
    step = step_count[0].astype(jnp.float32)
    new_small = adam(
        jnp.stack([1 - BETA_ONE**step, 1 - BETA_TWO**step]),
        rows.reshape(32, -1, BLOCK),
        grad_io,
        scalars,
        mod_table,
        mod_mom,
        mod_var,
        mod_ema,
        io_weight,
        io_mom,
        io_var,
        io_ema,
    )
    new_mod, new_io = new_small[:4], new_small[4:8]
    grad_norm, loss_sum, noised_total = (value.reshape(()) for value in new_small[8:])
    mat_grad, new_mat_weight, new_stat_left, new_stat_right, new_mat_ema = shampoo_blocks(
        owned, mat_weight, mat_ema, stat_left, stat_right, root_left, root_right
    )
    return (
        loss_sum,
        noised_total,
        grad_norm,
        mat_grad,
        new_mat_weight,
        new_stat_left,
        new_stat_right,
        new_mat_ema,
        new_mod[0],
        new_mod[1],
        new_mod[2],
        new_mod[3],
        new_io[0],
        new_io[1],
        new_io[2],
        new_io[3],
    )


def solution(mesh):
    tuned = dict(mesh.shape) == {"frame": 16, "rep": 2}
    body = on_grid if tuned else on_device
    in_specs = (
        P("rep", "frame", None, None),
        P("rep", "frame", None, None),
        P("rep", "frame"),
        P("rep", "frame"),
        P(),
        P(),
        P(),
        P(("frame", "rep"), None, None),
        P(("frame", "rep"), None, None),
        P(("frame", "rep"), None, None),
        P(("frame", "rep"), None, None),
        P(("frame", "rep"), None, None),
        P(("frame", "rep"), None, None),
        P(),
        P(),
        P(),
        P(),
        P(),
        P(),
        P(),
        P(),
    )
    out_specs = (
        P(),
        P(),
        P(),
        P(("frame", "rep"), None, None),
        P(("frame", "rep"), None, None),
        P(("frame", "rep"), None, None),
        P(("frame", "rep"), None, None),
        P(("frame", "rep"), None, None),
        P(),
        P(),
        P(),
        P(),
        P(),
        P(),
        P(),
        P(),
    )
    return jax.shard_map(
        body, mesh=mesh, in_specs=in_specs, out_specs=out_specs, check_vma=False
    )
```
